32 devices in a mesh: fsdp: 8 (over y, x, core), seq: 4 (over z).
Axes of the slice: x: 2, y: 2, z: 4, core: 2. Of those that a mesh axis runs over, the one named last changes fastest.
Arguments:
- tokens: bfloat16 [8192, 1536], P(('fsdp', 'seq')), may hold values from -6 to 6
- cotangent: bfloat16 [8192, 1536], P(('fsdp', 'seq')), may hold values from -6 to 6
- lengths: int32 [8, 2], P('fsdp'), may hold values from 0 to 1024, as said below
- w_qkv: float32 [2, 1536, 3072], P(None, ('fsdp', 'seq')), may hold values from -0.15625 to 0.15625
- w_out: float32 [2, 1536, 1536], P(None, ('fsdp', 'seq')), may hold values from -0.625 to 0.625
- w_gateup: float32 [2, 1536, 8192], P(None, ('fsdp', 'seq')), may hold values from -0.15625 to 0.15625
- w_down: float32 [2, 4096, 1536], P(None, ('fsdp', 'seq')), may hold values from -0.09375 to 0.09375
- norm_gains: float32 [2, 2, 1536], P(None, None, ('fsdp', 'seq')), may hold values from 0.5 to 1.5
- first_qkv: float32 [2, 1536, 3072], P(None, ('fsdp', 'seq')), may hold values from -64 to 64
- first_out: float32 [2, 1536, 1536], P(None, ('fsdp', 'seq')), may hold values from -64 to 64
- first_gateup: float32 [2, 1536, 8192], P(None, ('fsdp', 'seq')), may hold values from -64 to 64
- first_down: float32 [2, 4096, 1536], P(None, ('fsdp', 'seq')), may hold values from -64 to 64
- first_gains: float32 [2, 2, 1536], P(None, None, ('fsdp', 'seq')), may hold values from -64 to 64
- second_qkv: float32 [2, 1536, 3072], P(None, ('fsdp', 'seq')), may hold values from 81.92 to 819.2
- second_out: float32 [2, 1536, 1536], P(None, ('fsdp', 'seq')), may hold values from 81.92 to 819.2
- second_gateup: float32 [2, 1536, 8192], P(None, ('fsdp', 'seq')), may hold values from 81.92 to 819.2
- second_down: float32 [2, 4096, 1536], P(None, ('fsdp', 'seq')), may hold values from 81.92 to 819.2
- second_gains: float32 [2, 2, 1536], P(None, None, ('fsdp', 'seq')), may hold values from 81.92 to 819.2
Outputs:
- layer_output: bfloat16 [8192, 1536], P(('fsdp', 'seq'))
- input_grad: float32 [8192, 1536], P(('fsdp', 'seq'))
- new_qkv: float32 [2, 1536, 3072], P(None, ('fsdp', 'seq'))
- new_out: float32 [2, 1536, 1536], P(None, ('fsdp', 'seq'))
- new_gateup: float32 [2, 1536, 8192], P(None, ('fsdp', 'seq'))
- new_down: float32 [2, 4096, 1536], P(None, ('fsdp', 'seq'))
- new_gains: float32 [2, 2, 1536], P(None, None, ('fsdp', 'seq'))
- first_qkv_out: float32 [2, 1536, 3072], P(None, ('fsdp', 'seq'))
- first_out_out: float32 [2, 1536, 1536], P(None, ('fsdp', 'seq'))
- first_gateup_out: float32 [2, 1536, 8192], P(None, ('fsdp', 'seq'))
- first_down_out: float32 [2, 4096, 1536], P(None, ('fsdp', 'seq'))
- first_gains_out: float32 [2, 2, 1536], P(None, None, ('fsdp', 'seq'))
- second_qkv_out: float32 [2, 1536, 3072], P(None, ('fsdp', 'seq'))
- second_out_out: float32 [2, 1536, 1536], P(None, ('fsdp', 'seq'))
- second_gateup_out: float32 [2, 1536, 8192], P(None, ('fsdp', 'seq'))
- second_down_out: float32 [2, 4096, 1536], P(None, ('fsdp', 'seq'))
- second_gains_out: float32 [2, 2, 1536], P(None, None, ('fsdp', 'seq'))
The draws below stay inside these ranges and needn't reach their ends.
Inputs may be any that keep to these rules, and one draw needn't show every extreme that they name: `lengths`: row f holds the length of group f's sequence, 1024 to 1024 tokens, then the rest of the group's 1024 tokens, which form a segment of their own; the rows sum to 1024, and in some group the sequence fills all 1024 tokens.
All inputs are finite; a program needn't handle non-finite values.
Results may differ from the reference program's by a relative error of at most 0.019.
Values may be sent and summed in bfloat16 or wider, within the bound.
A program may use at most 512 MiB of HBM per device.

```python
import math
import jax
import jax.numpy as jnp
from jax import lax

D = 1536
QUERY_HEAD_COUNT = 16
KEY_VALUE_HEADS = 8
HEAD_SIZE = 96
FF = 4096
LAYERS = 2
SHORTEST = 1024
STEP = 6
TOK_DEV = 256
GROUP_TOKENS = 1024
TOTAL_TOKENS = 8192
QKV = 3072
N_FSDP = 8


def draw_lengths(key, part):
    key = jax.random.fold_in(key, 7)
    length_key, full_key = jax.random.split(key)
    least_len = max(min(SHORTEST, GROUP_TOKENS), GROUP_TOKENS - TOK_DEV + 1)
    first = jax.random.randint(length_key, (N_FSDP,), least_len, GROUP_TOKENS + 1, dtype=jnp.int32)
    full_group = jax.random.randint(full_key, (), 0, N_FSDP, dtype=jnp.int32)
    first = jnp.where(jnp.arange(N_FSDP, dtype=jnp.int32) == full_group, GROUP_TOKENS, first)
    return jnp.stack([first, GROUP_TOKENS - first], axis=1)


def level_of(own_key, shape, cuts, least, top_value):
    factor_of, own = 1.0, jax.random.fold_in(own_key, 6)
    for position, blocks in cuts:
        draws = jnp.exp(jax.random.uniform(jax.random.fold_in(own, position), (blocks,), jnp.float32, least / len(cuts), top_value / len(cuts)))
        factor_of = factor_of * jnp.repeat(draws, shape[position] // blocks).reshape([-1 if axis == position else 1 for axis in range(len(shape))])
    return factor_of


def centred(stream_key, dims, deviation, reach, cuts=(), held_as=jnp.bfloat16):
    values = jax.random.normal(stream_key, dims, jnp.float32) * deviation
    if len(cuts) > 0:
        values = level_of(stream_key, dims, cuts, -0.22, 0.18) * values
    return jnp.clip(values, min=-reach, max=reach).astype(held_as)


def setup_inputs(seed: int = 0) -> dict:
    seeds = jax.random.split(jax.random.key(seed), 19)
    return {
        "tokens": centred(seeds[0], (TOTAL_TOKENS, D), 1.0, 6.0, ((0, 32),)),
        "cotangent": centred(seeds[1], (TOTAL_TOKENS, D), 1.0, 6.0, ((0, 32),)),
        "lengths": draw_lengths(jax.random.fold_in(seeds[18], 71), 0),
        "w_qkv": centred(seeds[3], (LAYERS, D, QKV), D ** -0.5, 0.15625, ((1, 32),), jnp.float32),
        "w_out": centred(seeds[4], (LAYERS, D, D), (D // 16) ** -0.5, 0.625, ((1, 32),), jnp.float32),
        "w_gateup": centred(seeds[5], (LAYERS, D, 2 * FF), D ** -0.5, 0.15625, ((1, 32),), jnp.float32),
        "w_down": centred(seeds[6], (LAYERS, FF, D), FF ** -0.5, 0.09375, ((1, 32),), jnp.float32),
        "norm_gains": jnp.clip(1.0 + 0.1 * jax.random.normal(seeds[7], (LAYERS, 2, D), jnp.float32), 0.5, 1.5),
        "first_qkv": centred(seeds[8], (LAYERS, D, QKV), (TOTAL_TOKENS ** 0.5 / 9), 64.0, ((1, 32),), jnp.float32),
        "first_out": centred(seeds[9], (LAYERS, D, D), (TOTAL_TOKENS ** 0.5 / 9), 64.0, ((1, 32),), jnp.float32),
        "first_gateup": centred(seeds[10], (LAYERS, D, 2 * FF), (TOTAL_TOKENS ** 0.5 / 9), 64.0, ((1, 32),), jnp.float32),
        "first_down": centred(seeds[11], (LAYERS, FF, D), (TOTAL_TOKENS ** 0.5 / 9), 64.0, ((1, 32),), jnp.float32),
        "first_gains": centred(seeds[12], (LAYERS, 2, D), (TOTAL_TOKENS ** 0.5 / 9), 64.0, ((2, 32),), jnp.float32),
        "second_qkv": jnp.clip(jnp.exp(math.log(819.2) - 2.3025851 * jax.random.uniform(seeds[13], (LAYERS, D, QKV), jnp.float32) ** level_of(seeds[13], (LAYERS, D, QKV), ((1, 32),), -0.2, 0.2)), 81.92, 819.2),
        "second_out": jnp.clip(jnp.exp(math.log(819.2) - 2.3025851 * jax.random.uniform(seeds[14], (LAYERS, D, D), jnp.float32) ** level_of(seeds[14], (LAYERS, D, D), ((1, 32),), -0.2, 0.2)), 81.92, 819.2),
        "second_gateup": jnp.clip(jnp.exp(math.log(819.2) - 2.3025851 * jax.random.uniform(seeds[15], (LAYERS, D, 2 * FF), jnp.float32) ** level_of(seeds[15], (LAYERS, D, 2 * FF), ((1, 32),), -0.2, 0.2)), 81.92, 819.2),
        "second_down": jnp.clip(jnp.exp(math.log(819.2) - 2.3025851 * jax.random.uniform(seeds[16], (LAYERS, FF, D), jnp.float32) ** level_of(seeds[16], (LAYERS, FF, D), ((1, 32),), -0.2, 0.2)), 81.92, 819.2),
        "second_gains": jnp.clip(jnp.exp(math.log(819.2) - 2.3025851 * jax.random.uniform(seeds[17], (LAYERS, 2, D), jnp.float32) ** level_of(seeds[17], (LAYERS, 2, D), ((2, 32),), -0.2, 0.2)), 81.92, 819.2),
    }


@jax.custom_vjp
def lower_half(v):
    return lax.optimization_barrier(v.astype(jnp.bfloat16)).astype(jnp.float32)

@jax.custom_vjp
def low_back(v):
    return v

def low_keep(v):
    return (lower_half(v), None)

def low_pass(kept, grad):
    return (grad,)

def back_keep(v):
    return (v, None)

def back_low(kept, grad):
    return (lower_half(grad),)
lower_half.defvjp(low_keep, low_pass)
low_back.defvjp(back_keep, back_low)
highest = lax.Precision.HIGHEST
eps_norm = 1e-05
rope_base = 100000.0
beta_one = 0.9
beta_two = 0.95
adam_eps = 1e-08
decay_rate = 0.1
masked_score = -1e+30

def layout(length_row, places):
    seq_ends = jnp.cumsum(length_row, dtype=jnp.int32)
    passed = (places[:, None] >= seq_ends[None, :]).astype(jnp.int32)
    segment = lax.optimization_barrier(jnp.sum(passed, axis=1, dtype=jnp.int32))
    begins = lax.optimization_barrier(jnp.sum(passed * length_row[None, :], axis=1, dtype=jnp.int32))
    return (segment, places - begins)

def tables(positions):
    freq_index = jnp.arange(HEAD_SIZE // 2, dtype=jnp.float32)
    inverse = rope_base ** (-2.0 * freq_index / HEAD_SIZE)
    angles = positions.astype(jnp.float32)[:, None] * inverse[None, :]
    angles = jnp.concatenate([angles, angles], axis=-1)
    return (jnp.cos(angles)[:, None, :], jnp.sin(angles)[:, None, :])

def apply_rotary(values, rotary_cosines, rotary_sines):
    half_width = values.shape[-1] // 2
    turned = jnp.concatenate([-values[..., half_width:], values[..., :half_width]], axis=-1)
    return values * rotary_cosines + turned * rotary_sines

def normalize(residual):
    return residual * lax.rsqrt(lax.optimization_barrier(jnp.mean(residual * residual, axis=-1, keepdims=True)) + eps_norm)

def group_attention(packed):
    query_head_rows, key_head_rows, value_head_rows, segment = packed
    key_order = jnp.arange(GROUP_TOKENS, dtype=jnp.int32)
    scores = jnp.einsum('qgrd,kgd->grqk', query_head_rows, key_head_rows, precision=highest) * HEAD_SIZE ** (-0.5)
    scores = low_back(scores)
    allowed = (segment[:, None] == segment[None, :]) & (key_order[None, :] <= key_order[:, None])
    scores = jnp.where(allowed[None, None], scores, masked_score)
    attn_weights = lower_half(jax.nn.softmax(scores, axis=-1))
    return jnp.einsum('grqk,kgd->qgrd', attn_weights, value_head_rows, precision=highest)

def layer(residual, w_qkv, w_out, w_gateup, w_down, gain_pair, segments, rotary_cosines, rotary_sines):
    heads_per_group = QUERY_HEAD_COUNT // KEY_VALUE_HEADS
    input_one = lower_half(normalize(residual) * lower_half(gain_pair[0]))
    query_key_value_rows = low_back(jnp.dot(input_one, lower_half(w_qkv), precision=highest))
    query_head_rows = query_key_value_rows[:, :QUERY_HEAD_COUNT * HEAD_SIZE].reshape(TOTAL_TOKENS, QUERY_HEAD_COUNT, HEAD_SIZE)
    key_row_block = query_key_value_rows[:, QUERY_HEAD_COUNT * HEAD_SIZE:(QUERY_HEAD_COUNT + KEY_VALUE_HEADS) * HEAD_SIZE].reshape(TOTAL_TOKENS, KEY_VALUE_HEADS, HEAD_SIZE)
    value_row_block = query_key_value_rows[:, (QUERY_HEAD_COUNT + KEY_VALUE_HEADS) * HEAD_SIZE:].reshape(TOTAL_TOKENS, KEY_VALUE_HEADS, HEAD_SIZE)
    query_head_rows = lower_half(apply_rotary(query_head_rows, rotary_cosines, rotary_sines)).reshape(N_FSDP, GROUP_TOKENS, KEY_VALUE_HEADS, heads_per_group, HEAD_SIZE)
    key_row_block = lower_half(apply_rotary(key_row_block, rotary_cosines, rotary_sines)).reshape(N_FSDP, GROUP_TOKENS, KEY_VALUE_HEADS, HEAD_SIZE)
    value_row_block = lower_half(value_row_block).reshape(N_FSDP, GROUP_TOKENS, KEY_VALUE_HEADS, HEAD_SIZE)
    attended = lax.map(jax.checkpoint(group_attention), (query_head_rows, key_row_block, value_row_block, segments))
    attended = lower_half(low_back(attended.reshape(TOTAL_TOKENS, QUERY_HEAD_COUNT * HEAD_SIZE)))
    middle = residual + low_back(jnp.dot(attended, lower_half(w_out), precision=highest))
    input_two = lower_half(normalize(middle) * lower_half(gain_pair[1]))
    gate_up = low_back(jnp.dot(input_two, lower_half(w_gateup), precision=highest))
    hidden = lower_half(jax.nn.silu(gate_up[:, :FF]) * gate_up[:, FF:])
    return middle + low_back(jnp.dot(hidden, lower_half(w_down), precision=highest))

def adam_step(weight, gradient, first_moment, second_moment, step_rate, shrink):
    first_moment = beta_one * first_moment + (1.0 - beta_one) * gradient
    second_moment = beta_two * second_moment + (1.0 - beta_two) * gradient * gradient
    first_hat = first_moment / (1.0 - beta_one ** STEP)
    second_hat = second_moment / (1.0 - beta_two ** STEP)
    weight = weight - step_rate * (first_hat / (jnp.sqrt(second_hat) + adam_eps) + shrink * weight)
    return (weight, first_moment, second_moment)

def reference(tokens, cotangent, lengths, w_qkv, w_out, w_gateup, w_down, norm_gains, first_qkv, first_out, first_gateup, first_down, first_gains, second_qkv, second_out, second_gateup, second_down, second_gains):
    places = jnp.arange(GROUP_TOKENS, dtype=jnp.int32)
    segments, positions = jax.vmap(lambda length_row: layout(length_row, places))(lengths)
    rotary_cosines, rotary_sines = tables(positions.reshape(TOTAL_TOKENS))

    def forward(residual, all_qkv, all_out, all_gateup, all_down, all_gains):
        for layer_index in range(LAYERS):
            residual = layer(residual, all_qkv[layer_index], all_out[layer_index], all_gateup[layer_index], all_down[layer_index], all_gains[layer_index], segments, rotary_cosines, rotary_sines)
        return residual
    layer_out, pullback = jax.vjp(forward, tokens.astype(jnp.float32), w_qkv, w_out, w_gateup, w_down, norm_gains)
    gradients = pullback(cotangent.astype(jnp.float32))
    step_rates = (D ** (-0.5), 4.0 * D ** (-0.5), D ** (-0.5), FF ** (-0.5), 0.5)
    shrinks = (decay_rate, decay_rate, decay_rate, decay_rate, 0.0)
    weights = (w_qkv, w_out, w_gateup, w_down, norm_gains)
    firsts = (first_qkv, first_out, first_gateup, first_down, first_gains)
    seconds = (second_qkv, second_out, second_gateup, second_down, second_gains)
    results = [adam_step(weights[kind_index], gradients[kind_index + 1], firsts[kind_index], seconds[kind_index], step_rates[kind_index], shrinks[kind_index]) for kind_index in range(5)]
    return (layer_out.astype(jnp.bfloat16), gradients[0], results[0][0], results[1][0], results[2][0], results[3][0], results[4][0], results[0][1], results[1][1], results[2][1], results[3][1], results[4][1], results[0][2], results[1][2], results[2][2], results[3][2], results[4][2])
```

```python
import functools

import jax
import jax.numpy as jnp
from jax import lax
from jax.experimental import pallas as pl
from jax.experimental.pallas import tpu as pltpu
from jax.sharding import PartitionSpec as P

D = 1536
QUERY_HEAD_COUNT = 16
KEY_VALUE_HEADS = 8
HEAD_SIZE = 96
FF = 4096
LAYERS = 2
STEP = 6


eps_norm = 1e-05
rope_base = 100000.0
beta_one = 0.9
beta_two = 0.95
adam_eps = 1e-08
decay_rate = 0.1
masked_score = -1e30
lane_width = 128


def layout(length_row, places):
    seq_ends = jnp.cumsum(length_row, dtype=jnp.int32)
    passed = (places[:, None] >= seq_ends[None, :]).astype(jnp.int32)
    segment = jnp.sum(passed, axis=1, dtype=jnp.int32)
    begins = jnp.sum(passed * length_row[None, :], axis=1, dtype=jnp.int32)
    return (segment, places - begins)


def tables(positions):
    freq_index = jnp.arange(HEAD_SIZE // 2, dtype=jnp.float32)
    inverse = rope_base ** (-2.0 * freq_index / HEAD_SIZE)
    angles = positions.astype(jnp.float32)[:, None] * inverse[None, :]
    angles = jnp.concatenate([angles, angles], axis=-1)
    return (jnp.cos(angles)[:, None, :], jnp.sin(angles)[:, None, :])


def apply_rotary(values, rotary_cosines, rotary_sines):
    half_width = values.shape[-1] // 2
    turned = jnp.concatenate([-values[..., half_width:], values[..., :half_width]], axis=-1)
    return values * rotary_cosines + turned * rotary_sines


def invert_rotary(values, rotary_cosines, rotary_sines):
    half_width = values.shape[-1] // 2
    scaled_sine = values * rotary_sines
    turned = jnp.concatenate(
        [scaled_sine[..., half_width:], -scaled_sine[..., :half_width]], axis=-1
    )
    return values * rotary_cosines + turned


def normalize(residual):
    return residual * lax.rsqrt(jnp.mean(residual * residual, axis=-1, keepdims=True) + eps_norm)


def norm_back(grad_normed, normed, residual):
    inverse = lax.rsqrt(jnp.mean(residual * residual, axis=-1, keepdims=True) + eps_norm)
    return inverse * (grad_normed - normed * jnp.mean(grad_normed * normed, axis=-1, keepdims=True))


def product(lhs_matrix, rhs_matrix):
    return jnp.dot(lhs_matrix, rhs_matrix, preferred_element_type=jnp.float32)


def attention_scores(query_head_rows, key_head_rows, allowed):
    scores = jnp.einsum(
        "qgrd,kgd->grqk", query_head_rows, key_head_rows, preferred_element_type=jnp.float32
    ) * HEAD_SIZE ** (-0.5)
    return jnp.where(allowed[None, None], scores, masked_score)


def wire_pieces(stacked, layer_index):
    return tuple((shard_piece[layer_index].astype(jnp.bfloat16) for shard_piece in stacked))


def fetch_forward(stacked, layer_index):
    qkv_piece, out_piece, gateup_piece, down_piece, gain_piece = wire_pieces(stacked, layer_index)
    return (
        lax.all_gather(qkv_piece, ("fsdp", "seq"), axis=0, tiled=True),
        lax.all_gather(out_piece, ("fsdp", "seq"), axis=0, tiled=True),
        lax.all_gather(gateup_piece, ("fsdp", "seq"), axis=0, tiled=True),
        lax.all_gather(down_piece, ("fsdp", "seq"), axis=0, tiled=True),
        lax.all_gather(gain_piece, ("fsdp", "seq"), axis=1, tiled=True),
    )


def fetch_backward(stacked, layer_index):
    qkv_piece, out_piece, gateup_piece, down_piece, gain_piece = wire_pieces(stacked, layer_index)
    return (
        lax.all_gather(qkv_piece, ("fsdp", "seq"), axis=0, tiled=True),
        lax.all_gather(out_piece, ("fsdp", "seq"), axis=0, tiled=True),
        lax.all_gather(gateup_piece, ("fsdp", "seq"), axis=0, tiled=True),
        lax.all_gather(down_piece, ("fsdp", "seq"), axis=0, tiled=True),
        lax.all_gather(gain_piece, ("fsdp", "seq"), axis=1, tiled=True),
    )


def flat_lanes(matrix):
    return matrix.reshape(-1, lane_width)


def reduce_grads(grad_terms):
    grad_qkv, grad_out_proj, grad_gateup, grad_down, grad_gains = grad_terms
    widths = (grad_qkv.shape[1], grad_out_proj.shape[1], grad_gateup.shape[1], grad_down.shape[1])
    flat_qkv = flat_lanes(grad_qkv)
    flat_out = flat_lanes(grad_out_proj)
    flat_gateup = flat_lanes(grad_gateup)
    flat_down = flat_lanes(grad_down)
    summed = (
        lax.psum_scatter(flat_qkv, ("fsdp", "seq"), scatter_dimension=0, tiled=True),
        lax.psum_scatter(flat_out, ("fsdp", "seq"), scatter_dimension=0, tiled=True),
        lax.psum_scatter(flat_gateup, ("fsdp", "seq"), scatter_dimension=0, tiled=True),
        lax.psum_scatter(flat_down, ("fsdp", "seq"), scatter_dimension=0, tiled=True),
        lax.psum_scatter(grad_gains, ("fsdp", "seq"), scatter_dimension=1, tiled=True),
    )
    owned = tuple((summed[kind_index].reshape(-1, widths[kind_index]) for kind_index in range(4)))
    return owned + (summed[4],)


def layer_forward(residual, gathered, allowed, rotary_cosines, rotary_sines):
    w_qkv, w_out, w_gateup, w_down, gain_pair = gathered
    count_of_rows = residual.shape[0]
    heads_per_group = QUERY_HEAD_COUNT // KEY_VALUE_HEADS
    gain_float = gain_pair.astype(jnp.float32)
    normed_one = normalize(residual)
    input_one = (normed_one * gain_float[0]).astype(jnp.bfloat16)
    query_key_value_rows = product(input_one, w_qkv)
    query_head_rows = apply_rotary(
        query_key_value_rows[:, : QUERY_HEAD_COUNT * HEAD_SIZE].reshape(
            count_of_rows, QUERY_HEAD_COUNT, HEAD_SIZE
        ),
        rotary_cosines,
        rotary_sines,
    ).astype(jnp.bfloat16)
    key_row_block = apply_rotary(
        query_key_value_rows[
            :, QUERY_HEAD_COUNT * HEAD_SIZE : (QUERY_HEAD_COUNT + KEY_VALUE_HEADS) * HEAD_SIZE
        ].reshape(count_of_rows, KEY_VALUE_HEADS, HEAD_SIZE),
        rotary_cosines,
        rotary_sines,
    ).astype(jnp.bfloat16)
    value_row_block = query_key_value_rows[
        :, (QUERY_HEAD_COUNT + KEY_VALUE_HEADS) * HEAD_SIZE :
    ].astype(jnp.bfloat16)
    every_key, every_value = (
        lax.all_gather(
            key_row_block.reshape(count_of_rows, KEY_VALUE_HEADS * HEAD_SIZE),
            "seq",
            axis=0,
            tiled=True,
        ),
        lax.all_gather(value_row_block, "seq", axis=0, tiled=True),
    )
    key_head_rows = every_key.reshape(-1, KEY_VALUE_HEADS, HEAD_SIZE)
    value_head_rows = every_value.reshape(-1, KEY_VALUE_HEADS, HEAD_SIZE)
    query_head_rows = query_head_rows.reshape(
        count_of_rows, KEY_VALUE_HEADS, heads_per_group, HEAD_SIZE
    )
    scores = attention_scores(query_head_rows, key_head_rows, allowed)
    row_max = jnp.max(scores, axis=-1, keepdims=True)
    shifted = jnp.exp(scores - row_max)
    row_sum = jnp.sum(shifted, axis=-1, keepdims=True)
    log_total = row_max + jnp.log(row_sum)
    attn_weights = (shifted / row_sum).astype(jnp.bfloat16)
    attended = jnp.einsum(
        "grqk,kgd->qgrd", attn_weights, value_head_rows, preferred_element_type=jnp.float32
    )
    attended = attended.reshape(count_of_rows, QUERY_HEAD_COUNT * HEAD_SIZE).astype(jnp.bfloat16)
    middle = residual + product(attended, w_out)
    normed_two = normalize(middle)
    input_two = (normed_two * gain_float[1]).astype(jnp.bfloat16)
    gate_up = product(input_two, w_gateup)
    gate_pre = gate_up[:, :FF]
    up_proj = gate_up[:, FF:]
    hidden = (jax.nn.silu(gate_pre) * up_proj).astype(jnp.bfloat16)
    layer_out = middle + product(hidden, w_down)
    saved_layer = (
        residual,
        normed_one,
        input_one,
        query_head_rows,
        key_head_rows,
        value_head_rows,
        log_total,
        attended,
        middle,
        normed_two,
        input_two,
        gate_pre,
        up_proj,
        hidden,
    )
    return (saved_layer, layer_out)


def layer_backward(grad_out, saved_layer, gathered, allowed, rotary_cosines, rotary_sines):
    w_qkv, w_out, w_gateup, w_down, gain_pair = gathered
    (
        residual,
        normed_one,
        input_one,
        query_head_rows,
        key_head_rows,
        value_head_rows,
        log_total,
        attended,
        middle,
        normed_two,
        input_two,
        gate_pre,
        up_proj,
        hidden,
    ) = saved_layer
    count_of_rows = grad_out.shape[0]
    heads_per_group = QUERY_HEAD_COUNT // KEY_VALUE_HEADS
    gain_float = gain_pair.astype(jnp.float32)
    grad_branch = grad_out.astype(jnp.bfloat16)
    grad_down = jnp.einsum("tf,td->fd", hidden, grad_branch, preferred_element_type=jnp.float32)
    grad_hidden = jnp.einsum("td,fd->tf", grad_branch, w_down, preferred_element_type=jnp.float32)
    sigmoid_gate = jax.nn.sigmoid(gate_pre)
    grad_gate = grad_hidden * up_proj * sigmoid_gate * (1.0 + gate_pre * (1.0 - sigmoid_gate))
    grad_up = grad_hidden * gate_pre * sigmoid_gate
    grad_pair = jnp.concatenate([grad_gate, grad_up], axis=1).astype(jnp.bfloat16)
    grad_gateup = jnp.einsum("td,tf->df", input_two, grad_pair, preferred_element_type=jnp.float32)
    grad_input_two = jnp.einsum(
        "tf,df->td", grad_pair, w_gateup, preferred_element_type=jnp.float32
    )
    grad_gain_two = jnp.sum(grad_input_two * normed_two, axis=0)
    grad_middle = grad_out + norm_back(grad_input_two * gain_float[1], normed_two, middle)
    grad_branch_two = grad_middle.astype(jnp.bfloat16)
    grad_out_proj = jnp.einsum(
        "te,td->ed", attended, grad_branch_two, preferred_element_type=jnp.float32
    )
    attended_gradient = jnp.einsum(
        "td,ed->te", grad_branch_two, w_out, preferred_element_type=jnp.float32
    )
    attended_gradient = attended_gradient.astype(jnp.bfloat16).reshape(
        count_of_rows, KEY_VALUE_HEADS, heads_per_group, HEAD_SIZE
    )
    scores = attention_scores(query_head_rows, key_head_rows, allowed)
    attn_float = jnp.exp(scores - log_total)
    value_gradient = jnp.einsum(
        "grqk,qgrd->kgd",
        attn_float.astype(jnp.bfloat16),
        attended_gradient,
        preferred_element_type=jnp.float32,
    )
    grad_weights = jnp.einsum(
        "qgrd,kgd->grqk", attended_gradient, value_head_rows, preferred_element_type=jnp.float32
    )
    inner_sum = jnp.sum(attn_float * grad_weights, axis=-1, keepdims=True)
    grad_scores = (attn_float * (grad_weights - inner_sum)).astype(jnp.bfloat16)
    grad_query = jnp.einsum(
        "grqk,kgd->qgrd", grad_scores, key_head_rows, preferred_element_type=jnp.float32
    ) * HEAD_SIZE ** (-0.5)
    gradient_keys = jnp.einsum(
        "grqk,qgrd->kgd", grad_scores, query_head_rows, preferred_element_type=jnp.float32
    ) * HEAD_SIZE ** (-0.5)
    shared_keys, value_share = (
        lax.psum_scatter(
            gradient_keys.reshape(-1, KEY_VALUE_HEADS * HEAD_SIZE).astype(jnp.bfloat16),
            "seq",
            scatter_dimension=0,
            tiled=True,
        ).astype(jnp.float32),
        lax.psum_scatter(
            value_gradient.reshape(-1, KEY_VALUE_HEADS * HEAD_SIZE).astype(jnp.bfloat16),
            "seq",
            scatter_dimension=0,
            tiled=True,
        ).astype(jnp.float32),
    )
    grad_q = invert_rotary(
        grad_query.reshape(count_of_rows, QUERY_HEAD_COUNT, HEAD_SIZE), rotary_cosines, rotary_sines
    ).reshape(count_of_rows, QUERY_HEAD_COUNT * HEAD_SIZE)
    key_gradient = invert_rotary(
        shared_keys.reshape(count_of_rows, KEY_VALUE_HEADS, HEAD_SIZE), rotary_cosines, rotary_sines
    ).reshape(count_of_rows, KEY_VALUE_HEADS * HEAD_SIZE)
    grad_rows = jnp.concatenate([grad_q, key_gradient, value_share], axis=1).astype(jnp.bfloat16)
    grad_qkv = jnp.einsum("td,tf->df", input_one, grad_rows, preferred_element_type=jnp.float32)
    grad_input_one = jnp.einsum("tf,df->td", grad_rows, w_qkv, preferred_element_type=jnp.float32)
    grad_gain_one = jnp.sum(grad_input_one * normed_one, axis=0)
    grad_in = grad_middle + norm_back(grad_input_one * gain_float[0], normed_one, residual)
    return (
        grad_in,
        (
            grad_qkv,
            grad_out_proj,
            grad_gateup,
            grad_down,
            jnp.stack([grad_gain_one, grad_gain_two]),
        ),
    )


def adam_step(weight, gradient, first_moment, second_moment, step_rate, shrink):
    first_moment = beta_one * first_moment + (1.0 - beta_one) * gradient
    second_moment = beta_two * second_moment + (1.0 - beta_two) * gradient * gradient
    first_hat = first_moment / (1.0 - beta_one**STEP)
    second_hat = second_moment / (1.0 - beta_two**STEP)
    weight = weight - step_rate * (first_hat / (jnp.sqrt(second_hat) + adam_eps) + shrink * weight)
    return (weight, first_moment, second_moment)


def shards(
    tokens,
    cotangent,
    lengths,
    w_qkv,
    w_out,
    w_gateup,
    w_down,
    norm_gains,
    first_qkv,
    first_out,
    first_gateup,
    first_down,
    first_gains,
    second_qkv,
    second_out,
    second_gateup,
    second_down,
    second_gains,
):
    count_of_rows = tokens.shape[0]
    group_rows = count_of_rows * lax.axis_size("seq")
    place_rows = lax.axis_index("seq") * count_of_rows + jnp.arange(count_of_rows, dtype=jnp.int32)
    key_places = jnp.arange(group_rows, dtype=jnp.int32)
    seg_rows, positions = layout(lengths[0], place_rows)
    seg_keys = layout(lengths[0], key_places)[0]
    allowed = (seg_rows[:, None] == seg_keys[None, :]) & (
        key_places[None, :] <= place_rows[:, None]
    )
    rotary_cosines, rotary_sines = tables(positions)
    stacked = (w_qkv, w_out, w_gateup, w_down, norm_gains)
    residual = tokens.astype(jnp.float32)
    saved_all = []
    for layer_index in range(LAYERS):
        gathered = fetch_forward(stacked, layer_index)
        saved_layer, residual = layer_forward(
            residual, gathered, allowed, rotary_cosines, rotary_sines
        )
        saved_all.append(saved_layer)
    grad_state = cotangent.astype(jnp.float32)
    updates = [None] * LAYERS
    for layer_index in reversed(range(LAYERS)):
        gathered = fetch_backward(stacked, layer_index)
        grad_state, grad_terms = layer_backward(
            grad_state, saved_all[layer_index], gathered, allowed, rotary_cosines, rotary_sines
        )
        updates[layer_index] = reduce_grads(grad_terms)
    step_rates = (D ** (-0.5), 4.0 * D ** (-0.5), D ** (-0.5), FF ** (-0.5), 0.5)
    shrinks = (decay_rate, decay_rate, decay_rate, decay_rate, 0.0)
    firsts = (first_qkv, first_out, first_gateup, first_down, first_gains)
    seconds = (second_qkv, second_out, second_gateup, second_down, second_gains)
    new_weights = []
    new_firsts = []
    new_seconds = []
    for kind_index in range(5):
        grads_kind = jnp.stack([updates[layer_index][kind_index] for layer_index in range(LAYERS)])
        weight, first_moment, second_moment = adam_step(
            stacked[kind_index],
            grads_kind,
            firsts[kind_index],
            seconds[kind_index],
            step_rates[kind_index],
            shrinks[kind_index],
        )
        new_weights.append(weight)
        new_firsts.append(first_moment)
        new_seconds.append(second_moment)
    outputs = [residual.astype(jnp.bfloat16), grad_state] + new_weights + new_firsts + new_seconds
    return tuple(outputs)


MESH = pl.DeviceIdType.MESH
BF = jnp.bfloat16
F32 = jnp.float32
KV_RANK = KEY_VALUE_HEADS // 4
Q_RANK = QUERY_HEAD_COUNT // 4
ANY = pl.BlockSpec(memory_space=pl.ANY)
VM = pl.BlockSpec(memory_space=pltpu.VMEM)
DMA = pltpu.SemaphoreType.DMA


class Place:
    def __init__(self):
        f, z = lax.axis_index("fsdp"), lax.axis_index("seq")
        self.y, self.x, self.c = lax.div(f, 4), lax.rem(lax.div(f, 2), 2), lax.rem(f, 2)
        self.z1, self.z0 = lax.div(z, 2), lax.rem(z, 2)
        self.rank = 2 * self.c + self.z0
        self.peer = {
            "y": (f + 4 - 8 * self.y, z),
            "x": (f + 2 - 4 * self.x, z),
            "c": (f + 1 - 2 * self.c, z),
            "z1": (f, z + 2 - 4 * self.z1),
            "z0": (f, z + 1 - 2 * self.z0),
            "cz": (f + 1 - 2 * self.c, z + 1 - 2 * self.z0),
        }


def greet(place, names):
    barrier = pltpu.get_barrier_semaphore()
    for name in names:
        pl.semaphore_signal(barrier, inc=1, device_id=place.peer[name], device_id_type=MESH)
    pl.semaphore_wait(barrier, len(names))


def remote(src, dst, send_sem, recv_sem, device):
    return pltpu.make_async_remote_copy(
        src_ref=src, dst_ref=dst, send_sem=send_sem, recv_sem=recv_sem, device_id=device, device_id_type=MESH
    )


def columns_index(y, x, z1, h):
    return ((y * 2 + x) * 2 + h) * 2 + z1


def rows_index(y, x, z1, h):
    return ((y * 2 + x) * 2 + z1) * 2 + h


class Gather:
    def __init__(self, place, ref, index, send, recv):
        self.p, self.ref, self.index, self.send, self.recv = place, ref, index, send, recv

    def at(self, flips, h):
        p = self.p
        flip = lambda v, name: 1 - v if name in flips else v
        return self.ref.at[self.index(flip(p.y, "y"), flip(p.x, "x"), flip(p.z1, "z1"), h)]

    def route(self, h):
        a, b = ("y", "x") if h == 0 else ("x", "y")
        return (
            ("z1", ()),
            (a, ()),
            (a, ("z1",)),
            (b, ()),
            (b, ("z1",)),
            (b, (a,)),
            (b, (a, "z1")),
        )

    def out(self, h, m):
        axis, flips = self.route(h)[m]
        ref = self.at(flips, h)
        return remote(ref, ref, self.send.at[7 * h + m], self.recv.at[7 * h + m], self.p.peer[axis])

    def into(self, h, m):
        axis, flips = self.route(h)[m]
        ref = self.at(flips + (axis,), h)
        return remote(ref, ref, self.send.at[7 * h + m], self.recv.at[7 * h + m], self.p.peer[axis])

    def steps(self):
        def first():
            for m in (0, 1, 3):
                for h in (0, 1):
                    self.out(h, m).start()

        def then(got, gives):
            def step():
                for h in (0, 1):
                    self.into(h, got).wait_recv()
                    for m in gives:
                        self.out(h, m).start()

            return step

        def last():
            for h in (0, 1):
                for m in (3, 4, 5, 6):
                    self.into(h, m).wait_recv()
                for m in range(7):
                    self.out(h, m).wait_send()

        return [first, then(0, (2, 4)), then(1, (5,)), then(2, (6,)), last]


class Spread:
    def __init__(self, place, src, target, send, recv, local):
        self.p, self.src, self.target, self.send, self.recv, self.local = place, src, target, send, recv, local

    def copy(self, k, arriving=False):
        p = self.p
        name, fc, fz = (("c", 1, 0), ("z0", 0, 1), ("cz", 1, 1))[k]
        c = 1 - p.c if fc else p.c
        z0 = 1 - p.z0 if fz else p.z0
        src = self.src(c, z0)
        dst = self.target(c, z0) if arriving else self.target(p.c, p.z0)
        return remote(src, dst, self.send.at[k], self.recv.at[k], p.peer[name])

    def own(self):
        p = self.p
        return pltpu.make_async_copy(self.src(p.c, p.z0), self.target(p.c, p.z0), self.local)

    def start(self):
        for k in range(3):
            self.copy(k).start()
        self.own().start()

    def wait(self):
        for k in range(3):
            self.copy(k, True).wait_recv()
        self.own().wait()

    def finish(self):
        for k in range(3):
            self.copy(k).wait_send()


def add_to(dst, src):
    dst[...] = (dst[...].astype(F32) + src[...].astype(F32)).astype(dst.dtype)


class Reduce:
    def __init__(self, place, ref, index, one, two, three, send, recv):
        self.p, self.ref, self.index = place, ref, index
        self.one, self.two, self.three, self.send, self.recv = one, two, three, send, recv

    def block(self, h, a, b, z1):
        y, x = (b, a) if h == 0 else (a, b)
        return self.ref.at[self.index(y, x, z1, h)]

    def axes(self, h):
        p = self.p
        return ("x", "y", p.x, p.y) if h == 0 else ("y", "x", p.y, p.x)

    def copy(self, h, m):
        p = self.p
        name_a, name_b, a, b = self.axes(h)
        sems = self.send.at[7 * h + m], self.recv.at[7 * h + m]
        if m < 4:
            at_b, at_z = (1 - b if m < 2 else b), m % 2
            return remote(self.block(h, 1 - a, at_b, at_z), self.one.at[h, m], *sems, p.peer[name_a])
        if m < 6:
            return remote(self.one.at[h, m - 4], self.two.at[h, m - 4], *sems, p.peer[name_b])
        return remote(self.two.at[h, 1 - p.z1], self.three.at[h], *sems, p.peer["z1"])

    def steps(self):
        def first():
            for m in range(4):
                for h in (0, 1):
                    self.copy(h, m).start()

        def second(ms):
            def step():
                for m in ms:
                    for h in (0, 1):
                        _, _, a, b = self.axes(h)
                        self.copy(h, m).wait_recv()
                        at_b = 1 - b if m < 2 else b
                        add_to(self.one.at[h, m], self.block(h, a, at_b, m % 2))
                        if m < 2:
                            self.copy(h, 4 + m).start()

            return step

        def third():
            for h in (0, 1):
                for k in (0, 1):
                    self.copy(h, 4 + k).wait_recv()
                    add_to(self.two.at[h, k], self.one.at[h, 2 + k])
                self.copy(h, 6).start()

        def last():
            for h in (0, 1):
                self.copy(h, 6).wait_recv()
                add_to(self.three.at[h], self.two.at[h, self.p.z1])
                for m in range(7):
                    self.copy(h, m).wait_send()

        return [first, second((0, 1)), second((2, 3)), third, last]


def run_together(*programs):
    for k in range(max(len(p) for p in programs)):
        for p in programs:
            if k < len(p):
                p[k]()


def out_gather_steps(p, src, ref, send, recv, local):
    home = p.x == p.z0
    here = p.y * 2 + p.z1
    at = lambda fy, fz: ref.at[(1 - p.y if fy else p.y) * 2 + (1 - p.z1 if fz else p.z1)]
    pair = lambda half: remote(src, ref.at[here, half], send.at[0], recv.at[0], p.peer["z0"])
    z1_copy = lambda fz: remote(at(0, fz), at(0, fz), send.at[1], recv.at[1], p.peer["z1"])
    y_copy = lambda k, fy: remote(at(fy, k), at(fy, k), send.at[2 + k], recv.at[2 + k], p.peer["y"])
    x_copy = lambda k: remote(at(k // 2, k % 2), at(k // 2, k % 2), send.at[4 + k], recv.at[4 + k], p.peer["x"])
    own = pltpu.make_async_copy(src, ref.at[here, p.z0], local)

    def zero():
        @pl.when(home)
        def _():
            own.start()

        @pl.when(jnp.logical_not(home))
        def _():
            pair(p.z0).start()

    def one():
        @pl.when(home)
        def _():
            own.wait()
            pair(1 - p.z0).wait_recv()
            z1_copy(0).start()
            y_copy(0, 0).start()
            x_copy(0).start()

    def two():
        @pl.when(home)
        def _():
            z1_copy(1).wait_recv()
            y_copy(1, 0).start()
            x_copy(1).start()

    def three():
        @pl.when(home)
        def _():
            for k in (0, 1):
                y_copy(k, 1).wait_recv()
                x_copy(2 + k).start()

    def last():
        @pl.when(home)
        def _():
            z1_copy(0).wait_send()
            for k in (0, 1):
                y_copy(k, 0).wait_send()
            for k in range(4):
                x_copy(k).wait_send()

        @pl.when(jnp.logical_not(home))
        def _():
            pair(p.z0).wait_send()
            for k in range(4):
                x_copy(k).wait_recv()

    return [zero, one, two, three, last]


def out_reduce_steps(p, ref, one, two, three, got, out, send, recv):
    home = p.x == p.z0
    away = jnp.logical_not(home)
    x_copy = lambda k: remote(ref.at[k], one.at[k], send.at[k], recv.at[k], p.peer["x"])
    y_copy = lambda k: remote(one.at[(1 - p.y) * 2 + k], two.at[k], send.at[4 + k], recv.at[4 + k], p.peer["y"])
    z1_copy = remote(two.at[1 - p.z1], three, send.at[6], recv.at[6], p.peer["z1"])
    rows = three.shape[0] // 2
    half = lambda z0: three.at[pl.ds(pl.multiple_of(z0 * rows, rows), rows)]
    pair = remote(half(1 - p.z0), got, send.at[7], recv.at[7], p.peer["z0"])

    def zero():
        @pl.when(away)
        def _():
            for k in range(4):
                x_copy(k).start()

    def first():
        @pl.when(home)
        def _():
            for k in range(4):
                x_copy(k).wait_recv()
                add_to(one.at[k], ref.at[k])
            for k in (0, 1):
                y_copy(k).start()

    def second():
        @pl.when(home)
        def _():
            for k in (0, 1):
                y_copy(k).wait_recv()
                add_to(two.at[k], one.at[p.y * 2 + k])
            z1_copy.start()

    def third():
        @pl.when(home)
        def _():
            z1_copy.wait_recv()
            add_to(three, two.at[p.z1])
            pair.start()

    def last():
        @pl.when(home)
        def _():
            out[...] = half(p.z0)[...]
            for k in (0, 1):
                y_copy(k).wait_send()
            z1_copy.wait_send()
            pair.wait_send()

        @pl.when(away)
        def _():
            pair.wait_recv()
            out[...] = got[...]
            for k in range(4):
                x_copy(k).wait_send()

    return [zero, first, second, third, last]


def gains_gather(p, src, ref, send, recv, local):
    me = ((p.y * 2 + p.x) * 2 + p.c) * 4 + p.z1 * 2 + p.z0
    own = pltpu.make_async_copy(src, ref.at[me], local)
    names = ("z0", "z1", "c", "x", "y")

    def span(k, other):
        size = 1 << k
        start = lax.div(me, size) * size
        if other:
            bit = lax.rem(lax.div(me, size), 2)
            start = start + size - 2 * size * bit
        return ref.at[pl.ds(start, size)]

    def copy(k, other):
        return remote(span(k, other), span(k, other), send.at[k], recv.at[k], p.peer[names[k]])

    def step(k):
        def run():
            if k == 0:
                own.start()
                own.wait()
            else:
                copy(k - 1, True).wait_recv()
            if k < 5:
                copy(k, False).start()
            else:
                for j in range(5):
                    copy(j, False).wait_send()

        return run

    return [step(k) for k in range(6)]


def gains_reduce(p, ref, halves, out, send, recv):
    names, bits = ("y", "x", "c", "z1", "z0"), (p.y, p.x, p.c, p.z1, p.z0)

    def part(k, bit):
        source, size = (ref if k == 0 else halves[k - 1]), 16 >> k
        return source.at[pl.ds(bit * size, size)]

    def copy(k):
        return remote(part(k, 1 - bits[k]), halves[k], send.at[k], recv.at[k], p.peer[names[k]])

    def step(k):
        def run():
            if k > 0:
                copy(k - 1).wait_recv()
                halves[k - 1][...] += part(k - 1, bits[k - 1])[...]
            if k < 5:
                copy(k).start()
            else:
                out[...] = halves[4][0]
                for j in range(5):
                    copy(j).wait_send()

        return run

    return [step(k) for k in range(6)]


GROUP = ("c", "z0", "cz")
EIGHT = ("z1", "y", "x")


def gather_attention(qkv, out, gains, collective_id):
    _, rows, width = qkv.shape

    def body(*refs):
        refs = list(refs)
        qkv_ref, out_ref = refs[:2]
        del refs[:2]
        gains_ref = refs.pop(0) if gains is not None else None
        all_qkv, all_out = refs[:2]
        del refs[:2]
        all_gains = refs.pop(0) if gains is not None else None
        send, recv, local, s_send, s_recv, o_send, o_recv = refs[:7]
        p = Place()
        greet(p, GROUP + EIGHT)
        at = lambda c, z0: all_qkv.at[columns_index(p.y, p.x, p.z1, c), z0]
        spread = Spread(p, lambda c, z0: qkv_ref.at[2 * c + z0], at, s_send, s_recv, local.at[0])
        out_steps = out_gather_steps(p, out_ref, all_out, o_send, o_recv, local.at[1])
        programs = [out_steps]
        spread.start()
        out_steps[0]()
        spread.wait()
        programs = [Gather(p, all_qkv, columns_index, send, recv).steps(), out_steps[1:]]
        if gains is not None:
            programs.append(gains_gather(p, gains_ref, all_gains, refs[7], refs[8], local.at[2]))
        run_together(*programs)
        spread.finish()

    shapes = [
        jax.ShapeDtypeStruct((16, 2, rows, width), BF),
        jax.ShapeDtypeStruct((4, 2) + out.shape, BF),
    ]
    args = [qkv, out]
    scratch = [DMA((14,)), DMA((14,)), DMA((3,)), DMA((3,)), DMA((3,)), DMA((8,)), DMA((8,))]
    if gains is not None:
        args.append(gains)
        shapes.append(jax.ShapeDtypeStruct((32,) + gains.shape, BF))
        scratch += [DMA((5,)), DMA((5,))]
    return pl.pallas_call(
        body,
        out_shape=shapes,
        in_specs=[ANY] * len(args),
        out_specs=[ANY] * len(shapes),
        scratch_shapes=scratch,
        compiler_params=pltpu.CompilerParams(collective_id=collective_id, has_side_effects=True),
        name="gather_attention",
    )(*args)


def gather_feed(gateup, down, collective_id):
    _, rows, width = gateup.shape

    def body(gu_ref, down_ref, all_gu, all_down, send, recv, local, s_send, s_recv, d_send, d_recv):
        p = Place()
        greet(p, GROUP + EIGHT)
        at = lambda c, z0: all_gu.at[columns_index(p.y, p.x, p.z1, c), z0]
        spread = Spread(p, lambda c, z0: gu_ref.at[2 * c + z0], at, s_send, s_recv, local.at[0])
        spread.start()
        own = pltpu.make_async_copy(down_ref, all_down.at[pl.ds(rows_index(p.y, p.x, p.z1, 0), 2)], local.at[1])
        own.start()
        own.wait()
        down_steps = Gather(p, all_down, rows_index, d_send, d_recv).steps()
        down_steps[0]()
        spread.wait()
        run_together(Gather(p, all_gu, columns_index, send, recv).steps(), down_steps[1:])
        spread.finish()

    return pl.pallas_call(
        body,
        out_shape=[
            jax.ShapeDtypeStruct((16, 2, rows, width), BF),
            jax.ShapeDtypeStruct((16,) + down.shape[1:], BF),
        ],
        in_specs=[ANY] * 2,
        out_specs=[ANY] * 2,
        scratch_shapes=[DMA((14,)), DMA((14,)), DMA((2,)), DMA((3,)), DMA((3,)), DMA((14,)), DMA((14,))],
        compiler_params=pltpu.CompilerParams(collective_id=collective_id, has_side_effects=True),
        name="gather_feed",
    )(gateup, down)


def reduce_scratch(block):
    return [
        pltpu.VMEM((2, 4) + block, BF),
        pltpu.VMEM((2, 2) + block, BF),
        pltpu.VMEM((2,) + block, BF),
        DMA((14,)),
        DMA((14,)),
    ]


def reduce_attention(qkv, out, gains, collective_id):
    block, rows = qkv.shape[1:], qkv.shape[1] // 2

    def body(*refs):
        refs = list(refs)
        qkv_ref, out_ref = refs[:2]
        del refs[:2]
        gains_ref = refs.pop(0) if gains is not None else None
        qkv_sum, out_sum = refs[:2]
        del refs[:2]
        gains_sum = refs.pop(0) if gains is not None else None
        one, two, three, send, recv, o1, o2, o3, got, o_send, o_recv, s_send, s_recv, local = refs[:14]
        p = Place()
        greet(p, GROUP + EIGHT)
        programs = [
            Reduce(p, qkv_ref, columns_index, one, two, three, send, recv).steps(),
            out_reduce_steps(p, out_ref, o1, o2, o3, got, out_sum, o_send, o_recv),
        ]
        if gains is not None:
            programs.append(gains_reduce(p, gains_ref, refs[14:19], gains_sum, refs[19], refs[20]))
        run_together(*programs)
        part = lambda c, z0: three.at[c, pl.ds(pl.multiple_of(z0 * rows, rows), rows)]
        spread = Spread(p, part, lambda c, z0: qkv_sum.at[2 * c + z0], s_send, s_recv, local.at[0])
        spread.start()
        spread.wait()
        spread.finish()

    shapes = [jax.ShapeDtypeStruct((4, rows, block[1]), BF), jax.ShapeDtypeStruct((rows, out.shape[2]), BF)]
    args = [qkv, out]
    wide = out.shape[1:]
    scratch = reduce_scratch(block) + [
        pltpu.VMEM((4,) + wide, BF),
        pltpu.VMEM((2,) + wide, BF),
        pltpu.VMEM(wide, BF),
        pltpu.VMEM((rows, wide[1]), BF),
        DMA((8,)),
        DMA((8,)),
        DMA((3,)),
        DMA((3,)),
        DMA((1,)),
    ]
    if gains is not None:
        args.append(gains)
        shapes.append(jax.ShapeDtypeStruct(gains.shape[1:], F32))
        scratch += [pltpu.VMEM((16 >> k,) + gains.shape[1:], F32) for k in range(5)] + [DMA((5,)), DMA((5,))]
    return pl.pallas_call(
        body,
        out_shape=shapes,
        in_specs=[VM] * len(args),
        out_specs=[VM] * len(shapes),
        scratch_shapes=scratch,
        compiler_params=pltpu.CompilerParams(
            collective_id=collective_id, has_side_effects=True, vmem_limit_bytes=50 * 2**20
        ),
        name="reduce_attention",
    )(*args)


def reduce_feed(gateup, down, collective_id):
    block, rows, thin = gateup.shape[1:], gateup.shape[1] // 2, down.shape[1:]

    def body(gu_ref, down_ref, gu_sum, down_sum, one, two, three, send, recv, d1, d2, d3, d_send, d_recv, s_send, s_recv, local):
        p = Place()
        greet(p, GROUP + EIGHT)
        run_together(
            Reduce(p, gu_ref, columns_index, one, two, three, send, recv).steps(),
            Reduce(p, down_ref, rows_index, d1, d2, d3, d_send, d_recv).steps(),
        )
        part = lambda c, z0: three.at[c, pl.ds(pl.multiple_of(z0 * rows, rows), rows)]
        spread = Spread(p, part, lambda c, z0: gu_sum.at[2 * c + z0], s_send, s_recv, local.at[0])
        spread.start()
        down_sum[...] = d3[...]
        spread.wait()
        spread.finish()

    return pl.pallas_call(
        body,
        out_shape=[jax.ShapeDtypeStruct((4, rows, block[1]), BF), jax.ShapeDtypeStruct((2,) + thin, BF)],
        in_specs=[VM] * 2,
        out_specs=[VM] * 2,
        scratch_shapes=reduce_scratch(block) + reduce_scratch(thin) + [DMA((3,)), DMA((3,)), DMA((1,))],
        compiler_params=pltpu.CompilerParams(
            collective_id=collective_id, has_side_effects=True, vmem_limit_bytes=60 * 2**20
        ),
        name="reduce_feed",
    )(gateup, down)


CHUNKS = 4


class ShareRows:
    def __init__(self, p, src, dst, send, recv, local):
        self.p, self.src, self.dst, self.send, self.recv, self.local = p, src, dst, send, recv, local
        self.rows = src.shape[0] // CHUNKS

    def chunk(self, rank, k):
        return self.dst.at[rank, pl.ds(k * self.rows, self.rows)]

    def over(self, k, arriving=False):
        p = self.p
        src = self.src.at[pl.ds(k * self.rows, self.rows)]
        rank = 2 * p.c + 1 - p.z0 if arriving else p.rank
        return remote(src, self.chunk(rank, k), self.send.at[k], self.recv.at[k], p.peer["z0"])

    def across(self, arriving=False):
        p = self.p
        rank = 2 * (1 - p.c) + p.z0 if arriving else p.rank
        return remote(self.src, self.dst.at[rank], self.send.at[CHUNKS], self.recv.at[CHUNKS], p.peer["c"])

    def onward(self, k, arriving=False):
        p = self.p
        ours, theirs = 2 * p.c + 1 - p.z0, 2 * (1 - p.c) + 1 - p.z0
        ref = self.chunk(theirs if arriving else ours, k)
        return remote(ref, ref, self.send.at[CHUNKS + 1 + k], self.recv.at[CHUNKS + 1 + k], p.peer["c"])

    def own(self):
        return pltpu.make_async_copy(self.src, self.dst.at[self.p.rank], self.local)

    def start(self):
        for k in range(CHUNKS):
            self.over(k).start()
        self.across().start()
        self.own().start()

    def near(self):
        self.own().wait()
        self.across(True).wait_recv()

    def pass_on(self, k):
        self.over(k, True).wait_recv()
        self.onward(k).start()

    def far(self, k):
        self.onward(k, True).wait_recv()

    def finish(self):
        for k in range(CHUNKS):
            self.over(k).wait_send()
            self.onward(k).wait_send()
        self.across().wait_send()


def share_rows(rows, collective_id):
    def body(src, dst, send, recv, local):
        p = Place()
        greet(p, ("c", "z0"))
        share = ShareRows(p, src, dst, send, recv, local.at[0])
        share.start()
        share.near()
        for k in range(CHUNKS):
            share.pass_on(k)
        for k in range(CHUNKS):
            share.far(k)
        share.finish()

    return pl.pallas_call(
        body,
        out_shape=jax.ShapeDtypeStruct((4,) + rows.shape, rows.dtype),
        in_specs=[ANY],
        out_specs=ANY,
        scratch_shapes=[DMA((2 * CHUNKS + 1,)), DMA((2 * CHUNKS + 1,)), DMA((1,))],
        compiler_params=pltpu.CompilerParams(collective_id=collective_id, has_side_effects=True),
        name="share_rows",
    )(rows)


class SumRows:
    def __init__(self, p, terms, near, cross, far, send, recv):
        self.p, self.terms, self.near, self.cross, self.far, self.send, self.recv = p, terms, near, cross, far, send, recv
        self.rows = near.shape[0] // CHUNKS

    def diagonal(self, k):
        p = self.p
        part = pl.ds(k * self.rows, self.rows)
        rank = 2 * (1 - p.c) + 1 - p.z0
        return remote(self.terms.at[rank, part], self.cross.at[part], self.send.at[k], self.recv.at[k], p.peer["c"])

    def sibling(self):
        p = self.p
        rank, at = 2 * (1 - p.c) + p.z0, CHUNKS
        return remote(self.terms.at[rank], self.near, self.send.at[at], self.recv.at[at], p.peer["c"])

    def over(self, k):
        p, at = self.p, CHUNKS + 1 + k
        part = pl.ds(k * self.rows, self.rows)
        return remote(self.cross.at[part], self.far.at[part], self.send.at[at], self.recv.at[at], p.peer["z0"])

    def relay(self, k):
        p = self.p
        self.diagonal(k).wait_recv()
        part = pl.ds(k * self.rows, self.rows)
        add_to(self.cross.at[part], self.terms.at[2 * p.c + 1 - p.z0, part])
        self.over(k).start()

    def finish(self):
        for k in range(CHUNKS):
            self.diagonal(k).wait_send()
            self.over(k).wait_send()
        self.sibling().wait_send()


def sum_rows(terms, collective_id):
    _, rows, width = terms.shape

    def body(terms_ref, out_ref, near, cross, far, send, recv):
        p = Place()
        greet(p, ("c", "z0"))
        total = SumRows(p, terms_ref, near, cross, far, send, recv)
        for k in range(CHUNKS):
            total.diagonal(k).start()
        total.sibling().start()
        for k in range(CHUNKS):
            total.relay(k)
        total.sibling().wait_recv()
        out_ref[...] = terms_ref[p.rank].astype(F32) + near[...].astype(F32)
        for k in range(CHUNKS):
            total.over(k).wait_recv()
        out_ref[...] += far[...].astype(F32)
        total.finish()

    part = pltpu.VMEM((rows, width), BF)
    return pl.pallas_call(
        body,
        out_shape=jax.ShapeDtypeStruct((rows, width), F32),
        in_specs=[VM],
        out_specs=VM,
        scratch_shapes=[part, part, part, DMA((2 * CHUNKS + 1,)), DMA((2 * CHUNKS + 1,))],
        compiler_params=pltpu.CompilerParams(
            collective_id=collective_id, has_side_effects=True, vmem_limit_bytes=40 * 2**20
        ),
        name="sum_rows",
    )(terms)


def pack_qkv(shard):
    rows = shard.shape[0]
    q = shard[:, : QUERY_HEAD_COUNT * HEAD_SIZE].reshape(rows, 2, 2, 2, 2, HEAD_SIZE)
    q = q.transpose(3, 2, 0, 1, 4, 5).reshape(4, rows, Q_RANK * HEAD_SIZE)
    kv = shard[:, QUERY_HEAD_COUNT * HEAD_SIZE :].reshape(rows, 2, 2, 2, 2, HEAD_SIZE)
    kv = kv.transpose(4, 3, 0, 1, 2, 5).reshape(4, rows, 2 * KV_RANK * HEAD_SIZE)
    return jnp.concatenate([q, kv], axis=2).astype(BF)


def unpack_qkv(parts):
    rows = parts.shape[1]
    q = parts[..., : Q_RANK * HEAD_SIZE].reshape(2, 2, rows, 2, 2, HEAD_SIZE)
    q = q.transpose(2, 3, 1, 0, 4, 5).reshape(rows, QUERY_HEAD_COUNT * HEAD_SIZE)
    kv = parts[..., Q_RANK * HEAD_SIZE :].reshape(2, 2, rows, 2, 2, HEAD_SIZE)
    kv = kv.transpose(2, 3, 4, 1, 0, 5).reshape(rows, 2 * KEY_VALUE_HEADS * HEAD_SIZE)
    return jnp.concatenate([q, kv], axis=1)


def pack_gateup(shard):
    rows = shard.shape[0]
    parts = shard.reshape(rows, 2, 2, 2, 2, 2, 2, -1).transpose(4, 6, 0, 1, 2, 3, 5, 7)
    return parts.reshape(4, rows, -1).astype(BF)


def unpack_gateup(parts):
    rows = parts.shape[1]
    return parts.reshape(2, 2, rows, 2, 2, 2, 2, -1).transpose(2, 3, 4, 5, 0, 6, 1, 7).reshape(rows, -1)


def swap_pairs(count_fsdp, count_seq):
    pairs = []
    for f in range(count_fsdp):
        for z in range(count_seq):
            c, z1 = f % 2, z // 2
            pairs.append((f * count_seq + z, (f - c + z1) * count_seq + c * 2 + z % 2))
    return pairs


def rank_tables(length_row, count):
    places = jnp.arange(count, dtype=jnp.int32)
    segment, positions = layout(length_row, places)
    allowed = (segment[:, None] == segment[None, :]) & (places[None, :] <= places[:, None])
    cosines, sines = tables(positions)
    return allowed, cosines, sines


def rank_scores(q, k, allowed):
    return attention_scores(q, k, allowed)


def attention_forward(residual, gain, w_qkv, w_out, allowed, cosines, sines):
    normed = normalize(residual)
    own = (normed * gain).astype(BF)
    every = share_rows(own, 4).reshape(-1, D)
    count = every.shape[0]
    qkv = product(every, w_qkv)
    split = Q_RANK * HEAD_SIZE
    q = apply_rotary(qkv[:, :split].reshape(count, Q_RANK, HEAD_SIZE), cosines, sines).astype(BF)
    k = apply_rotary(
        qkv[:, split : split + KV_RANK * HEAD_SIZE].reshape(count, KV_RANK, HEAD_SIZE), cosines, sines
    ).astype(BF)
    v = qkv[:, split + KV_RANK * HEAD_SIZE :].reshape(count, KV_RANK, HEAD_SIZE).astype(BF)
    q = q.reshape(count, KV_RANK, Q_RANK // KV_RANK, HEAD_SIZE)
    scores = attention_scores(q, k, allowed)
    row_max = jnp.max(scores, axis=-1, keepdims=True)
    shifted = jnp.exp(scores - row_max)
    row_sum = jnp.sum(shifted, axis=-1, keepdims=True)
    log_total = row_max + jnp.log(row_sum)
    weights = (shifted / row_sum).astype(BF)
    attended = jnp.einsum("grqk,kgd->qgrd", weights, v, preferred_element_type=F32)
    attended = attended.reshape(count, split).astype(BF)
    terms = product(attended, w_out).astype(BF).reshape(4, -1, D)
    middle = residual + sum_rows(terms, 5)
    return middle, (residual, every, q, k, v, log_total, attended)


def feed_forward(middle, gain, w_gateup, w_down):
    own = (normalize(middle) * gain).astype(BF)
    every = share_rows(own, 4).reshape(-1, D)
    gate_up = product(every, w_gateup)
    wide = gate_up.shape[1] // 2
    gate, up = gate_up[:, :wide], gate_up[:, wide:]
    hidden = (jax.nn.silu(gate) * up).astype(BF)
    terms = product(hidden, w_down).astype(BF).reshape(4, -1, D)
    return middle + sum_rows(terms, 5), (middle, every, gate, up, hidden)


def feed_backward(grad, gain, w_gateup, w_down, kept):
    middle, every, gate, up, hidden = kept
    e = share_rows(grad.astype(BF), 4).reshape(-1, D)
    grad_down = jnp.einsum("tf,td->fd", hidden, e, preferred_element_type=F32).astype(BF)
    grad_hidden = jnp.einsum("td,fd->tf", e, w_down, preferred_element_type=F32)
    sigmoid = jax.nn.sigmoid(gate)
    grad_gate = grad_hidden * up * sigmoid * (1.0 + gate * (1.0 - sigmoid))
    grad_up = grad_hidden * gate * sigmoid
    pair = jnp.concatenate([grad_gate, grad_up], axis=1).astype(BF)
    grad_gateup = jnp.einsum("td,tf->df", every, pair, preferred_element_type=F32).astype(BF)
    terms = jnp.einsum("tf,df->td", pair, w_gateup, preferred_element_type=F32).astype(BF)
    grad_input = sum_rows(terms.reshape(4, -1, D), 5)
    normed = normalize(middle)
    grad_gain = jnp.sum(grad_input * normed, axis=0)
    return grad + norm_back(grad_input * gain, normed, middle), grad_gateup, grad_down, grad_gain


def attention_backward(grad, gain, w_qkv, w_out, kept, allowed, cosines, sines):
    residual, every, q, k, v, log_total, attended = kept
    e = share_rows(grad.astype(BF), 4).reshape(-1, D)
    count = e.shape[0]
    grad_out = jnp.einsum("te,td->ed", attended, e, preferred_element_type=F32).astype(BF)
    grad_attended = jnp.einsum("td,ed->te", e, w_out, preferred_element_type=F32).astype(BF)
    grad_attended = grad_attended.reshape(count, KV_RANK, Q_RANK // KV_RANK, HEAD_SIZE)
    weights = jnp.exp(attention_scores(q, k, allowed) - log_total)
    grad_v = jnp.einsum("grqk,qgrd->kgd", weights.astype(BF), grad_attended, preferred_element_type=F32)
    grad_weights = jnp.einsum("qgrd,kgd->grqk", grad_attended, v, preferred_element_type=F32)
    inner = jnp.sum(weights * grad_weights, axis=-1, keepdims=True)
    grad_scores = (weights * (grad_weights - inner)).astype(BF)
    scale = HEAD_SIZE ** (-0.5)
    grad_q = jnp.einsum("grqk,kgd->qgrd", grad_scores, k, preferred_element_type=F32) * scale
    grad_k = jnp.einsum("grqk,qgrd->kgd", grad_scores, q, preferred_element_type=F32) * scale
    grad_q = invert_rotary(grad_q.reshape(count, Q_RANK, HEAD_SIZE), cosines, sines).reshape(count, -1)
    grad_k = invert_rotary(grad_k, cosines, sines).reshape(count, -1)
    rows = jnp.concatenate([grad_q, grad_k, grad_v.reshape(count, -1)], axis=1).astype(BF)
    grad_qkv = jnp.einsum("td,tf->df", every, rows, preferred_element_type=F32).astype(BF)
    terms = jnp.einsum("tf,df->td", rows, w_qkv, preferred_element_type=F32).astype(BF)
    grad_input = sum_rows(terms.reshape(4, -1, D), 5)
    normed = normalize(residual)
    grad_gain = jnp.sum(grad_input * normed, axis=0)
    return grad + norm_back(grad_input * gain, normed, residual), grad_qkv, grad_out, grad_gain


def fast_shards(
    tokens, cotangent, lengths, w_qkv, w_out, w_gateup, w_down, norm_gains, *moments
):
    axes = ("fsdp", "seq")
    pairs = swap_pairs(lax.axis_size("fsdp"), lax.axis_size("seq"))
    tokens = lax.ppermute(tokens, axes, pairs)
    lengths = lax.ppermute(lengths, axes, pairs)
    cotangent = lax.ppermute(cotangent, axes, pairs)
    allowed, cosines, sines = rank_tables(lengths[0], 4 * tokens.shape[0])
    rows, owned = w_qkv.shape[1], norm_gains.shape[2]
    own_gains = jnp.pad(
        norm_gains.reshape(2 * LAYERS, owned).astype(BF), ((0, 16 - 2 * LAYERS), (0, lane_width - owned))
    )
    weights = []
    for l in range(LAYERS):
        got = gather_attention(pack_qkv(w_qkv[l]), w_out[l].astype(BF), own_gains if l == 0 else None, l)
        if l == 0:
            all_gains = got[2][:, : 2 * LAYERS, :owned].transpose(1, 0, 2).reshape(LAYERS, 2, D).astype(F32)
        gu, down = gather_feed(pack_gateup(w_gateup[l]), w_down[l].astype(BF).reshape(2, -1, D), 2)
        weights.append((got[0].reshape(D, -1), got[1].reshape(-1, D), gu.reshape(D, -1), down.reshape(-1, D)))
    residual = tokens.astype(F32)
    kept = []
    for l in range(LAYERS):
        qkv, out, gateup, down = weights[l]
        residual, first = attention_forward(residual, all_gains[l, 0], qkv, out, allowed, cosines, sines)
        residual, second = feed_forward(residual, all_gains[l, 1], gateup, down)
        kept.append((first, second))
    layer_output = lax.ppermute(residual.astype(BF), axes, pairs)
    grad = cotangent.astype(F32)
    updates = [None] * LAYERS
    gain_terms = [None] * LAYERS
    for l in reversed(range(LAYERS)):
        qkv, out, gateup, down = weights[l]
        grad, g_gateup, g_down, gain_two = feed_backward(grad, all_gains[l, 1], gateup, down, kept[l][1])
        grad, g_qkv, g_out, gain_one = attention_backward(
            grad, all_gains[l, 0], qkv, out, kept[l][0], allowed, cosines, sines
        )
        gain_terms[l] = jnp.stack([gain_one, gain_two])
        feed = reduce_feed(g_gateup.reshape(16, 2 * rows, -1), g_down.reshape(16, -1, D), 3)
        terms = None
        if l == 0:
            terms = jnp.concatenate(gain_terms).reshape(2 * LAYERS, -1, owned).transpose(1, 0, 2)
            terms = jnp.pad(terms, ((0, 0), (0, 8 - 2 * LAYERS), (0, lane_width - owned)))
        heads = reduce_attention(
            g_qkv.reshape(16, 2 * rows, -1), g_out.reshape(4, 2 * rows, D), terms, 6 + (l == 0)
        )
        updates[l] = (
            unpack_qkv(heads[0]).astype(F32),
            heads[1].astype(F32),
            unpack_gateup(feed[0]).astype(F32),
            feed[1].reshape(-1, D).astype(F32),
        )
    grad_gains = heads[2][: 2 * LAYERS, :owned].reshape(LAYERS, 2, owned)
    input_grad = lax.ppermute(grad.astype(BF), axes, pairs).astype(F32)
    step_rates = (D ** (-0.5), 4.0 * D ** (-0.5), D ** (-0.5), FF ** (-0.5), 0.5)
    shrinks = (decay_rate, decay_rate, decay_rate, decay_rate, 0.0)
    stacked = (w_qkv, w_out, w_gateup, w_down, norm_gains)
    results = []
    for kind in range(5):
        grads = grad_gains if kind == 4 else jnp.stack([updates[l][kind] for l in range(LAYERS)])
        results.append(
            adam_step(stacked[kind], grads, moments[kind], moments[5 + kind], step_rates[kind], shrinks[kind])
        )
    return (layer_output, input_grad) + tuple(results[kind][part] for part in range(3) for kind in range(5))


def solution(mesh):
    in_specs = (
        P(("fsdp", "seq"), None),
        P(("fsdp", "seq"), None),
        P("fsdp", None),
        P(None, ("fsdp", "seq"), None),
        P(None, ("fsdp", "seq"), None),
        P(None, ("fsdp", "seq"), None),
        P(None, ("fsdp", "seq"), None),
        P(None, None, ("fsdp", "seq")),
        P(None, ("fsdp", "seq"), None),
        P(None, ("fsdp", "seq"), None),
        P(None, ("fsdp", "seq"), None),
        P(None, ("fsdp", "seq"), None),
        P(None, None, ("fsdp", "seq")),
        P(None, ("fsdp", "seq"), None),
        P(None, ("fsdp", "seq"), None),
        P(None, ("fsdp", "seq"), None),
        P(None, ("fsdp", "seq"), None),
        P(None, None, ("fsdp", "seq")),
    )
    out_specs = (
        P(("fsdp", "seq"), None),
        P(("fsdp", "seq"), None),
        P(None, ("fsdp", "seq"), None),
        P(None, ("fsdp", "seq"), None),
        P(None, ("fsdp", "seq"), None),
        P(None, ("fsdp", "seq"), None),
        P(None, None, ("fsdp", "seq")),
        P(None, ("fsdp", "seq"), None),
        P(None, ("fsdp", "seq"), None),
        P(None, ("fsdp", "seq"), None),
        P(None, ("fsdp", "seq"), None),
        P(None, None, ("fsdp", "seq")),
        P(None, ("fsdp", "seq"), None),
        P(None, ("fsdp", "seq"), None),
        P(None, ("fsdp", "seq"), None),
        P(None, ("fsdp", "seq"), None),
        P(None, None, ("fsdp", "seq")),
    )
    whole_tiles = (D // mesh.size) % 16 == 0 and mesh.shape["seq"] == 4 and mesh.size == 32
    body = fast_shards if whole_tiles else shards
    return jax.shard_map(body, mesh=mesh, in_specs=in_specs, out_specs=out_specs, check_vma=False)
```

```python
import functools

import jax
import jax.numpy as jnp
from jax import lax
from jax.experimental import pallas as pl
from jax.experimental.pallas import tpu as pltpu
from jax.sharding import PartitionSpec as P

D = 1536
QUERY_HEAD_COUNT = 16
KEY_VALUE_HEADS = 8
HEAD_SIZE = 96
FF = 4096
LAYERS = 2
STEP = 6


eps_norm = 1e-05
rope_base = 100000.0
beta_one = 0.9
beta_two = 0.95
adam_eps = 1e-08
decay_rate = 0.1
masked_score = -1e30
lane_width = 128


def layout(length_row, places):
    seq_ends = jnp.cumsum(length_row, dtype=jnp.int32)
    passed = (places[:, None] >= seq_ends[None, :]).astype(jnp.int32)
    segment = jnp.sum(passed, axis=1, dtype=jnp.int32)
    begins = jnp.sum(passed * length_row[None, :], axis=1, dtype=jnp.int32)
    return (segment, places - begins)


def tables(positions):
    freq_index = jnp.arange(HEAD_SIZE // 2, dtype=jnp.float32)
    inverse = rope_base ** (-2.0 * freq_index / HEAD_SIZE)
    angles = positions.astype(jnp.float32)[:, None] * inverse[None, :]
    angles = jnp.concatenate([angles, angles], axis=-1)
    return (jnp.cos(angles)[:, None, :], jnp.sin(angles)[:, None, :])


def apply_rotary(values, rotary_cosines, rotary_sines):
    half_width = values.shape[-1] // 2
    turned = jnp.concatenate([-values[..., half_width:], values[..., :half_width]], axis=-1)
    return values * rotary_cosines + turned * rotary_sines


def invert_rotary(values, rotary_cosines, rotary_sines):
    half_width = values.shape[-1] // 2
    scaled_sine = values * rotary_sines
    turned = jnp.concatenate(
        [scaled_sine[..., half_width:], -scaled_sine[..., :half_width]], axis=-1
    )
    return values * rotary_cosines + turned


def normalize(residual):
    return residual * lax.rsqrt(jnp.mean(residual * residual, axis=-1, keepdims=True) + eps_norm)


def norm_back(grad_normed, normed, residual):
    inverse = lax.rsqrt(jnp.mean(residual * residual, axis=-1, keepdims=True) + eps_norm)
    return inverse * (grad_normed - normed * jnp.mean(grad_normed * normed, axis=-1, keepdims=True))


def product(lhs_matrix, rhs_matrix):
    return jnp.dot(lhs_matrix, rhs_matrix, preferred_element_type=jnp.float32)


def attention_scores(query_head_rows, key_head_rows, allowed):
    scores = jnp.einsum(
        "qgrd,kgd->grqk", query_head_rows, key_head_rows, preferred_element_type=jnp.float32
    ) * HEAD_SIZE ** (-0.5)
    return jnp.where(allowed[None, None], scores, masked_score)


def wire_pieces(stacked, layer_index):
    return tuple((shard_piece[layer_index].astype(jnp.bfloat16) for shard_piece in stacked))


def fetch_forward(stacked, layer_index):
    qkv_piece, out_piece, gateup_piece, down_piece, gain_piece = wire_pieces(stacked, layer_index)
    return (
        lax.all_gather(qkv_piece, ("fsdp", "seq"), axis=0, tiled=True),
        lax.all_gather(out_piece, ("fsdp", "seq"), axis=0, tiled=True),
        lax.all_gather(gateup_piece, ("fsdp", "seq"), axis=0, tiled=True),
        lax.all_gather(down_piece, ("fsdp", "seq"), axis=0, tiled=True),
        lax.all_gather(gain_piece, ("fsdp", "seq"), axis=1, tiled=True),
    )


def fetch_backward(stacked, layer_index):
    qkv_piece, out_piece, gateup_piece, down_piece, gain_piece = wire_pieces(stacked, layer_index)
    return (
        lax.all_gather(qkv_piece, ("fsdp", "seq"), axis=0, tiled=True),
        lax.all_gather(out_piece, ("fsdp", "seq"), axis=0, tiled=True),
        lax.all_gather(gateup_piece, ("fsdp", "seq"), axis=0, tiled=True),
        lax.all_gather(down_piece, ("fsdp", "seq"), axis=0, tiled=True),
        lax.all_gather(gain_piece, ("fsdp", "seq"), axis=1, tiled=True),
    )


def flat_lanes(matrix):
    return matrix.reshape(-1, lane_width)


def reduce_grads(grad_terms):
    grad_qkv, grad_out_proj, grad_gateup, grad_down, grad_gains = grad_terms
    widths = (grad_qkv.shape[1], grad_out_proj.shape[1], grad_gateup.shape[1], grad_down.shape[1])
    flat_qkv = flat_lanes(grad_qkv)
    flat_out = flat_lanes(grad_out_proj)
    flat_gateup = flat_lanes(grad_gateup)
    flat_down = flat_lanes(grad_down)
    summed = (
        lax.psum_scatter(flat_qkv, ("fsdp", "seq"), scatter_dimension=0, tiled=True),
        lax.psum_scatter(flat_out, ("fsdp", "seq"), scatter_dimension=0, tiled=True),
        lax.psum_scatter(flat_gateup, ("fsdp", "seq"), scatter_dimension=0, tiled=True),
        lax.psum_scatter(flat_down, ("fsdp", "seq"), scatter_dimension=0, tiled=True),
        lax.psum_scatter(grad_gains, ("fsdp", "seq"), scatter_dimension=1, tiled=True),
    )
    owned = tuple((summed[kind_index].reshape(-1, widths[kind_index]) for kind_index in range(4)))
    return owned + (summed[4],)


def layer_forward(residual, gathered, allowed, rotary_cosines, rotary_sines):
    w_qkv, w_out, w_gateup, w_down, gain_pair = gathered
    count_of_rows = residual.shape[0]
    heads_per_group = QUERY_HEAD_COUNT // KEY_VALUE_HEADS
    gain_float = gain_pair.astype(jnp.float32)
    normed_one = normalize(residual)
    input_one = (normed_one * gain_float[0]).astype(jnp.bfloat16)
    query_key_value_rows = product(input_one, w_qkv)
    query_head_rows = apply_rotary(
        query_key_value_rows[:, : QUERY_HEAD_COUNT * HEAD_SIZE].reshape(
            count_of_rows, QUERY_HEAD_COUNT, HEAD_SIZE
        ),
        rotary_cosines,
        rotary_sines,
    ).astype(jnp.bfloat16)
    key_row_block = apply_rotary(
        query_key_value_rows[
            :, QUERY_HEAD_COUNT * HEAD_SIZE : (QUERY_HEAD_COUNT + KEY_VALUE_HEADS) * HEAD_SIZE
        ].reshape(count_of_rows, KEY_VALUE_HEADS, HEAD_SIZE),
        rotary_cosines,
        rotary_sines,
    ).astype(jnp.bfloat16)
    value_row_block = query_key_value_rows[
        :, (QUERY_HEAD_COUNT + KEY_VALUE_HEADS) * HEAD_SIZE :
    ].astype(jnp.bfloat16)
    every_key, every_value = (
        lax.all_gather(
            key_row_block.reshape(count_of_rows, KEY_VALUE_HEADS * HEAD_SIZE),
            "seq",
            axis=0,
            tiled=True,
        ),
        lax.all_gather(value_row_block, "seq", axis=0, tiled=True),
    )
    key_head_rows = every_key.reshape(-1, KEY_VALUE_HEADS, HEAD_SIZE)
    value_head_rows = every_value.reshape(-1, KEY_VALUE_HEADS, HEAD_SIZE)
    query_head_rows = query_head_rows.reshape(
        count_of_rows, KEY_VALUE_HEADS, heads_per_group, HEAD_SIZE
    )
    scores = attention_scores(query_head_rows, key_head_rows, allowed)
    row_max = jnp.max(scores, axis=-1, keepdims=True)
    shifted = jnp.exp(scores - row_max)
    row_sum = jnp.sum(shifted, axis=-1, keepdims=True)
    log_total = row_max + jnp.log(row_sum)
    attn_weights = (shifted / row_sum).astype(jnp.bfloat16)
    attended = jnp.einsum(
        "grqk,kgd->qgrd", attn_weights, value_head_rows, preferred_element_type=jnp.float32
    )
    attended = attended.reshape(count_of_rows, QUERY_HEAD_COUNT * HEAD_SIZE).astype(jnp.bfloat16)
    middle = residual + product(attended, w_out)
    normed_two = normalize(middle)
    input_two = (normed_two * gain_float[1]).astype(jnp.bfloat16)
    gate_up = product(input_two, w_gateup)
    gate_pre = gate_up[:, :FF]
    up_proj = gate_up[:, FF:]
    hidden = (jax.nn.silu(gate_pre) * up_proj).astype(jnp.bfloat16)
    layer_out = middle + product(hidden, w_down)
    saved_layer = (
        residual,
        normed_one,
        input_one,
        query_head_rows,
        key_head_rows,
        value_head_rows,
        log_total,
        attended,
        middle,
        normed_two,
        input_two,
        gate_pre,
        up_proj,
        hidden,
    )
    return (saved_layer, layer_out)


def layer_backward(grad_out, saved_layer, gathered, allowed, rotary_cosines, rotary_sines):
    w_qkv, w_out, w_gateup, w_down, gain_pair = gathered
    (
        residual,
        normed_one,
        input_one,
        query_head_rows,
        key_head_rows,
        value_head_rows,
        log_total,
        attended,
        middle,
        normed_two,
        input_two,
        gate_pre,
        up_proj,
        hidden,
    ) = saved_layer
    count_of_rows = grad_out.shape[0]
    heads_per_group = QUERY_HEAD_COUNT // KEY_VALUE_HEADS
    gain_float = gain_pair.astype(jnp.float32)
    grad_branch = grad_out.astype(jnp.bfloat16)
    grad_down = jnp.einsum("tf,td->fd", hidden, grad_branch, preferred_element_type=jnp.float32)
    grad_hidden = jnp.einsum("td,fd->tf", grad_branch, w_down, preferred_element_type=jnp.float32)
    sigmoid_gate = jax.nn.sigmoid(gate_pre)
    grad_gate = grad_hidden * up_proj * sigmoid_gate * (1.0 + gate_pre * (1.0 - sigmoid_gate))
    grad_up = grad_hidden * gate_pre * sigmoid_gate
    grad_pair = jnp.concatenate([grad_gate, grad_up], axis=1).astype(jnp.bfloat16)
    grad_gateup = jnp.einsum("td,tf->df", input_two, grad_pair, preferred_element_type=jnp.float32)
    grad_input_two = jnp.einsum(
        "tf,df->td", grad_pair, w_gateup, preferred_element_type=jnp.float32
    )
    grad_gain_two = jnp.sum(grad_input_two * normed_two, axis=0)
    grad_middle = grad_out + norm_back(grad_input_two * gain_float[1], normed_two, middle)
    grad_branch_two = grad_middle.astype(jnp.bfloat16)
    grad_out_proj = jnp.einsum(
        "te,td->ed", attended, grad_branch_two, preferred_element_type=jnp.float32
    )
    attended_gradient = jnp.einsum(
        "td,ed->te", grad_branch_two, w_out, preferred_element_type=jnp.float32
    )
    attended_gradient = attended_gradient.astype(jnp.bfloat16).reshape(
        count_of_rows, KEY_VALUE_HEADS, heads_per_group, HEAD_SIZE
    )
    scores = attention_scores(query_head_rows, key_head_rows, allowed)
    attn_float = jnp.exp(scores - log_total)
    value_gradient = jnp.einsum(
        "grqk,qgrd->kgd",
        attn_float.astype(jnp.bfloat16),
        attended_gradient,
        preferred_element_type=jnp.float32,
    )
    grad_weights = jnp.einsum(
        "qgrd,kgd->grqk", attended_gradient, value_head_rows, preferred_element_type=jnp.float32
    )
    inner_sum = jnp.sum(attn_float * grad_weights, axis=-1, keepdims=True)
    grad_scores = (attn_float * (grad_weights - inner_sum)).astype(jnp.bfloat16)
    grad_query = jnp.einsum(
        "grqk,kgd->qgrd", grad_scores, key_head_rows, preferred_element_type=jnp.float32
    ) * HEAD_SIZE ** (-0.5)
    gradient_keys = jnp.einsum(
        "grqk,qgrd->kgd", grad_scores, query_head_rows, preferred_element_type=jnp.float32
    ) * HEAD_SIZE ** (-0.5)
    shared_keys, value_share = (
        lax.psum_scatter(
            gradient_keys.reshape(-1, KEY_VALUE_HEADS * HEAD_SIZE).astype(jnp.bfloat16),
            "seq",
            scatter_dimension=0,
            tiled=True,
        ).astype(jnp.float32),
        lax.psum_scatter(
            value_gradient.reshape(-1, KEY_VALUE_HEADS * HEAD_SIZE).astype(jnp.bfloat16),
            "seq",
            scatter_dimension=0,
            tiled=True,
        ).astype(jnp.float32),
    )
    grad_q = invert_rotary(
        grad_query.reshape(count_of_rows, QUERY_HEAD_COUNT, HEAD_SIZE), rotary_cosines, rotary_sines
    ).reshape(count_of_rows, QUERY_HEAD_COUNT * HEAD_SIZE)
    key_gradient = invert_rotary(
        shared_keys.reshape(count_of_rows, KEY_VALUE_HEADS, HEAD_SIZE), rotary_cosines, rotary_sines
    ).reshape(count_of_rows, KEY_VALUE_HEADS * HEAD_SIZE)
    grad_rows = jnp.concatenate([grad_q, key_gradient, value_share], axis=1).astype(jnp.bfloat16)
    grad_qkv = jnp.einsum("td,tf->df", input_one, grad_rows, preferred_element_type=jnp.float32)
    grad_input_one = jnp.einsum("tf,df->td", grad_rows, w_qkv, preferred_element_type=jnp.float32)
    grad_gain_one = jnp.sum(grad_input_one * normed_one, axis=0)
    grad_in = grad_middle + norm_back(grad_input_one * gain_float[0], normed_one, residual)
    return (
        grad_in,
        (
            grad_qkv,
            grad_out_proj,
            grad_gateup,
            grad_down,
            jnp.stack([grad_gain_one, grad_gain_two]),
        ),
    )


def adam_step(weight, gradient, first_moment, second_moment, step_rate, shrink):
    first_moment = beta_one * first_moment + (1.0 - beta_one) * gradient
    second_moment = beta_two * second_moment + (1.0 - beta_two) * gradient * gradient
    first_hat = first_moment / (1.0 - beta_one**STEP)
    second_hat = second_moment / (1.0 - beta_two**STEP)
    weight = weight - step_rate * (first_hat / (jnp.sqrt(second_hat) + adam_eps) + shrink * weight)
    return (weight, first_moment, second_moment)


def shards(
    tokens,
    cotangent,
    lengths,
    w_qkv,
    w_out,
    w_gateup,
    w_down,
    norm_gains,
    first_qkv,
    first_out,
    first_gateup,
    first_down,
    first_gains,
    second_qkv,
    second_out,
    second_gateup,
    second_down,
    second_gains,
):
    count_of_rows = tokens.shape[0]
    group_rows = count_of_rows * lax.axis_size("seq")
    place_rows = lax.axis_index("seq") * count_of_rows + jnp.arange(count_of_rows, dtype=jnp.int32)
    key_places = jnp.arange(group_rows, dtype=jnp.int32)
    seg_rows, positions = layout(lengths[0], place_rows)
    seg_keys = layout(lengths[0], key_places)[0]
    allowed = (seg_rows[:, None] == seg_keys[None, :]) & (
        key_places[None, :] <= place_rows[:, None]
    )
    rotary_cosines, rotary_sines = tables(positions)
    stacked = (w_qkv, w_out, w_gateup, w_down, norm_gains)
    residual = tokens.astype(jnp.float32)
    saved_all = []
    for layer_index in range(LAYERS):
        gathered = fetch_forward(stacked, layer_index)
        saved_layer, residual = layer_forward(
            residual, gathered, allowed, rotary_cosines, rotary_sines
        )
        saved_all.append(saved_layer)
    grad_state = cotangent.astype(jnp.float32)
    updates = [None] * LAYERS
    for layer_index in reversed(range(LAYERS)):
        gathered = fetch_backward(stacked, layer_index)
        grad_state, grad_terms = layer_backward(
            grad_state, saved_all[layer_index], gathered, allowed, rotary_cosines, rotary_sines
        )
        updates[layer_index] = reduce_grads(grad_terms)
    step_rates = (D ** (-0.5), 4.0 * D ** (-0.5), D ** (-0.5), FF ** (-0.5), 0.5)
    shrinks = (decay_rate, decay_rate, decay_rate, decay_rate, 0.0)
    firsts = (first_qkv, first_out, first_gateup, first_down, first_gains)
    seconds = (second_qkv, second_out, second_gateup, second_down, second_gains)
    new_weights = []
    new_firsts = []
    new_seconds = []
    for kind_index in range(5):
        grads_kind = jnp.stack([updates[layer_index][kind_index] for layer_index in range(LAYERS)])
        weight, first_moment, second_moment = adam_step(
            stacked[kind_index],
            grads_kind,
            firsts[kind_index],
            seconds[kind_index],
            step_rates[kind_index],
            shrinks[kind_index],
        )
        new_weights.append(weight)
        new_firsts.append(first_moment)
        new_seconds.append(second_moment)
    outputs = [residual.astype(jnp.bfloat16), grad_state] + new_weights + new_firsts + new_seconds
    return tuple(outputs)


MESH = pl.DeviceIdType.MESH
BF = jnp.bfloat16
F32 = jnp.float32
KV_RANK = KEY_VALUE_HEADS // 4
Q_RANK = QUERY_HEAD_COUNT // 4
ANY = pl.BlockSpec(memory_space=pl.ANY)
VM = pl.BlockSpec(memory_space=pltpu.VMEM)
DMA = pltpu.SemaphoreType.DMA


class Place:
    def __init__(self):
        f, z = lax.axis_index("fsdp"), lax.axis_index("seq")
        self.y, self.x, self.c = lax.div(f, 4), lax.rem(lax.div(f, 2), 2), lax.rem(f, 2)
        self.z1, self.z0 = lax.div(z, 2), lax.rem(z, 2)
        self.rank = 2 * self.c + self.z0
        self.peer = {
            "y": (f + 4 - 8 * self.y, z),
            "x": (f + 2 - 4 * self.x, z),
            "c": (f + 1 - 2 * self.c, z),
            "z1": (f, z + 2 - 4 * self.z1),
            "z0": (f, z + 1 - 2 * self.z0),
            "cz": (f + 1 - 2 * self.c, z + 1 - 2 * self.z0),
        }


def greet(place, names):
    barrier = pltpu.get_barrier_semaphore()
    for name in names:
        pl.semaphore_signal(barrier, inc=1, device_id=place.peer[name], device_id_type=MESH)
    pl.semaphore_wait(barrier, len(names))


def remote(src, dst, send_sem, recv_sem, device):
    return pltpu.make_async_remote_copy(
        src_ref=src, dst_ref=dst, send_sem=send_sem, recv_sem=recv_sem, device_id=device, device_id_type=MESH
    )


def columns_index(y, x, z1, h):
    return ((y * 2 + x) * 2 + h) * 2 + z1


def rows_index(y, x, z1, h):
    return ((y * 2 + x) * 2 + z1) * 2 + h


class Gather:
    def __init__(self, place, ref, index, send, recv, src=None, local=None):
        self.p, self.ref, self.index, self.send, self.recv = place, ref, index, send, recv
        self.src, self.local = src, local

    def at(self, flips, h):
        p = self.p
        flip = lambda v, name: 1 - v if name in flips else v
        return self.ref.at[self.index(flip(p.y, "y"), flip(p.x, "x"), flip(p.z1, "z1"), h)]

    def route(self, h):
        a, b = ("y", "x") if h == 0 else ("x", "y")
        return (
            ("z1", ()),
            (a, ()),
            (a, ("z1",)),
            (b, ()),
            (b, ("z1",)),
            (b, (a,)),
            (b, (a, "z1")),
        )

    def out(self, h, m):
        axis, flips = self.route(h)[m]
        dst = self.at(flips, h)
        src = self.src.at[h] if self.src is not None and not flips else dst
        return remote(src, dst, self.send.at[7 * h + m], self.recv.at[7 * h + m], self.p.peer[axis])

    def into(self, h, m):
        axis, flips = self.route(h)[m]
        ref = self.at(flips + (axis,), h)
        return remote(ref, ref, self.send.at[7 * h + m], self.recv.at[7 * h + m], self.p.peer[axis])

    def own(self, h):
        return pltpu.make_async_copy(self.src.at[h], self.at((), h), self.local.at[h])

    def first(self, messages):
        for m in messages:
            for h in (0, 1):
                self.out(h, m).start()
        if self.src is not None and 0 not in messages:
            for h in (0, 1):
                self.own(h).start()

    def on(self, h, got, gives):
        self.into(h, got).wait_recv()
        for m in gives:
            self.out(h, m).start()

    def last(self):
        for h in (0, 1):
            for m in (3, 4, 5, 6):
                self.into(h, m).wait_recv()
            for m in range(7):
                self.out(h, m).wait_send()
            if self.src is not None:
                self.own(h).wait()


class Spread:
    def __init__(self, place, src, target, send, recv, local):
        self.p, self.src, self.target, self.send, self.recv, self.local = place, src, target, send, recv, local

    def copy(self, k, arriving=False):
        p = self.p
        name, fc, fz = (("c", 1, 0), ("z0", 0, 1), ("cz", 1, 1))[k]
        c = 1 - p.c if fc else p.c
        z0 = 1 - p.z0 if fz else p.z0
        src = self.src(c, z0)
        dst = self.target(c, z0) if arriving else self.target(p.c, p.z0)
        return remote(src, dst, self.send.at[k], self.recv.at[k], p.peer[name])

    def own(self):
        p = self.p
        return pltpu.make_async_copy(self.src(p.c, p.z0), self.target(p.c, p.z0), self.local)

    def start(self):
        for k in range(3):
            self.copy(k).start()
        self.own().start()

    def wait(self):
        for k in range(3):
            self.copy(k, True).wait_recv()
        self.own().wait()

    def finish(self):
        for k in range(3):
            self.copy(k).wait_send()


def add_to(dst, src):
    dst[...] = (dst[...].astype(F32) + src[...].astype(F32)).astype(dst.dtype)


class Reduce:
    def __init__(self, place, ref, index, out, mine, one, two, three, send, recv, local):
        self.p, self.ref, self.index, self.result = place, ref, index, out
        self.mine, self.one, self.two, self.three = mine, one, two, three
        self.send, self.recv, self.local = send, recv, local

    def block(self, h, far_a, m):
        p = self.p
        a, b = (p.x, p.y) if h == 0 else (p.y, p.x)
        a = 1 - a if far_a else a
        b = 1 - b if m < 2 else b
        z1 = 1 - p.z1 if m % 2 == 0 else p.z1
        y, x = (b, a) if h == 0 else (a, b)
        return self.ref.at[self.index(y, x, z1, h)]

    def copy(self, h, m):
        p = self.p
        name_a, name_b = ("x", "y") if h == 0 else ("y", "x")
        sems = self.send.at[7 * h + m], self.recv.at[7 * h + m]
        if m < 4:
            return remote(self.block(h, True, m), self.one.at[h, m], *sems, p.peer[name_a])
        if m < 6:
            return remote(self.one.at[h, m - 4], self.two.at[h, m - 4], *sems, p.peer[name_b])
        return remote(self.two.at[h, 0], self.three.at[h], *sems, p.peer["z1"])

    def load(self, h, m):
        return pltpu.make_async_copy(self.block(h, False, m), self.mine.at[h, m], self.local.at[4 * h + m])

    def first(self):
        for m in range(4):
            for h in (0, 1):
                self.copy(h, m).start()
                self.load(h, m).start()

    def second(self, h, m):
        self.copy(h, m).wait_recv()
        self.load(h, m).wait()
        add_to(self.one.at[h, m], self.mine.at[h, m])
        if m < 2:
            self.copy(h, 4 + m).start()

    def third(self, h, k):
        self.copy(h, 4 + k).wait_recv()
        add_to(self.two.at[h, k], self.one.at[h, 2 + k])
        if k == 0:
            self.copy(h, 6).start()

    def fourth(self, h):
        self.copy(h, 6).wait_recv()
        add_to(self.three.at[h], self.two.at[h, 1])

    def finish(self):
        for h in (0, 1):
            for m in range(7):
                self.copy(h, m).wait_send()

    def store(self):
        return pltpu.make_async_copy(self.three, self.result, self.local.at[8])


def out_gather_steps(p, src, ref, send, recv, local):
    home = p.x == p.z0
    here = p.y * 2 + p.z1
    at = lambda fy, fz: ref.at[(1 - p.y if fy else p.y) * 2 + (1 - p.z1 if fz else p.z1)]
    pair = lambda half: remote(src, ref.at[here, half], send.at[0], recv.at[0], p.peer["z0"])
    z1_copy = lambda fz: remote(at(0, fz), at(0, fz), send.at[1], recv.at[1], p.peer["z1"])
    y_copy = lambda k, fy: remote(at(fy, k), at(fy, k), send.at[2 + k], recv.at[2 + k], p.peer["y"])
    x_copy = lambda k: remote(at(k // 2, k % 2), at(k // 2, k % 2), send.at[4 + k], recv.at[4 + k], p.peer["x"])
    own = pltpu.make_async_copy(src, ref.at[here, p.z0], local)

    def zero():
        @pl.when(home)
        def _():
            own.start()

        @pl.when(jnp.logical_not(home))
        def _():
            pair(p.z0).start()

    def one():
        @pl.when(home)
        def _():
            own.wait()
            pair(1 - p.z0).wait_recv()
            z1_copy(0).start()
            y_copy(0, 0).start()
            x_copy(0).start()

    def two():
        @pl.when(home)
        def _():
            z1_copy(1).wait_recv()
            y_copy(1, 0).start()
            x_copy(1).start()

    def three():
        @pl.when(home)
        def _():
            for k in (0, 1):
                y_copy(k, 1).wait_recv()
                x_copy(2 + k).start()

    def last():
        @pl.when(home)
        def _():
            z1_copy(0).wait_send()
            for k in (0, 1):
                y_copy(k, 0).wait_send()
            for k in range(4):
                x_copy(k).wait_send()

        @pl.when(jnp.logical_not(home))
        def _():
            pair(p.z0).wait_send()
            for k in range(4):
                x_copy(k).wait_recv()

    return [zero, one, two, three, last]


def out_reduce_steps(p, ref, out, mine, one, two, three, got, send, recv, local):
    home = p.x == p.z0
    away = jnp.logical_not(home)
    x_copy = lambda k: remote(ref.at[k], one.at[k], send.at[k], recv.at[k], p.peer["x"])
    y_copy = lambda k: remote(one.at[(1 - p.y) * 2 + k], two.at[k], send.at[4 + k], recv.at[4 + k], p.peer["y"])
    z1_copy = remote(two.at[1 - p.z1], three, send.at[6], recv.at[6], p.peer["z1"])
    rows = three.shape[0] // 2
    half = lambda z0: three.at[pl.ds(pl.multiple_of(z0 * rows, rows), rows)]
    pair = remote(half(1 - p.z0), got, send.at[7], recv.at[7], p.peer["z0"])
    load = lambda k: pltpu.make_async_copy(ref.at[k], mine.at[k], local.at[k])
    keep = pltpu.make_async_copy(half(p.z0), out, local.at[4])
    take = pltpu.make_async_copy(got, out, local.at[4])

    def zero():
        @pl.when(away)
        def _():
            for k in range(4):
                x_copy(k).start()

        @pl.when(home)
        def _():
            for k in range(4):
                load(k).start()

    def first():
        @pl.when(home)
        def _():
            for k in range(4):
                x_copy(k).wait_recv()
                load(k).wait()
                add_to(one.at[k], mine.at[k])
            for k in (0, 1):
                y_copy(k).start()

    def second():
        @pl.when(home)
        def _():
            for k in (0, 1):
                y_copy(k).wait_recv()
                add_to(two.at[k], one.at[p.y * 2 + k])
            z1_copy.start()

    def third():
        @pl.when(home)
        def _():
            z1_copy.wait_recv()
            add_to(three, two.at[p.z1])
            pair.start()
            keep.start()

    def last():
        @pl.when(home)
        def _():
            keep.wait()
            for k in (0, 1):
                y_copy(k).wait_send()
            z1_copy.wait_send()
            pair.wait_send()

        @pl.when(away)
        def _():
            pair.wait_recv()
            take.start()
            for k in range(4):
                x_copy(k).wait_send()
            take.wait()

    return [zero, first, second, third, last]


def gains_gather(p, src, ref, send, recv, local):
    me = ((p.y * 2 + p.x) * 2 + p.c) * 4 + p.z1 * 2 + p.z0
    own = pltpu.make_async_copy(src, ref.at[me], local)
    names = ("z0", "z1", "c", "x", "y")

    def span(k, other):
        size = 1 << k
        start = lax.div(me, size) * size
        if other:
            bit = lax.rem(lax.div(me, size), 2)
            start = start + size - 2 * size * bit
        return ref.at[pl.ds(start, size)]

    def copy(k, other):
        return remote(span(k, other), span(k, other), send.at[k], recv.at[k], p.peer[names[k]])

    def step(k):
        def run():
            if k == 0:
                own.start()
                own.wait()
            else:
                copy(k - 1, True).wait_recv()
            if k < 5:
                copy(k, False).start()
            else:
                for j in range(5):
                    copy(j, False).wait_send()

        return run

    return [step(k) for k in range(6)]


def gains_reduce(p, src, out, base, halves, send, recv, local):
    names, bits = ("y", "x", "c", "z1", "z0"), (p.y, p.x, p.c, p.z1, p.z0)
    load = pltpu.make_async_copy(src, base, local.at[0])
    keep = pltpu.make_async_copy(halves[4].at[0], out, local.at[0])

    def part(k, bit):
        source, size = (base if k == 0 else halves[k - 1]), 16 >> k
        return source.at[pl.ds(bit * size, size)]

    def copy(k):
        return remote(part(k, 1 - bits[k]), halves[k], send.at[k], recv.at[k], p.peer[names[k]])

    def step(k):
        def run():
            if k > 0:
                copy(k - 1).wait_recv()
                halves[k - 1][...] += part(k - 1, bits[k - 1])[...]
            else:
                load.start()
                load.wait()
            if k < 5:
                copy(k).start()
            else:
                keep.start()
                for j in range(5):
                    copy(j).wait_send()
                keep.wait()

        return run

    return [step(k) for k in range(6)]


GROUP = ("c", "z0", "cz")
EIGHT = ("z1", "y", "x")


CHUNKS = 2


class ShareRows:
    def __init__(self, p, src, dst, send, recv, local):
        self.p, self.src, self.dst, self.send, self.recv, self.local = p, src, dst, send, recv, local
        self.rows = src.shape[0] // CHUNKS

    def chunk(self, rank, k):
        return self.dst.at[rank, pl.ds(k * self.rows, self.rows)]

    def over(self, k, arriving=False):
        p = self.p
        src = self.src.at[pl.ds(k * self.rows, self.rows)]
        rank = 2 * p.c + 1 - p.z0 if arriving else p.rank
        return remote(src, self.chunk(rank, k), self.send.at[k], self.recv.at[k], p.peer["z0"])

    def across(self, arriving=False):
        p = self.p
        rank = 2 * (1 - p.c) + p.z0 if arriving else p.rank
        return remote(self.src, self.dst.at[rank], self.send.at[CHUNKS], self.recv.at[CHUNKS], p.peer["c"])

    def onward(self, k, arriving=False):
        p = self.p
        ours, theirs = 2 * p.c + 1 - p.z0, 2 * (1 - p.c) + 1 - p.z0
        ref = self.chunk(theirs if arriving else ours, k)
        return remote(ref, ref, self.send.at[CHUNKS + 1 + k], self.recv.at[CHUNKS + 1 + k], p.peer["c"])

    def own(self):
        return pltpu.make_async_copy(self.src, self.dst.at[self.p.rank], self.local)

    def start(self):
        for k in range(CHUNKS):
            self.over(k).start()
        self.across().start()
        self.own().start()

    def near(self):
        self.own().wait()
        self.across(True).wait_recv()

    def pass_on(self, k):
        self.over(k, True).wait_recv()
        self.onward(k).start()

    def far(self, k):
        self.onward(k, True).wait_recv()

    def finish(self):
        for k in range(CHUNKS):
            self.over(k).wait_send()
            self.onward(k).wait_send()
        self.across().wait_send()


class SumRows:
    def __init__(self, p, terms, near, cross, far, send, recv):
        self.p, self.terms, self.near, self.cross, self.far, self.send, self.recv = p, terms, near, cross, far, send, recv
        self.rows = near.shape[0] // CHUNKS

    def diagonal(self, k):
        p = self.p
        part = pl.ds(k * self.rows, self.rows)
        rank = 2 * (1 - p.c) + 1 - p.z0
        return remote(self.terms.at[rank, part], self.cross.at[part], self.send.at[k], self.recv.at[k], p.peer["c"])

    def sibling(self):
        p = self.p
        rank, at = 2 * (1 - p.c) + p.z0, CHUNKS
        return remote(self.terms.at[rank], self.near, self.send.at[at], self.recv.at[at], p.peer["c"])

    def over(self, k):
        p, at = self.p, CHUNKS + 1 + k
        part = pl.ds(k * self.rows, self.rows)
        return remote(self.cross.at[part], self.far.at[part], self.send.at[at], self.recv.at[at], p.peer["z0"])

    def relay(self, k):
        p = self.p
        self.diagonal(k).wait_recv()
        part = pl.ds(k * self.rows, self.rows)
        add_to(self.cross.at[part], self.terms.at[2 * p.c + 1 - p.z0, part])
        self.over(k).start()

    def finish(self):
        for k in range(CHUNKS):
            self.diagonal(k).wait_send()
            self.over(k).wait_send()
        self.sibling().wait_send()


def pack_qkv(shard):
    rows = shard.shape[0]
    q = shard[:, : QUERY_HEAD_COUNT * HEAD_SIZE].reshape(rows, 2, 2, 2, 2, HEAD_SIZE)
    q = q.transpose(3, 2, 0, 1, 4, 5).reshape(4, rows, Q_RANK * HEAD_SIZE)
    kv = shard[:, QUERY_HEAD_COUNT * HEAD_SIZE :].reshape(rows, 2, 2, 2, 2, HEAD_SIZE)
    kv = kv.transpose(4, 3, 0, 1, 2, 5).reshape(4, rows, 2 * KV_RANK * HEAD_SIZE)
    return jnp.concatenate([q, kv], axis=2).astype(BF)


def unpack_qkv(parts):
    rows = parts.shape[1]
    q = parts[..., : Q_RANK * HEAD_SIZE].reshape(2, 2, rows, 2, 2, HEAD_SIZE)
    q = q.transpose(2, 3, 1, 0, 4, 5).reshape(rows, QUERY_HEAD_COUNT * HEAD_SIZE)
    kv = parts[..., Q_RANK * HEAD_SIZE :].reshape(2, 2, rows, 2, 2, HEAD_SIZE)
    kv = kv.transpose(2, 3, 4, 1, 0, 5).reshape(rows, 2 * KEY_VALUE_HEADS * HEAD_SIZE)
    return jnp.concatenate([q, kv], axis=1)


def pack_gateup(shard):
    rows = shard.shape[0]
    parts = shard.reshape(rows, 2, 2, 2, 2, 2, 2, -1).transpose(4, 6, 0, 1, 2, 3, 5, 7)
    return parts.reshape(4, rows, -1).astype(BF)


def unpack_gateup(parts):
    rows = parts.shape[1]
    return parts.reshape(2, 2, rows, 2, 2, 2, 2, -1).transpose(2, 3, 4, 5, 0, 6, 1, 7).reshape(rows, -1)


def swap_pairs(count_fsdp, count_seq):
    pairs = []
    for f in range(count_fsdp):
        for z in range(count_seq):
            c, z1 = f % 2, z // 2
            pairs.append((f * count_seq + z, (f - c + z1) * count_seq + c * 2 + z % 2))
    return pairs


TILE = 256
HALVES = 2


def wide_params(collective_id):
    return pltpu.CompilerParams(
        collective_id=collective_id, has_side_effects=True, vmem_limit_bytes=58 * 2**20
    )


def dot(a, b, contract=((1,), (0,))):
    return lax.dot_general(a, b, (contract, ((), ())), preferred_element_type=F32)


def row_normalize(ref, gain, out, rows=32):
    def step(k, _):
        at = pl.ds(pl.multiple_of(k * rows, rows), rows)
        value = ref[at, :].astype(F32)
        out[at, :] = (normalize(value) * gain[...]).astype(out.dtype)
        return 0

    lax.fori_loop(0, ref.shape[0] // rows, step, 0)


def column_tiles(width, tile, step):
    def run(j, _):
        step(pl.multiple_of(j * tile, tile))
        return 0

    lax.fori_loop(0, width // tile, run, 0)


def exchange(p, share, total, compute, steps, between=lambda: None):
    steps = list(steps)
    advance = lambda: steps.pop(0)() if steps else None
    rows = total.near.shape[0]
    part = rows // CHUNKS
    share.start()
    advance()
    share.own().wait()
    compute(p.rank, 0, rows)
    advance()
    share.across(True).wait_recv()
    sibling = 2 * (1 - p.c) + p.z0
    compute(sibling, 0, rows)
    total.sibling().start()
    advance()
    for k in range(CHUNKS):
        share.pass_on(k)
        compute(2 * p.c + 1 - p.z0, k * part, part)
        share.far(k)
        compute(2 * (1 - p.c) + 1 - p.z0, k * part, part)
        total.diagonal(k).start()
        total.relay(k)
        advance()
    between()
    while steps:
        advance()


def collect(p, total, write, rows=32):
    total.sibling().wait_recv()
    for k in range(CHUNKS):
        total.over(k).wait_recv()

        def step(j, _, k=k):
            at = pl.ds(pl.multiple_of(k * total.rows + j * rows, rows), rows)
            value = total.terms[p.rank, at, :].astype(F32) + total.near[at, :].astype(F32)
            write(at, value + total.far[at, :].astype(F32))
            return 0

        lax.fori_loop(0, total.rows // rows, step, 0)


def exchange_scratch(rows):
    part = pltpu.VMEM((rows, D), BF)
    sems = DMA((2 * CHUNKS + 1,))
    return [part, pltpu.VMEM((4, rows, D), BF), part, part, part, sems, sems, sems, sems, DMA((1,))]


def exchange_of(p, every, refs):
    own, terms, near, cross, far, send, recv, t_send, t_recv, local = refs
    share = ShareRows(p, own, every, send, recv, local.at[0])
    return own, terms, share, SumRows(p, terms, near, cross, far, t_send, t_recv)


class Nothing:
    names, args, shapes, scratch = (), (), (), ()

    def steps(self, p, ins, outs, scratch):
        return []


def beside_call(body, args, in_specs, shapes, out_specs, scratch, beside, name, collective_id, flops, peers=("c", "z0")):
    counts = [len(args), len(beside.args), len(shapes), len(beside.shapes), len(scratch), len(beside.scratch)]

    def whole(*refs):
        groups, at = [], 0
        for n in counts:
            groups.append(refs[at : at + n])
            at += n
        p = Place()
        greet(p, tuple(peers) + tuple(n for n in beside.names if n not in peers))
        body(p, groups[0], groups[2], groups[4], beside.steps(p, groups[1], groups[3], groups[5]))

    out = pl.pallas_call(
        whole,
        out_shape=list(shapes) + list(beside.shapes),
        in_specs=list(in_specs) + [ANY] * len(beside.args),
        out_specs=list(out_specs) + [ANY] * len(beside.shapes),
        scratch_shapes=list(scratch) + list(beside.scratch),
        compiler_params=wide_params(collective_id),
        cost_estimate=pl.CostEstimate(flops=flops, bytes_accessed=20 * 2**20, transcendentals=0),
        name=name,
    )(*args, *beside.args)
    return out[: len(shapes)], out[len(shapes) :]


def feed_forward_call(middle, gain, w_gateup, w_down, beside, collective_id):
    rows, wide = middle.shape[0], w_down.shape[0]

    def body(p, ins, outs, scratch, steps):
        mid_ref, gain_ref, gu_ref, down_ref = ins
        new_ref, every, gate_ref, up_ref, hid_ref = outs
        own, terms, share, total = exchange_of(p, every, scratch)

        def compute(rank, first, count):
            at = pl.ds(first, count)

            def up_tile(j):
                cols, far = pl.ds(j, TILE), pl.ds(wide + j, TILE)
                x = every[rank, at, :]
                gate, up = dot(x, gu_ref[:, cols]), dot(x, gu_ref[:, far])
                gate_ref[rank, at, cols] = gate
                up_ref[rank, at, cols] = up
                hid_ref[rank, at, cols] = (gate / (1.0 + jnp.exp(-gate)) * up).astype(BF)

            column_tiles(wide, TILE, up_tile)

            def down_tile(j):
                cols = pl.ds(j, TILE)
                terms[rank, at, cols] = dot(hid_ref[rank, at, :], down_ref[:, cols]).astype(BF)

            column_tiles(D, TILE, down_tile)

        row_normalize(mid_ref, gain_ref, own)
        exchange(p, share, total, compute, steps)

        def write(at, value):
            new_ref[at, :] = mid_ref[at, :] + value

        collect(p, total, write)
        share.finish()
        total.finish()

    return beside_call(
        body,
        (middle, gain.reshape(1, D), w_gateup, w_down),
        [VM] * 4,
        [
            jax.ShapeDtypeStruct((rows, D), F32),
            jax.ShapeDtypeStruct((4, rows, D), BF),
            jax.ShapeDtypeStruct((4, rows, wide), F32),
            jax.ShapeDtypeStruct((4, rows, wide), F32),
            jax.ShapeDtypeStruct((4, rows, wide), BF),
        ],
        [VM] * 5,
        exchange_scratch(rows),
        beside,
        "feed_forward",
        collective_id,
        6 * 4 * rows * wide * D,
    )


def feed_backward_call(grad, middle, gain, w_gateup, w_down, kept, beside, collective_id):
    every, gate, up, hidden = kept
    rows, wide = middle.shape[0], w_down.shape[0]

    def body(p, ins, outs, scratch, steps):
        grad_ref, mid_ref, gain_ref, gu_ref, down_ref, every_ref, gate_ref, up_ref, hid_ref = ins
        new_ref, gain_out, g_gu, g_down = outs
        e, pair = scratch[:2]
        own, terms, share, total = exchange_of(p, e, scratch[2:])

        def compute(rank, first, count):
            at = pl.ds(first, count)

            def up_tile(j):
                cols, far = pl.ds(j, TILE), pl.ds(wide + j, TILE)
                grad_hidden = dot(e[rank, at, :], down_ref[cols, :], ((1,), (1,)))
                g, u = gate_ref[rank, at, cols], up_ref[rank, at, cols]
                s = 1.0 / (1.0 + jnp.exp(-g))
                pair[rank, at, cols] = (grad_hidden * u * s * (1.0 + g * (1.0 - s))).astype(BF)
                pair[rank, at, far] = (grad_hidden * g * s).astype(BF)

            column_tiles(wide, TILE, up_tile)

            def down_tile(j):
                cols = pl.ds(j, TILE)
                terms[rank, at, cols] = dot(pair[rank, at, :], gu_ref[cols, :], ((1,), (1,))).astype(BF)

            column_tiles(D, TILE, down_tile)

        def weight_grads():
            tokens = 4 * rows
            e_all, pair_all, x_all, hid_all = (
                r.reshape(tokens, r.shape[2]) for r in (e, pair, every_ref, hid_ref)
            )

            def down_grad(j):
                cols = pl.ds(j, TILE)
                g_down[cols, :] = dot(hid_all[:, cols], e_all[...], ((0,), (0,))).astype(BF)

            column_tiles(wide, TILE, down_grad)

            def gu_grad(j):
                cols = pl.ds(j, TILE)
                g_gu[cols, :] = dot(x_all[:, cols], pair_all[...], ((0,), (0,))).astype(BF)

            column_tiles(D, TILE, gu_grad)

        def copy_own(k, _):
            at = pl.ds(pl.multiple_of(k * 32, 32), 32)
            own[at, :] = grad_ref[at, :].astype(BF)
            return 0

        lax.fori_loop(0, rows // 32, copy_own, 0)
        exchange(p, share, total, compute, steps, weight_grads)
        gain_out[...] = jnp.zeros_like(gain_out)

        def write(at, value):
            mid = mid_ref[at, :]
            normed = normalize(mid)
            gain_out[...] += jnp.sum(value * normed, axis=0, keepdims=True)
            new_ref[at, :] = grad_ref[at, :] + norm_back(value * gain_ref[...], normed, mid)

        collect(p, total, write)
        share.finish()
        total.finish()

    return beside_call(
        body,
        (grad, middle, gain.reshape(1, D), w_gateup, w_down, every, gate, up, hidden),
        [VM] * 9,
        [
            jax.ShapeDtypeStruct((rows, D), F32),
            jax.ShapeDtypeStruct((1, D), F32),
            jax.ShapeDtypeStruct((D, 2 * wide), BF),
            jax.ShapeDtypeStruct((wide, D), BF),
        ],
        [VM] * 4,
        [pltpu.VMEM((4, rows, D), BF), pltpu.VMEM((4, rows, 2 * wide), BF)] + exchange_scratch(rows),
        beside,
        "feed_backward",
        collective_id,
        12 * 4 * rows * wide * D,
    )


class Both:
    def __init__(self, *parts):
        self.parts = parts
        self.names = tuple(dict.fromkeys(n for p in parts for n in p.names))
        self.args = tuple(a for p in parts for a in p.args)
        self.shapes = tuple(s for p in parts for s in p.shapes)
        self.scratch = tuple(s for p in parts for s in p.scratch)

    def steps(self, p, ins, outs, scratch):
        lists, at = [], [0, 0, 0]
        for part in self.parts:
            ends = [at[0] + len(part.args), at[1] + len(part.shapes), at[2] + len(part.scratch)]
            lists.append(part.steps(p, ins[at[0] : ends[0]], outs[at[1] : ends[1]], scratch[at[2] : ends[2]]))
            at = ends

        def row(k):
            def run():
                for steps in lists:
                    if k < len(steps):
                        steps[k]()

            return run

        return [row(k) for k in range(max(len(s) for s in lists))]


class SpreadColumns:
    names = GROUP

    def __init__(self, *blocks):
        self.args = blocks
        self.shapes = tuple(jax.ShapeDtypeStruct((2, 2) + b.shape[1:], BF) for b in blocks)
        self.scratch = (DMA((3 * len(blocks),)), DMA((3 * len(blocks),)), DMA((len(blocks),)))

    def steps(self, p, ins, outs, scratch):
        send, recv, local = scratch
        made = []
        for k, (src, dst) in enumerate(zip(ins, outs)):
            sems = [s.at[pl.ds(3 * k, 3)] for s in (send, recv)]
            made.append(
                Spread(
                    p, lambda c, z0, s=src: s.at[2 * c + z0], lambda c, z0, d=dst: d.at[c, z0], *sems, local.at[k]
                )
            )

        def first():
            for m in made:
                m.start()

        def last():
            for m in made:
                m.wait()
                m.finish()

        return [first, lambda: None, lambda: None, lambda: None, last]


class CollectColumns:
    names = GROUP

    def __init__(self, *blocks):
        self.args = blocks
        self.shapes = tuple(jax.ShapeDtypeStruct((4,) + b.shape[2:], BF) for b in blocks)
        self.scratch = (DMA((3 * len(blocks),)), DMA((3 * len(blocks),)), DMA((len(blocks),)))

    def steps(self, p, ins, outs, scratch):
        send, recv, local = scratch
        made = []
        for k, (src, dst) in enumerate(zip(ins, outs)):
            sems = [s.at[pl.ds(3 * k, 3)] for s in (send, recv)]
            made.append(
                Spread(
                    p, lambda c, z0, s=src: s.at[c, z0], lambda c, z0, d=dst: d.at[2 * c + z0], *sems, local.at[k]
                )
            )

        def first():
            for m in made:
                m.start()

        def last():
            for m in made:
                m.wait()
                m.finish()

        return [first, lambda: None, lambda: None, lambda: None, last]


class GatherWeights:
    def __init__(self, columns=None, down=None, out=None, gains=None):
        self.has = columns is not None, down is not None, out is not None, gains is not None
        self.spread = columns is not None and columns.ndim == 3
        self.names = EIGHT + (GROUP if self.spread else ())
        self.args = tuple(a for a in (columns, down, out, gains) if a is not None)
        shapes, scratch = [], []
        sems = lambda n: [DMA((n,)), DMA((n,)), DMA((2,))]
        if columns is not None:
            shapes.append((16, 2) + columns.shape[-2:])
            scratch += sems(14) + sems(3)
        if down is not None:
            shapes.append((16,) + down.shape[1:])
            scratch += sems(14)
        if out is not None:
            shapes.append((4, 2) + out.shape)
            scratch += sems(8)
        if gains is not None:
            shapes.append((32,) + gains.shape)
            scratch += sems(5)
        self.shapes = tuple(jax.ShapeDtypeStruct(s, BF) for s in shapes)
        self.scratch = tuple(scratch)

    def steps(self, p, ins, outs, scratch):
        ins, outs, scratch = list(ins), list(outs), list(scratch)
        before, early, late, other, ends = [], [], [], [], []
        if self.has[0]:
            src, ref = ins.pop(0), outs.pop(0)
            send, recv, local, s_send, s_recv, s_local = (scratch.pop(0) for _ in range(6))
            if self.spread:
                at = lambda c, z0, ref=ref: ref.at[columns_index(p.y, p.x, p.z1, c), z0]
                spread = Spread(p, lambda c, z0, src=src: src.at[2 * c + z0], at, s_send, s_recv, s_local.at[0])
                gather = Gather(p, ref, columns_index, send, recv)
                before.append(spread.start)
                late.append((gather, [spread.wait]))
                ends.append(spread.finish)
            else:
                late.append((Gather(p, ref, columns_index, send, recv, src, local), []))
        if self.has[1]:
            src, ref = ins.pop(0), outs.pop(0)
            send, recv, local = (scratch.pop(0) for _ in range(3))
            early.append((Gather(p, ref, rows_index, send, recv, src, local), []))
        if self.has[2]:
            src, ref = ins.pop(0), outs.pop(0)
            send, recv, local = (scratch.pop(0) for _ in range(3))
            other.append(out_gather_steps(p, src, ref, send, recv, local.at[0]))
        if self.has[3]:
            src, ref = ins.pop(0), outs.pop(0)
            send, recv, local = (scratch.pop(0) for _ in range(3))
            other.append(gains_gather(p, src, ref, send, recv, local.at[0]))
        gathers = early + late
        waves = [[] for _ in range(8)]
        waves[0] += before
        for messages in ((0,), (1, 3)):
            for gather, first in gathers:
                waves[0] += (first if messages == (0,) else []) + [functools.partial(gather.first, messages)]
        for gather, _ in gathers:
            for h in (0, 1):
                waves[1 + h].append(functools.partial(gather.on, h, 0, (2, 4)))
                waves[3 + h].append(functools.partial(gather.on, h, 1, (5,)))
                waves[5 + h].append(functools.partial(gather.on, h, 2, (6,)))
            waves[7].append(gather.last)
        waves[7] += ends
        return in_waves(waves, other)


def in_waves(waves, lists):
    for steps in lists:
        for k, act in enumerate(steps):
            waves[min(k, len(waves) - 1)].append(act)

    def run(wave):
        for act in wave:
            act()

    return [functools.partial(run, wave) for wave in waves]


class ReduceWeights:
    def __init__(self, columns=None, down=None, out=None, gains=None, collect=False):
        self.names = EIGHT + (GROUP if collect else ())
        self.has = columns is not None, down is not None, out is not None, gains is not None
        self.collect = collect
        self.args = tuple(a for a in (columns, down, out, gains) if a is not None)
        shapes, scratch = [], []
        for block in (columns, down):
            if block is not None:
                b = block.shape[1:]
                shape = (4, b[0] // 2, b[1]) if collect and block is columns else (2,) + b
                shapes.append(jax.ShapeDtypeStruct(shape, BF))
                scratch += [pltpu.VMEM(n + b, BF) for n in ((2, 4), (2, 4), (2, 2), (2,))]
                scratch += [DMA((14,)), DMA((14,)), DMA((9,))]
        if collect:
            scratch += [DMA((3,)), DMA((3,)), DMA((1,))]
        if out is not None:
            wide, rows = out.shape[1:], out.shape[1] // 2
            shapes.append(jax.ShapeDtypeStruct((rows, wide[1]), BF))
            scratch += [pltpu.VMEM(n + wide, BF) for n in ((4,), (4,), (2,), ())]
            scratch += [pltpu.VMEM((rows, wide[1]), BF), DMA((8,)), DMA((8,)), DMA((5,))]
        if gains is not None:
            shapes.append(jax.ShapeDtypeStruct(gains.shape[1:], F32))
            scratch += [pltpu.VMEM(gains.shape, F32)]
            scratch += [pltpu.VMEM((16 >> k,) + gains.shape[1:], F32) for k in range(5)]
            scratch += [DMA((5,)), DMA((5,)), DMA((1,))]
        self.shapes, self.scratch = tuple(shapes), tuple(scratch)

    def steps(self, p, ins, outs, scratch):
        ins, outs, scratch = list(ins), list(outs), list(scratch)
        waves, lists = [[] for _ in range(7)], []
        for k, index in ((1, rows_index), (0, columns_index)):
            if self.has[k]:
                at = 0 if k == 0 or not self.has[0] else 1
                parts = [scratch[7 * at + n] for n in range(7)]
                r = Reduce(p, ins[at], index, outs[at], *parts)
                waves[0].append(r.first)
                for h in (0, 1):
                    waves[1].append(functools.partial(r.second, h, 0))
                    waves[2].append(functools.partial(r.second, h, 1))
                    waves[3] += [functools.partial(r.second, h, 2), functools.partial(r.third, h, 0)]
                    waves[4] += [functools.partial(r.second, h, 3), functools.partial(r.third, h, 1)]
                    waves[5].append(functools.partial(r.fourth, h))
                if k == 0 and self.collect:
                    send, recv, local = scratch[7 * (self.has[0] + self.has[1]) :][:3]
                    rows = r.three.shape[1] // 2
                    part = lambda c, z0, t=r.three: t.at[c, pl.ds(pl.multiple_of(z0 * rows, rows), rows)]
                    spread = Spread(p, part, lambda c, z0, o=outs[at]: o.at[2 * c + z0], send, recv, local.at[0])
                    waves[5].append(spread.start)
                    waves[6] += [spread.wait, spread.finish]
                else:
                    waves[5].append(lambda r=r: r.store().start())
                    waves[6].append(lambda r=r: r.store().wait())
                waves[6].append(r.finish)
        done = self.has[0] + self.has[1]
        ins, outs, scratch = ins[done:], outs[done:], scratch[7 * done + 3 * self.collect :]
        if self.has[2]:
            parts = [scratch.pop(0) for _ in range(8)]
            lists.append(out_reduce_steps(p, ins.pop(0), outs.pop(0), *parts))
        if self.has[3]:
            parts = [scratch.pop(0) for _ in range(9)]
            lists.append(gains_reduce(p, ins.pop(0), outs.pop(0), parts[0], parts[1:6], *parts[6:]))
        return in_waves(waves, lists)


LANES = 128
HEADS = Q_RANK + 2 * KV_RANK


def head_lanes():
    half = HEAD_SIZE // 2
    column = jnp.arange(HEADS * HEAD_SIZE, dtype=jnp.int32)
    head, inner = column // HEAD_SIZE, column % HEAD_SIZE
    lane = head * LANES + jnp.where(inner < half, inner, inner - half + LANES // 2)
    return (lane[:, None] == jnp.arange(HEADS * LANES, dtype=jnp.int32)[None, :]).astype(BF)


def lane_tables(length_row, count):
    places = jnp.arange(count, dtype=jnp.int32)
    segment, positions = layout(length_row, places)
    cosines, sines = tables(positions)
    cosines, sines = cosines[:, 0], sines[:, 0]
    half, space = HEAD_SIZE // 2, LANES // 2 - HEAD_SIZE // 2
    spread = lambda a, b: jnp.concatenate(
        [jnp.pad(a, ((0, 0), (0, space))), jnp.pad(b, ((0, 0), (0, space)))], axis=1
    )
    return (
        spread(cosines[:, :half], cosines[:, half:]),
        spread(-sines[:, :half], sines[:, half:]),
        (places - positions)[:, None],
    )


def pad_weights(lanes_ref, qkv_ref, out_ref, qkv_wide, out_wide):
    def qkv_tile(j):
        at = pl.ds(j, TILE)
        qkv_wide[at, :] = dot(qkv_ref[at, :], lanes_ref[...]).astype(BF)

    column_tiles(D, TILE, qkv_tile)
    heads = lanes_ref[: Q_RANK * HEAD_SIZE, : Q_RANK * LANES]

    def out_tile(j):
        cols = pl.ds(j, TILE)
        out_wide[:, cols] = dot(heads, out_ref[:, cols], ((0,), (0,))).astype(BF)

    column_tiles(D, TILE, out_tile)


def masked(scores, first, start_ref):
    count, keys = scores.shape
    query = lax.broadcasted_iota(jnp.int32, scores.shape, 0) + first
    key = lax.broadcasted_iota(jnp.int32, scores.shape, 1)
    start = start_ref[first : first + count, :]
    return jnp.where((key <= query) & (key >= start), scores, masked_score)


def attention_forward_call(residual, gain, w_qkv, w_out, common, beside, collective_id):
    lanes, cosines, sines, starts = common
    rows = residual.shape[0]
    count = 4 * rows
    scale = HEAD_SIZE ** (-0.5)

    def body(p, ins, outs, scratch, steps):
        res_ref, gain_ref, qkv_ref, out_ref, lanes_ref, cos_ref, sin_ref, start_ref = ins
        new_ref, every, heads_ref, att_ref, log_ref = outs
        qkv_wide, out_wide = scratch[:2]
        own, terms, share, total = exchange_of(p, every, scratch[2:])
        steps = list(steps)
        advance = lambda: steps.pop(0)() if steps else None

        def project(rank, first, n):
            at = pl.ds(first, n)
            here = pl.ds(pl.multiple_of(rank * rows + first, n), n)
            cos, sin = cos_ref[here, :], sin_ref[here, :]
            for j in range(0, HEADS, 2):
                both = dot(every[rank, at, :], qkv_wide[:, j * LANES : (j + 2) * LANES])
                for k in (0, 1):
                    value = both[:, k * LANES : (k + 1) * LANES]
                    if j + k < Q_RANK + KV_RANK:
                        value = value * cos + pltpu.roll(value, LANES // 2, 1) * sin
                    heads_ref[j + k, here, :] = value.astype(BF)

        def attend(j, _):
            g = lax.div(j, Q_RANK // KV_RANK)
            for first in range(0, count, rows):
                n = first + rows
                q = heads_ref[j, first:n, :]
                scores = dot(q, heads_ref[Q_RANK + g, :n, :], ((1,), (1,))) * scale
                scores = masked(scores, first, start_ref)
                top = jnp.max(scores, axis=1, keepdims=True)
                shifted = jnp.exp(scores - top)
                amount = jnp.sum(shifted, axis=1, keepdims=True)
                log_ref[j, first:n, :] = top + jnp.log(amount)
                weights = (shifted / amount).astype(BF)
                att_ref[j, first:n, :] = dot(weights, heads_ref[Q_RANK + KV_RANK + g, :n, :]).astype(BF)
            return 0

        def project_out(rank, first, n):
            here = pl.ds(pl.multiple_of(rank * rows + first, n), n)
            wide = jnp.concatenate([att_ref[j, here, :] for j in range(Q_RANK)], axis=1)

            def tile(j):
                cols = pl.ds(j, TILE)
                terms[rank, pl.ds(first, n), cols] = dot(wide, out_wide[:, cols]).astype(BF)

            column_tiles(D, TILE, tile)

        sib, over, diag = 2 * (1 - p.c) + p.z0, 2 * p.c + 1 - p.z0, 2 * (1 - p.c) + 1 - p.z0
        row_normalize(res_ref, gain_ref, own)
        share.start()
        advance()
        pad_weights(lanes_ref, qkv_ref, out_ref, qkv_wide, out_wide)
        share.own().wait()
        project(p.rank, 0, rows)
        share.across(True).wait_recv()
        project(sib, 0, rows)
        advance()
        part = rows // CHUNKS
        for k in range(CHUNKS):
            share.pass_on(k)
            project(over, k * part, part)
            share.far(k)
            project(diag, k * part, part)
            advance()
        for j in range(0, Q_RANK, 2):
            lax.fori_loop(j, j + 2, attend, 0)
            advance()
        for k in range(CHUNKS):
            project_out(diag, k * part, part)
            total.diagonal(k).start()
            project_out(over, k * part, part)
            total.relay(k)
            advance()
        project_out(sib, 0, rows)
        total.sibling().start()
        project_out(p.rank, 0, rows)
        while steps:
            advance()

        def write(at, value):
            new_ref[at, :] = res_ref[at, :] + value

        collect(p, total, write)
        share.finish()
        total.finish()

    return beside_call(
        body,
        (residual, gain.reshape(1, D), w_qkv, w_out, lanes, cosines, sines, starts),
        [VM] * 8,
        [
            jax.ShapeDtypeStruct((rows, D), F32),
            jax.ShapeDtypeStruct((4, rows, D), BF),
            jax.ShapeDtypeStruct((HEADS, count, LANES), BF),
            jax.ShapeDtypeStruct((Q_RANK, count, LANES), BF),
            jax.ShapeDtypeStruct((Q_RANK, count, 1), F32),
        ],
        [VM] * 5,
        [pltpu.VMEM((D, HEADS * LANES), BF), pltpu.VMEM((Q_RANK * LANES, D), BF)] + exchange_scratch(rows),
        beside,
        "attention_forward",
        collective_id,
        2 * count * D * (HEADS + Q_RANK) * LANES,
    )


def attention_backward_call(grad, residual, gain, w_qkv, w_out, kept, common, beside, collective_id):
    lanes, cosines, sines, starts = common
    every, heads, attended, logs = kept
    rows = residual.shape[0]
    count = 4 * rows
    scale = HEAD_SIZE ** (-0.5)

    def body(p, ins, outs, scratch, steps):
        (grad_ref, res_ref, gain_ref, qkv_ref, out_ref, lanes_ref, cos_ref, sin_ref, start_ref) = ins[:9]
        every_ref, heads_ref, att_ref, log_ref = ins[9:]
        new_ref, gain_out, g_qkv, g_out = outs
        qkv_wide, out_wide, e, d_att, d_k, d_v, d_heads = scratch[:7]
        own, terms, share, total = exchange_of(p, e, scratch[7:])
        steps = list(steps)
        advance = lambda: steps.pop(0)() if steps else None

        def copy_own(k, _):
            at = pl.ds(pl.multiple_of(k * 32, 32), 32)
            own[at, :] = grad_ref[at, :].astype(BF)
            return 0

        lax.fori_loop(0, rows // 32, copy_own, 0)

        def back_out(rank, first, n):
            here = pl.ds(pl.multiple_of(rank * rows + first, n), n)
            for j in range(0, Q_RANK, 2):
                both = dot(e[rank, pl.ds(first, n), :], out_wide[j * LANES : (j + 2) * LANES, :], ((1,), (1,)))
                for k in (0, 1):
                    d_att[j + k, here, :] = both[:, k * LANES : (k + 1) * LANES].astype(BF)

        def attend(j, _):
            g = lax.div(j, Q_RANK // KV_RANK)
            for first in range(0, count, rows):
                n = first + rows
                q, d_o = heads_ref[j, first:n, :], d_att[j, first:n, :]
                k, v = heads_ref[Q_RANK + g, :n, :], heads_ref[Q_RANK + KV_RANK + g, :n, :]
                scores = masked(dot(q, k, ((1,), (1,))) * scale, first, start_ref)
                weights = jnp.exp(scores - log_ref[j, first:n, :])
                d_weights = dot(d_o, v, ((1,), (1,)))
                inner = jnp.sum(weights * d_weights, axis=1, keepdims=True)
                d_scores = (weights * (d_weights - inner)).astype(BF)
                d_v[g, :n, :] += dot(weights.astype(BF), d_o, ((0,), (0,)))
                d_k[g, :n, :] += dot(d_scores, q, ((0,), (0,)))
                d_q = dot(d_scores, k) * scale
                d_heads[j, first:n, :] = turn_back(d_q, cos_ref[first:n, :], sin_ref[first:n, :])
            return 0

        def turn_back(value, cos, sin):
            return (value * cos - pltpu.roll(value, LANES // 2, 1) * sin).astype(BF)

        def keys_back():
            for g in range(KV_RANK):
                for first in range(0, count, rows):
                    at = slice(first, first + rows)
                    d_heads[Q_RANK + g, at, :] = turn_back(d_k[g, at, :] * scale, cos_ref[at, :], sin_ref[at, :])
                    d_heads[Q_RANK + KV_RANK + g, at, :] = d_v[g, at, :].astype(BF)

        def project_back(rank, first, n):
            here = pl.ds(pl.multiple_of(rank * rows + first, n), n)
            wide = jnp.concatenate([d_heads[j, here, :] for j in range(HEADS)], axis=1)

            def tile(j):
                cols = pl.ds(j, TILE)
                terms[rank, pl.ds(first, n), cols] = dot(wide, qkv_wide[cols, :], ((1,), (1,))).astype(BF)

            column_tiles(D, TILE, tile)

        def weight_grads():
            e_all, x_all = e.reshape(count, D), every_ref.reshape(count, D)
            pairs = LANES * 2

            def out_grad(j):
                cols = pl.ds(j, TILE)
                wide = jnp.concatenate(
                    [dot(att_ref[h], e_all[:, cols], ((0,), (0,))) for h in range(Q_RANK)], axis=0
                ).astype(BF)
                g_out[:, cols] = dot(lanes_ref[: Q_RANK * HEAD_SIZE, : Q_RANK * LANES], wide).astype(BF)

            column_tiles(D, TILE, out_grad)

            def qkv_grad(j):
                cols = pl.ds(j, TILE)
                wide = jnp.concatenate(
                    [dot(x_all[:, cols], d_heads[h], ((0,), (0,))) for h in range(HEADS)], axis=1
                ).astype(BF)
                g_qkv[cols, :] = dot(wide, lanes_ref[...], ((1,), (1,))).astype(BF)

            column_tiles(D, TILE, qkv_grad)

        sib, over, diag = 2 * (1 - p.c) + p.z0, 2 * p.c + 1 - p.z0, 2 * (1 - p.c) + 1 - p.z0
        share.start()
        advance()
        pad_weights(lanes_ref, qkv_ref, out_ref, qkv_wide, out_wide)
        d_k[...] = jnp.zeros_like(d_k)
        d_v[...] = jnp.zeros_like(d_v)
        share.own().wait()
        back_out(p.rank, 0, rows)
        share.across(True).wait_recv()
        back_out(sib, 0, rows)
        advance()
        part = rows // CHUNKS
        for k in range(CHUNKS):
            share.pass_on(k)
            back_out(over, k * part, part)
            share.far(k)
            back_out(diag, k * part, part)
            advance()
        for j in range(0, Q_RANK, 2):
            lax.fori_loop(j, j + 2, attend, 0)
            advance()
        keys_back()
        for k in range(CHUNKS):
            project_back(diag, k * part, part)
            total.diagonal(k).start()
            project_back(over, k * part, part)
            total.relay(k)
            advance()
        project_back(sib, 0, rows)
        total.sibling().start()
        project_back(p.rank, 0, rows)
        advance()
        weight_grads()
        while steps:
            advance()
        gain_out[...] = jnp.zeros_like(gain_out)

        def write(at, value):
            res = res_ref[at, :]
            normed = normalize(res)
            gain_out[...] += jnp.sum(value * normed, axis=0, keepdims=True)
            new_ref[at, :] = grad_ref[at, :] + norm_back(value * gain_ref[...], normed, res)

        collect(p, total, write)
        share.finish()
        total.finish()

    return beside_call(
        body,
        (grad, residual, gain.reshape(1, D), w_qkv, w_out, lanes, cosines, sines, starts, every, heads, attended, logs),
        [VM] * 13,
        [
            jax.ShapeDtypeStruct((rows, D), F32),
            jax.ShapeDtypeStruct((1, D), F32),
            jax.ShapeDtypeStruct((D, HEADS * HEAD_SIZE), BF),
            jax.ShapeDtypeStruct((Q_RANK * HEAD_SIZE, D), BF),
        ],
        [VM] * 4,
        [
            pltpu.VMEM((D, HEADS * LANES), BF),
            pltpu.VMEM((Q_RANK * LANES, D), BF),
            pltpu.VMEM((4, rows, D), BF),
            pltpu.VMEM((Q_RANK, count, LANES), BF),
            pltpu.VMEM((KV_RANK, count, LANES), F32),
            pltpu.VMEM((KV_RANK, count, LANES), F32),
            pltpu.VMEM((HEADS, count, LANES), BF),
        ]
        + exchange_scratch(rows),
        beside,
        "attention_backward",
        collective_id,
        6 * count * D * (HEADS + Q_RANK) * LANES,
    )


def links_call(beside, name, collective_id):
    return beside_call(
        lambda p, ins, outs, scratch, steps: [step() for step in steps] and None,
        (), [], [], [], [], beside, name, collective_id, 0, peers=(),
    )[1]


def fast_shards(
    tokens, cotangent, lengths, w_qkv, w_out, w_gateup, w_down, norm_gains, *moments
):
    axes = ("fsdp", "seq")
    pairs = swap_pairs(lax.axis_size("fsdp"), lax.axis_size("seq"))
    tokens = lax.ppermute(tokens, axes, pairs)
    lengths = lax.ppermute(lengths, axes, pairs)
    cotangent = lax.ppermute(cotangent, axes, pairs)
    common = (head_lanes(),) + lane_tables(lengths[0], 4 * tokens.shape[0])
    rows, owned = w_qkv.shape[1], norm_gains.shape[2]
    own_gains = jnp.pad(
        norm_gains.reshape(2 * LAYERS, owned).astype(BF), ((0, 16 - 2 * LAYERS), (0, lane_width - owned))
    )
    qkv_parts = [pack_qkv(w_qkv[l]) for l in range(LAYERS)]
    gateup_parts = [pack_gateup(w_gateup[l]) for l in range(LAYERS)]
    down_parts = [w_down[l].astype(BF).reshape(2, -1, D) for l in range(LAYERS)]
    out_parts = [w_out[l].astype(BF) for l in range(LAYERS)]
    qkv0, out0, got_gains, *columns = links_call(
        Both(
            GatherWeights(columns=qkv_parts[0], out=out_parts[0], gains=own_gains),
            SpreadColumns(gateup_parts[0], qkv_parts[1], gateup_parts[1]),
        ),
        "first_weights",
        0,
    )
    all_gains = got_gains[:, : 2 * LAYERS, :owned].transpose(1, 0, 2).reshape(LAYERS, 2, D).astype(F32)
    matrix = lambda g: g.reshape(D, -1)
    stack = lambda g: g.reshape(-1, D)
    start = tokens.astype(F32)
    (middle0, *first0), (gu0, down0) = attention_forward_call(
        start, all_gains[0, 0], matrix(qkv0), stack(out0), common, GatherWeights(columns=columns[0], down=down_parts[0]), 1
    )
    (later0, *second0), (qkv1, down1, out1) = feed_forward_call(
        middle0, all_gains[0, 1], matrix(gu0), stack(down0),
        GatherWeights(columns=columns[1], down=down_parts[1], out=out_parts[1]), 2,
    )
    (middle1, *first1), (gu1,) = attention_forward_call(
        later0, all_gains[1, 0], matrix(qkv1), stack(out1), common, GatherWeights(columns=columns[2]), 3
    )
    (later1, *second1), _ = feed_forward_call(
        middle1, all_gains[1, 1], matrix(gu1), stack(down1), Nothing(), 4
    )
    layer_output = lax.ppermute(later1.astype(BF), axes, pairs)
    wide = lambda g: g.reshape(16, 2 * rows, -1)
    tall = lambda g: g.reshape(16, -1, D)
    heads = lambda g: g.reshape(4, 2 * rows, D)
    (grad, gain11, g_gu1, g_down1), _ = feed_backward_call(
        cotangent.astype(F32), middle1, all_gains[1, 1], matrix(gu1), stack(down1), second1, Nothing(), 5
    )
    (grad, gain10, g_qkv1, g_out1), (s_gu1, s_down1) = attention_backward_call(
        grad, later0, all_gains[1, 0], matrix(qkv1), stack(out1), first1, common,
        ReduceWeights(columns=wide(g_gu1), down=tall(g_down1)), 6,
    )
    (grad, gain01, g_gu0, g_down0), (s_qkv1, s_out1) = feed_backward_call(
        grad, middle0, all_gains[0, 1], matrix(gu0), stack(down0), second0,
        ReduceWeights(columns=wide(g_qkv1), out=heads(g_out1)), 7,
    )
    (grad, gain00, g_qkv0, g_out0), (s_gu0, s_down0) = attention_backward_call(
        grad, start, all_gains[0, 0], matrix(qkv0), stack(out0), first0, common,
        ReduceWeights(columns=wide(g_gu0), down=tall(g_down0)), 8,
    )
    terms = jnp.concatenate([gain00, gain01, gain10, gain11]).reshape(2 * LAYERS, -1, owned).transpose(1, 0, 2)
    terms = jnp.pad(terms, ((0, 0), (0, 8 - 2 * LAYERS), (0, lane_width - owned)))
    split = lambda g: g.reshape(2, 2, rows, -1)
    s_qkv0, s_out0, s_gains, s_gu1, s_qkv1, s_gu0 = links_call(
        Both(
            ReduceWeights(columns=wide(g_qkv0), out=heads(g_out0), gains=terms, collect=True),
            CollectColumns(split(s_gu1), split(s_qkv1), split(s_gu0)),
        ),
        "last_gradients",
        9,
    )
    updates = [
        (unpack_qkv(q).astype(F32), o.astype(F32), unpack_gateup(g).astype(F32), stack(d).astype(F32))
        for q, o, g, d in ((s_qkv0, s_out0, s_gu0, s_down0), (s_qkv1, s_out1, s_gu1, s_down1))
    ]
    grad_gains = s_gains[: 2 * LAYERS, :owned].reshape(LAYERS, 2, owned)
    input_grad = lax.ppermute(grad.astype(BF), axes, pairs).astype(F32)
    return (layer_output, input_grad) + update_all(
        (w_qkv, w_out, w_gateup, w_down, norm_gains), moments, updates, grad_gains
    )


def update_all(stacked, moments, updates, grad_gains):
    step_rates = (D ** (-0.5), 4.0 * D ** (-0.5), D ** (-0.5), FF ** (-0.5), 0.5)
    shrinks = (decay_rate, decay_rate, decay_rate, decay_rate, 0.0)
    results = []
    for kind in range(5):
        grads = grad_gains if kind == 4 else jnp.stack([updates[l][kind] for l in range(LAYERS)])
        results.append(
            adam_step(stacked[kind], grads, moments[kind], moments[5 + kind], step_rates[kind], shrinks[kind])
        )
    return tuple(results[kind][part] for part in range(3) for kind in range(5))


def solution(mesh):
    in_specs = (
        P(("fsdp", "seq"), None),
        P(("fsdp", "seq"), None),
        P("fsdp", None),
        P(None, ("fsdp", "seq"), None),
        P(None, ("fsdp", "seq"), None),
        P(None, ("fsdp", "seq"), None),
        P(None, ("fsdp", "seq"), None),
        P(None, None, ("fsdp", "seq")),
        P(None, ("fsdp", "seq"), None),
        P(None, ("fsdp", "seq"), None),
        P(None, ("fsdp", "seq"), None),
        P(None, ("fsdp", "seq"), None),
        P(None, None, ("fsdp", "seq")),
        P(None, ("fsdp", "seq"), None),
        P(None, ("fsdp", "seq"), None),
        P(None, ("fsdp", "seq"), None),
        P(None, ("fsdp", "seq"), None),
        P(None, None, ("fsdp", "seq")),
    )
    out_specs = (
        P(("fsdp", "seq"), None),
        P(("fsdp", "seq"), None),
        P(None, ("fsdp", "seq"), None),
        P(None, ("fsdp", "seq"), None),
        P(None, ("fsdp", "seq"), None),
        P(None, ("fsdp", "seq"), None),
        P(None, None, ("fsdp", "seq")),
        P(None, ("fsdp", "seq"), None),
        P(None, ("fsdp", "seq"), None),
        P(None, ("fsdp", "seq"), None),
        P(None, ("fsdp", "seq"), None),
        P(None, None, ("fsdp", "seq")),
        P(None, ("fsdp", "seq"), None),
        P(None, ("fsdp", "seq"), None),
        P(None, ("fsdp", "seq"), None),
        P(None, ("fsdp", "seq"), None),
        P(None, None, ("fsdp", "seq")),
    )
    whole_tiles = (D // mesh.size) % 16 == 0 and mesh.shape["seq"] == 4 and mesh.size == 32
    body = fast_shards if whole_tiles else shards
    return jax.shard_map(body, mesh=mesh, in_specs=in_specs, out_specs=out_specs, check_vma=False)
```

```python
import functools

import jax
import jax.numpy as jnp
from jax import lax
from jax.experimental import pallas as pl
from jax.experimental.pallas import tpu as pltpu
from jax.sharding import PartitionSpec as P

D = 1536
QUERY_HEAD_COUNT = 16
KEY_VALUE_HEADS = 8
HEAD_SIZE = 96
FF = 4096
LAYERS = 2
STEP = 6


eps_norm = 1e-05
rope_base = 100000.0
beta_one = 0.9
beta_two = 0.95
adam_eps = 1e-08
decay_rate = 0.1
masked_score = -1e30
lane_width = 128


def layout(length_row, places):
    seq_ends = jnp.cumsum(length_row, dtype=jnp.int32)
    passed = (places[:, None] >= seq_ends[None, :]).astype(jnp.int32)
    segment = jnp.sum(passed, axis=1, dtype=jnp.int32)
    begins = jnp.sum(passed * length_row[None, :], axis=1, dtype=jnp.int32)
    return (segment, places - begins)


def tables(positions):
    freq_index = jnp.arange(HEAD_SIZE // 2, dtype=jnp.float32)
    inverse = rope_base ** (-2.0 * freq_index / HEAD_SIZE)
    angles = positions.astype(jnp.float32)[:, None] * inverse[None, :]
    angles = jnp.concatenate([angles, angles], axis=-1)
    return (jnp.cos(angles)[:, None, :], jnp.sin(angles)[:, None, :])


def apply_rotary(values, rotary_cosines, rotary_sines):
    half_width = values.shape[-1] // 2
    turned = jnp.concatenate([-values[..., half_width:], values[..., :half_width]], axis=-1)
    return values * rotary_cosines + turned * rotary_sines


def invert_rotary(values, rotary_cosines, rotary_sines):
    half_width = values.shape[-1] // 2
    scaled_sine = values * rotary_sines
    turned = jnp.concatenate(
        [scaled_sine[..., half_width:], -scaled_sine[..., :half_width]], axis=-1
    )
    return values * rotary_cosines + turned


def normalize(residual):
    return residual * lax.rsqrt(jnp.mean(residual * residual, axis=-1, keepdims=True) + eps_norm)


def norm_back(grad_normed, normed, residual):
    inverse = lax.rsqrt(jnp.mean(residual * residual, axis=-1, keepdims=True) + eps_norm)
    return inverse * (grad_normed - normed * jnp.mean(grad_normed * normed, axis=-1, keepdims=True))


def product(lhs_matrix, rhs_matrix):
    return jnp.dot(lhs_matrix, rhs_matrix, preferred_element_type=jnp.float32)


def attention_scores(query_head_rows, key_head_rows, allowed):
    scores = jnp.einsum(
        "qgrd,kgd->grqk", query_head_rows, key_head_rows, preferred_element_type=jnp.float32
    ) * HEAD_SIZE ** (-0.5)
    return jnp.where(allowed[None, None], scores, masked_score)


def wire_pieces(stacked, layer_index):
    return tuple((shard_piece[layer_index].astype(jnp.bfloat16) for shard_piece in stacked))


def fetch_forward(stacked, layer_index):
    qkv_piece, out_piece, gateup_piece, down_piece, gain_piece = wire_pieces(stacked, layer_index)
    return (
        lax.all_gather(qkv_piece, ("fsdp", "seq"), axis=0, tiled=True),
        lax.all_gather(out_piece, ("fsdp", "seq"), axis=0, tiled=True),
        lax.all_gather(gateup_piece, ("fsdp", "seq"), axis=0, tiled=True),
        lax.all_gather(down_piece, ("fsdp", "seq"), axis=0, tiled=True),
        lax.all_gather(gain_piece, ("fsdp", "seq"), axis=1, tiled=True),
    )


def fetch_backward(stacked, layer_index):
    qkv_piece, out_piece, gateup_piece, down_piece, gain_piece = wire_pieces(stacked, layer_index)
    return (
        lax.all_gather(qkv_piece, ("fsdp", "seq"), axis=0, tiled=True),
        lax.all_gather(out_piece, ("fsdp", "seq"), axis=0, tiled=True),
        lax.all_gather(gateup_piece, ("fsdp", "seq"), axis=0, tiled=True),
        lax.all_gather(down_piece, ("fsdp", "seq"), axis=0, tiled=True),
        lax.all_gather(gain_piece, ("fsdp", "seq"), axis=1, tiled=True),
    )


def flat_lanes(matrix):
    return matrix.reshape(-1, lane_width)


def reduce_grads(grad_terms):
    grad_qkv, grad_out_proj, grad_gateup, grad_down, grad_gains = grad_terms
    widths = (grad_qkv.shape[1], grad_out_proj.shape[1], grad_gateup.shape[1], grad_down.shape[1])
    flat_qkv = flat_lanes(grad_qkv)
    flat_out = flat_lanes(grad_out_proj)
    flat_gateup = flat_lanes(grad_gateup)
    flat_down = flat_lanes(grad_down)
    summed = (
        lax.psum_scatter(flat_qkv, ("fsdp", "seq"), scatter_dimension=0, tiled=True),
        lax.psum_scatter(flat_out, ("fsdp", "seq"), scatter_dimension=0, tiled=True),
        lax.psum_scatter(flat_gateup, ("fsdp", "seq"), scatter_dimension=0, tiled=True),
        lax.psum_scatter(flat_down, ("fsdp", "seq"), scatter_dimension=0, tiled=True),
        lax.psum_scatter(grad_gains, ("fsdp", "seq"), scatter_dimension=1, tiled=True),
    )
    owned = tuple((summed[kind_index].reshape(-1, widths[kind_index]) for kind_index in range(4)))
    return owned + (summed[4],)


def layer_forward(residual, gathered, allowed, rotary_cosines, rotary_sines):
    w_qkv, w_out, w_gateup, w_down, gain_pair = gathered
    count_of_rows = residual.shape[0]
    heads_per_group = QUERY_HEAD_COUNT // KEY_VALUE_HEADS
    gain_float = gain_pair.astype(jnp.float32)
    normed_one = normalize(residual)
    input_one = (normed_one * gain_float[0]).astype(jnp.bfloat16)
    query_key_value_rows = product(input_one, w_qkv)
    query_head_rows = apply_rotary(
        query_key_value_rows[:, : QUERY_HEAD_COUNT * HEAD_SIZE].reshape(
            count_of_rows, QUERY_HEAD_COUNT, HEAD_SIZE
        ),
        rotary_cosines,
        rotary_sines,
    ).astype(jnp.bfloat16)
    key_row_block = apply_rotary(
        query_key_value_rows[
            :, QUERY_HEAD_COUNT * HEAD_SIZE : (QUERY_HEAD_COUNT + KEY_VALUE_HEADS) * HEAD_SIZE
        ].reshape(count_of_rows, KEY_VALUE_HEADS, HEAD_SIZE),
        rotary_cosines,
        rotary_sines,
    ).astype(jnp.bfloat16)
    value_row_block = query_key_value_rows[
        :, (QUERY_HEAD_COUNT + KEY_VALUE_HEADS) * HEAD_SIZE :
    ].astype(jnp.bfloat16)
    every_key, every_value = (
        lax.all_gather(
            key_row_block.reshape(count_of_rows, KEY_VALUE_HEADS * HEAD_SIZE),
            "seq",
            axis=0,
            tiled=True,
        ),
        lax.all_gather(value_row_block, "seq", axis=0, tiled=True),
    )
    key_head_rows = every_key.reshape(-1, KEY_VALUE_HEADS, HEAD_SIZE)
    value_head_rows = every_value.reshape(-1, KEY_VALUE_HEADS, HEAD_SIZE)
    query_head_rows = query_head_rows.reshape(
        count_of_rows, KEY_VALUE_HEADS, heads_per_group, HEAD_SIZE
    )
    scores = attention_scores(query_head_rows, key_head_rows, allowed)
    row_max = jnp.max(scores, axis=-1, keepdims=True)
    shifted = jnp.exp(scores - row_max)
    row_sum = jnp.sum(shifted, axis=-1, keepdims=True)
    log_total = row_max + jnp.log(row_sum)
    attn_weights = (shifted / row_sum).astype(jnp.bfloat16)
    attended = jnp.einsum(
        "grqk,kgd->qgrd", attn_weights, value_head_rows, preferred_element_type=jnp.float32
    )
    attended = attended.reshape(count_of_rows, QUERY_HEAD_COUNT * HEAD_SIZE).astype(jnp.bfloat16)
    middle = residual + product(attended, w_out)
    normed_two = normalize(middle)
    input_two = (normed_two * gain_float[1]).astype(jnp.bfloat16)
    gate_up = product(input_two, w_gateup)
    gate_pre = gate_up[:, :FF]
    up_proj = gate_up[:, FF:]
    hidden = (jax.nn.silu(gate_pre) * up_proj).astype(jnp.bfloat16)
    layer_out = middle + product(hidden, w_down)
    saved_layer = (
        residual,
        normed_one,
        input_one,
        query_head_rows,
        key_head_rows,
        value_head_rows,
        log_total,
        attended,
        middle,
        normed_two,
        input_two,
        gate_pre,
        up_proj,
        hidden,
    )
    return (saved_layer, layer_out)


def layer_backward(grad_out, saved_layer, gathered, allowed, rotary_cosines, rotary_sines):
    w_qkv, w_out, w_gateup, w_down, gain_pair = gathered
    (
        residual,
        normed_one,
        input_one,
        query_head_rows,
        key_head_rows,
        value_head_rows,
        log_total,
        attended,
        middle,
        normed_two,
        input_two,
        gate_pre,
        up_proj,
        hidden,
    ) = saved_layer
    count_of_rows = grad_out.shape[0]
    heads_per_group = QUERY_HEAD_COUNT // KEY_VALUE_HEADS
    gain_float = gain_pair.astype(jnp.float32)
    grad_branch = grad_out.astype(jnp.bfloat16)
    grad_down = jnp.einsum("tf,td->fd", hidden, grad_branch, preferred_element_type=jnp.float32)
    grad_hidden = jnp.einsum("td,fd->tf", grad_branch, w_down, preferred_element_type=jnp.float32)
    sigmoid_gate = jax.nn.sigmoid(gate_pre)
    grad_gate = grad_hidden * up_proj * sigmoid_gate * (1.0 + gate_pre * (1.0 - sigmoid_gate))
    grad_up = grad_hidden * gate_pre * sigmoid_gate
    grad_pair = jnp.concatenate([grad_gate, grad_up], axis=1).astype(jnp.bfloat16)
    grad_gateup = jnp.einsum("td,tf->df", input_two, grad_pair, preferred_element_type=jnp.float32)
    grad_input_two = jnp.einsum(
        "tf,df->td", grad_pair, w_gateup, preferred_element_type=jnp.float32
    )
    grad_gain_two = jnp.sum(grad_input_two * normed_two, axis=0)
    grad_middle = grad_out + norm_back(grad_input_two * gain_float[1], normed_two, middle)
    grad_branch_two = grad_middle.astype(jnp.bfloat16)
    grad_out_proj = jnp.einsum(
        "te,td->ed", attended, grad_branch_two, preferred_element_type=jnp.float32
    )
    attended_gradient = jnp.einsum(
        "td,ed->te", grad_branch_two, w_out, preferred_element_type=jnp.float32
    )
    attended_gradient = attended_gradient.astype(jnp.bfloat16).reshape(
        count_of_rows, KEY_VALUE_HEADS, heads_per_group, HEAD_SIZE
    )
    scores = attention_scores(query_head_rows, key_head_rows, allowed)
    attn_float = jnp.exp(scores - log_total)
    value_gradient = jnp.einsum(
        "grqk,qgrd->kgd",
        attn_float.astype(jnp.bfloat16),
        attended_gradient,
        preferred_element_type=jnp.float32,
    )
    grad_weights = jnp.einsum(
        "qgrd,kgd->grqk", attended_gradient, value_head_rows, preferred_element_type=jnp.float32
    )
    inner_sum = jnp.sum(attn_float * grad_weights, axis=-1, keepdims=True)
    grad_scores = (attn_float * (grad_weights - inner_sum)).astype(jnp.bfloat16)
    grad_query = jnp.einsum(
        "grqk,kgd->qgrd", grad_scores, key_head_rows, preferred_element_type=jnp.float32
    ) * HEAD_SIZE ** (-0.5)
    gradient_keys = jnp.einsum(
        "grqk,qgrd->kgd", grad_scores, query_head_rows, preferred_element_type=jnp.float32
    ) * HEAD_SIZE ** (-0.5)
    shared_keys, value_share = (
        lax.psum_scatter(
            gradient_keys.reshape(-1, KEY_VALUE_HEADS * HEAD_SIZE).astype(jnp.bfloat16),
            "seq",
            scatter_dimension=0,
            tiled=True,
        ).astype(jnp.float32),
        lax.psum_scatter(
            value_gradient.reshape(-1, KEY_VALUE_HEADS * HEAD_SIZE).astype(jnp.bfloat16),
            "seq",
            scatter_dimension=0,
            tiled=True,
        ).astype(jnp.float32),
    )
    grad_q = invert_rotary(
        grad_query.reshape(count_of_rows, QUERY_HEAD_COUNT, HEAD_SIZE), rotary_cosines, rotary_sines
    ).reshape(count_of_rows, QUERY_HEAD_COUNT * HEAD_SIZE)
    key_gradient = invert_rotary(
        shared_keys.reshape(count_of_rows, KEY_VALUE_HEADS, HEAD_SIZE), rotary_cosines, rotary_sines
    ).reshape(count_of_rows, KEY_VALUE_HEADS * HEAD_SIZE)
    grad_rows = jnp.concatenate([grad_q, key_gradient, value_share], axis=1).astype(jnp.bfloat16)
    grad_qkv = jnp.einsum("td,tf->df", input_one, grad_rows, preferred_element_type=jnp.float32)
    grad_input_one = jnp.einsum("tf,df->td", grad_rows, w_qkv, preferred_element_type=jnp.float32)
    grad_gain_one = jnp.sum(grad_input_one * normed_one, axis=0)
    grad_in = grad_middle + norm_back(grad_input_one * gain_float[0], normed_one, residual)
    return (
        grad_in,
        (
            grad_qkv,
            grad_out_proj,
            grad_gateup,
            grad_down,
            jnp.stack([grad_gain_one, grad_gain_two]),
        ),
    )


def adam_step(weight, gradient, first_moment, second_moment, step_rate, shrink):
    first_moment = beta_one * first_moment + (1.0 - beta_one) * gradient
    second_moment = beta_two * second_moment + (1.0 - beta_two) * gradient * gradient
    first_hat = first_moment / (1.0 - beta_one**STEP)
    second_hat = second_moment / (1.0 - beta_two**STEP)
    weight = weight - step_rate * (first_hat / (jnp.sqrt(second_hat) + adam_eps) + shrink * weight)
    return (weight, first_moment, second_moment)


def shards(
    tokens,
    cotangent,
    lengths,
    w_qkv,
    w_out,
    w_gateup,
    w_down,
    norm_gains,
    first_qkv,
    first_out,
    first_gateup,
    first_down,
    first_gains,
    second_qkv,
    second_out,
    second_gateup,
    second_down,
    second_gains,
):
    count_of_rows = tokens.shape[0]
    group_rows = count_of_rows * lax.axis_size("seq")
    place_rows = lax.axis_index("seq") * count_of_rows + jnp.arange(count_of_rows, dtype=jnp.int32)
    key_places = jnp.arange(group_rows, dtype=jnp.int32)
    seg_rows, positions = layout(lengths[0], place_rows)
    seg_keys = layout(lengths[0], key_places)[0]
    allowed = (seg_rows[:, None] == seg_keys[None, :]) & (
        key_places[None, :] <= place_rows[:, None]
    )
    rotary_cosines, rotary_sines = tables(positions)
    stacked = (w_qkv, w_out, w_gateup, w_down, norm_gains)
    residual = tokens.astype(jnp.float32)
    saved_all = []
    for layer_index in range(LAYERS):
        gathered = fetch_forward(stacked, layer_index)
        saved_layer, residual = layer_forward(
            residual, gathered, allowed, rotary_cosines, rotary_sines
        )
        saved_all.append(saved_layer)
    grad_state = cotangent.astype(jnp.float32)
    updates = [None] * LAYERS
    for layer_index in reversed(range(LAYERS)):
        gathered = fetch_backward(stacked, layer_index)
        grad_state, grad_terms = layer_backward(
            grad_state, saved_all[layer_index], gathered, allowed, rotary_cosines, rotary_sines
        )
        updates[layer_index] = reduce_grads(grad_terms)
    step_rates = (D ** (-0.5), 4.0 * D ** (-0.5), D ** (-0.5), FF ** (-0.5), 0.5)
    shrinks = (decay_rate, decay_rate, decay_rate, decay_rate, 0.0)
    firsts = (first_qkv, first_out, first_gateup, first_down, first_gains)
    seconds = (second_qkv, second_out, second_gateup, second_down, second_gains)
    new_weights = []
    new_firsts = []
    new_seconds = []
    for kind_index in range(5):
        grads_kind = jnp.stack([updates[layer_index][kind_index] for layer_index in range(LAYERS)])
        weight, first_moment, second_moment = adam_step(
            stacked[kind_index],
            grads_kind,
            firsts[kind_index],
            seconds[kind_index],
            step_rates[kind_index],
            shrinks[kind_index],
        )
        new_weights.append(weight)
        new_firsts.append(first_moment)
        new_seconds.append(second_moment)
    outputs = [residual.astype(jnp.bfloat16), grad_state] + new_weights + new_firsts + new_seconds
    return tuple(outputs)


MESH = pl.DeviceIdType.MESH
BF = jnp.bfloat16
F32 = jnp.float32
KV_RANK = KEY_VALUE_HEADS // 4
Q_RANK = QUERY_HEAD_COUNT // 4
ANY = pl.BlockSpec(memory_space=pl.ANY)
VM = pl.BlockSpec(memory_space=pltpu.VMEM)
DMA = pltpu.SemaphoreType.DMA


class Place:
    def __init__(self):
        f, z = lax.axis_index("fsdp"), lax.axis_index("seq")
        self.y, self.x, self.c = lax.div(f, 4), lax.rem(lax.div(f, 2), 2), lax.rem(f, 2)
        self.z1, self.z0 = lax.div(z, 2), lax.rem(z, 2)
        self.rank = 2 * self.c + self.z0
        self.inner = self.z1 != self.z0
        self.sibling, self.over = 2 * (1 - self.c) + self.z0, 2 * self.c + 1 - self.z0
        self.diagonal = 2 * (1 - self.c) + 1 - self.z0
        self.peer = {
            "y": (f + 4 - 8 * self.y, z),
            "x": (f + 2 - 4 * self.x, z),
            "c": (f + 1 - 2 * self.c, z),
            "z1": (f, z + 2 - 4 * self.z1),
            "z0": (f, z + 1 - 2 * self.z0),
            "cz": (f + 1 - 2 * self.c, z + 1 - 2 * self.z0),
            "swap": (f - self.c + self.z1, 2 * self.c + self.z0),
            "mid": (f, 3 - z),
        }


def greet(place, names):
    barrier = pltpu.get_barrier_semaphore()
    partial = {"swap": place.c != place.z1, "mid": place.inner}
    amount = len([n for n in names if n not in partial])
    for name in names:
        if name not in partial:
            pl.semaphore_signal(barrier, inc=1, device_id=place.peer[name], device_id_type=MESH)
    for name, holds in partial.items():
        if name in names:
            amount = amount + holds.astype(jnp.int32)

            @pl.when(holds)
            def _(name=name):
                pl.semaphore_signal(barrier, inc=1, device_id=place.peer[name], device_id_type=MESH)

    pl.semaphore_wait(barrier, amount)


def remote(src, dst, send_sem, recv_sem, device):
    return pltpu.make_async_remote_copy(
        src_ref=src, dst_ref=dst, send_sem=send_sem, recv_sem=recv_sem, device_id=device, device_id_type=MESH
    )


def columns_index(y, x, z1, h):
    return ((y * 2 + x) * 2 + h) * 2 + z1


def rows_index(y, x, z1, h):
    return ((y * 2 + x) * 2 + z1) * 2 + h


class Cross:
    def __init__(self, place, src, dst_there, dst_here, relay, send, recv):
        self.p, self.src, self.dst_there, self.dst_here, self.relay = place, src, dst_there, dst_here, relay
        self.send, self.recv = send, recv

    def copy(self, k):
        p, relay = self.p, self.relay
        src, dst, peer = (
            (self.src, relay.at[0], "z0"),
            (self.src, relay.at[1], "mid"),
            (relay.at[0], self.dst_there, "mid"),
            (relay.at[1], self.dst_here, "z0"),
        )[k]
        return remote(src, dst, self.send.at[k], self.recv.at[k], p.peer[peer])

    def start(self):
        @pl.when(self.p.inner)
        def _():
            self.copy(1).start()

        @pl.when(jnp.logical_not(self.p.inner))
        def _():
            self.copy(0).start()

    def bring(self):
        @pl.when(self.p.inner)
        def _():
            self.copy(1).wait_recv()
            self.copy(3).start()

    def take(self):
        @pl.when(self.p.inner)
        def _():
            self.copy(0).wait_recv()
            self.copy(2).start()

    def wait(self):
        @pl.when(self.p.inner)
        def _():
            self.copy(2).wait_recv()

        @pl.when(jnp.logical_not(self.p.inner))
        def _():
            self.copy(3).wait_recv()

    def finish(self):
        @pl.when(self.p.inner)
        def _():
            for k in (1, 2, 3):
                self.copy(k).wait_send()

        @pl.when(jnp.logical_not(self.p.inner))
        def _():
            self.copy(0).wait_send()


class Gather:
    def __init__(self, place, ref, index, send, recv, local, relay, src=None):
        self.p, self.ref, self.index, self.send, self.recv = place, ref, index, send, recv
        self.local, self.src = local, src
        self.cross = []
        for h in (0, 1):
            block = self.at((), h)
            self.cross.append(
                Cross(
                    place,
                    block if src is None else src.at[h],
                    block,
                    self.at(("z1",), h),
                    relay.at[h],
                    *[s.at[pl.ds(14 + 4 * h, 4)] for s in (send, recv)],
                )
            )

    def at(self, flips, h):
        p = self.p
        flip = lambda v, name: 1 - v if name in flips else v
        return self.ref.at[self.index(flip(p.y, "y"), flip(p.x, "x"), flip(p.z1, "z1"), h)]

    def route(self, h):
        a, b = ("y", "x") if h == 0 else ("x", "y")
        return (
            ("z1", ()),
            (a, ()),
            (a, ("z1",)),
            (b, ()),
            (b, ("z1",)),
            (b, (a,)),
            (b, (a, "z1")),
        )

    def out(self, h, m):
        axis, flips = self.route(h)[m]
        dst = src = self.at(flips, h)
        if self.src is not None and not flips:
            src = self.src.at[h]
        return remote(src, dst, self.send.at[7 * h + m], self.recv.at[7 * h + m], self.p.peer[axis])

    def into(self, h, m):
        axis, flips = self.route(h)[m]
        ref = self.at(flips + (axis,), h)
        return remote(ref, ref, self.send.at[7 * h + m], self.recv.at[7 * h + m], self.p.peer[axis])

    def keep(self, h):
        return pltpu.make_async_copy(self.src.at[h], self.at((), h), self.local.at[h])

    def first(self):
        for c in self.cross:
            c.start()

    def second(self):
        for m in (1, 3):
            for h in (0, 1):
                self.out(h, m).start()
        if self.src is not None:
            for h in (0, 1):
                self.keep(h).start()

    def turned(self, h):
        self.cross[h].wait()
        for m in (2, 4):
            self.out(h, m).start()

    def on(self, h, got, gives):
        self.into(h, got).wait_recv()
        for m in gives:
            self.out(h, m).start()

    def last(self):
        for h in (0, 1):
            for m in (3, 4, 5, 6):
                self.into(h, m).wait_recv()
            for m in range(1, 7):
                self.out(h, m).wait_send()
            self.cross[h].finish()
            if self.src is not None:
                self.keep(h).wait()

    def steps(self, when):
        part = functools.partial
        acts = [(when["start"], self.first), (when["start"], self.second)]
        for h in (0, 1):
            acts.append((when["bring"][h], self.cross[h].bring))
            acts.append((when["take"][h], self.cross[h].take))
            acts.append((when["turn"][h], part(self.turned, h)))
            acts.append((when["five"], part(self.on, h, 1, (5,))))
            acts.append((when["six"][h], part(self.on, h, 2, (6,))))
        return acts + [(when["last"], self.last)]


def times(start, bring, take, five, turn, six, last=99):
    return dict(start=start, bring=bring, take=take, five=five, turn=turn, six=six, last=last)


class Spread:
    def __init__(self, place, src, target, send, recv, local):
        self.p, self.src, self.target, self.send, self.recv, self.local = place, src, target, send, recv, local

    def copy(self, k, arriving=False):
        p = self.p
        name, fc, fz = (("c", 1, 0), ("z0", 0, 1), ("cz", 1, 1))[k]
        c = 1 - p.c if fc else p.c
        z0 = 1 - p.z0 if fz else p.z0
        src = self.src(c, z0)
        dst = self.target(c, z0) if arriving else self.target(p.c, p.z0)
        return remote(src, dst, self.send.at[k], self.recv.at[k], p.peer[name])

    def own(self):
        p = self.p
        return pltpu.make_async_copy(self.src(p.c, p.z0), self.target(p.c, p.z0), self.local)

    def start(self):
        for k in range(3):
            self.copy(k).start()
        self.own().start()

    def wait(self):
        for k in range(3):
            self.copy(k, True).wait_recv()
        self.own().wait()

    def finish(self):
        for k in range(3):
            self.copy(k).wait_send()


def add_to(dst, src):
    dst[...] = (dst[...].astype(F32) + src[...].astype(F32)).astype(dst.dtype)


class Reduce:
    def __init__(self, place, ref, index, out, mine, one, two, three, relay, send, recv, local):
        self.cross = [
            Cross(
                place, two.at[h, 0], three.at[h], three.at[h], relay.at[h], *[s.at[pl.ds(14 + 4 * h, 4)] for s in (send, recv)]
            )
            for h in ((0, 1) if out.shape != two.shape else ())
        ]
        self.p, self.ref, self.index, self.result = place, ref, index, out
        self.mine, self.one, self.two, self.three = mine, one, two, three
        self.send, self.recv, self.local = send, recv, local
        self.open = out.shape == two.shape

    def block(self, h, far_a, m):
        p = self.p
        a, b = (p.x, p.y) if h == 0 else (p.y, p.x)
        a = 1 - a if far_a else a
        b = 1 - b if m < 2 else b
        z1 = 1 - p.z1 if m % 2 == 0 else p.z1
        y, x = (b, a) if h == 0 else (a, b)
        return self.ref.at[self.index(y, x, z1, h)]

    def copy(self, h, m):
        p = self.p
        name_a, name_b = ("x", "y") if h == 0 else ("y", "x")
        sems = self.send.at[7 * h + m], self.recv.at[7 * h + m]
        if m < 4:
            return remote(self.block(h, True, m), self.one.at[h, m], *sems, p.peer[name_a])
        return remote(self.one.at[h, m - 4], self.two.at[h, m - 4], *sems, p.peer[name_b])

    def near(self, h, m):
        return self.block(h, False, m) if self.mine is None else self.mine.at[h, m]

    def load(self, h, m):
        return pltpu.make_async_copy(self.block(h, False, m), self.mine.at[h, m], self.local.at[4 * h + m])

    def first(self):
        for m in range(4):
            for h in (0, 1):
                self.copy(h, m).start()
                if self.mine is not None:
                    self.load(h, m).start()

    def second(self, h, m):
        self.copy(h, m).wait_recv()
        if self.mine is not None:
            self.load(h, m).wait()
        add_to(self.one.at[h, m], self.near(h, m))
        if m < 2:
            self.copy(h, 4 + m).start()

    def third(self, h, k):
        self.copy(h, 4 + k).wait_recv()
        add_to(self.two.at[h, k], self.one.at[h, 2 + k])
        if k == 0 and not self.open:
            self.cross[h].start()

    def fourth(self, h):
        self.cross[h].wait()
        add_to(self.three.at[h], self.two.at[h, 1])

    def finish(self):
        for h in (0, 1):
            for m in range(6):
                self.copy(h, m).wait_send()
            if not self.open:
                self.cross[h].finish()

    def store(self):
        src = self.two if self.result.shape == self.two.shape else self.three
        return pltpu.make_async_copy(src, self.result, self.local.at[8])


def out_gather_steps(p, src, ref, send, recv, local):
    home = p.x == p.z0
    away = jnp.logical_not(home)
    at = lambda fy, fz: ref.at[(1 - p.y if fy else p.y) * 2 + (1 - p.z1 if fz else p.z1)]
    pair = lambda half: remote(src, at(0, 0).at[half], send.at[0], recv.at[0], p.peer["z0"])
    z1_copy = lambda fz: remote(at(0, fz), at(0, fz), send.at[1], recv.at[1], p.peer["z1"])
    x_copy = lambda k: remote(at(0, k), at(0, k), send.at[2 + k], recv.at[2 + k], p.peer["x"])
    y_copy = lambda k, fy: remote(at(fy, k), at(fy, k), send.at[4 + k], recv.at[4 + k], p.peer["y"])
    own = pltpu.make_async_copy(src, at(0, 0).at[p.z0], local)

    def zero():
        @pl.when(home)
        def _():
            own.start()

        @pl.when(away)
        def _():
            pair(p.z0).start()

    def one():
        @pl.when(home)
        def _():
            own.wait()
            pair(1 - p.z0).wait_recv()
            z1_copy(0).start()
            x_copy(0).start()
            y_copy(0, 0).start()

    def two():
        @pl.when(home)
        def _():
            z1_copy(1).wait_recv()
            x_copy(1).start()
            y_copy(1, 0).start()

    def three():
        @pl.when(away)
        def _():
            for k in (0, 1):
                x_copy(k).wait_recv()
                y_copy(k, 0).start()

    def last():
        for k in (0, 1):
            y_copy(k, 1).wait_recv()
            y_copy(k, 0).wait_send()

        @pl.when(home)
        def _():
            z1_copy(0).wait_send()
            for k in (0, 1):
                x_copy(k).wait_send()

        @pl.when(away)
        def _():
            pair(p.z0).wait_send()

    return [zero, one, two, three, last]


def out_reduce_steps(p, ref, out, one, two, three, got, send, recv, local):
    home = p.x == p.z0
    away = jnp.logical_not(home)
    y_copy = lambda k: remote(ref.at[(1 - p.y) * 2 + k], one.at[k], send.at[k], recv.at[k], p.peer["y"])
    x_copy = lambda k: remote(one.at[k], two.at[k], send.at[2 + k], recv.at[2 + k], p.peer["x"])
    z1_copy = remote(two.at[1 - p.z1], three, send.at[4], recv.at[4], p.peer["z1"])
    rows = three.shape[0] // 2
    half = lambda z0: three.at[pl.ds(pl.multiple_of(z0 * rows, rows), rows)]
    pair = remote(half(1 - p.z0), got, send.at[5], recv.at[5], p.peer["z0"])
    keep = pltpu.make_async_copy(half(p.z0), out, local.at[0])
    take = pltpu.make_async_copy(got, out, local.at[0])

    def zero():
        for k in (0, 1):
            y_copy(k).start()

    def first():
        for k in (0, 1):
            y_copy(k).wait_recv()
            add_to(one.at[k], ref.at[p.y * 2 + k])

            @pl.when(away)
            def _(k=k):
                x_copy(k).start()

    def second():
        @pl.when(home)
        def _():
            for k in (0, 1):
                x_copy(k).wait_recv()
                add_to(two.at[k], one.at[k])
            z1_copy.start()

    def third():
        @pl.when(home)
        def _():
            z1_copy.wait_recv()
            add_to(three, two.at[p.z1])
            pair.start()
            keep.start()

    def last():
        for k in (0, 1):
            y_copy(k).wait_send()

        @pl.when(home)
        def _():
            keep.wait()
            z1_copy.wait_send()
            pair.wait_send()

        @pl.when(away)
        def _():
            pair.wait_recv()
            take.start()
            for k in (0, 1):
                x_copy(k).wait_send()
            take.wait()

    return [zero, first, second, third, last]


def out_reduce_scratch(wide):
    return [
        pltpu.VMEM((4,) + wide, BF),
        pltpu.VMEM((2,) + wide, BF),
        pltpu.VMEM((2,) + wide, BF),
        pltpu.VMEM(wide, BF),
        pltpu.VMEM((wide[0] // 2, wide[1]), BF),
        DMA((6,)),
        DMA((6,)),
        DMA((1,)),
    ]


def gains_gather(p, src, ref, send, recv, local):
    me = ((p.y * 2 + p.x) * 2 + p.c) * 4 + p.z1 * 2 + p.z0
    own = pltpu.make_async_copy(src, ref.at[me], local)
    names = ("z0", "z1", "c", "x", "y")

    def span(k, other):
        size = 1 << k
        start = lax.div(me, size) * size
        if other:
            bit = lax.rem(lax.div(me, size), 2)
            start = start + size - 2 * size * bit
        return ref.at[pl.ds(start, size)]

    def copy(k, other):
        return remote(span(k, other), span(k, other), send.at[k], recv.at[k], p.peer[names[k]])

    def step(k):
        def run():
            if k == 0:
                own.start()
                own.wait()
            else:
                copy(k - 1, True).wait_recv()
            if k < 5:
                copy(k, False).start()
            else:
                for j in range(5):
                    copy(j, False).wait_send()

        return run

    return [step(k) for k in range(6)]


def gains_reduce(p, src, out, base, halves, send, recv, local):
    names, bits = ("y", "x", "c", "z1", "z0"), (p.y, p.x, p.c, p.z1, p.z0)
    load = pltpu.make_async_copy(src, base, local.at[0])
    keep = pltpu.make_async_copy(halves[4].at[0], out, local.at[0])

    def part(k, bit):
        source, size = (base if k == 0 else halves[k - 1]), 16 >> k
        return source.at[pl.ds(bit * size, size)]

    def copy(k):
        return remote(part(k, 1 - bits[k]), halves[k], send.at[k], recv.at[k], p.peer[names[k]])

    def step(k):
        def run():
            if k > 0:
                copy(k - 1).wait_recv()
                halves[k - 1][...] += part(k - 1, bits[k - 1])[...]
            else:
                load.start()
                load.wait()
            if k < 5:
                copy(k).start()
            else:
                keep.start()
                for j in range(5):
                    copy(j).wait_send()
                keep.wait()

        return run

    return [step(k) for k in range(6)]


GROUP = ("c", "z0", "cz")
EIGHT = ("z1", "y", "x")


CHUNKS = 2


class ShareRows:
    def __init__(self, p, dst, send, recv):
        self.p, self.dst, self.send, self.recv = p, dst, send, recv
        self.rows = dst.shape[1] // CHUNKS

    def chunk(self, rank, k):
        return self.dst.at[rank, pl.ds(k * self.rows, self.rows)]

    def over(self, k, arriving=False):
        p = self.p
        ref = self.chunk(p.over if arriving else p.rank, k)
        return remote(ref, ref, self.send.at[k], self.recv.at[k], p.peer["z0"])

    def across(self, arriving=False):
        p = self.p
        ref = self.dst.at[p.sibling if arriving else p.rank]
        return remote(ref, ref, self.send.at[CHUNKS], self.recv.at[CHUNKS], p.peer["c"])

    def onward(self, k, arriving=False):
        p = self.p
        ours, theirs = 2 * p.c + 1 - p.z0, 2 * (1 - p.c) + 1 - p.z0
        ref = self.chunk(theirs if arriving else ours, k)
        return remote(ref, ref, self.send.at[CHUNKS + 1 + k], self.recv.at[CHUNKS + 1 + k], p.peer["c"])

    def start(self):
        for k in range(CHUNKS):
            self.over(k).start()
        self.across().start()

    def pass_on(self, k):
        self.over(k, True).wait_recv()
        self.onward(k).start()

    def far(self, k):
        self.onward(k, True).wait_recv()

    def finish(self):
        for k in range(CHUNKS):
            self.over(k).wait_send()
            self.onward(k).wait_send()
        self.across().wait_send()


class SumRows:
    def __init__(self, p, terms, near, cross, far, send, recv):
        self.p, self.terms, self.near, self.cross, self.far, self.send, self.recv = p, terms, near, cross, far, send, recv
        self.rows = near.shape[0] // CHUNKS

    def diagonal(self, k):
        p = self.p
        part = pl.ds(k * self.rows, self.rows)
        rank = 2 * (1 - p.c) + 1 - p.z0
        return remote(self.terms.at[rank, part], self.cross.at[part], self.send.at[k], self.recv.at[k], p.peer["c"])

    def sibling(self):
        p = self.p
        rank, at = 2 * (1 - p.c) + p.z0, CHUNKS
        return remote(self.terms.at[rank], self.near, self.send.at[at], self.recv.at[at], p.peer["c"])

    def over(self, k):
        p, at = self.p, CHUNKS + 1 + k
        part = pl.ds(k * self.rows, self.rows)
        return remote(self.cross.at[part], self.far.at[part], self.send.at[at], self.recv.at[at], p.peer["z0"])

    def relay(self, k):
        p = self.p
        self.diagonal(k).wait_recv()
        part = pl.ds(k * self.rows, self.rows)
        add_to(self.cross.at[part], self.terms.at[2 * p.c + 1 - p.z0, part])
        self.over(k).start()

    def finish(self):
        for k in range(CHUNKS):
            self.diagonal(k).wait_send()
            self.over(k).wait_send()
        self.sibling().wait_send()


def swap_pairs(count_fsdp, count_seq):
    pairs = []
    for f in range(count_fsdp):
        for z in range(count_seq):
            c, z1 = f % 2, z // 2
            pairs.append((f * count_seq + z, (f - c + z1) * count_seq + c * 2 + z % 2))
    return pairs


TILE = 256
UP_TILE = 512
DOWN_TILE = 768
GRAD_TILE = 512
HALVES = 2


def wide_params(collective_id):
    return pltpu.CompilerParams(
        collective_id=collective_id, has_side_effects=True, vmem_limit_bytes=58 * 2**20
    )


def dot(a, b, contract=((1,), (0,))):
    return lax.dot_general(a, b, (contract, ((), ())), preferred_element_type=F32)


def row_normalize(ref, gain, out, rows=32):
    def step(k, _):
        at = pl.ds(pl.multiple_of(k * rows, rows), rows)
        value = ref[at, :].astype(F32)
        out[at, :] = (normalize(value) * gain[...]).astype(out.dtype)
        return 0

    lax.fori_loop(0, ref.shape[0] // rows, step, 0)


def column_tiles(width, tile, step):
    def run(j, _):
        step(pl.multiple_of(j * tile, tile))
        return 0

    lax.fori_loop(0, width // tile, run, 0)


def exchange(p, share, total, compute, advance):
    rows = total.near.shape[0]
    part = rows // CHUNKS
    share.start()
    advance()
    compute([(p.rank, 0)], rows)
    advance()
    share.across(True).wait_recv()
    compute([(p.sibling, 0)], rows)
    total.sibling().start()
    advance()
    for k in range(CHUNKS):
        share.pass_on(k)
        share.far(k)
        compute([(p.diagonal, k * part), (p.over, k * part)], part)
        total.diagonal(k).start()
        total.relay(k)
        advance()


def gather_pieces(ref, pieces, count, *index):
    parts = [ref[(rank, pl.ds(first, count)) + index] for rank, first in pieces]
    return parts[0] if len(parts) == 1 else jnp.concatenate(parts, axis=0)


def scatter_pieces(ref, pieces, count, value, *index):
    for k, (rank, first) in enumerate(pieces):
        ref[(rank, pl.ds(first, count)) + index] = value[k * count : (k + 1) * count]


def token_rows(pieces, count, rows):
    return [pl.ds(pl.multiple_of(rank * rows + first, count), count) for rank, first in pieces]


def collect(p, total, write, rows=32):
    total.sibling().wait_recv()
    for k in range(CHUNKS):
        total.over(k).wait_recv()

        def step(j, _, k=k):
            at = pl.ds(pl.multiple_of(k * total.rows + j * rows, rows), rows)
            value = total.terms[p.rank, at, :].astype(F32) + total.near[at, :].astype(F32)
            write(at, value + total.far[at, :].astype(F32))
            return 0

        lax.fori_loop(0, total.rows // rows, step, 0)


def exchange_scratch(rows):
    part = pltpu.VMEM((rows, D), BF)
    sems = DMA((2 * CHUNKS + 1,))
    return [pltpu.VMEM((4, rows, D), BF), part, part, part, sems, sems, sems, sems]


def exchange_of(p, every, refs):
    terms, near, cross, far, send, recv, t_send, t_recv = refs
    share = ShareRows(p, every, send, recv)
    return every.at[p.rank], terms, share, SumRows(p, terms, near, cross, far, t_send, t_recv)


class Nothing:
    names, args, specs, shapes, scratch = (), (), (), (), ()

    def steps(self, p, ins, outs, scratch):
        return []


class Clock:
    def __init__(self, steps):
        self.steps, self.now = sorted(steps, key=lambda s: s[0]), 0

    def __call__(self):
        while self.steps and self.steps[0][0] <= self.now:
            self.steps.pop(0)[1]()
        self.now += 1

    def finish(self):
        for _, act in self.steps:
            act()
        self.steps = []


class Staged:
    def __init__(self, ins, in_sems, outs, out_sems):
        self.loads = {k: pltpu.make_async_copy(src, dst, in_sems.at[n]) for n, (k, src, dst) in enumerate(ins)}
        self.stores = {k: pltpu.make_async_copy(src, dst, out_sems.at[n]) for n, (k, src, dst) in enumerate(outs)}
        self.started = []
        for load in self.loads.values():
            load.start()

    def ready(self, *ks):
        for k in ks:
            if k in self.loads:
                self.loads.pop(k).wait()

    def flush(self, *ks):
        for k in ks:
            store = self.stores.pop(k)
            store.start()
            self.started.append(store)

    def finish(self):
        self.ready(*list(self.loads))
        self.flush(*list(self.stores))
        for store in self.started:
            store.wait()


def beside_call(
    body, args, late, shapes, later, scratch, beside, name, collective_id, flops, peers=("c", "z0"), specs=None
):
    n_ins, n_outs = len(args), len(shapes)
    buffers = [pltpu.VMEM(args[k].shape, args[k].dtype) for k in late]
    buffers += [pltpu.VMEM(shapes[k].shape, shapes[k].dtype) for k in later]
    sems = [DMA((max(len(late), 1),)), DMA((max(len(later), 1),))]
    counts = [n_ins, len(beside.args), n_outs, len(beside.shapes), len(scratch), len(buffers), 2, len(beside.scratch)]

    def whole(*refs):
        groups, at = [], 0
        for n in counts:
            groups.append(list(refs[at : at + n]))
            at += n
        ins, b_ins, outs, b_outs, own, held, (in_sems, out_sems), b_scratch = groups
        moved_in = [(k, ins[k], held[n]) for n, k in enumerate(late)]
        moved_out = [(k, held[len(late) + n], outs[k]) for n, k in enumerate(later)]
        staged = Staged(moved_in, in_sems, moved_out, out_sems)
        for k, _, dst in moved_in:
            ins[k] = dst
        for k, src, _ in moved_out:
            outs[k] = src
        p = Place()
        greet(p, tuple(peers) + tuple(n for n in beside.names if n not in peers))
        body(p, ins, outs, own, Clock(beside.steps(p, b_ins, b_outs, b_scratch)), staged)
        staged.finish()

    specs = specs or {}
    out = pl.pallas_call(
        whole,
        out_shape=list(shapes) + list(beside.shapes),
        in_specs=[ANY if k in late else VM for k in range(n_ins)] + list(beside.specs),
        out_specs=[ANY if k in later else specs.get(k, VM) for k in range(n_outs)] + [ANY] * len(beside.shapes),
        scratch_shapes=list(scratch) + buffers + sems + list(beside.scratch),
        compiler_params=wide_params(collective_id),
        cost_estimate=pl.CostEstimate(flops=flops, bytes_accessed=20 * 2**20, transcendentals=0),
        name=name,
    )(*args, *beside.args)
    return out[:n_outs], out[n_outs:]


def feed_forward_call(middle, gain, w_gateup, w_down, beside, collective_id, dtype=F32):
    rows, wide = middle.shape[0], w_down.shape[0]

    def body(p, ins, outs, scratch, advance, staged):
        mid_ref, gain_ref, gu_ref, down_ref = ins
        new_ref, every, gate_ref, up_ref, hid_ref = outs
        own, terms, share, total = exchange_of(p, every, scratch)

        def compute(pieces, count):
            staged.ready(2, 3)

            def up_tile(j):
                cols, far = pl.ds(j, UP_TILE), pl.ds(wide + j, UP_TILE)
                x = gather_pieces(every, pieces, count)
                gate, up = dot(x, gu_ref[:, cols]), dot(x, gu_ref[:, far])
                scatter_pieces(gate_ref, pieces, count, gate.astype(BF), cols)
                scatter_pieces(up_ref, pieces, count, up.astype(BF), cols)
                hidden = (gate / (1.0 + jnp.exp(-gate)) * up).astype(BF)
                scatter_pieces(hid_ref, pieces, count, hidden, cols)

            column_tiles(wide, UP_TILE, up_tile)

            def down_tile(j):
                cols = pl.ds(j, DOWN_TILE)
                value = dot(gather_pieces(hid_ref, pieces, count), down_ref[:, cols]).astype(BF)
                scatter_pieces(terms, pieces, count, value, cols)

            column_tiles(D, DOWN_TILE, down_tile)

        row_normalize(mid_ref, gain_ref, own)
        exchange(p, share, total, compute, advance)
        staged.flush(1, 2, 3, 4)

        def write(at, value):
            new_ref[at, :] = (mid_ref[at, :] + value).astype(dtype)

        collect(p, total, write)
        advance.finish()
        share.finish()
        total.finish()

    return beside_call(
        body,
        (middle, gain.reshape(1, D), w_gateup, w_down),
        (2, 3),
        [
            jax.ShapeDtypeStruct((rows, D), dtype),
            jax.ShapeDtypeStruct((4, rows, D), BF),
            jax.ShapeDtypeStruct((4, rows, wide), BF),
            jax.ShapeDtypeStruct((4, rows, wide), BF),
            jax.ShapeDtypeStruct((4, rows, wide), BF),
        ],
        (1, 2, 3, 4),
        exchange_scratch(rows),
        beside,
        "feed_forward",
        collective_id,
        6 * 4 * rows * wide * D,
    )


def feed_backward_call(grad, middle, gain, w_gateup, w_down, kept, beside, collective_id):
    every, gate, up, hidden = kept
    rows, wide = middle.shape[0], w_down.shape[0]
    block = (wide // 16, D)

    def body(p, ins, outs, scratch, advance, staged):
        grad_ref, mid_ref, gain_ref, gu_ref, down_ref, every_ref, gate_ref, up_ref, hid_ref = ins
        new_ref, gain_out, g_gu, two_down = outs
        e, pair, g_down, one, two, send, recv, local = scratch[:8]
        own, terms, share, total = exchange_of(p, e, scratch[8:])
        reduce = Reduce(p, g_down, rows_index, two_down, None, one, two, None, None, send, recv, local)

        def compute(pieces, count):
            staged.ready(4, 6, 7, 3)

            def up_tile(j):
                cols, far = pl.ds(j, UP_TILE), pl.ds(wide + j, UP_TILE)
                grad_hidden = dot(gather_pieces(e, pieces, count), down_ref[cols, :], ((1,), (1,)))
                g = gather_pieces(gate_ref, pieces, count, cols).astype(F32)
                u = gather_pieces(up_ref, pieces, count, cols).astype(F32)
                s = 1.0 / (1.0 + jnp.exp(-g))
                grad_gate = (grad_hidden * u * s * (1.0 + g * (1.0 - s))).astype(BF)
                scatter_pieces(pair, pieces, count, grad_gate, cols)
                scatter_pieces(pair, pieces, count, (grad_hidden * g * s).astype(BF), far)

            column_tiles(wide, UP_TILE, up_tile)

            def down_tile(j):
                cols = pl.ds(j, DOWN_TILE)
                value = dot(gather_pieces(pair, pieces, count), gu_ref[cols, :], ((1,), (1,))).astype(BF)
                scatter_pieces(terms, pieces, count, value, cols)

            column_tiles(D, DOWN_TILE, down_tile)

        def weight_grads():
            tokens = 4 * rows
            e_all, pair_all, x_all, hid_all = (
                r.reshape(tokens, r.shape[2]) for r in (e, pair, every_ref, hid_ref)
            )

            part = g_down.shape[1]
            staged.ready(8, 5)

            def down_grad(j):
                value = dot(hid_all[:, pl.ds(j, GRAD_TILE)], e_all[...], ((0,), (0,))).astype(BF)
                g_down[pl.ds(lax.div(j, part), GRAD_TILE // part)] = value.reshape(GRAD_TILE // part, part, D)

            column_tiles(wide, GRAD_TILE, down_grad)
            reduce.first()
            for k in range(D // GRAD_TILE):
                cols = slice(k * GRAD_TILE, (k + 1) * GRAD_TILE)
                g_gu[cols, :] = dot(x_all[:, cols], pair_all[...], ((0,), (0,))).astype(BF)
                advance()
                if k < 2:
                    for m in (2 * k, 2 * k + 1):
                        for h in (0, 1):
                            reduce.second(h, m)
            staged.flush(2)

        def copy_own(k, _):
            at = pl.ds(pl.multiple_of(k * 32, 32), 32)
            own[at, :] = grad_ref[at, :].astype(BF)
            return 0

        lax.fori_loop(0, rows // 32, copy_own, 0)
        exchange(p, share, total, compute, advance)
        weight_grads()
        gain_out[...] = jnp.zeros_like(gain_out)

        def write(at, value):
            mid = mid_ref[at, :]
            normed = normalize(mid)
            gain_out[...] += jnp.sum(value * normed, axis=0, keepdims=True)
            new_ref[at, :] = grad_ref[at, :] + norm_back(value * gain_ref[...], normed, mid)

        collect(p, total, write)
        for k in (0, 1):
            for h in (0, 1):
                reduce.third(h, k)
        advance.finish()
        reduce.store().start()
        reduce.finish()
        reduce.store().wait()
        share.finish()
        total.finish()

    return beside_call(
        body,
        (grad, middle, gain.reshape(1, D), w_gateup, w_down, every, gate, up, hidden),
        (4, 6, 7, 3, 8, 5),
        [
            jax.ShapeDtypeStruct((rows, D), F32),
            jax.ShapeDtypeStruct((1, D), F32),
            jax.ShapeDtypeStruct((D, 2 * wide), BF),
            jax.ShapeDtypeStruct((2, 2) + block, BF),
        ],
        (2,),
        [
            pltpu.VMEM((4, rows, D), BF),
            pltpu.VMEM((4, rows, 2 * wide), BF),
            pltpu.VMEM((16,) + block, BF),
            pltpu.VMEM((2, 4) + block, BF),
            pltpu.VMEM((2, 2) + block, BF),
            DMA((14,)),
            DMA((14,)),
            DMA((9,)),
        ]
        + exchange_scratch(rows),
        beside,
        "feed_backward",
        collective_id,
        12 * 4 * rows * wide * D,
        ("c", "z0", "x", "y"),
        {3: ANY},
    )


class Both:
    def __init__(self, *parts):
        self.parts = parts
        self.names = tuple(dict.fromkeys(n for p in parts for n in p.names))
        self.args = tuple(a for p in parts for a in p.args)
        self.specs = tuple(a for p in parts for a in p.specs)
        self.shapes = tuple(s for p in parts for s in p.shapes)
        self.scratch = tuple(s for p in parts for s in p.scratch)

    def steps(self, p, ins, outs, scratch):
        waves, at = [], [0, 0, 0]
        for part in self.parts:
            ends = [at[0] + len(part.args), at[1] + len(part.shapes), at[2] + len(part.scratch)]
            waves += part.steps(p, ins[at[0] : ends[0]], outs[at[1] : ends[1]], scratch[at[2] : ends[2]])
            at = ends
        return waves


class SwapRows:
    names = ("swap",)

    def __init__(self, rows, at=0):
        self.args, self.specs, self.time = (rows,), (VM,), at
        self.shapes = (jax.ShapeDtypeStruct(rows.shape, rows.dtype),)
        self.scratch = (DMA((1,)), DMA((1,)), DMA((1,)))

    def steps(self, p, ins, outs, scratch):
        send, recv, local = (s.at[0] for s in scratch)
        away = p.c != p.z1
        move = remote(ins[0], outs[0], send, recv, p.peer["swap"])
        stay = pltpu.make_async_copy(ins[0], outs[0], local)

        def first():
            @pl.when(away)
            def _():
                move.start()

            @pl.when(jnp.logical_not(away))
            def _():
                stay.start()

        def last():
            @pl.when(away)
            def _():
                move.wait()

            @pl.when(jnp.logical_not(away))
            def _():
                stay.wait()

        return [(self.time, first), (99, last)]


class SpreadColumns:
    names = GROUP

    def __init__(self, *blocks):
        self.args, self.specs = blocks, (VM,) * len(blocks)
        self.shapes = tuple(jax.ShapeDtypeStruct((2, 2) + b.shape[1:], BF) for b in blocks)
        self.scratch = (DMA((3 * len(blocks),)), DMA((3 * len(blocks),)), DMA((len(blocks),)))

    def steps(self, p, ins, outs, scratch):
        send, recv, local = scratch
        made = []
        for k, (src, dst) in enumerate(zip(ins, outs)):
            sems = [s.at[pl.ds(3 * k, 3)] for s in (send, recv)]
            made.append(
                Spread(
                    p, lambda c, z0, s=src: s.at[2 * c + z0], lambda c, z0, d=dst: d.at[c, z0], *sems, local.at[k]
                )
            )

        def first():
            for m in made:
                m.start()

        def last():
            for m in made:
                m.wait()
                m.finish()

        return [(0, first), (99, last)]


class CollectColumns:
    names = GROUP

    def __init__(self, *blocks):
        self.args, self.specs = blocks, (VM,) * len(blocks)
        self.shapes = tuple(jax.ShapeDtypeStruct((4,) + b.shape[2:], BF) for b in blocks)
        self.scratch = (DMA((3 * len(blocks),)), DMA((3 * len(blocks),)), DMA((len(blocks),)))

    def steps(self, p, ins, outs, scratch):
        send, recv, local = scratch
        made = []
        for k, (src, dst) in enumerate(zip(ins, outs)):
            sems = [s.at[pl.ds(3 * k, 3)] for s in (send, recv)]
            made.append(
                Spread(
                    p, lambda c, z0, s=src: s.at[c, z0], lambda c, z0, d=dst: d.at[2 * c + z0], *sems, local.at[k]
                )
            )

        def first():
            for m in made:
                m.start()

        def last():
            for m in made:
                m.wait()
                m.finish()

        return [(0, first), (99, last)]


class GatherWeights:
    def __init__(self, columns=None, down=None, out=None, gains=None, columns_at=None, down_at=None, out_at=None, gains_at=None):
        self.has = columns is not None, down is not None, out is not None, gains is not None
        self.spread = columns is not None and len(columns.shape) == 3
        self.times = columns_at, down_at, out_at, gains_at
        self.names = EIGHT + ("mid", "z0") + (GROUP if self.spread else ())
        self.args = tuple(a for a in (columns, down, out, gains) if a is not None)
        self.specs = (VM,) * len(self.args)
        shapes, scratch = [], []
        sems = lambda n: [DMA((n,)), DMA((n,)), DMA((4,))]
        if columns is not None:
            block = (2,) + columns.shape[-2:]
            shapes.append((16,) + block)
            scratch += sems(22) + [pltpu.VMEM((2, 2) + block, BF)] + sems(3)
        if down is not None:
            shapes.append((16,) + down.shape[1:])
            scratch += sems(22) + [pltpu.VMEM((2, 2) + down.shape[1:], BF)]
        if out is not None:
            shapes.append((4, 2) + out.shape)
            scratch += sems(8)
        if gains is not None:
            shapes.append((32,) + gains.shape)
            scratch += sems(5)
        self.shapes = tuple(jax.ShapeDtypeStruct(s, BF) for s in shapes)
        self.scratch = tuple(scratch)

    def steps(self, p, ins, outs, scratch):
        ins, outs, scratch = list(ins), list(outs), list(scratch)
        take = lambda n: [scratch.pop(0) for _ in range(n)]
        acts = []
        if self.has[0]:
            src, ref = ins.pop(0), outs.pop(0)
            sems, s_sems, when = take(4), take(3), self.times[0]
            if self.spread:
                at = lambda c, z0, ref=ref: ref.at[columns_index(p.y, p.x, p.z1, c), z0]
                spread = Spread(p, lambda c, z0, src=src: src.at[2 * c + z0], at, *s_sems[:2], s_sems[2].at[0])
                acts += [(-1, spread.start), (when["start"], spread.wait), (99, spread.finish)]
                src = None
            acts += Gather(p, ref, columns_index, *sems, src).steps(when)
        if self.has[1]:
            src, ref = ins.pop(0), outs.pop(0)
            acts += Gather(p, ref, rows_index, *take(4), src).steps(self.times[1])
        if self.has[2]:
            acts += zip(self.times[2], out_gather_steps(p, ins.pop(0), outs.pop(0), *take(2), take(1)[0].at[0]))
        if self.has[3]:
            acts += zip(self.times[3], gains_gather(p, ins.pop(0), outs.pop(0), *take(2), take(1)[0].at[0]))
        return acts


class ReduceWeights:
    def __init__(self, columns, gains=None, collect=False, open=False, at=range(8)):
        self.gains = gains is not None
        self.collect, self.open, self.times = collect, open, tuple(at)
        self.names = EIGHT + ("mid", "z0") + (GROUP if collect else ())
        self.args = tuple(a for a in (columns, gains) if a is not None)
        self.specs = (ANY,) * len(self.args)
        shapes, scratch = [], []
        b = columns.shape[1:]
        shape = (4, b[0] // 2, b[1]) if collect else (2, 2) + b if open else (2,) + b
        shapes.append(jax.ShapeDtypeStruct(shape, BF))
        scratch += [pltpu.VMEM(n + b, BF) for n in ((2, 4), (2, 4), (2, 2), (2,))]
        scratch += [pltpu.VMEM((1, 1, 16, 128) if open else (2, 2) + b, BF), DMA((22,)), DMA((22,)), DMA((9,))]
        if collect:
            scratch += [DMA((3,)), DMA((3,)), DMA((1,))]
        if gains is not None:
            shapes.append(jax.ShapeDtypeStruct(gains.shape[1:], F32))
            scratch += [pltpu.VMEM(gains.shape, F32)]
            scratch += [pltpu.VMEM((16 >> k,) + gains.shape[1:], F32) for k in range(5)]
            scratch += [DMA((5,)), DMA((5,)), DMA((1,))]
        self.shapes, self.scratch = tuple(shapes), tuple(scratch)

    def steps(self, p, ins, outs, scratch):
        ins, outs, scratch = list(ins), list(outs), list(scratch)
        take = lambda n: [scratch.pop(0) for _ in range(n)]
        waves = [[] for _ in range(8)]
        part = functools.partial
        both = (0, 1)
        columns = Reduce(p, ins.pop(0), columns_index, outs.pop(0), *take(8))
        waves[0].append(columns.first)
        for m in range(4):
            waves[1 + m] += [part(columns.second, h, m) for h in both]
        for k in both:
            waves[5 + k] += [part(columns.third, h, k) for h in both]
        if self.collect:
            send, recv, local = take(3)
            rows = columns.three.shape[1] // 2
            piece = lambda c, z0: columns.three.at[c, pl.ds(pl.multiple_of(z0 * rows, rows), rows)]
            spread = Spread(p, piece, lambda c, z0: columns.result.at[2 * c + z0], send, recv, local.at[0])
            waves[7] += [c.bring for c in columns.cross] + [c.take for c in columns.cross]
            waves[7] += [part(columns.fourth, h) for h in both] + [spread.start, spread.wait, spread.finish]
        elif not self.open:
            waves[7] += [c.bring for c in columns.cross] + [c.take for c in columns.cross]
            waves[7] += [part(columns.fourth, h) for h in both]
        if not self.collect:
            waves[7] += [lambda: columns.store().start(), lambda: columns.store().wait()]
        waves[7].append(columns.finish)
        if self.gains:
            parts = take(9)
            steps = gains_reduce(p, ins.pop(0), outs.pop(0), parts[0], parts[1:6], *parts[6:])
            for k, act in zip((0, 2, 3, 4, 6, 7), steps):
                waves[k].append(act)
        return [(t, act) for t, wave in zip(self.times, waves) for act in wave]


class FinishColumns:
    def __init__(self, two, collect=False, at=(0, 1, 2, 99)):
        self.names = ("mid", "z0") + (GROUP if collect else ())
        self.collect, self.times = collect, at
        b = two.shape[2:]
        self.args, self.specs = (two,), (ANY,)
        self.shapes = (jax.ShapeDtypeStruct((4, b[0] // 2, b[1]) if collect else (2,) + b, BF),)
        self.scratch = (pltpu.VMEM((2,) + b, BF), pltpu.VMEM((2,) + b, BF), pltpu.VMEM((2, 2) + b, BF))
        self.scratch += (DMA((8,)), DMA((8,)), DMA((3,)), DMA((3,)), DMA((3,)), DMA((1,)))

    def steps(self, p, ins, outs, scratch):
        mine, three, relay, send, recv, local, s_send, s_recv, s_local = scratch
        two, result = ins[0], outs[0]
        crosses = [
            Cross(p, two.at[h, 0], three.at[h], three.at[h], relay.at[h], *[s.at[pl.ds(4 * h, 4)] for s in (send, recv)])
            for h in (0, 1)
        ]
        loads = [pltpu.make_async_copy(two.at[h, 1], mine.at[h], local.at[h]) for h in (0, 1)]
        rows = three.shape[1] // 2
        piece = lambda c, z0: three.at[c, pl.ds(pl.multiple_of(z0 * rows, rows), rows)]
        spread = Spread(p, piece, lambda c, z0: result.at[2 * c + z0], s_send, s_recv, s_local.at[0])
        store = lambda: pltpu.make_async_copy(three, result, local.at[2])

        def first():
            for c in crosses + loads:
                c.start()

        def last():
            for h in (0, 1):
                crosses[h].wait()
                loads[h].wait()
                add_to(three.at[h], mine.at[h])
            if self.collect:
                spread.start()
                spread.wait()
                spread.finish()
            else:
                store().start()
                store().wait()
            for c in crosses:
                c.finish()

        acts = [(self.times[0], first)]
        acts += [(self.times[1], c.bring) for c in crosses] + [(self.times[2], c.take) for c in crosses]
        return acts + [(self.times[3], last)]


LANES = 128
HEADS = Q_RANK + 2 * KV_RANK


def head_lanes():
    half = HEAD_SIZE // 2
    column = jnp.arange(HEADS * HEAD_SIZE, dtype=jnp.int32)
    head, inner = column // HEAD_SIZE, column % HEAD_SIZE
    lane = head * LANES + jnp.where(inner < half, inner, inner - half + LANES // 2)
    return (lane[:, None] == jnp.arange(HEADS * LANES, dtype=jnp.int32)[None, :]).astype(BF)


def pad_weights(lanes_ref, qkv_ref, out_ref, qkv_wide, out_wide):
    def qkv_tile(j):
        at = pl.ds(j, TILE)
        qkv_wide[at, :] = dot(qkv_ref[at, :], lanes_ref[...]).astype(BF)

    column_tiles(D, TILE, qkv_tile)
    heads = lanes_ref[: Q_RANK * HEAD_SIZE, : Q_RANK * LANES]

    def out_tile(j):
        cols = pl.ds(j, TILE)
        out_wide[:, cols] = dot(heads, out_ref[:, cols], ((0,), (0,))).astype(BF)

    column_tiles(D, TILE, out_tile)


def masked(scores, first, start_ref):
    count, keys = scores.shape
    query = lax.broadcasted_iota(jnp.int32, scores.shape, 0) + first
    key = lax.broadcasted_iota(jnp.int32, scores.shape, 1)
    start = start_ref[first : first + count, :]
    return jnp.where((key <= query) & (key >= start), scores, masked_score)


def attention_forward_call(residual, gain, w_qkv, w_out, common, beside, collective_id):
    lanes, cosines, sines, starts = common
    rows = residual.shape[0]
    count = 4 * rows
    scale = HEAD_SIZE ** (-0.5)

    def body(p, ins, outs, scratch, advance, staged):
        res_ref, gain_ref, qkv_ref, out_ref, lanes_ref, cos_ref, sin_ref, start_ref = ins
        new_ref, every, heads_ref, att_ref, log_ref = outs
        qkv_wide, out_wide = scratch[:2]
        own, terms, share, total = exchange_of(p, every, scratch[2:])

        def project(pieces, n):
            places = token_rows(pieces, n, rows)
            both = lambda ref: jnp.concatenate([ref[at, :] for at in places], axis=0)
            cos, sin = both(cos_ref), both(sin_ref)
            x = gather_pieces(every, pieces, n)
            for j in range(0, HEADS, 4):
                wide = dot(x, qkv_wide[:, j * LANES : (j + 4) * LANES])
                for k in range(4):
                    value = wide[:, k * LANES : (k + 1) * LANES]
                    if j + k < Q_RANK + KV_RANK:
                        value = value * cos + pltpu.roll(value, LANES // 2, 1) * sin
                    for m, at in enumerate(places):
                        heads_ref[j + k, at, :] = value[m * n : (m + 1) * n].astype(BF)

        def attend(j, _):
            g = lax.div(j, Q_RANK // KV_RANK)
            for first in range(0, count, rows):
                n = first + rows
                q = heads_ref[j, first:n, :]
                scores = dot(q, heads_ref[Q_RANK + g, :n, :], ((1,), (1,))) * scale
                scores = masked(scores, first, start_ref)
                top = jnp.max(scores, axis=1, keepdims=True)
                shifted = jnp.exp(scores - top)
                amount = jnp.sum(shifted, axis=1, keepdims=True)
                log_ref[j, first:n, :] = top + jnp.log(amount)
                weights = (shifted / amount).astype(BF)
                att_ref[j, first:n, :] = dot(weights, heads_ref[Q_RANK + KV_RANK + g, :n, :]).astype(BF)
            return 0

        def project_out(pieces, n):
            places = token_rows(pieces, n, rows)
            wide = jnp.concatenate(
                [jnp.concatenate([att_ref[j, at, :] for j in range(Q_RANK)], axis=1) for at in places], axis=0
            )

            def tile(j):
                cols = pl.ds(j, DOWN_TILE)
                scatter_pieces(terms, pieces, n, dot(wide, out_wide[:, cols]).astype(BF), cols)

            column_tiles(D, DOWN_TILE, tile)

        row_normalize(res_ref, gain_ref, own)
        share.start()
        advance()
        staged.ready(2, 3, 4)
        pad_weights(lanes_ref, qkv_ref, out_ref, qkv_wide, out_wide)
        staged.ready(5, 6)
        project([(p.rank, 0)], rows)
        share.across(True).wait_recv()
        project([(p.sibling, 0)], rows)
        advance()
        part = rows // CHUNKS
        for k in range(CHUNKS):
            share.pass_on(k)
            share.far(k)
            project([(p.diagonal, k * part), (p.over, k * part)], part)
            advance()
        staged.flush(1, 2)
        for j in range(0, Q_RANK, 2):
            lax.fori_loop(j, j + 2, attend, 0)
            advance()
        for k in range(CHUNKS):
            project_out([(p.diagonal, k * part), (p.over, k * part)], part)
            total.diagonal(k).start()
            total.relay(k)
            advance()
        staged.flush(3)
        project_out([(p.sibling, 0)], rows)
        total.sibling().start()
        project_out([(p.rank, 0)], rows)
        advance()

        def write(at, value):
            new_ref[at, :] = res_ref[at, :] + value

        collect(p, total, write)
        advance.finish()
        share.finish()
        total.finish()

    return beside_call(
        body,
        (residual, gain.reshape(1, D), w_qkv, w_out, lanes, cosines, sines, starts),
        (4, 2, 3, 5, 6),
        [
            jax.ShapeDtypeStruct((rows, D), F32),
            jax.ShapeDtypeStruct((4, rows, D), BF),
            jax.ShapeDtypeStruct((HEADS, count, LANES), BF),
            jax.ShapeDtypeStruct((Q_RANK, count, LANES), BF),
            jax.ShapeDtypeStruct((Q_RANK, count, 1), F32),
        ],
        (1, 2, 3),
        [pltpu.VMEM((D, HEADS * LANES), BF), pltpu.VMEM((Q_RANK * LANES, D), BF)] + exchange_scratch(rows),
        beside,
        "attention_forward",
        collective_id,
        2 * count * D * (HEADS + Q_RANK) * LANES,
    )


def attention_backward_call(grad, residual, gain, w_qkv, w_out, kept, common, beside, collective_id, dtype=F32):
    lanes, cosines, sines, starts = common
    every, heads, attended, logs = kept
    rows = residual.shape[0]
    count = 4 * rows
    scale = HEAD_SIZE ** (-0.5)

    def body(p, ins, outs, scratch, advance, staged):
        (grad_ref, res_ref, gain_ref, qkv_ref, out_ref, lanes_ref, cos_ref, sin_ref, start_ref) = ins[:9]
        every_ref, heads_ref, att_ref, log_ref = ins[9:]
        new_ref, gain_out, g_qkv, s_out = outs
        qkv_wide, out_wide, e, d_att, d_k, d_v, d_heads = scratch[:7]
        g_out = scratch[7]
        reduce = out_reduce_steps(p, g_out, s_out, *scratch[8:15])
        own, terms, share, total = exchange_of(p, e, scratch[15:])

        def copy_own(k, _):
            at = pl.ds(pl.multiple_of(k * 32, 32), 32)
            own[at, :] = grad_ref[at, :].astype(BF)
            return 0

        lax.fori_loop(0, rows // 32, copy_own, 0)

        def back_out(pieces, n):
            wide = dot(gather_pieces(e, pieces, n), out_wide[...], ((1,), (1,)))
            for m, at in enumerate(token_rows(pieces, n, rows)):
                for j in range(Q_RANK):
                    d_att[j, at, :] = wide[m * n : (m + 1) * n, j * LANES : (j + 1) * LANES].astype(BF)

        def attend(j, _):
            g = lax.div(j, Q_RANK // KV_RANK)
            for first in range(0, count, rows):
                n = first + rows
                q, d_o = heads_ref[j, first:n, :], d_att[j, first:n, :]
                k, v = heads_ref[Q_RANK + g, :n, :], heads_ref[Q_RANK + KV_RANK + g, :n, :]
                scores = masked(dot(q, k, ((1,), (1,))) * scale, first, start_ref)
                weights = jnp.exp(scores - log_ref[j, first:n, :])
                d_weights = dot(d_o, v, ((1,), (1,)))
                inner = jnp.sum(weights * d_weights, axis=1, keepdims=True)
                d_scores = (weights * (d_weights - inner)).astype(BF)
                d_v[g, :n, :] += dot(weights.astype(BF), d_o, ((0,), (0,)))
                d_k[g, :n, :] += dot(d_scores, q, ((0,), (0,)))
                d_q = dot(d_scores, k) * scale
                d_heads[j, first:n, :] = turn_back(d_q, cos_ref[first:n, :], sin_ref[first:n, :])
            return 0

        def turn_back(value, cos, sin):
            return (value * cos - pltpu.roll(value, LANES // 2, 1) * sin).astype(BF)

        def keys_back():
            for g in range(KV_RANK):
                for first in range(0, count, rows):
                    at = slice(first, first + rows)
                    d_heads[Q_RANK + g, at, :] = turn_back(d_k[g, at, :] * scale, cos_ref[at, :], sin_ref[at, :])
                    d_heads[Q_RANK + KV_RANK + g, at, :] = d_v[g, at, :].astype(BF)

        def project_back(pieces, n):
            wide = jnp.concatenate(
                [
                    jnp.concatenate([d_heads[j, at, :] for j in range(HEADS)], axis=1)
                    for at in token_rows(pieces, n, rows)
                ],
                axis=0,
            )

            def tile(j):
                cols = pl.ds(j, DOWN_TILE)
                value = dot(wide, qkv_wide[cols, :], ((1,), (1,))).astype(BF)
                scatter_pieces(terms, pieces, n, value, cols)

            column_tiles(D, DOWN_TILE, tile)

        def out_grads():
            e_all = e.reshape(count, D)

            def out_grad(j):
                cols = pl.ds(j, TILE)
                wide = jnp.concatenate(
                    [dot(att_ref[h], e_all[:, cols], ((0,), (0,))) for h in range(Q_RANK)], axis=0
                ).astype(BF)
                value = dot(lanes_ref[: Q_RANK * HEAD_SIZE, : Q_RANK * LANES], wide).astype(BF)
                for h in range(Q_RANK):
                    g_out[h, :, cols] = value[h * HEAD_SIZE : (h + 1) * HEAD_SIZE]

            column_tiles(D, TILE, out_grad)

        def weight_grads():
            x_all = every_ref.reshape(count, D)

            def qkv_grad(j):
                cols = pl.ds(j, TILE)
                wide = jnp.concatenate(
                    [dot(x_all[:, cols], d_heads[h], ((0,), (0,))) for h in range(HEADS)], axis=1
                ).astype(BF)
                g_qkv[cols, :] = dot(wide, lanes_ref[...], ((1,), (1,))).astype(BF)

            column_tiles(D, TILE, qkv_grad)

        share.start()
        advance()
        staged.ready(3, 4, 5)
        pad_weights(lanes_ref, qkv_ref, out_ref, qkv_wide, out_wide)
        d_k[...] = jnp.zeros_like(d_k)
        d_v[...] = jnp.zeros_like(d_v)
        back_out([(p.rank, 0)], rows)
        share.across(True).wait_recv()
        back_out([(p.sibling, 0)], rows)
        advance()
        part = rows // CHUNKS
        for k in range(CHUNKS):
            share.pass_on(k)
            share.far(k)
            back_out([(p.diagonal, k * part), (p.over, k * part)], part)
            advance()
        staged.ready(11)
        out_grads()
        reduce[0]()
        staged.ready(6, 7, 10)
        for j in range(0, Q_RANK, 2):
            lax.fori_loop(j, j + 2, attend, 0)
            advance()
        reduce[1]()
        keys_back()
        for k in range(CHUNKS):
            project_back([(p.diagonal, k * part), (p.over, k * part)], part)
            total.diagonal(k).start()
            total.relay(k)
            advance()
        project_back([(p.sibling, 0)], rows)
        total.sibling().start()
        project_back([(p.rank, 0)], rows)
        advance()
        reduce[2]()
        staged.ready(9)
        weight_grads()
        staged.flush(2)
        reduce[3]()
        advance()
        gain_out[...] = jnp.zeros_like(gain_out)

        def write(at, value):
            res = res_ref[at, :].astype(F32)
            normed = normalize(res)
            gain_out[...] += jnp.sum(value * normed, axis=0, keepdims=True)
            back = norm_back(value * gain_ref[...], normed, res)
            new_ref[at, :] = (grad_ref[at, :] + back).astype(dtype)

        collect(p, total, write)
        advance.finish()
        reduce[4]()
        share.finish()
        total.finish()

    return beside_call(
        body,
        (grad, residual, gain.reshape(1, D), w_qkv, w_out, lanes, cosines, sines, starts, every, heads, attended, logs),
        (5, 3, 4, 11, 6, 7, 10, 9),
        [
            jax.ShapeDtypeStruct((rows, D), dtype),
            jax.ShapeDtypeStruct((1, D), F32),
            jax.ShapeDtypeStruct((D, HEADS * HEAD_SIZE), BF),
            jax.ShapeDtypeStruct((HEAD_SIZE // 2, D), BF),
        ],
        (2,),
        [
            pltpu.VMEM((D, HEADS * LANES), BF),
            pltpu.VMEM((Q_RANK * LANES, D), BF),
            pltpu.VMEM((4, rows, D), BF),
            pltpu.VMEM((Q_RANK, count, LANES), BF),
            pltpu.VMEM((KV_RANK, count, LANES), F32),
            pltpu.VMEM((KV_RANK, count, LANES), F32),
            pltpu.VMEM((HEADS, count, LANES), BF),
        ]
        + out_reduce_scratch((HEAD_SIZE, D))
        + exchange_scratch(rows),
        beside,
        "attention_backward",
        collective_id,
        6 * count * D * (HEADS + Q_RANK) * LANES,
        ("c", "z0", "x", "y", "z1"),
        {3: ANY},
    )


def lane_rows():
    half, space = HEAD_SIZE // 2, LANES // 2 - HEAD_SIZE // 2
    index = jnp.arange(half, dtype=jnp.float32)
    inverse = jnp.pad(rope_base ** (-2.0 * index / HEAD_SIZE), (0, space))
    ones = jnp.pad(jnp.ones(half, F32), (0, space))
    row = lambda a, b: jnp.concatenate([a, b])
    return jnp.stack([row(inverse, inverse), row(ones, ones), row(-ones, ones)])


def rank_columns(ref, l, c, x):
    pieces = []
    for start, width in (
        (0, 2 * HEAD_SIZE),
        (QUERY_HEAD_COUNT * HEAD_SIZE, HEAD_SIZE),
        ((QUERY_HEAD_COUNT + KEY_VALUE_HEADS) * HEAD_SIZE, HEAD_SIZE),
    ):
        for y in (0, 1):
            at = start + (4 * y + 2 * x + c) * width
            pieces.append(ref[l][:, at : at + width])
    return jnp.concatenate(pieces, axis=1).astype(BF)


def first_call(tokens, lengths, w_qkv, w_out, w_gateup, w_down, gains, collective_id):
    rows = w_qkv.shape[1]
    count = 4 * tokens.shape[0]
    ranks = lambda w: jax.ShapeDtypeStruct((4, rows, w.shape[2] // 4), BF)
    shard = jax.ShapeDtypeStruct(w_out.shape[1:], BF)
    gather = GatherWeights(
        columns=ranks(w_qkv), out=shard, gains=gains, columns_at=times(1, (2, 2), (2, 2), 3, (4, 4), (6, 6)),
        out_at=(-1, 1, 3, 5, 99), gains_at=(1, 2, 3, 4, 5, 99),
    )
    spread = SpreadColumns(ranks(w_gateup), ranks(w_qkv), ranks(w_gateup))
    swap = SwapRows(tokens)
    works = (gather, spread, swap)
    unit = w_gateup.shape[2] // 64
    down_rows = w_down.shape[1] // 2

    def body(*refs):
        refs = list(refs)
        take = lambda n: [refs.pop(0) for _ in range(n)]
        tokens_ref, lengths_ref, qkv_ref, out_ref, gu_ref, down_ref, gains_ref, lanes_ref = take(8)
        down0, down1, out1, cos_ref, sin_ref, start_ref = take(6)
        outs = [take(len(w.shapes)) for w in works]
        qkv0, qkv1, gu0, gu1, out0 = take(5)
        scratch = [take(len(w.scratch)) for w in works]
        p = Place()
        greet(p, EIGHT + GROUP + ("swap", "mid"))
        clock = Clock(gather.steps(p, [qkv0, out0, gains_ref], outs[0], scratch[0]))

        def pack_heads(l, dst):
            for c in (0, 1):
                for x in (0, 1):
                    dst[2 * c + x] = rank_columns(qkv_ref, l, c, x)

        def pack_units(l, dst):
            for chunk in range(64):
                z0, z1, c, rest = chunk % 2, chunk // 2 % 2, chunk // 4 % 2, chunk // 8
                at = (rest * 2 + z1) * unit
                dst[2 * c + z0, :, at : at + unit] = gu_ref[l, :, chunk * unit : (chunk + 1) * unit].astype(BF)

        pack_heads(0, qkv0)
        out0[...] = out_ref[0].astype(BF)
        clock()
        pack_units(0, gu0)
        clock()
        pack_heads(1, qkv1)
        pack_units(1, gu1)
        later = Clock(
            spread.steps(p, [gu0, qkv1, gu1], outs[1], scratch[1]) + swap.steps(p, [tokens_ref], outs[2], scratch[2])
        )
        later()
        out1[...] = out_ref[1].astype(BF)
        for h in (0, 1):
            part = slice(h * down_rows, (h + 1) * down_rows)
            down0[h] = down_ref[0, part, :].astype(BF)
            down1[h] = down_ref[1, part, :].astype(BF)
        clock()

        def begin(places):
            start, end = jnp.zeros_like(places), 0
            for k in range(lengths.shape[1]):
                length = lengths_ref[0, k]
                end = end + length
                start = start + jnp.where(places >= end, length, 0)
            return start

        def table(k, _):
            at = pl.ds(pl.multiple_of(k * TILE, TILE), TILE)
            places = lax.broadcasted_iota(jnp.int32, (TILE, LANES), 0) + k * TILE
            angles = (places - begin(places)).astype(F32) * lanes_ref[0:1, :]
            cos_ref[at, :] = jnp.cos(angles) * lanes_ref[1:2, :]
            sin_ref[at, :] = jnp.sin(angles) * lanes_ref[2:3, :]
            start_ref[at, :] = begin(lax.broadcasted_iota(jnp.int32, (TILE, 1), 0) + k * TILE)
            return 0

        lax.fori_loop(0, count // TILE, table, 0)
        clock.finish()
        later.finish()

    vmem = lambda s: pltpu.VMEM(s.shape, BF)
    half = jax.ShapeDtypeStruct((2, down_rows, D), BF)
    made = [half, half, shard, *([jax.ShapeDtypeStruct((count, LANES), F32)] * 2), jax.ShapeDtypeStruct((count, 1), jnp.int32)]
    out = pl.pallas_call(
        body,
        out_shape=made + [s for w in works for s in w.shapes],
        in_specs=[VM, pl.BlockSpec(memory_space=pltpu.SMEM)] + [VM] * 6,
        out_specs=[VM] * len(made) + [ANY for w in works for _ in w.shapes],
        scratch_shapes=[vmem(ranks(w_qkv)), vmem(ranks(w_qkv)), vmem(ranks(w_gateup)), vmem(ranks(w_gateup)), vmem(shard)]
        + [s for w in works for s in w.scratch],
        compiler_params=wide_params(collective_id),
        name="first_weights",
    )(tokens, lengths, w_qkv, w_out, w_gateup, w_down, gains, lane_rows())
    return out


def stepped(weight, gradient, first, second, rate, shrink):
    return adam_step(weight, gradient.astype(F32), first, second, rate, shrink)


def update_gateup(weight, first, second, parts, rate, shrink):
    rows, columns = weight.shape[1:]
    blocks = 8
    wide, thin = columns // blocks, columns // 4 // blocks
    unit = thin // 2

    def body(w_ref, m_ref, v_ref, *refs):
        grads, (w_out, m_out, v_out) = refs[:-3], refs[-3:]

        def run(g_ref):
            for c in (0, 1):
                for z1 in (0, 1):
                    for z0 in (0, 1):
                        at = pl.ds(((c * 2 + z1) * 2 + z0) * unit, unit)
                        grad = g_ref[2 * c + z0, :, pl.ds(z1 * unit, unit)]
                        new = stepped(w_ref[0, :, at], grad, m_ref[0, :, at], v_ref[0, :, at], rate, shrink)
                        w_out[0, :, at], m_out[0, :, at], v_out[0, :, at] = new

        for l, g_ref in enumerate(grads):
            pl.when(pl.program_id(0) == l)(functools.partial(run, g_ref))

    big = pl.BlockSpec((1, rows, wide), lambda l, j: (l, 0, j))
    small = [
        pl.BlockSpec((4, rows, thin), lambda l, j, k=k: (0, 0, jnp.where(l == k, j, 0 if k else blocks - 1)))
        for k in range(LAYERS)
    ]
    return pl.pallas_call(
        body,
        grid=(LAYERS, blocks),
        in_specs=[big] * 3 + small,
        out_specs=[big] * 3,
        out_shape=[jax.ShapeDtypeStruct(weight.shape, F32)] * 3,
        compiler_params=pltpu.CompilerParams(vmem_limit_bytes=32 * 2**20),
        name="update_gateup",
    )(weight, first, second, *parts)


def update_rows(weight, first, second, parts, rate, shrink):
    rows, columns = weight.shape[1:]
    blocks = 2
    wide = columns // blocks

    def body(w_ref, m_ref, v_ref, *refs):
        grads, (w_out, m_out, v_out) = refs[:-3], refs[-3:]

        def run(g_ref):
            w_out[0], m_out[0], v_out[0] = stepped(w_ref[0], g_ref[...], m_ref[0], v_ref[0], rate, shrink)

        for l, g_ref in enumerate(grads):
            pl.when(pl.program_id(0) == l)(functools.partial(run, g_ref))

    big = pl.BlockSpec((1, rows, wide), lambda l, j: (l, 0, j))
    small = [
        pl.BlockSpec((rows, wide), lambda l, j, k=k: (0, jnp.where(l == k, j, 0 if k else blocks - 1)))
        for k in range(LAYERS)
    ]
    return pl.pallas_call(
        body,
        grid=(LAYERS, blocks),
        in_specs=[big] * 3 + small,
        out_specs=[big] * 3,
        out_shape=[jax.ShapeDtypeStruct(weight.shape, F32)] * 3,
        compiler_params=pltpu.CompilerParams(vmem_limit_bytes=32 * 2**20),
        name="update_rows",
    )(weight, first, second, *parts)


def update_qkv(weight, first, second, parts, rate, shrink):
    rows, columns = weight.shape[1:]
    q_wide, kv_wide = QUERY_HEAD_COUNT * HEAD_SIZE, KEY_VALUE_HEADS * HEAD_SIZE

    def body(w_ref, m_ref, v_ref, *refs):
        grads, (w_out, m_out, v_out) = refs[:-3], refs[-3:]

        def run(g_ref):
            pieces = []
            for start, width in ((0, 2 * HEAD_SIZE), (4 * HEAD_SIZE, HEAD_SIZE), (6 * HEAD_SIZE, HEAD_SIZE)):
                for y in (0, 1):
                    for x in (0, 1):
                        for c in (0, 1):
                            at = start + y * width
                            pieces.append(g_ref[2 * c + x].astype(F32)[:, at : at + width])
            grad = jnp.concatenate(pieces, axis=1)
            w_out[0], m_out[0], v_out[0] = stepped(w_ref[0], grad, m_ref[0], v_ref[0], rate, shrink)

        for l, g_ref in enumerate(grads):
            pl.when(pl.program_id(0) == l)(functools.partial(run, g_ref))

    big = pl.BlockSpec((1, rows, columns), lambda l: (l, 0, 0))
    small = [pl.BlockSpec((4, rows, columns // 4), lambda l: (0, 0, 0))] * LAYERS
    return pl.pallas_call(
        body,
        grid=(LAYERS,),
        in_specs=[big] * 3 + small,
        out_specs=[big] * 3,
        out_shape=[jax.ShapeDtypeStruct(weight.shape, F32)] * 3,
        compiler_params=pltpu.CompilerParams(vmem_limit_bytes=32 * 2**20),
        name="update_qkv",
    )(weight, first, second, *parts)


def links_call(beside, name, collective_id):
    return beside_call(
        lambda p, ins, outs, scratch, advance, staged: advance.finish(),
        (), (), [], (), [], beside, name, collective_id, 0, peers=(),
    )[1]


def fast_shards(
    tokens, cotangent, lengths, w_qkv, w_out, w_gateup, w_down, norm_gains, *moments
):
    axes = ("fsdp", "seq")
    pairs = swap_pairs(lax.axis_size("fsdp"), lax.axis_size("seq"))
    lengths = lax.ppermute(lengths, axes, pairs)
    rows, owned = w_qkv.shape[1], norm_gains.shape[2]
    own_gains = jnp.pad(
        norm_gains.reshape(2 * LAYERS, owned).astype(BF), ((0, 16 - 2 * LAYERS), (0, lane_width - owned))
    )
    down_parts, out_parts, columns = [None] * 2, [None] * 2, [None] * 3
    down_parts[0], down_parts[1], out_parts[1], *places, qkv0, out0, got_gains, columns[0], columns[1], columns[2], start = (
        first_call(tokens, lengths, w_qkv, w_out, w_gateup, w_down, own_gains, 0)
    )
    common = (head_lanes(), *places)
    all_gains = got_gains[:, : 2 * LAYERS, :owned].transpose(1, 0, 2).reshape(LAYERS, 2, D).astype(F32)
    matrix = lambda g: g.reshape(D, -1)
    small = times(0, (1, 1), (4, 4), 4, (5, 5), (7, 7))
    large = times(0, (2, 4), (5, 6), 4, (7, 8), (8, 9))
    alone = times(0, (1, 2), (4, 5), 4, (5, 6), (7, 8))
    stack = lambda g: g.reshape(-1, D)
    (middle0, *first0), (gu0, down0, cotangent) = attention_forward_call(
        start, all_gains[0, 0], matrix(qkv0), stack(out0), common,
        Both(
            GatherWeights(columns=columns[0], down=down_parts[0], columns_at=large, down_at=small),
            SwapRows(cotangent, 7),
        ), 1,
    )
    (later0, *second0), (qkv1, down1, out1) = feed_forward_call(
        middle0, all_gains[0, 1], matrix(gu0), stack(down0),
        GatherWeights(
            columns=columns[1], down=down_parts[1], out=out_parts[1],
            columns_at=times(0, (2, 2), (3, 3), 3, (4, 4), (5, 5)),
            down_at=times(0, (2, 2), (3, 3), 3, (4, 4), (5, 5)),
            out_at=(0, 2, 3, 4, 5),
        ), 2,
    )
    (middle1, *first1), (gu1,) = attention_forward_call(
        later0, all_gains[1, 0], matrix(qkv1), stack(out1), common,
        GatherWeights(columns=columns[2], columns_at=alone), 3,
    )
    (later1, *second1), _ = feed_forward_call(
        middle1, all_gains[1, 1], matrix(gu1), stack(down1), Nothing(), 4, BF
    )
    wide = lambda g: g.reshape(16, 2 * rows, -1)
    (grad, gain11, g_gu1, two_down1), _ = feed_backward_call(
        cotangent, middle1, all_gains[1, 1], matrix(gu1), stack(down1), second1, Nothing(), 5
    )
    (grad, gain10, g_qkv1, s_out1), (two_gu1, s_down1, layer_output) = attention_backward_call(
        grad, later0, all_gains[1, 0], matrix(qkv1), stack(out1), first1, common,
        Both(
            ReduceWeights(columns=wide(g_gu1), open=True, at=(0, 3, 3, 4, 5, 9, 10, 11)),
            FinishColumns(two_down1, at=(3, 4, 5, 6)),
            SwapRows(later1, 7),
        ), 6,
    )
    (grad, gain01, g_gu0, two_down0), (s_gu1, s_qkv1) = feed_backward_call(
        grad, middle0, all_gains[0, 1], matrix(gu0), stack(down0), second0,
        Both(
            FinishColumns(two_gu1, at=(0, 3, 4, 5)),
            ReduceWeights(columns=wide(g_qkv1), at=(0, 2, 3, 3, 4, 5, 6, 7)),
        ), 7,
    )
    (grad, gain00, g_qkv0, s_out0), (two_gu0, s_down0) = attention_backward_call(
        grad, start, all_gains[0, 0], matrix(qkv0), stack(out0), first0, common,
        Both(
            ReduceWeights(columns=wide(g_gu0), open=True, at=(0, 3, 3, 4, 5, 9, 10, 11)),
            FinishColumns(two_down0, at=(3, 4, 5, 6)),
        ), 8, BF,
    )
    terms = jnp.concatenate([gain00, gain01, gain10, gain11]).reshape(2 * LAYERS, -1, owned).transpose(1, 0, 2)
    terms = jnp.pad(terms, ((0, 0), (0, 8 - 2 * LAYERS), (0, lane_width - owned)))
    split = lambda g: g.reshape(2, 2, rows, -1)
    s_gu0, s_qkv0, s_gains, s_gu1, s_qkv1, input_grad = links_call(
        Both(
            FinishColumns(two_gu0, collect=True, at=(0, 1, 2, 6)),
            ReduceWeights(columns=wide(g_qkv0), gains=terms, collect=True),
            CollectColumns(split(s_gu1), split(s_qkv1)),
            SwapRows(grad),
        ),
        "last_gradients",
        9,
    )
    flat = lambda g: g.reshape(-1, D)
    update = {
        "qkv": (s_qkv0, s_qkv1),
        "out": (s_out0, s_out1),
        "gateup": (s_gu0, s_gu1),
        "down": (flat(s_down0), flat(s_down1)),
        "gains": s_gains[: 2 * LAYERS, :owned].reshape(LAYERS, 2, owned),
    }
    return (layer_output, input_grad.astype(F32)) + update_all(
        (w_qkv, w_out, w_gateup, w_down, norm_gains), moments, update
    )


def update_all(stacked, moments, update):
    step_rates = (D ** (-0.5), 4.0 * D ** (-0.5), D ** (-0.5), FF ** (-0.5), 0.5)
    shrinks = (decay_rate, decay_rate, decay_rate, decay_rate, 0.0)
    ways = (update_qkv, update_rows, update_gateup, update_rows, adam_step)
    results = []
    for kind, (name, way) in enumerate(zip(update, ways)):
        weight, first, second = stacked[kind], moments[kind], moments[5 + kind]
        if kind == 4:
            results.append(way(weight, update[name], first, second, step_rates[kind], shrinks[kind]))
        else:
            results.append(way(weight, first, second, update[name], step_rates[kind], shrinks[kind]))
    return tuple(results[kind][part] for part in range(3) for kind in range(5))


def solution(mesh):
    in_specs = (
        P(("fsdp", "seq"), None),
        P(("fsdp", "seq"), None),
        P("fsdp", None),
        P(None, ("fsdp", "seq"), None),
        P(None, ("fsdp", "seq"), None),
        P(None, ("fsdp", "seq"), None),
        P(None, ("fsdp", "seq"), None),
        P(None, None, ("fsdp", "seq")),
        P(None, ("fsdp", "seq"), None),
        P(None, ("fsdp", "seq"), None),
        P(None, ("fsdp", "seq"), None),
        P(None, ("fsdp", "seq"), None),
        P(None, None, ("fsdp", "seq")),
        P(None, ("fsdp", "seq"), None),
        P(None, ("fsdp", "seq"), None),
        P(None, ("fsdp", "seq"), None),
        P(None, ("fsdp", "seq"), None),
        P(None, None, ("fsdp", "seq")),
    )
    out_specs = (
        P(("fsdp", "seq"), None),
        P(("fsdp", "seq"), None),
        P(None, ("fsdp", "seq"), None),
        P(None, ("fsdp", "seq"), None),
        P(None, ("fsdp", "seq"), None),
        P(None, ("fsdp", "seq"), None),
        P(None, None, ("fsdp", "seq")),
        P(None, ("fsdp", "seq"), None),
        P(None, ("fsdp", "seq"), None),
        P(None, ("fsdp", "seq"), None),
        P(None, ("fsdp", "seq"), None),
        P(None, None, ("fsdp", "seq")),
        P(None, ("fsdp", "seq"), None),
        P(None, ("fsdp", "seq"), None),
        P(None, ("fsdp", "seq"), None),
        P(None, ("fsdp", "seq"), None),
        P(None, None, ("fsdp", "seq")),
    )
    whole_tiles = (D // mesh.size) % 16 == 0 and mesh.shape["seq"] == 4 and mesh.size == 32
    body = fast_shards if whole_tiles else shards
    return jax.shard_map(body, mesh=mesh, in_specs=in_specs, out_specs=out_specs, check_vma=False)
```

```python
import functools

import jax
import jax.numpy as jnp
from jax import lax
from jax.experimental import pallas as pl
from jax.experimental.pallas import tpu as pltpu
from jax.sharding import PartitionSpec as P

D = 1536
QUERY_HEAD_COUNT = 16
KEY_VALUE_HEADS = 8
HEAD_SIZE = 96
FF = 4096
LAYERS = 2
STEP = 6


eps_norm = 1e-05
rope_base = 100000.0
beta_one = 0.9
beta_two = 0.95
adam_eps = 1e-08
decay_rate = 0.1
masked_score = -1e30
lane_width = 128


def layout(length_row, places):
    seq_ends = jnp.cumsum(length_row, dtype=jnp.int32)
    passed = (places[:, None] >= seq_ends[None, :]).astype(jnp.int32)
    segment = jnp.sum(passed, axis=1, dtype=jnp.int32)
    begins = jnp.sum(passed * length_row[None, :], axis=1, dtype=jnp.int32)
    return (segment, places - begins)


def tables(positions):
    freq_index = jnp.arange(HEAD_SIZE // 2, dtype=jnp.float32)
    inverse = rope_base ** (-2.0 * freq_index / HEAD_SIZE)
    angles = positions.astype(jnp.float32)[:, None] * inverse[None, :]
    angles = jnp.concatenate([angles, angles], axis=-1)
    return (jnp.cos(angles)[:, None, :], jnp.sin(angles)[:, None, :])


def apply_rotary(values, rotary_cosines, rotary_sines):
    half_width = values.shape[-1] // 2
    turned = jnp.concatenate([-values[..., half_width:], values[..., :half_width]], axis=-1)
    return values * rotary_cosines + turned * rotary_sines


def invert_rotary(values, rotary_cosines, rotary_sines):
    half_width = values.shape[-1] // 2
    scaled_sine = values * rotary_sines
    turned = jnp.concatenate(
        [scaled_sine[..., half_width:], -scaled_sine[..., :half_width]], axis=-1
    )
    return values * rotary_cosines + turned


def normalize(residual):
    return residual * lax.rsqrt(jnp.mean(residual * residual, axis=-1, keepdims=True) + eps_norm)


def norm_back(grad_normed, normed, residual):
    inverse = lax.rsqrt(jnp.mean(residual * residual, axis=-1, keepdims=True) + eps_norm)
    return inverse * (grad_normed - normed * jnp.mean(grad_normed * normed, axis=-1, keepdims=True))


def product(lhs_matrix, rhs_matrix):
    return jnp.dot(lhs_matrix, rhs_matrix, preferred_element_type=jnp.float32)


def attention_scores(query_head_rows, key_head_rows, allowed):
    scores = jnp.einsum(
        "qgrd,kgd->grqk", query_head_rows, key_head_rows, preferred_element_type=jnp.float32
    ) * HEAD_SIZE ** (-0.5)
    return jnp.where(allowed[None, None], scores, masked_score)


def wire_pieces(stacked, layer_index):
    return tuple((shard_piece[layer_index].astype(jnp.bfloat16) for shard_piece in stacked))


def fetch_forward(stacked, layer_index):
    qkv_piece, out_piece, gateup_piece, down_piece, gain_piece = wire_pieces(stacked, layer_index)
    return (
        lax.all_gather(qkv_piece, ("fsdp", "seq"), axis=0, tiled=True),
        lax.all_gather(out_piece, ("fsdp", "seq"), axis=0, tiled=True),
        lax.all_gather(gateup_piece, ("fsdp", "seq"), axis=0, tiled=True),
        lax.all_gather(down_piece, ("fsdp", "seq"), axis=0, tiled=True),
        lax.all_gather(gain_piece, ("fsdp", "seq"), axis=1, tiled=True),
    )


def fetch_backward(stacked, layer_index):
    qkv_piece, out_piece, gateup_piece, down_piece, gain_piece = wire_pieces(stacked, layer_index)
    return (
        lax.all_gather(qkv_piece, ("fsdp", "seq"), axis=0, tiled=True),
        lax.all_gather(out_piece, ("fsdp", "seq"), axis=0, tiled=True),
        lax.all_gather(gateup_piece, ("fsdp", "seq"), axis=0, tiled=True),
        lax.all_gather(down_piece, ("fsdp", "seq"), axis=0, tiled=True),
        lax.all_gather(gain_piece, ("fsdp", "seq"), axis=1, tiled=True),
    )


def flat_lanes(matrix):
    return matrix.reshape(-1, lane_width)


def reduce_grads(grad_terms):
    grad_qkv, grad_out_proj, grad_gateup, grad_down, grad_gains = grad_terms
    widths = (grad_qkv.shape[1], grad_out_proj.shape[1], grad_gateup.shape[1], grad_down.shape[1])
    flat_qkv = flat_lanes(grad_qkv)
    flat_out = flat_lanes(grad_out_proj)
    flat_gateup = flat_lanes(grad_gateup)
    flat_down = flat_lanes(grad_down)
    summed = (
        lax.psum_scatter(flat_qkv, ("fsdp", "seq"), scatter_dimension=0, tiled=True),
        lax.psum_scatter(flat_out, ("fsdp", "seq"), scatter_dimension=0, tiled=True),
        lax.psum_scatter(flat_gateup, ("fsdp", "seq"), scatter_dimension=0, tiled=True),
        lax.psum_scatter(flat_down, ("fsdp", "seq"), scatter_dimension=0, tiled=True),
        lax.psum_scatter(grad_gains, ("fsdp", "seq"), scatter_dimension=1, tiled=True),
    )
    owned = tuple((summed[kind_index].reshape(-1, widths[kind_index]) for kind_index in range(4)))
    return owned + (summed[4],)


def layer_forward(residual, gathered, allowed, rotary_cosines, rotary_sines):
    w_qkv, w_out, w_gateup, w_down, gain_pair = gathered
    count_of_rows = residual.shape[0]
    heads_per_group = QUERY_HEAD_COUNT // KEY_VALUE_HEADS
    gain_float = gain_pair.astype(jnp.float32)
    normed_one = normalize(residual)
    input_one = (normed_one * gain_float[0]).astype(jnp.bfloat16)
    query_key_value_rows = product(input_one, w_qkv)
    query_head_rows = apply_rotary(
        query_key_value_rows[:, : QUERY_HEAD_COUNT * HEAD_SIZE].reshape(
            count_of_rows, QUERY_HEAD_COUNT, HEAD_SIZE
        ),
        rotary_cosines,
        rotary_sines,
    ).astype(jnp.bfloat16)
    key_row_block = apply_rotary(
        query_key_value_rows[
            :, QUERY_HEAD_COUNT * HEAD_SIZE : (QUERY_HEAD_COUNT + KEY_VALUE_HEADS) * HEAD_SIZE
        ].reshape(count_of_rows, KEY_VALUE_HEADS, HEAD_SIZE),
        rotary_cosines,
        rotary_sines,
    ).astype(jnp.bfloat16)
    value_row_block = query_key_value_rows[
        :, (QUERY_HEAD_COUNT + KEY_VALUE_HEADS) * HEAD_SIZE :
    ].astype(jnp.bfloat16)
    every_key, every_value = (
        lax.all_gather(
            key_row_block.reshape(count_of_rows, KEY_VALUE_HEADS * HEAD_SIZE),
            "seq",
            axis=0,
            tiled=True,
        ),
        lax.all_gather(value_row_block, "seq", axis=0, tiled=True),
    )
    key_head_rows = every_key.reshape(-1, KEY_VALUE_HEADS, HEAD_SIZE)
    value_head_rows = every_value.reshape(-1, KEY_VALUE_HEADS, HEAD_SIZE)
    query_head_rows = query_head_rows.reshape(
        count_of_rows, KEY_VALUE_HEADS, heads_per_group, HEAD_SIZE
    )
    scores = attention_scores(query_head_rows, key_head_rows, allowed)
    row_max = jnp.max(scores, axis=-1, keepdims=True)
    shifted = jnp.exp(scores - row_max)
    row_sum = jnp.sum(shifted, axis=-1, keepdims=True)
    log_total = row_max + jnp.log(row_sum)
    attn_weights = (shifted / row_sum).astype(jnp.bfloat16)
    attended = jnp.einsum(
        "grqk,kgd->qgrd", attn_weights, value_head_rows, preferred_element_type=jnp.float32
    )
    attended = attended.reshape(count_of_rows, QUERY_HEAD_COUNT * HEAD_SIZE).astype(jnp.bfloat16)
    middle = residual + product(attended, w_out)
    normed_two = normalize(middle)
    input_two = (normed_two * gain_float[1]).astype(jnp.bfloat16)
    gate_up = product(input_two, w_gateup)
    gate_pre = gate_up[:, :FF]
    up_proj = gate_up[:, FF:]
    hidden = (jax.nn.silu(gate_pre) * up_proj).astype(jnp.bfloat16)
    layer_out = middle + product(hidden, w_down)
    saved_layer = (
        residual,
        normed_one,
        input_one,
        query_head_rows,
        key_head_rows,
        value_head_rows,
        log_total,
        attended,
        middle,
        normed_two,
        input_two,
        gate_pre,
        up_proj,
        hidden,
    )
    return (saved_layer, layer_out)


def layer_backward(grad_out, saved_layer, gathered, allowed, rotary_cosines, rotary_sines):
    w_qkv, w_out, w_gateup, w_down, gain_pair = gathered
    (
        residual,
        normed_one,
        input_one,
        query_head_rows,
        key_head_rows,
        value_head_rows,
        log_total,
        attended,
        middle,
        normed_two,
        input_two,
        gate_pre,
        up_proj,
        hidden,
    ) = saved_layer
    count_of_rows = grad_out.shape[0]
    heads_per_group = QUERY_HEAD_COUNT // KEY_VALUE_HEADS
    gain_float = gain_pair.astype(jnp.float32)
    grad_branch = grad_out.astype(jnp.bfloat16)
    grad_down = jnp.einsum("tf,td->fd", hidden, grad_branch, preferred_element_type=jnp.float32)
    grad_hidden = jnp.einsum("td,fd->tf", grad_branch, w_down, preferred_element_type=jnp.float32)
    sigmoid_gate = jax.nn.sigmoid(gate_pre)
    grad_gate = grad_hidden * up_proj * sigmoid_gate * (1.0 + gate_pre * (1.0 - sigmoid_gate))
    grad_up = grad_hidden * gate_pre * sigmoid_gate
    grad_pair = jnp.concatenate([grad_gate, grad_up], axis=1).astype(jnp.bfloat16)
    grad_gateup = jnp.einsum("td,tf->df", input_two, grad_pair, preferred_element_type=jnp.float32)
    grad_input_two = jnp.einsum(
        "tf,df->td", grad_pair, w_gateup, preferred_element_type=jnp.float32
    )
    grad_gain_two = jnp.sum(grad_input_two * normed_two, axis=0)
    grad_middle = grad_out + norm_back(grad_input_two * gain_float[1], normed_two, middle)
    grad_branch_two = grad_middle.astype(jnp.bfloat16)
    grad_out_proj = jnp.einsum(
        "te,td->ed", attended, grad_branch_two, preferred_element_type=jnp.float32
    )
    attended_gradient = jnp.einsum(
        "td,ed->te", grad_branch_two, w_out, preferred_element_type=jnp.float32
    )
    attended_gradient = attended_gradient.astype(jnp.bfloat16).reshape(
        count_of_rows, KEY_VALUE_HEADS, heads_per_group, HEAD_SIZE
    )
    scores = attention_scores(query_head_rows, key_head_rows, allowed)
    attn_float = jnp.exp(scores - log_total)
    value_gradient = jnp.einsum(
        "grqk,qgrd->kgd",
        attn_float.astype(jnp.bfloat16),
        attended_gradient,
        preferred_element_type=jnp.float32,
    )
    grad_weights = jnp.einsum(
        "qgrd,kgd->grqk", attended_gradient, value_head_rows, preferred_element_type=jnp.float32
    )
    inner_sum = jnp.sum(attn_float * grad_weights, axis=-1, keepdims=True)
    grad_scores = (attn_float * (grad_weights - inner_sum)).astype(jnp.bfloat16)
    grad_query = jnp.einsum(
        "grqk,kgd->qgrd", grad_scores, key_head_rows, preferred_element_type=jnp.float32
    ) * HEAD_SIZE ** (-0.5)
    gradient_keys = jnp.einsum(
        "grqk,qgrd->kgd", grad_scores, query_head_rows, preferred_element_type=jnp.float32
    ) * HEAD_SIZE ** (-0.5)
    shared_keys, value_share = (
        lax.psum_scatter(
            gradient_keys.reshape(-1, KEY_VALUE_HEADS * HEAD_SIZE).astype(jnp.bfloat16),
            "seq",
            scatter_dimension=0,
            tiled=True,
        ).astype(jnp.float32),
        lax.psum_scatter(
            value_gradient.reshape(-1, KEY_VALUE_HEADS * HEAD_SIZE).astype(jnp.bfloat16),
            "seq",
            scatter_dimension=0,
            tiled=True,
        ).astype(jnp.float32),
    )
    grad_q = invert_rotary(
        grad_query.reshape(count_of_rows, QUERY_HEAD_COUNT, HEAD_SIZE), rotary_cosines, rotary_sines
    ).reshape(count_of_rows, QUERY_HEAD_COUNT * HEAD_SIZE)
    key_gradient = invert_rotary(
        shared_keys.reshape(count_of_rows, KEY_VALUE_HEADS, HEAD_SIZE), rotary_cosines, rotary_sines
    ).reshape(count_of_rows, KEY_VALUE_HEADS * HEAD_SIZE)
    grad_rows = jnp.concatenate([grad_q, key_gradient, value_share], axis=1).astype(jnp.bfloat16)
    grad_qkv = jnp.einsum("td,tf->df", input_one, grad_rows, preferred_element_type=jnp.float32)
    grad_input_one = jnp.einsum("tf,df->td", grad_rows, w_qkv, preferred_element_type=jnp.float32)
    grad_gain_one = jnp.sum(grad_input_one * normed_one, axis=0)
    grad_in = grad_middle + norm_back(grad_input_one * gain_float[0], normed_one, residual)
    return (
        grad_in,
        (
            grad_qkv,
            grad_out_proj,
            grad_gateup,
            grad_down,
            jnp.stack([grad_gain_one, grad_gain_two]),
        ),
    )


def adam_step(weight, gradient, first_moment, second_moment, step_rate, shrink):
    first_moment = beta_one * first_moment + (1.0 - beta_one) * gradient
    second_moment = beta_two * second_moment + (1.0 - beta_two) * gradient * gradient
    first_hat = first_moment / (1.0 - beta_one**STEP)
    second_hat = second_moment / (1.0 - beta_two**STEP)
    weight = weight - step_rate * (first_hat / (jnp.sqrt(second_hat) + adam_eps) + shrink * weight)
    return (weight, first_moment, second_moment)


def shards(
    tokens,
    cotangent,
    lengths,
    w_qkv,
    w_out,
    w_gateup,
    w_down,
    norm_gains,
    first_qkv,
    first_out,
    first_gateup,
    first_down,
    first_gains,
    second_qkv,
    second_out,
    second_gateup,
    second_down,
    second_gains,
):
    count_of_rows = tokens.shape[0]
    group_rows = count_of_rows * lax.axis_size("seq")
    place_rows = lax.axis_index("seq") * count_of_rows + jnp.arange(count_of_rows, dtype=jnp.int32)
    key_places = jnp.arange(group_rows, dtype=jnp.int32)
    seg_rows, positions = layout(lengths[0], place_rows)
    seg_keys = layout(lengths[0], key_places)[0]
    allowed = (seg_rows[:, None] == seg_keys[None, :]) & (
        key_places[None, :] <= place_rows[:, None]
    )
    rotary_cosines, rotary_sines = tables(positions)
    stacked = (w_qkv, w_out, w_gateup, w_down, norm_gains)
    residual = tokens.astype(jnp.float32)
    saved_all = []
    for layer_index in range(LAYERS):
        gathered = fetch_forward(stacked, layer_index)
        saved_layer, residual = layer_forward(
            residual, gathered, allowed, rotary_cosines, rotary_sines
        )
        saved_all.append(saved_layer)
    grad_state = cotangent.astype(jnp.float32)
    updates = [None] * LAYERS
    for layer_index in reversed(range(LAYERS)):
        gathered = fetch_backward(stacked, layer_index)
        grad_state, grad_terms = layer_backward(
            grad_state, saved_all[layer_index], gathered, allowed, rotary_cosines, rotary_sines
        )
        updates[layer_index] = reduce_grads(grad_terms)
    step_rates = (D ** (-0.5), 4.0 * D ** (-0.5), D ** (-0.5), FF ** (-0.5), 0.5)
    shrinks = (decay_rate, decay_rate, decay_rate, decay_rate, 0.0)
    firsts = (first_qkv, first_out, first_gateup, first_down, first_gains)
    seconds = (second_qkv, second_out, second_gateup, second_down, second_gains)
    new_weights = []
    new_firsts = []
    new_seconds = []
    for kind_index in range(5):
        grads_kind = jnp.stack([updates[layer_index][kind_index] for layer_index in range(LAYERS)])
        weight, first_moment, second_moment = adam_step(
            stacked[kind_index],
            grads_kind,
            firsts[kind_index],
            seconds[kind_index],
            step_rates[kind_index],
            shrinks[kind_index],
        )
        new_weights.append(weight)
        new_firsts.append(first_moment)
        new_seconds.append(second_moment)
    outputs = [residual.astype(jnp.bfloat16), grad_state] + new_weights + new_firsts + new_seconds
    return tuple(outputs)


MESH = pl.DeviceIdType.MESH
BF = jnp.bfloat16
F32 = jnp.float32
KV_RANK = KEY_VALUE_HEADS // 4
Q_RANK = QUERY_HEAD_COUNT // 4
ANY = pl.BlockSpec(memory_space=pl.ANY)
VM = pl.BlockSpec(memory_space=pltpu.VMEM)
DMA = pltpu.SemaphoreType.DMA


class Place:
    def __init__(self):
        f, z = lax.axis_index("fsdp"), lax.axis_index("seq")
        self.y, self.x, self.c = lax.div(f, 4), lax.rem(lax.div(f, 2), 2), lax.rem(f, 2)
        self.z1, self.z0 = lax.div(z, 2), lax.rem(z, 2)
        self.rank = 2 * self.c + self.z0
        self.inner = self.z1 != self.z0
        self.sibling, self.over = 2 * (1 - self.c) + self.z0, 2 * self.c + 1 - self.z0
        self.diagonal = 2 * (1 - self.c) + 1 - self.z0
        self.peer = {
            "y": (f + 4 - 8 * self.y, z),
            "x": (f + 2 - 4 * self.x, z),
            "c": (f + 1 - 2 * self.c, z),
            "z1": (f, z + 2 - 4 * self.z1),
            "z0": (f, z + 1 - 2 * self.z0),
            "cz": (f + 1 - 2 * self.c, z + 1 - 2 * self.z0),
            "swap": (f - self.c + self.z1, 2 * self.c + self.z0),
            "mid": (f, 3 - z),
        }


def greet(place, names):
    barrier = pltpu.get_barrier_semaphore()
    partial = {"swap": place.c != place.z1, "mid": place.inner}
    amount = len([n for n in names if n not in partial])
    for name in names:
        if name not in partial:
            pl.semaphore_signal(barrier, inc=1, device_id=place.peer[name], device_id_type=MESH)
    for name, holds in partial.items():
        if name in names:
            amount = amount + holds.astype(jnp.int32)

            @pl.when(holds)
            def _(name=name):
                pl.semaphore_signal(barrier, inc=1, device_id=place.peer[name], device_id_type=MESH)

    pl.semaphore_wait(barrier, amount)


def remote(src, dst, send_sem, recv_sem, device):
    return pltpu.make_async_remote_copy(
        src_ref=src, dst_ref=dst, send_sem=send_sem, recv_sem=recv_sem, device_id=device, device_id_type=MESH
    )


def columns_index(y, x, z1, h):
    return ((y * 2 + x) * 2 + h) * 2 + z1


def rows_index(y, x, z1, h):
    return ((y * 2 + x) * 2 + z1) * 2 + h


class Cross:
    def __init__(self, place, src, dst_there, dst_here, relay, send, recv):
        self.p, self.src, self.dst_there, self.dst_here, self.relay = place, src, dst_there, dst_here, relay
        self.send, self.recv = send, recv

    def copy(self, k):
        p, relay = self.p, self.relay
        src, dst, peer = (
            (self.src, relay.at[0], "z0"),
            (self.src, relay.at[1], "mid"),
            (relay.at[0], self.dst_there, "mid"),
            (relay.at[1], self.dst_here, "z0"),
        )[k]
        return remote(src, dst, self.send.at[k], self.recv.at[k], p.peer[peer])

    def start(self):
        @pl.when(self.p.inner)
        def _():
            self.copy(1).start()

        @pl.when(jnp.logical_not(self.p.inner))
        def _():
            self.copy(0).start()

    def bring(self):
        @pl.when(self.p.inner)
        def _():
            self.copy(1).wait_recv()
            self.copy(3).start()

    def take(self):
        @pl.when(self.p.inner)
        def _():
            self.copy(0).wait_recv()
            self.copy(2).start()

    def wait(self):
        @pl.when(self.p.inner)
        def _():
            self.copy(2).wait_recv()

        @pl.when(jnp.logical_not(self.p.inner))
        def _():
            self.copy(3).wait_recv()

    def finish(self):
        @pl.when(self.p.inner)
        def _():
            for k in (1, 2, 3):
                self.copy(k).wait_send()

        @pl.when(jnp.logical_not(self.p.inner))
        def _():
            self.copy(0).wait_send()


class Gather:
    def __init__(self, place, ref, index, send, recv, local, relay, src=None, met=None):
        self.p, self.ref, self.index, self.send, self.recv = place, ref, index, send, recv
        self.local, self.src, self.met = local, src, met
        self.cross = []
        for h in (0, 1) if met is None else ():
            block = self.at((), h)
            self.cross.append(
                Cross(
                    place,
                    block if src is None else src.at[h],
                    block,
                    self.at(("z1",), h),
                    relay.at[h],
                    *[s.at[pl.ds(14 + 4 * h, 4)] for s in (send, recv)],
                )
            )

    def at(self, flips, h):
        p = self.p
        flip = lambda v, name: 1 - v if name in flips else v
        return self.ref.at[self.index(flip(p.y, "y"), flip(p.x, "x"), flip(p.z1, "z1"), h)]

    def route(self, h):
        a, b = ("y", "x") if h == 0 else ("x", "y")
        return (
            ("z1", ()),
            (a, ()),
            (a, ("z1",)),
            (b, ()),
            (b, ("z1",)),
            (b, (a,)),
            (b, (a, "z1")),
        )

    def out(self, h, m):
        axis, flips = self.route(h)[m]
        dst = src = self.at(flips, h)
        if self.src is not None and not flips:
            src = self.src.at[h]
        if self.met is not None and flips == ("z1",):
            src = self.met.at[h]
        return remote(src, dst, self.send.at[7 * h + m], self.recv.at[7 * h + m], self.p.peer[axis])

    def into(self, h, m):
        axis, flips = self.route(h)[m]
        ref = self.at(flips + (axis,), h)
        return remote(ref, ref, self.send.at[7 * h + m], self.recv.at[7 * h + m], self.p.peer[axis])

    def keep(self, h):
        kept = []
        if self.src is not None:
            kept.append(pltpu.make_async_copy(self.src.at[h], self.at((), h), self.local.at[h]))
        if self.met is not None:
            kept.append(pltpu.make_async_copy(self.met.at[h], self.at(("z1",), h), self.local.at[2 + h]))
        return kept

    def first(self):
        for c in self.cross:
            c.start()

    def second(self):
        for m in (1, 3) if self.met is None else (1, 3, 2, 4):
            for h in (0, 1):
                self.out(h, m).start()
        for h in (0, 1):
            for copy in self.keep(h):
                copy.start()

    def turned(self, h):
        self.cross[h].wait()
        for m in (2, 4):
            self.out(h, m).start()

    def on(self, h, got, gives):
        self.into(h, got).wait_recv()
        for m in gives:
            self.out(h, m).start()

    def last(self):
        for h in (0, 1):
            for m in (3, 4, 5, 6):
                self.into(h, m).wait_recv()
            for m in range(1, 7):
                self.out(h, m).wait_send()
            if self.met is None:
                self.cross[h].finish()
            for copy in self.keep(h):
                copy.wait()

    def steps(self, when):
        part = functools.partial
        acts = [(when["start"], self.first), (when["start"], self.second)]
        for h in (0, 1):
            if self.met is None:
                acts.append((when["bring"][h], self.cross[h].bring))
                acts.append((when["take"][h], self.cross[h].take))
                acts.append((when["turn"][h], part(self.turned, h)))
            acts.append((when["five"], part(self.on, h, 1, (5,))))
            acts.append((when["six"][h], part(self.on, h, 2, (6,))))
        return acts + [(when["last"], self.last)]


def times(start, bring, take, five, turn, six, last=99):
    return dict(start=start, bring=bring, take=take, five=five, turn=turn, six=six, last=last)


class Spread:
    def __init__(self, place, src, target, send, recv, local):
        self.p, self.src, self.target, self.send, self.recv, self.local = place, src, target, send, recv, local

    def copy(self, k, arriving=False):
        p = self.p
        name, fc, fz = (("c", 1, 0), ("z0", 0, 1), ("cz", 1, 1))[k]
        c = 1 - p.c if fc else p.c
        z0 = 1 - p.z0 if fz else p.z0
        src = self.src(c, z0)
        dst = self.target(c, z0) if arriving else self.target(p.c, p.z0)
        return remote(src, dst, self.send.at[k], self.recv.at[k], p.peer[name])

    def own(self):
        p = self.p
        return pltpu.make_async_copy(self.src(p.c, p.z0), self.target(p.c, p.z0), self.local)

    def start(self):
        for k in range(3):
            self.copy(k).start()
        self.own().start()

    def wait(self):
        for k in range(3):
            self.copy(k, True).wait_recv()
        self.own().wait()

    def finish(self):
        for k in range(3):
            self.copy(k).wait_send()


def add_to(dst, src):
    dst[...] = (dst[...].astype(F32) + src[...].astype(F32)).astype(dst.dtype)


class Reduce:
    def __init__(self, place, ref, index, out, mine, one, two, three, relay, send, recv, local):
        self.cross = [
            Cross(
                place, two.at[h, 0], three.at[h], three.at[h], relay.at[h], *[s.at[pl.ds(14 + 4 * h, 4)] for s in (send, recv)]
            )
            for h in ((0, 1) if out.shape != two.shape else ())
        ]
        self.p, self.ref, self.index, self.result = place, ref, index, out
        self.mine, self.one, self.two, self.three = mine, one, two, three
        self.send, self.recv, self.local = send, recv, local
        self.open = out.shape == two.shape

    def block(self, h, far_a, m):
        p = self.p
        a, b = (p.x, p.y) if h == 0 else (p.y, p.x)
        a = 1 - a if far_a else a
        b = 1 - b if m < 2 else b
        z1 = 1 - p.z1 if m % 2 == 0 else p.z1
        y, x = (b, a) if h == 0 else (a, b)
        return self.ref.at[self.index(y, x, z1, h)]

    def copy(self, h, m):
        p = self.p
        name_a, name_b = ("x", "y") if h == 0 else ("y", "x")
        sems = self.send.at[7 * h + m], self.recv.at[7 * h + m]
        if m < 4:
            return remote(self.block(h, True, m), self.one.at[h, m], *sems, p.peer[name_a])
        return remote(self.one.at[h, m - 4], self.two.at[h, m - 4], *sems, p.peer[name_b])

    def near(self, h, m):
        return self.block(h, False, m) if self.mine is None else self.mine.at[h, m]

    def load(self, h, m):
        return pltpu.make_async_copy(self.block(h, False, m), self.mine.at[h, m], self.local.at[4 * h + m])

    def first(self):
        for m in range(4):
            for h in (0, 1):
                self.copy(h, m).start()
                if self.mine is not None:
                    self.load(h, m).start()

    def second(self, h, m):
        self.copy(h, m).wait_recv()
        if self.mine is not None:
            self.load(h, m).wait()
        add_to(self.one.at[h, m], self.near(h, m))
        if m < 2:
            self.copy(h, 4 + m).start()

    def third(self, h, k):
        self.copy(h, 4 + k).wait_recv()
        add_to(self.two.at[h, k], self.one.at[h, 2 + k])
        if k == 0 and not self.open:
            self.cross[h].start()

    def fourth(self, h):
        self.cross[h].wait()
        add_to(self.three.at[h], self.two.at[h, 1])

    def finish(self):
        for h in (0, 1):
            for m in range(6):
                self.copy(h, m).wait_send()
            if not self.open:
                self.cross[h].finish()

    def store(self):
        src = self.two if self.result.shape == self.two.shape else self.three
        return pltpu.make_async_copy(src, self.result, self.local.at[8])


def out_gather_steps(p, src, ref, send, recv, local):
    home = p.x == p.z0
    away = jnp.logical_not(home)
    at = lambda fy, fz: ref.at[(1 - p.y if fy else p.y) * 2 + (1 - p.z1 if fz else p.z1)]
    pair = lambda half: remote(src, at(0, 0).at[half], send.at[0], recv.at[0], p.peer["z0"])
    z1_copy = lambda fz: remote(at(0, fz), at(0, fz), send.at[1], recv.at[1], p.peer["z1"])
    x_copy = lambda k: remote(at(0, k), at(0, k), send.at[2 + k], recv.at[2 + k], p.peer["x"])
    y_copy = lambda k, fy: remote(at(fy, k), at(fy, k), send.at[4 + k], recv.at[4 + k], p.peer["y"])
    own = pltpu.make_async_copy(src, at(0, 0).at[p.z0], local)

    def zero():
        @pl.when(home)
        def _():
            own.start()

        @pl.when(away)
        def _():
            pair(p.z0).start()

    def one():
        @pl.when(home)
        def _():
            own.wait()
            pair(1 - p.z0).wait_recv()
            z1_copy(0).start()
            x_copy(0).start()
            y_copy(0, 0).start()

    def two():
        @pl.when(home)
        def _():
            z1_copy(1).wait_recv()
            x_copy(1).start()
            y_copy(1, 0).start()

    def three():
        @pl.when(away)
        def _():
            for k in (0, 1):
                x_copy(k).wait_recv()
                y_copy(k, 0).start()

    def last():
        for k in (0, 1):
            y_copy(k, 1).wait_recv()
            y_copy(k, 0).wait_send()

        @pl.when(home)
        def _():
            z1_copy(0).wait_send()
            for k in (0, 1):
                x_copy(k).wait_send()

        @pl.when(away)
        def _():
            pair(p.z0).wait_send()

    return [zero, one, two, three, last]


def out_reduce_steps(p, ref, out, one, two, three, got, send, recv, local):
    home = p.x == p.z0
    away = jnp.logical_not(home)
    y_copy = lambda k: remote(ref.at[(1 - p.y) * 2 + k], one.at[k], send.at[k], recv.at[k], p.peer["y"])
    x_copy = lambda k: remote(one.at[k], two.at[k], send.at[2 + k], recv.at[2 + k], p.peer["x"])
    z1_copy = remote(two.at[1 - p.z1], three, send.at[4], recv.at[4], p.peer["z1"])
    rows = three.shape[0] // 2
    half = lambda z0: three.at[pl.ds(pl.multiple_of(z0 * rows, rows), rows)]
    pair = remote(half(1 - p.z0), got, send.at[5], recv.at[5], p.peer["z0"])
    keep = pltpu.make_async_copy(half(p.z0), out, local.at[0])
    take = pltpu.make_async_copy(got, out, local.at[0])

    def zero():
        for k in (0, 1):
            y_copy(k).start()

    def first():
        for k in (0, 1):
            y_copy(k).wait_recv()
            add_to(one.at[k], ref.at[p.y * 2 + k])

            @pl.when(away)
            def _(k=k):
                x_copy(k).start()

    def second():
        @pl.when(home)
        def _():
            for k in (0, 1):
                x_copy(k).wait_recv()
                add_to(two.at[k], one.at[k])
            z1_copy.start()

    def third():
        @pl.when(home)
        def _():
            z1_copy.wait_recv()
            add_to(three, two.at[p.z1])
            pair.start()
            keep.start()

    def last():
        for k in (0, 1):
            y_copy(k).wait_send()

        @pl.when(home)
        def _():
            keep.wait()
            z1_copy.wait_send()
            pair.wait_send()

        @pl.when(away)
        def _():
            pair.wait_recv()
            take.start()
            for k in (0, 1):
                x_copy(k).wait_send()
            take.wait()

    return [zero, first, second, third, last]


def out_reduce_scratch(wide):
    return [
        pltpu.VMEM((4,) + wide, BF),
        pltpu.VMEM((2,) + wide, BF),
        pltpu.VMEM((2,) + wide, BF),
        pltpu.VMEM(wide, BF),
        pltpu.VMEM((wide[0] // 2, wide[1]), BF),
        DMA((6,)),
        DMA((6,)),
        DMA((1,)),
    ]


def gains_gather(p, src, ref, send, recv, local):
    me = ((p.y * 2 + p.x) * 2 + p.c) * 4 + p.z1 * 2 + p.z0
    own = pltpu.make_async_copy(src, ref.at[me], local)
    names = ("z0", "z1", "c", "x", "y")

    def span(k, other):
        size = 1 << k
        start = lax.div(me, size) * size
        if other:
            bit = lax.rem(lax.div(me, size), 2)
            start = start + size - 2 * size * bit
        return ref.at[pl.ds(start, size)]

    def copy(k, other):
        return remote(span(k, other), span(k, other), send.at[k], recv.at[k], p.peer[names[k]])

    def step(k):
        def run():
            if k == 0:
                own.start()
                own.wait()
            else:
                copy(k - 1, True).wait_recv()
            if k < 5:
                copy(k, False).start()
            else:
                for j in range(5):
                    copy(j, False).wait_send()

        return run

    return [step(k) for k in range(6)]


def gains_reduce(p, src, out, base, halves, send, recv, local):
    names, bits = ("y", "x", "c", "z1", "z0"), (p.y, p.x, p.c, p.z1, p.z0)
    load = pltpu.make_async_copy(src, base, local.at[0])
    keep = pltpu.make_async_copy(halves[4].at[0], out, local.at[0])

    def part(k, bit):
        source, size = (base if k == 0 else halves[k - 1]), 16 >> k
        return source.at[pl.ds(bit * size, size)]

    def copy(k):
        return remote(part(k, 1 - bits[k]), halves[k], send.at[k], recv.at[k], p.peer[names[k]])

    def step(k):
        def run():
            if k > 0:
                copy(k - 1).wait_recv()
                halves[k - 1][...] += part(k - 1, bits[k - 1])[...]
            else:
                load.start()
                load.wait()
            if k < 5:
                copy(k).start()
            else:
                keep.start()
                for j in range(5):
                    copy(j).wait_send()
                keep.wait()

        return run

    return [step(k) for k in range(6)]


GROUP = ("c", "z0", "cz")
EIGHT = ("z1", "y", "x")


CHUNKS = 2


class ShareRows:
    def __init__(self, p, dst, send, recv):
        self.p, self.dst, self.send, self.recv = p, dst, send, recv
        self.rows = dst.shape[1] // CHUNKS

    def chunk(self, rank, k):
        return self.dst.at[rank, pl.ds(k * self.rows, self.rows)]

    def over(self, k, arriving=False):
        p = self.p
        ref = self.chunk(p.over if arriving else p.rank, k)
        return remote(ref, ref, self.send.at[k], self.recv.at[k], p.peer["z0"])

    def across(self, arriving=False):
        p = self.p
        ref = self.dst.at[p.sibling if arriving else p.rank]
        return remote(ref, ref, self.send.at[CHUNKS], self.recv.at[CHUNKS], p.peer["c"])

    def onward(self, k, arriving=False):
        p = self.p
        ours, theirs = 2 * p.c + 1 - p.z0, 2 * (1 - p.c) + 1 - p.z0
        ref = self.chunk(theirs if arriving else ours, k)
        return remote(ref, ref, self.send.at[CHUNKS + 1 + k], self.recv.at[CHUNKS + 1 + k], p.peer["c"])

    def start(self):
        for k in range(CHUNKS):
            self.over(k).start()
        self.across().start()

    def pass_on(self, k):
        self.over(k, True).wait_recv()
        self.onward(k).start()

    def far(self, k):
        self.onward(k, True).wait_recv()

    def finish(self):
        for k in range(CHUNKS):
            self.over(k).wait_send()
            self.onward(k).wait_send()
        self.across().wait_send()


class SumRows:
    def __init__(self, p, terms, near, cross, far, send, recv):
        self.p, self.terms, self.near, self.cross, self.far, self.send, self.recv = p, terms, near, cross, far, send, recv
        self.rows = near.shape[0] // CHUNKS

    def diagonal(self, k):
        p = self.p
        part = pl.ds(k * self.rows, self.rows)
        rank = 2 * (1 - p.c) + 1 - p.z0
        return remote(self.terms.at[rank, part], self.cross.at[part], self.send.at[k], self.recv.at[k], p.peer["c"])

    def sibling(self):
        p = self.p
        rank, at = 2 * (1 - p.c) + p.z0, CHUNKS
        return remote(self.terms.at[rank], self.near, self.send.at[at], self.recv.at[at], p.peer["c"])

    def over(self, k):
        p, at = self.p, CHUNKS + 1 + k
        part = pl.ds(k * self.rows, self.rows)
        return remote(self.cross.at[part], self.far.at[part], self.send.at[at], self.recv.at[at], p.peer["z0"])

    def relay(self, k):
        p = self.p
        self.diagonal(k).wait_recv()
        part = pl.ds(k * self.rows, self.rows)
        add_to(self.cross.at[part], self.terms.at[2 * p.c + 1 - p.z0, part])
        self.over(k).start()

    def finish(self):
        for k in range(CHUNKS):
            self.diagonal(k).wait_send()
            self.over(k).wait_send()
        self.sibling().wait_send()


def swap_pairs(count_fsdp, count_seq):
    pairs = []
    for f in range(count_fsdp):
        for z in range(count_seq):
            c, z1 = f % 2, z // 2
            pairs.append((f * count_seq + z, (f - c + z1) * count_seq + c * 2 + z % 2))
    return pairs


TILE = 256
UP_TILE = 512
DOWN_TILE = 768
GRAD_TILE = 512
HALVES = 2


def wide_params(collective_id):
    return pltpu.CompilerParams(
        collective_id=collective_id, has_side_effects=True, vmem_limit_bytes=61 * 2**20
    )


def dot(a, b, contract=((1,), (0,))):
    return lax.dot_general(a, b, (contract, ((), ())), preferred_element_type=F32)


def row_normalize(ref, gain, out, rows=32):
    def step(k, _):
        at = pl.ds(pl.multiple_of(k * rows, rows), rows)
        value = ref[at, :].astype(F32)
        out[at, :] = (normalize(value) * gain[...]).astype(out.dtype)
        return 0

    lax.fori_loop(0, ref.shape[0] // rows, step, 0)


def column_tiles(width, tile, step):
    def run(j, _):
        step(pl.multiple_of(j * tile, tile))
        return 0

    lax.fori_loop(0, width // tile, run, 0)


def exchange(p, share, total, compute, advance):
    rows = total.near.shape[0]
    part = rows // CHUNKS
    share.start()
    advance()
    compute([(p.rank, 0)], rows)
    advance()
    share.across(True).wait_recv()
    compute([(p.sibling, 0)], rows)
    total.sibling().start()
    advance()
    for k in range(CHUNKS):
        share.pass_on(k)
        share.far(k)
        compute([(p.diagonal, k * part), (p.over, k * part)], part)
        total.diagonal(k).start()
        total.relay(k)
        advance()


def gather_pieces(ref, pieces, count, *index):
    parts = [ref[(rank, pl.ds(first, count)) + index] for rank, first in pieces]
    return parts[0] if len(parts) == 1 else jnp.concatenate(parts, axis=0)


def scatter_pieces(ref, pieces, count, value, *index):
    for k, (rank, first) in enumerate(pieces):
        ref[(rank, pl.ds(first, count)) + index] = value[k * count : (k + 1) * count]


def token_rows(pieces, count, rows):
    return [pl.ds(pl.multiple_of(rank * rows + first, count), count) for rank, first in pieces]


def collect(p, total, write, rows=32):
    total.sibling().wait_recv()
    for k in range(CHUNKS):
        total.over(k).wait_recv()

        def step(j, _, k=k):
            at = pl.ds(pl.multiple_of(k * total.rows + j * rows, rows), rows)
            value = total.terms[p.rank, at, :].astype(F32) + total.near[at, :].astype(F32)
            write(at, value + total.far[at, :].astype(F32))
            return 0

        lax.fori_loop(0, total.rows // rows, step, 0)


def exchange_scratch(rows):
    part = pltpu.VMEM((rows, D), BF)
    sems = DMA((2 * CHUNKS + 1,))
    return [pltpu.VMEM((4, rows, D), BF), part, part, part, sems, sems, sems, sems]


def exchange_of(p, every, refs):
    terms, near, cross, far, send, recv, t_send, t_recv = refs
    share = ShareRows(p, every, send, recv)
    return every.at[p.rank], terms, share, SumRows(p, terms, near, cross, far, t_send, t_recv)


class Nothing:
    names, args, specs, shapes, scratch = (), (), (), (), ()

    def steps(self, p, ins, outs, scratch):
        return []


class Clock:
    def __init__(self, steps):
        self.steps, self.now = sorted(steps, key=lambda s: s[0]), 0

    def __call__(self):
        while self.steps and self.steps[0][0] <= self.now:
            self.steps.pop(0)[1]()
        self.now += 1

    def finish(self):
        for _, act in self.steps:
            act()
        self.steps = []


class Staged:
    def __init__(self, ins, in_sems, outs, out_sems):
        self.loads = {k: pltpu.make_async_copy(src, dst, in_sems.at[n]) for n, (k, src, dst) in enumerate(ins)}
        self.stores = {k: pltpu.make_async_copy(src, dst, out_sems.at[n]) for n, (k, src, dst) in enumerate(outs)}
        self.started = []
        for load in self.loads.values():
            load.start()

    def ready(self, *ks):
        for k in ks:
            if k in self.loads:
                self.loads.pop(k).wait()

    def flush(self, *ks):
        for k in ks:
            store = self.stores.pop(k)
            store.start()
            self.started.append(store)

    def finish(self):
        self.ready(*list(self.loads))
        self.flush(*list(self.stores))
        for store in self.started:
            store.wait()


def beside_call(
    body, args, late, shapes, later, scratch, beside, name, collective_id, flops, peers=("c", "z0"), specs=None
):
    n_ins, n_outs = len(args), len(shapes)
    buffers = [pltpu.VMEM(args[k].shape, args[k].dtype) for k in late]
    buffers += [pltpu.VMEM(shapes[k].shape, shapes[k].dtype) for k in later]
    sems = [DMA((max(len(late), 1),)), DMA((max(len(later), 1),))]
    counts = [n_ins, len(beside.args), n_outs, len(beside.shapes), len(scratch), len(buffers), 2, len(beside.scratch)]

    def whole(*refs):
        groups, at = [], 0
        for n in counts:
            groups.append(list(refs[at : at + n]))
            at += n
        ins, b_ins, outs, b_outs, own, held, (in_sems, out_sems), b_scratch = groups
        moved_in = [(k, ins[k], held[n]) for n, k in enumerate(late)]
        moved_out = [(k, held[len(late) + n], outs[k]) for n, k in enumerate(later)]
        staged = Staged(moved_in, in_sems, moved_out, out_sems)
        for k, _, dst in moved_in:
            ins[k] = dst
        for k, src, _ in moved_out:
            outs[k] = src
        p = Place()
        greet(p, tuple(peers) + tuple(n for n in beside.names if n not in peers))
        body(p, ins, outs, own, Clock(beside.steps(p, b_ins, b_outs, b_scratch)), staged)
        staged.finish()

    specs = specs or {}
    out = pl.pallas_call(
        whole,
        out_shape=list(shapes) + list(beside.shapes),
        in_specs=[ANY if k in late else VM for k in range(n_ins)] + list(beside.specs),
        out_specs=[ANY if k in later else specs.get(k, VM) for k in range(n_outs)] + [ANY] * len(beside.shapes),
        scratch_shapes=list(scratch) + buffers + sems + list(beside.scratch),
        compiler_params=wide_params(collective_id),
        cost_estimate=pl.CostEstimate(flops=flops, bytes_accessed=20 * 2**20, transcendentals=0),
        name=name,
    )(*args, *beside.args)
    return out[:n_outs], out[n_outs:]


def feed_forward_call(middle, gain, w_gateup, w_down, beside, collective_id, dtype=F32):
    rows, wide = middle.shape[0], w_down.shape[0]

    def body(p, ins, outs, scratch, advance, staged):
        mid_ref, gain_ref, gu_ref, down_ref = ins
        new_ref, every, gate_ref, up_ref, hid_ref = outs
        own, terms, share, total = exchange_of(p, every, scratch)

        def compute(pieces, count):
            staged.ready(2, 3)

            def up_tile(j):
                cols, far = pl.ds(j, UP_TILE), pl.ds(wide + j, UP_TILE)
                x = gather_pieces(every, pieces, count)
                gate, up = dot(x, gu_ref[:, cols]), dot(x, gu_ref[:, far])
                scatter_pieces(gate_ref, pieces, count, gate.astype(BF), cols)
                scatter_pieces(up_ref, pieces, count, up.astype(BF), cols)
                hidden = (gate / (1.0 + jnp.exp(-gate)) * up).astype(BF)
                scatter_pieces(hid_ref, pieces, count, hidden, cols)

            column_tiles(wide, UP_TILE, up_tile)

            def down_tile(j):
                cols = pl.ds(j, DOWN_TILE)
                value = dot(gather_pieces(hid_ref, pieces, count), down_ref[:, cols]).astype(BF)
                scatter_pieces(terms, pieces, count, value, cols)

            column_tiles(D, DOWN_TILE, down_tile)

        row_normalize(mid_ref, gain_ref, own)
        exchange(p, share, total, compute, advance)
        staged.flush(1, 2, 3, 4)

        def write(at, value):
            new_ref[at, :] = (mid_ref[at, :] + value).astype(dtype)

        collect(p, total, write)
        advance.finish()
        share.finish()
        total.finish()

    return beside_call(
        body,
        (middle, gain.reshape(1, D), w_gateup, w_down),
        (2, 3),
        [
            jax.ShapeDtypeStruct((rows, D), dtype),
            jax.ShapeDtypeStruct((4, rows, D), BF),
            jax.ShapeDtypeStruct((4, rows, wide), BF),
            jax.ShapeDtypeStruct((4, rows, wide), BF),
            jax.ShapeDtypeStruct((4, rows, wide), BF),
        ],
        (1, 2, 3, 4),
        exchange_scratch(rows),
        beside,
        "feed_forward",
        collective_id,
        6 * 4 * rows * wide * D,
    )


def feed_backward_call(grad, middle, gain, w_gateup, w_down, kept, beside, collective_id):
    every, gate, up, hidden = kept
    rows, wide = middle.shape[0], w_down.shape[0]
    block = (wide // 16, D)

    def body(p, ins, outs, scratch, advance, staged):
        grad_ref, mid_ref, gain_ref, gu_ref, down_ref, every_ref, gate_ref, up_ref, hid_ref = ins
        new_ref, gain_out, g_gu, two_down = outs
        e, pair, g_down, one, two, send, recv, local = scratch[:8]
        own, terms, share, total = exchange_of(p, e, scratch[8:])
        reduce = Reduce(p, g_down, rows_index, two_down, None, one, two, None, None, send, recv, local)

        def compute(pieces, count):
            staged.ready(4, 6, 7, 3)

            def up_tile(j):
                cols, far = pl.ds(j, UP_TILE), pl.ds(wide + j, UP_TILE)
                grad_hidden = dot(gather_pieces(e, pieces, count), down_ref[cols, :], ((1,), (1,)))
                g = gather_pieces(gate_ref, pieces, count, cols).astype(F32)
                u = gather_pieces(up_ref, pieces, count, cols).astype(F32)
                s = 1.0 / (1.0 + jnp.exp(-g))
                grad_gate = (grad_hidden * u * s * (1.0 + g * (1.0 - s))).astype(BF)
                scatter_pieces(pair, pieces, count, grad_gate, cols)
                scatter_pieces(pair, pieces, count, (grad_hidden * g * s).astype(BF), far)

            column_tiles(wide, UP_TILE, up_tile)

            def down_tile(j):
                cols = pl.ds(j, DOWN_TILE)
                value = dot(gather_pieces(pair, pieces, count), gu_ref[cols, :], ((1,), (1,))).astype(BF)
                scatter_pieces(terms, pieces, count, value, cols)

            column_tiles(D, DOWN_TILE, down_tile)

        def weight_grads():
            tokens = 4 * rows
            e_all, pair_all, x_all, hid_all = (
                r.reshape(tokens, r.shape[2]) for r in (e, pair, every_ref, hid_ref)
            )

            part = g_down.shape[1]
            staged.ready(8, 5)

            def down_grad(j):
                value = dot(hid_all[:, pl.ds(j, GRAD_TILE)], e_all[...], ((0,), (0,))).astype(BF)
                g_down[pl.ds(lax.div(j, part), GRAD_TILE // part)] = value.reshape(GRAD_TILE // part, part, D)

            column_tiles(wide, GRAD_TILE, down_grad)
            reduce.first()
            for k in range(D // GRAD_TILE):
                cols = slice(k * GRAD_TILE, (k + 1) * GRAD_TILE)
                g_gu[cols, :] = dot(x_all[:, cols], pair_all[...], ((0,), (0,))).astype(BF)
                advance()
                if k < 2:
                    for m in (2 * k, 2 * k + 1):
                        for h in (0, 1):
                            reduce.second(h, m)
            staged.flush(2)

        def copy_own(k, _):
            at = pl.ds(pl.multiple_of(k * 32, 32), 32)
            own[at, :] = grad_ref[at, :].astype(BF)
            return 0

        lax.fori_loop(0, rows // 32, copy_own, 0)
        exchange(p, share, total, compute, advance)
        weight_grads()
        gain_out[...] = jnp.zeros_like(gain_out)

        def write(at, value):
            mid = mid_ref[at, :]
            normed = normalize(mid)
            gain_out[...] += jnp.sum(value * normed, axis=0, keepdims=True)
            new_ref[at, :] = grad_ref[at, :] + norm_back(value * gain_ref[...], normed, mid)

        collect(p, total, write)
        for k in (0, 1):
            for h in (0, 1):
                reduce.third(h, k)
        advance.finish()
        reduce.store().start()
        reduce.finish()
        reduce.store().wait()
        share.finish()
        total.finish()

    return beside_call(
        body,
        (grad, middle, gain.reshape(1, D), w_gateup, w_down, every, gate, up, hidden),
        (4, 6, 7, 3, 8, 5),
        [
            jax.ShapeDtypeStruct((rows, D), F32),
            jax.ShapeDtypeStruct((1, D), F32),
            jax.ShapeDtypeStruct((D, 2 * wide), BF),
            jax.ShapeDtypeStruct((2, 2) + block, BF),
        ],
        (2,),
        [
            pltpu.VMEM((4, rows, D), BF),
            pltpu.VMEM((4, rows, 2 * wide), BF),
            pltpu.VMEM((16,) + block, BF),
            pltpu.VMEM((2, 4) + block, BF),
            pltpu.VMEM((2, 2) + block, BF),
            DMA((14,)),
            DMA((14,)),
            DMA((9,)),
        ]
        + exchange_scratch(rows),
        beside,
        "feed_backward",
        collective_id,
        12 * 4 * rows * wide * D,
        ("c", "z0", "x", "y"),
        {3: ANY},
    )


class Both:
    def __init__(self, *parts):
        self.parts = parts
        self.names = tuple(dict.fromkeys(n for p in parts for n in p.names))
        self.args = tuple(a for p in parts for a in p.args)
        self.specs = tuple(a for p in parts for a in p.specs)
        self.shapes = tuple(s for p in parts for s in p.shapes)
        self.scratch = tuple(s for p in parts for s in p.scratch)

    def steps(self, p, ins, outs, scratch):
        waves, at = [], [0, 0, 0]
        for part in self.parts:
            ends = [at[0] + len(part.args), at[1] + len(part.shapes), at[2] + len(part.scratch)]
            waves += part.steps(p, ins[at[0] : ends[0]], outs[at[1] : ends[1]], scratch[at[2] : ends[2]])
            at = ends
        return waves


class SwapRows:
    names = ("swap",)

    def __init__(self, rows, at=0):
        self.args, self.specs, self.time = (rows,), (VM,), at
        self.shapes = (jax.ShapeDtypeStruct(rows.shape, rows.dtype),)
        self.scratch = (DMA((1,)), DMA((1,)), DMA((1,)))

    def steps(self, p, ins, outs, scratch):
        send, recv, local = (s.at[0] for s in scratch)
        away = p.c != p.z1
        move = remote(ins[0], outs[0], send, recv, p.peer["swap"])
        stay = pltpu.make_async_copy(ins[0], outs[0], local)

        def first():
            @pl.when(away)
            def _():
                move.start()

            @pl.when(jnp.logical_not(away))
            def _():
                stay.start()

        def last():
            @pl.when(away)
            def _():
                move.wait()

            @pl.when(jnp.logical_not(away))
            def _():
                stay.wait()

        return [(self.time, first), (99, last)]


class SpreadColumns:
    names = GROUP

    def __init__(self, *blocks):
        self.args, self.specs = blocks, (VM,) * len(blocks)
        self.shapes = tuple(jax.ShapeDtypeStruct((2, 2) + b.shape[1:], BF) for b in blocks)
        self.scratch = (DMA((3 * len(blocks),)), DMA((3 * len(blocks),)), DMA((len(blocks),)))

    def steps(self, p, ins, outs, scratch):
        send, recv, local = scratch
        made = []
        for k, (src, dst) in enumerate(zip(ins, outs)):
            sems = [s.at[pl.ds(3 * k, 3)] for s in (send, recv)]
            made.append(
                Spread(
                    p, lambda c, z0, s=src: s.at[2 * c + z0], lambda c, z0, d=dst: d.at[c, z0], *sems, local.at[k]
                )
            )

        def first():
            for m in made:
                m.start()

        def last():
            for m in made:
                m.wait()
                m.finish()

        return [(0, first), (99, last)]


class CollectColumns:
    names = GROUP

    def __init__(self, *blocks, at=0):
        self.time = at
        self.args, self.specs = blocks, (VM,) * len(blocks)
        self.shapes = tuple(jax.ShapeDtypeStruct((4,) + b.shape[2:], BF) for b in blocks)
        self.scratch = (DMA((3 * len(blocks),)), DMA((3 * len(blocks),)), DMA((len(blocks),)))

    def steps(self, p, ins, outs, scratch):
        send, recv, local = scratch
        made = []
        for k, (src, dst) in enumerate(zip(ins, outs)):
            sems = [s.at[pl.ds(3 * k, 3)] for s in (send, recv)]
            made.append(
                Spread(
                    p, lambda c, z0, s=src: s.at[c, z0], lambda c, z0, d=dst: d.at[2 * c + z0], *sems, local.at[k]
                )
            )

        def first():
            for m in made:
                m.start()

        def last():
            for m in made:
                m.wait()
                m.finish()

        return [(self.time, first), (99, last)]


class MeetBlocks:
    names = ("mid", "z0")

    def __init__(self, *blocks, at=(0, 1, 2)):
        self.args, self.specs, self.times = blocks, (VM,) * len(blocks), at
        self.shapes = tuple(jax.ShapeDtypeStruct(b.shape, BF) for b in blocks)
        self.scratch = tuple(pltpu.VMEM((2,) + b.shape, BF) for b in blocks)
        self.scratch += (DMA((8 * len(blocks),)), DMA((8 * len(blocks),)))

    def steps(self, p, ins, outs, scratch):
        relays, (send, recv) = scratch[:-2], scratch[-2:]
        acts = []
        for k, (src, dst, relay) in enumerate(zip(ins, outs, relays)):
            for h in (0, 1):
                sems = [s.at[pl.ds(8 * k + 4 * h, 4)] for s in (send, recv)]
                c = Cross(p, src.at[h], dst.at[h], dst.at[h], relay.at[:, h], *sems)
                acts += list(zip(self.times, (c.start, c.bring, c.take))) + [(99, c.wait), (99, c.finish)]
        return acts


class MeetOut:
    names = ("z0", "z1")

    def __init__(self, out, at=(0, 4)):
        self.args, self.specs, self.times = (out,), (VM,), at
        self.shapes = (jax.ShapeDtypeStruct((2, 2) + out.shape, BF),)
        self.scratch = (DMA((2,)), DMA((2,)), DMA((1,)))

    def steps(self, p, ins, outs, scratch):
        src, met = ins[0], outs[0]
        send, recv, local = scratch
        home = p.x == p.z0
        away = jnp.logical_not(home)
        pair = lambda half: remote(src, met.at[0, half], send.at[0], recv.at[0], p.peer["z0"])
        over = remote(met.at[0], met.at[1], send.at[1], recv.at[1], p.peer["z1"])
        own = pltpu.make_async_copy(src, met.at[0, p.z0], local.at[0])

        def first():
            pl.when(home)(own.start)
            pl.when(away)(lambda: pair(p.z0).start())

        def second():
            @pl.when(home)
            def _():
                own.wait()
                pair(1 - p.z0).wait_recv()
                over.start()

        def last():
            pl.when(home)(over.wait)
            pl.when(away)(lambda: pair(p.z0).wait_send())

        return [(self.times[0], first), (self.times[1], second), (99, last)]


class GatherOut:
    names = ("x", "y")

    def __init__(self, met, at=(0, 3)):
        self.args, self.specs, self.times = (met,), (VM,), at
        self.shapes = (jax.ShapeDtypeStruct((4,) + met.shape[1:], BF),)
        self.scratch = (DMA((4,)), DMA((4,)), DMA((2,)))

    def steps(self, p, ins, outs, scratch):
        met, ref = ins[0], outs[0]
        send, recv, local = scratch
        home = p.x == p.z0
        away = jnp.logical_not(home)
        at = lambda fy, k: ref.at[(1 - p.y if fy else p.y) * 2 + (1 - p.z1 if k else p.z1)]
        x_copy = lambda k: remote(met.at[k], at(0, k), send.at[k], recv.at[k], p.peer["x"])
        y_copy = lambda k, src, fy=0: remote(src, at(fy, k), send.at[2 + k], recv.at[2 + k], p.peer["y"])
        keep = lambda k: pltpu.make_async_copy(met.at[k], at(0, k), local.at[k])

        def first():
            @pl.when(home)
            def _():
                for k in (0, 1):
                    x_copy(k).start()
                    y_copy(k, met.at[k]).start()
                    keep(k).start()

        def second():
            @pl.when(away)
            def _():
                for k in (0, 1):
                    x_copy(k).wait_recv()
                    y_copy(k, at(0, k)).start()

        def last():
            for k in (0, 1):
                y_copy(k, at(1, k), 1).wait_recv()
                y_copy(k, at(0, k)).wait_send()

            @pl.when(home)
            def _():
                for k in (0, 1):
                    x_copy(k).wait_send()
                    keep(k).wait()

        return [(self.times[0], first), (self.times[1], second), (99, last)]


class GatherWeights:
    def __init__(
        self, columns=None, down=None, out=None, gains=None, columns_at=None, down_at=None, out_at=None, gains_at=None, met=None
    ):
        self.has = columns is not None, down is not None, out is not None, gains is not None
        self.spread = columns is not None and len(columns.shape) == 3
        self.times = columns_at, down_at, out_at, gains_at
        self.names = EIGHT + (("mid",) if met is None else ()) + ("z0",) + (GROUP if self.spread else ())
        self.met = met is not None
        self.args = tuple(a for a in (columns, down, out, gains) if a is not None) + tuple(met or ())
        self.specs = (VM,) * len(self.args)
        shapes, scratch = [], []
        sems = lambda n: [DMA((n,)), DMA((n,)), DMA((4,))]
        if columns is not None:
            block = (2,) + columns.shape[-2:]
            shapes.append((16,) + block)
            scratch += sems(22) + [pltpu.VMEM((2, 2) + block, BF)] + sems(3)
        if down is not None:
            shapes.append((16,) + down.shape[1:])
            scratch += sems(22) + [pltpu.VMEM((2, 2) + down.shape[1:], BF)]
        if out is not None:
            shapes.append((4, 2) + out.shape)
            scratch += sems(8)
        if gains is not None:
            shapes.append((32,) + gains.shape)
            scratch += sems(5)
        self.shapes = tuple(jax.ShapeDtypeStruct(s, BF) for s in shapes)
        self.scratch = tuple(scratch)

    def steps(self, p, ins, outs, scratch):
        ins, outs, scratch = list(ins), list(outs), list(scratch)
        take = lambda n: [scratch.pop(0) for _ in range(n)]
        acts = []
        met = [ins.pop() if self.met and has else None for has in self.has[1::-1]][::-1]
        if self.has[0]:
            src, ref = ins.pop(0), outs.pop(0)
            sems, s_sems, when = take(4), take(3), self.times[0]
            if self.spread:
                at = lambda c, z0, ref=ref: ref.at[columns_index(p.y, p.x, p.z1, c), z0]
                spread = Spread(p, lambda c, z0, src=src: src.at[2 * c + z0], at, *s_sems[:2], s_sems[2].at[0])
                acts += [(-1, spread.start), (when["start"], spread.wait), (99, spread.finish)]
                src = None
            acts += Gather(p, ref, columns_index, *sems, src, met[0]).steps(when)
        if self.has[1]:
            src, ref = ins.pop(0), outs.pop(0)
            acts += Gather(p, ref, rows_index, *take(4), src, met[1]).steps(self.times[1])
        if self.has[2]:
            acts += zip(self.times[2], out_gather_steps(p, ins.pop(0), outs.pop(0), *take(2), take(1)[0].at[0]))
        if self.has[3]:
            acts += zip(self.times[3], gains_gather(p, ins.pop(0), outs.pop(0), *take(2), take(1)[0].at[0]))
        return acts


class ReduceWeights:
    def __init__(self, columns, gains=None, collect=False, open=False, at=range(9)):
        self.gains = gains is not None
        self.collect, self.open, self.times = collect, open, tuple(at)
        self.names = EIGHT + ("mid", "z0") + (GROUP if collect else ())
        self.args = tuple(a for a in (columns, gains) if a is not None)
        self.specs = (ANY,) * len(self.args)
        shapes, scratch = [], []
        b = columns.shape[1:]
        shape = (4, b[0] // 2, b[1]) if collect else (2, 2) + b if open else (2,) + b
        shapes.append(jax.ShapeDtypeStruct(shape, BF))
        scratch += [pltpu.VMEM(n + b, BF) for n in ((2, 4), (2, 4), (2, 2), (2,))]
        scratch += [pltpu.VMEM((1, 1, 16, 128) if open else (2, 2) + b, BF), DMA((22,)), DMA((22,)), DMA((9,))]
        if collect:
            scratch += [DMA((3,)), DMA((3,)), DMA((1,))]
        if gains is not None:
            shapes.append(jax.ShapeDtypeStruct(gains.shape[1:], F32))
            scratch += [pltpu.VMEM(gains.shape, F32)]
            scratch += [pltpu.VMEM((16 >> k,) + gains.shape[1:], F32) for k in range(5)]
            scratch += [DMA((5,)), DMA((5,)), DMA((1,))]
        self.shapes, self.scratch = tuple(shapes), tuple(scratch)

    def steps(self, p, ins, outs, scratch):
        ins, outs, scratch = list(ins), list(outs), list(scratch)
        take = lambda n: [scratch.pop(0) for _ in range(n)]
        waves = [[] for _ in range(9)]
        part = functools.partial
        both = (0, 1)
        columns = Reduce(p, ins.pop(0), columns_index, outs.pop(0), *take(8))
        waves[0].append(columns.first)
        for m in range(4):
            waves[1 + m] += [part(columns.second, h, m) for h in both]
        for k in both:
            waves[5 + k] += [part(columns.third, h, k) for h in both]
        if self.collect:
            send, recv, local = take(3)
            rows = columns.three.shape[1] // 2
            piece = lambda c, z0: columns.three.at[c, pl.ds(pl.multiple_of(z0 * rows, rows), rows)]
            spread = Spread(p, piece, lambda c, z0: columns.result.at[2 * c + z0], send, recv, local.at[0])
            waves[7] += [c.bring for c in columns.cross] + [c.take for c in columns.cross]
            waves[8] += [part(columns.fourth, h) for h in both] + [spread.start, spread.wait, spread.finish]
        elif not self.open:
            waves[7] += [c.bring for c in columns.cross] + [c.take for c in columns.cross]
            waves[8] += [part(columns.fourth, h) for h in both]
        if not self.collect:
            waves[8] += [lambda: columns.store().start(), lambda: columns.store().wait()]
        waves[8].append(columns.finish)
        if self.gains:
            parts = take(9)
            steps = gains_reduce(p, ins.pop(0), outs.pop(0), parts[0], parts[1:6], *parts[6:])
            for k, act in zip((0, 2, 3, 4, 6, 8), steps):
                waves[k].append(act)
        return [(t, act) for t, wave in zip(self.times, waves) for act in wave]


class FinishColumns:
    def __init__(self, two, collect=False, at=(0, 1, 2, 99)):
        self.names = ("mid", "z0") + (GROUP if collect else ())
        self.collect, self.times = collect, at
        b = two.shape[2:]
        self.args, self.specs = (two,), (ANY,)
        self.shapes = (jax.ShapeDtypeStruct((4, b[0] // 2, b[1]) if collect else (2,) + b, BF),)
        self.scratch = (pltpu.VMEM((2,) + b, BF), pltpu.VMEM((2,) + b, BF), pltpu.VMEM((2, 2) + b, BF))
        self.scratch += (DMA((8,)), DMA((8,)), DMA((3,)), DMA((3,)), DMA((3,)), DMA((1,)))

    def steps(self, p, ins, outs, scratch):
        mine, three, relay, send, recv, local, s_send, s_recv, s_local = scratch
        two, result = ins[0], outs[0]
        crosses = [
            Cross(p, two.at[h, 0], three.at[h], three.at[h], relay.at[h], *[s.at[pl.ds(4 * h, 4)] for s in (send, recv)])
            for h in (0, 1)
        ]
        loads = [pltpu.make_async_copy(two.at[h, 1], mine.at[h], local.at[h]) for h in (0, 1)]
        rows = three.shape[1] // 2
        piece = lambda c, z0: three.at[c, pl.ds(pl.multiple_of(z0 * rows, rows), rows)]
        spread = Spread(p, piece, lambda c, z0: result.at[2 * c + z0], s_send, s_recv, s_local.at[0])
        store = lambda: pltpu.make_async_copy(three, result, local.at[2])

        def first():
            for c in crosses + loads:
                c.start()

        def last():
            for h in (0, 1):
                crosses[h].wait()
                loads[h].wait()
                add_to(three.at[h], mine.at[h])
            if self.collect:
                spread.start()
                spread.wait()
                spread.finish()
            else:
                store().start()
                store().wait()
            for c in crosses:
                c.finish()

        acts = [(self.times[0], first)]
        acts += [(self.times[1], c.bring) for c in crosses] + [(self.times[2], c.take) for c in crosses]
        return acts + [(self.times[3], last)]


LANES = 128
HEADS = Q_RANK + 2 * KV_RANK


def head_lanes():
    half = HEAD_SIZE // 2
    column = jnp.arange(HEADS * HEAD_SIZE, dtype=jnp.int32)
    head, inner = column // HEAD_SIZE, column % HEAD_SIZE
    lane = head * LANES + jnp.where(inner < half, inner, inner - half + LANES // 2)
    return (lane[:, None] == jnp.arange(HEADS * LANES, dtype=jnp.int32)[None, :]).astype(BF)


def pad_weights(lanes_ref, qkv_ref, out_ref, qkv_wide, out_wide):
    def qkv_tile(j):
        at = pl.ds(j, TILE)
        qkv_wide[at, :] = dot(qkv_ref[at, :], lanes_ref[...]).astype(BF)

    column_tiles(D, TILE, qkv_tile)
    heads = lanes_ref[: Q_RANK * HEAD_SIZE, : Q_RANK * LANES]

    def out_tile(j):
        cols = pl.ds(j, TILE)
        out_wide[:, cols] = dot(heads, out_ref[:, cols], ((0,), (0,))).astype(BF)

    column_tiles(D, TILE, out_tile)


def masked(scores, first, start_ref):
    count, keys = scores.shape
    query = lax.broadcasted_iota(jnp.int32, scores.shape, 0) + first
    key = lax.broadcasted_iota(jnp.int32, scores.shape, 1)
    start = start_ref[first : first + count, :]
    return jnp.where((key <= query) & (key >= start), scores, masked_score)


def attention_forward_call(residual, gain, w_qkv, w_out, common, beside, collective_id):
    lanes, cosines, sines, starts = common
    rows = residual.shape[0]
    count = 4 * rows
    scale = HEAD_SIZE ** (-0.5)

    def body(p, ins, outs, scratch, advance, staged):
        res_ref, gain_ref, qkv_ref, out_ref, lanes_ref, cos_ref, sin_ref, start_ref = ins
        new_ref, every, heads_ref, att_ref = outs
        qkv_wide, out_wide = scratch[:2]
        own, terms, share, total = exchange_of(p, every, scratch[2:])

        def project(pieces, n):
            places = token_rows(pieces, n, rows)
            both = lambda ref: jnp.concatenate([ref[at, :] for at in places], axis=0)
            cos, sin = both(cos_ref), both(sin_ref)
            x = gather_pieces(every, pieces, n)
            for j in range(0, HEADS, 4):
                wide = dot(x, qkv_wide[:, j * LANES : (j + 4) * LANES])
                for k in range(4):
                    value = wide[:, k * LANES : (k + 1) * LANES]
                    if j + k < Q_RANK + KV_RANK:
                        value = value * cos + pltpu.roll(value, LANES // 2, 1) * sin
                    for m, at in enumerate(places):
                        heads_ref[j + k, at, :] = value[m * n : (m + 1) * n].astype(BF)

        def attend(j, _):
            g = lax.div(j, Q_RANK // KV_RANK)
            for first in range(0, count, rows):
                n = first + rows
                q = heads_ref[j, first:n, :]
                scores = dot(q, heads_ref[Q_RANK + g, :n, :], ((1,), (1,))) * scale
                scores = masked(scores, first, start_ref)
                top = jnp.max(scores, axis=1, keepdims=True)
                shifted = jnp.exp(scores - top)
                amount = jnp.sum(shifted, axis=1, keepdims=True)
                weights = (shifted / amount).astype(BF)
                att_ref[j, first:n, :] = dot(weights, heads_ref[Q_RANK + KV_RANK + g, :n, :]).astype(BF)
            return 0

        def project_out(pieces, n):
            places = token_rows(pieces, n, rows)
            wide = jnp.concatenate(
                [jnp.concatenate([att_ref[j, at, :] for j in range(Q_RANK)], axis=1) for at in places], axis=0
            )

            def tile(j):
                cols = pl.ds(j, DOWN_TILE)
                scatter_pieces(terms, pieces, n, dot(wide, out_wide[:, cols]).astype(BF), cols)

            column_tiles(D, DOWN_TILE, tile)

        row_normalize(res_ref, gain_ref, own)
        share.start()
        advance()
        staged.ready(2, 3, 4)
        pad_weights(lanes_ref, qkv_ref, out_ref, qkv_wide, out_wide)
        staged.ready(5, 6)
        project([(p.rank, 0)], rows)
        share.across(True).wait_recv()
        project([(p.sibling, 0)], rows)
        advance()
        part = rows // CHUNKS
        for k in range(CHUNKS):
            share.pass_on(k)
            share.far(k)
            project([(p.diagonal, k * part), (p.over, k * part)], part)
            advance()
        staged.flush(1, 2)
        for j in range(0, Q_RANK, 2):
            lax.fori_loop(j, j + 2, attend, 0)
            advance()
        for k in range(CHUNKS):
            project_out([(p.diagonal, k * part), (p.over, k * part)], part)
            total.diagonal(k).start()
            total.relay(k)
            advance()
        staged.flush(3)
        project_out([(p.sibling, 0)], rows)
        total.sibling().start()
        project_out([(p.rank, 0)], rows)
        advance()

        def write(at, value):
            new_ref[at, :] = res_ref[at, :] + value

        collect(p, total, write)
        advance.finish()
        share.finish()
        total.finish()

    return beside_call(
        body,
        (residual, gain.reshape(1, D), w_qkv, w_out, lanes, cosines, sines, starts),
        (4, 2, 3, 5, 6),
        [
            jax.ShapeDtypeStruct((rows, D), F32),
            jax.ShapeDtypeStruct((4, rows, D), BF),
            jax.ShapeDtypeStruct((HEADS, count, LANES), BF),
            jax.ShapeDtypeStruct((Q_RANK, count, LANES), BF),
        ],
        (1, 2, 3),
        [pltpu.VMEM((D, HEADS * LANES), BF), pltpu.VMEM((Q_RANK * LANES, D), BF)] + exchange_scratch(rows),
        beside,
        "attention_forward",
        collective_id,
        2 * count * D * (HEADS + Q_RANK) * LANES,
    )


def attention_backward_call(grad, residual, gain, w_qkv, w_out, kept, common, beside, collective_id, dtype=F32):
    lanes, cosines, sines, starts = common
    every, heads, attended = kept
    rows = residual.shape[0]
    count = 4 * rows
    scale = HEAD_SIZE ** (-0.5)

    def body(p, ins, outs, scratch, advance, staged):
        (grad_ref, res_ref, gain_ref, qkv_ref, out_ref, lanes_ref, cos_ref, sin_ref, start_ref) = ins[:9]
        every_ref, heads_ref, att_ref = ins[9:]
        new_ref, gain_out, g_qkv, s_out = outs
        qkv_wide, out_wide, e, d_att, d_k, d_v, d_heads = scratch[:7]
        soft, g_out = scratch[7:9]
        reduce = out_reduce_steps(p, g_out, s_out, *scratch[9:16])
        own, terms, share, total = exchange_of(p, e, scratch[16:])

        def copy_own(k, _):
            at = pl.ds(pl.multiple_of(k * 32, 32), 32)
            own[at, :] = grad_ref[at, :].astype(BF)
            return 0

        lax.fori_loop(0, rows // 32, copy_own, 0)

        def back_out(pieces, n):
            wide = dot(gather_pieces(e, pieces, n), out_wide[...], ((1,), (1,)))
            for m, at in enumerate(token_rows(pieces, n, rows)):
                for j in range(Q_RANK):
                    d_att[j, at, :] = wide[m * n : (m + 1) * n, j * LANES : (j + 1) * LANES].astype(BF)

        def attend(j, _):
            g = lax.div(j, Q_RANK // KV_RANK)
            for first in range(0, count, rows):
                n = first + rows
                q, d_o = heads_ref[j, first:n, :], d_att[j, first:n, :]
                k, v = heads_ref[Q_RANK + g, :n, :], heads_ref[Q_RANK + KV_RANK + g, :n, :]
                rounded = soft[j, :, soft_lanes(first)]
                weights = rounded.astype(F32)
                d_weights = dot(d_o, v, ((1,), (1,)))
                inner = jnp.sum(weights * d_weights, axis=1, keepdims=True)
                d_scores = (weights * (d_weights - inner)).astype(BF)
                d_v[g, :n, :] += dot(rounded, d_o, ((0,), (0,)))
                d_k[g, :n, :] += dot(d_scores, q, ((0,), (0,)))
                d_q = dot(d_scores, k) * scale
                d_heads[j, first:n, :] = turn_back(d_q, cos_ref[first:n, :], sin_ref[first:n, :])
            return 0

        def soft_lanes(first):
            k = first // rows
            at = k * (k + 1) // 2 * rows
            return slice(at, at + first + rows)

        def keep_weights(j, _):
            g = lax.div(j, Q_RANK // KV_RANK)
            for first in range(0, count, rows):
                n = first + rows
                scores = dot(heads_ref[j, first:n, :], heads_ref[Q_RANK + g, :n, :], ((1,), (1,))) * scale
                scores = masked(scores, first, start_ref)
                shifted = jnp.exp(scores - jnp.max(scores, axis=1, keepdims=True))
                amount = jnp.sum(shifted, axis=1, keepdims=True)
                soft[j, :, soft_lanes(first)] = (shifted / amount).astype(BF)
            return 0

        def turn_back(value, cos, sin):
            return (value * cos - pltpu.roll(value, LANES // 2, 1) * sin).astype(BF)

        def keys_back():
            for g in range(KV_RANK):
                for first in range(0, count, rows):
                    at = slice(first, first + rows)
                    d_heads[Q_RANK + g, at, :] = turn_back(d_k[g, at, :] * scale, cos_ref[at, :], sin_ref[at, :])
                    d_heads[Q_RANK + KV_RANK + g, at, :] = d_v[g, at, :].astype(BF)

        def project_back(pieces, n):
            wide = jnp.concatenate(
                [
                    jnp.concatenate([d_heads[j, at, :] for j in range(HEADS)], axis=1)
                    for at in token_rows(pieces, n, rows)
                ],
                axis=0,
            )

            def tile(j):
                cols = pl.ds(j, DOWN_TILE)
                value = dot(wide, qkv_wide[cols, :], ((1,), (1,))).astype(BF)
                scatter_pieces(terms, pieces, n, value, cols)

            column_tiles(D, DOWN_TILE, tile)

        def out_grads():
            e_all = e.reshape(count, D)

            def out_grad(j):
                cols = pl.ds(j, TILE)
                wide = jnp.concatenate(
                    [dot(att_ref[h], e_all[:, cols], ((0,), (0,))) for h in range(Q_RANK)], axis=0
                ).astype(BF)
                value = dot(lanes_ref[: Q_RANK * HEAD_SIZE, : Q_RANK * LANES], wide).astype(BF)
                for h in range(Q_RANK):
                    g_out[h, :, cols] = value[h * HEAD_SIZE : (h + 1) * HEAD_SIZE]

            column_tiles(D, TILE, out_grad)

        def weight_grads():
            x_all = every_ref.reshape(count, D)

            def qkv_grad(j):
                cols = pl.ds(j, TILE)
                wide = jnp.concatenate(
                    [dot(x_all[:, cols], d_heads[h], ((0,), (0,))) for h in range(HEADS)], axis=1
                ).astype(BF)
                g_qkv[cols, :] = dot(wide, lanes_ref[...], ((1,), (1,))).astype(BF)

            column_tiles(D, TILE, qkv_grad)

        share.start()
        advance()
        staged.ready(3, 4, 5)
        pad_weights(lanes_ref, qkv_ref, out_ref, qkv_wide, out_wide)
        staged.ready(10)
        lax.fori_loop(0, Q_RANK, keep_weights, 0)
        d_k[...] = jnp.zeros_like(d_k)
        d_v[...] = jnp.zeros_like(d_v)
        back_out([(p.rank, 0)], rows)
        share.across(True).wait_recv()
        back_out([(p.sibling, 0)], rows)
        advance()
        part = rows // CHUNKS
        for k in range(CHUNKS):
            share.pass_on(k)
            share.far(k)
            back_out([(p.diagonal, k * part), (p.over, k * part)], part)
            advance()
        staged.ready(11)
        out_grads()
        reduce[0]()
        staged.ready(6, 7)
        for j in range(0, Q_RANK, 2):
            lax.fori_loop(j, j + 2, attend, 0)
            advance()
        reduce[1]()
        keys_back()
        for k in range(CHUNKS):
            project_back([(p.diagonal, k * part), (p.over, k * part)], part)
            total.diagonal(k).start()
            total.relay(k)
            advance()
        project_back([(p.sibling, 0)], rows)
        total.sibling().start()
        project_back([(p.rank, 0)], rows)
        advance()
        reduce[2]()
        staged.ready(9)
        weight_grads()
        staged.flush(2)
        reduce[3]()
        advance()
        gain_out[...] = jnp.zeros_like(gain_out)

        def write(at, value):
            res = res_ref[at, :].astype(F32)
            normed = normalize(res)
            gain_out[...] += jnp.sum(value * normed, axis=0, keepdims=True)
            back = norm_back(value * gain_ref[...], normed, res)
            new_ref[at, :] = (grad_ref[at, :] + back).astype(dtype)

        collect(p, total, write)
        advance.finish()
        reduce[4]()
        share.finish()
        total.finish()

    return beside_call(
        body,
        (grad, residual, gain.reshape(1, D), w_qkv, w_out, lanes, cosines, sines, starts, every, heads, attended),
        (5, 3, 4, 10, 11, 6, 7, 9),
        [
            jax.ShapeDtypeStruct((rows, D), dtype),
            jax.ShapeDtypeStruct((1, D), F32),
            jax.ShapeDtypeStruct((D, HEADS * HEAD_SIZE), BF),
            jax.ShapeDtypeStruct((HEAD_SIZE // 2, D), BF),
        ],
        (2,),
        [
            pltpu.VMEM((D, HEADS * LANES), BF),
            pltpu.VMEM((Q_RANK * LANES, D), BF),
            pltpu.VMEM((4, rows, D), BF),
            pltpu.VMEM((Q_RANK, count, LANES), BF),
            pltpu.VMEM((KV_RANK, count, LANES), F32),
            pltpu.VMEM((KV_RANK, count, LANES), F32),
            pltpu.VMEM((HEADS, count, LANES), BF),
            pltpu.VMEM((Q_RANK, rows, 10 * rows), BF),
        ]
        + out_reduce_scratch((HEAD_SIZE, D))
        + exchange_scratch(rows),
        beside,
        "attention_backward",
        collective_id,
        6 * count * D * (HEADS + Q_RANK) * LANES,
        ("c", "z0", "x", "y", "z1"),
        {3: ANY},
    )


def lane_rows():
    half, space = HEAD_SIZE // 2, LANES // 2 - HEAD_SIZE // 2
    index = jnp.arange(half, dtype=jnp.float32)
    inverse = jnp.pad(rope_base ** (-2.0 * index / HEAD_SIZE), (0, space))
    ones = jnp.pad(jnp.ones(half, F32), (0, space))
    row = lambda a, b: jnp.concatenate([a, b])
    return jnp.stack([row(inverse, inverse), row(ones, ones), row(-ones, ones)])


def rank_columns(ref, l, c, x):
    pieces = []
    for start, width in (
        (0, 2 * HEAD_SIZE),
        (QUERY_HEAD_COUNT * HEAD_SIZE, HEAD_SIZE),
        ((QUERY_HEAD_COUNT + KEY_VALUE_HEADS) * HEAD_SIZE, HEAD_SIZE),
    ):
        for y in (0, 1):
            at = start + (4 * y + 2 * x + c) * width
            pieces.append(ref[l][:, at : at + width])
    return jnp.concatenate(pieces, axis=1).astype(BF)


def first_call(tokens, lengths, w_qkv, w_out, w_gateup, w_down, gains, collective_id):
    rows = w_qkv.shape[1]
    count = 4 * tokens.shape[0]
    ranks = lambda w: jax.ShapeDtypeStruct((4, rows, w.shape[2] // 4), BF)
    shard = jax.ShapeDtypeStruct(w_out.shape[1:], BF)
    down_rows = w_down.shape[1] // 2
    half = jax.ShapeDtypeStruct((2, down_rows, D), BF)
    gather = GatherWeights(
        columns=ranks(w_qkv), out=shard, gains=gains, columns_at=times(1, (2, 2), (2, 2), 3, (4, 4), (6, 6)),
        out_at=(-1, 1, 3, 5, 99), gains_at=(1, 2, 3, 4, 5, 99),
    )
    meet = MeetBlocks(half, at=(0, 1, 1))
    spread = SpreadColumns(ranks(w_gateup), ranks(w_qkv), ranks(w_gateup))
    swap = SwapRows(tokens)
    works = (gather, spread, swap, meet)
    unit = w_gateup.shape[2] // 64

    def body(*refs):
        refs = list(refs)
        take = lambda n: [refs.pop(0) for _ in range(n)]
        tokens_ref, lengths_ref, qkv_ref, out_ref, gu_ref, down_ref, gains_ref, lanes_ref = take(8)
        down0, down1, out1, cos_ref, sin_ref, start_ref = take(6)
        outs = [take(len(w.shapes)) for w in works]
        qkv0, qkv1, gu0, gu1, out0 = take(5)
        scratch = [take(len(w.scratch)) for w in works]
        p = Place()
        greet(p, EIGHT + GROUP + ("swap", "mid"))
        clock = Clock(gather.steps(p, [qkv0, out0, gains_ref], outs[0], scratch[0]))

        def pack_heads(l, dst):
            for c in (0, 1):
                for x in (0, 1):
                    dst[2 * c + x] = rank_columns(qkv_ref, l, c, x)

        def pack_units(l, dst):
            for chunk in range(64):
                z0, z1, c, rest = chunk % 2, chunk // 2 % 2, chunk // 4 % 2, chunk // 8
                at = (rest * 2 + z1) * unit
                dst[2 * c + z0, :, at : at + unit] = gu_ref[l, :, chunk * unit : (chunk + 1) * unit].astype(BF)

        pack_heads(0, qkv0)
        out0[...] = out_ref[0].astype(BF)
        clock()
        clock()
        for h in (0, 1):
            part = slice(h * down_rows, (h + 1) * down_rows)
            down0[h] = down_ref[0, part, :].astype(BF)
            down1[h] = down_ref[1, part, :].astype(BF)
        out1[...] = out_ref[1].astype(BF)
        pack_units(0, gu0)
        pack_heads(1, qkv1)
        pack_units(1, gu1)
        clock()
        later = Clock(
            spread.steps(p, [gu0, qkv1, gu1], outs[1], scratch[1])
            + meet.steps(p, [down0], outs[3], scratch[3])
            + swap.steps(p, [tokens_ref], outs[2], scratch[2])
        )
        later()

        def begin(places):
            start, end = jnp.zeros_like(places), 0
            for k in range(lengths.shape[1]):
                length = lengths_ref[0, k]
                end = end + length
                start = start + jnp.where(places >= end, length, 0)
            return start

        def table(k, _):
            at = pl.ds(pl.multiple_of(k * TILE, TILE), TILE)
            places = lax.broadcasted_iota(jnp.int32, (TILE, LANES), 0) + k * TILE
            angles = (places - begin(places)).astype(F32) * lanes_ref[0:1, :]
            cos_ref[at, :] = jnp.cos(angles) * lanes_ref[1:2, :]
            sin_ref[at, :] = jnp.sin(angles) * lanes_ref[2:3, :]
            start_ref[at, :] = begin(lax.broadcasted_iota(jnp.int32, (TILE, 1), 0) + k * TILE)
            return 0

        lax.fori_loop(0, count // TILE, table, 0)
        clock.finish()
        later.finish()

    vmem = lambda s: pltpu.VMEM(s.shape, BF)
    made = [half, half, shard, *([jax.ShapeDtypeStruct((count, LANES), F32)] * 2), jax.ShapeDtypeStruct((count, 1), jnp.int32)]
    out = pl.pallas_call(
        body,
        out_shape=made + [s for w in works for s in w.shapes],
        in_specs=[VM, pl.BlockSpec(memory_space=pltpu.SMEM)] + [VM] * 6,
        out_specs=[VM] * len(made) + [ANY for w in works for _ in w.shapes],
        scratch_shapes=[vmem(ranks(w_qkv)), vmem(ranks(w_qkv)), vmem(ranks(w_gateup)), vmem(ranks(w_gateup)), vmem(shard)]
        + [s for w in works for s in w.scratch],
        compiler_params=wide_params(collective_id),
        name="first_weights",
    )(tokens, lengths, w_qkv, w_out, w_gateup, w_down, gains, lane_rows())
    return out


def stepped(weight, gradient, first, second, rate, shrink):
    return adam_step(weight, gradient.astype(F32), first, second, rate, shrink)


def update_gateup(weight, first, second, parts, rate, shrink):
    rows, columns = weight.shape[1:]
    blocks = 8
    wide, thin = columns // blocks, columns // 4 // blocks
    unit = thin // 2

    def body(w_ref, m_ref, v_ref, *refs):
        grads, (w_out, m_out, v_out) = refs[:-3], refs[-3:]

        def run(g_ref):
            for c in (0, 1):
                for z1 in (0, 1):
                    for z0 in (0, 1):
                        at = pl.ds(((c * 2 + z1) * 2 + z0) * unit, unit)
                        grad = g_ref[2 * c + z0, :, pl.ds(z1 * unit, unit)]
                        new = stepped(w_ref[0, :, at], grad, m_ref[0, :, at], v_ref[0, :, at], rate, shrink)
                        w_out[0, :, at], m_out[0, :, at], v_out[0, :, at] = new

        for l, g_ref in enumerate(grads):
            pl.when(pl.program_id(0) == l)(functools.partial(run, g_ref))

    big = pl.BlockSpec((1, rows, wide), lambda l, j: (l, 0, j))
    small = [
        pl.BlockSpec((4, rows, thin), lambda l, j, k=k: (0, 0, jnp.where(l == k, j, 0 if k else blocks - 1)))
        for k in range(LAYERS)
    ]
    return pl.pallas_call(
        body,
        grid=(LAYERS, blocks),
        in_specs=[big] * 3 + small,
        out_specs=[big] * 3,
        out_shape=[jax.ShapeDtypeStruct(weight.shape, F32)] * 3,
        compiler_params=pltpu.CompilerParams(vmem_limit_bytes=32 * 2**20),
        name="update_gateup",
    )(weight, first, second, *parts)


def update_rows(weight, first, second, parts, rate, shrink):
    rows, columns = weight.shape[1:]
    blocks = 2
    wide = columns // blocks

    def body(w_ref, m_ref, v_ref, *refs):
        grads, (w_out, m_out, v_out) = refs[:-3], refs[-3:]

        def run(g_ref):
            w_out[0], m_out[0], v_out[0] = stepped(w_ref[0], g_ref[...], m_ref[0], v_ref[0], rate, shrink)

        for l, g_ref in enumerate(grads):
            pl.when(pl.program_id(0) == l)(functools.partial(run, g_ref))

    big = pl.BlockSpec((1, rows, wide), lambda l, j: (l, 0, j))
    small = [
        pl.BlockSpec((rows, wide), lambda l, j, k=k: (0, jnp.where(l == k, j, 0 if k else blocks - 1)))
        for k in range(LAYERS)
    ]
    return pl.pallas_call(
        body,
        grid=(LAYERS, blocks),
        in_specs=[big] * 3 + small,
        out_specs=[big] * 3,
        out_shape=[jax.ShapeDtypeStruct(weight.shape, F32)] * 3,
        compiler_params=pltpu.CompilerParams(vmem_limit_bytes=32 * 2**20),
        name="update_rows",
    )(weight, first, second, *parts)


def update_qkv(weight, first, second, parts, rate, shrink):
    rows, columns = weight.shape[1:]
    q_wide, kv_wide = QUERY_HEAD_COUNT * HEAD_SIZE, KEY_VALUE_HEADS * HEAD_SIZE

    def body(w_ref, m_ref, v_ref, *refs):
        grads, (w_out, m_out, v_out) = refs[:-3], refs[-3:]

        def run(g_ref):
            pieces = []
            for start, width in ((0, 2 * HEAD_SIZE), (4 * HEAD_SIZE, HEAD_SIZE), (6 * HEAD_SIZE, HEAD_SIZE)):
                for y in (0, 1):
                    for x in (0, 1):
                        for c in (0, 1):
                            at = start + y * width
                            pieces.append(g_ref[2 * c + x].astype(F32)[:, at : at + width])
            grad = jnp.concatenate(pieces, axis=1)
            w_out[0], m_out[0], v_out[0] = stepped(w_ref[0], grad, m_ref[0], v_ref[0], rate, shrink)

        for l, g_ref in enumerate(grads):
            pl.when(pl.program_id(0) == l)(functools.partial(run, g_ref))

    big = pl.BlockSpec((1, rows, columns), lambda l: (l, 0, 0))
    small = [pl.BlockSpec((4, rows, columns // 4), lambda l: (0, 0, 0))] * LAYERS
    return pl.pallas_call(
        body,
        grid=(LAYERS,),
        in_specs=[big] * 3 + small,
        out_specs=[big] * 3,
        out_shape=[jax.ShapeDtypeStruct(weight.shape, F32)] * 3,
        compiler_params=pltpu.CompilerParams(vmem_limit_bytes=32 * 2**20),
        name="update_qkv",
    )(weight, first, second, *parts)


def links_call(beside, name, collective_id):
    return beside_call(
        lambda p, ins, outs, scratch, advance, staged: advance.finish(),
        (), (), [], (), [], beside, name, collective_id, 0, peers=(),
    )[1]


def fast_shards(
    tokens, cotangent, lengths, w_qkv, w_out, w_gateup, w_down, norm_gains, *moments
):
    axes = ("fsdp", "seq")
    pairs = swap_pairs(lax.axis_size("fsdp"), lax.axis_size("seq"))
    lengths = lax.ppermute(lengths, axes, pairs)
    rows, owned = w_qkv.shape[1], norm_gains.shape[2]
    own_gains = jnp.pad(
        norm_gains.reshape(2 * LAYERS, owned).astype(BF), ((0, 16 - 2 * LAYERS), (0, lane_width - owned))
    )
    own_down0, own_down1, own_out1, *places, qkv0, out0, got_gains, own_gu0, own_qkv1, own_gu1, start, met_down0 = (
        first_call(tokens, lengths, w_qkv, w_out, w_gateup, w_down, own_gains, 0)
    )
    common = (head_lanes(), *places)
    all_gains = got_gains[:, : 2 * LAYERS, :owned].transpose(1, 0, 2).reshape(LAYERS, 2, D).astype(F32)
    matrix = lambda g: g.reshape(D, -1)
    stack = lambda g: g.reshape(-1, D)
    alone = times(0, (1, 1), (3, 4), 3, (4, 5), (7, 8))
    ahead = times(0, None, None, 3, None, (4, 4))
    (middle0, *first0), (gu0, down0, met_qkv1, met_down1, met_out1) = attention_forward_call(
        start, all_gains[0, 0], matrix(qkv0), stack(out0), common,
        Both(
            GatherWeights(columns=own_gu0, columns_at=alone),
            GatherWeights(down=own_down0, met=(met_down0,), down_at=times(0, None, None, 3, None, (5, 5))),
            MeetBlocks(own_qkv1, own_down1, at=(4, 7, 8)),
            MeetOut(own_out1, at=(4, 8)),
        ), 1,
    )
    (later0, *second0), (out1, qkv1, down1, met_gu1) = feed_forward_call(
        middle0, all_gains[0, 1], matrix(gu0), stack(down0),
        Both(
            GatherOut(met_out1),
            GatherWeights(columns=own_qkv1, met=(met_qkv1,), columns_at=ahead),
            GatherWeights(down=own_down1, met=(met_down1,), down_at=ahead),
            MeetBlocks(own_gu1, at=(0, 3, 4)),
        ), 2,
    )
    (middle1, *first1), (gu1, cotangent) = attention_forward_call(
        later0, all_gains[1, 0], matrix(qkv1), stack(out1), common,
        Both(
            GatherWeights(columns=own_gu1, met=(met_gu1,), columns_at=times(0, None, None, 3, None, (6, 7))),
            SwapRows(cotangent, 3),
        ), 3,
    )
    (later1, *second1), _ = feed_forward_call(
        middle1, all_gains[1, 1], matrix(gu1), stack(down1), Nothing(), 4, BF
    )
    wide = lambda g: g.reshape(16, 2 * rows, -1)
    (grad, gain11, g_gu1, two_down1), _ = feed_backward_call(
        cotangent, middle1, all_gains[1, 1], matrix(gu1), stack(down1), second1, Nothing(), 5
    )
    (grad, gain10, g_qkv1, s_out1), (two_gu1, s_down1, layer_output) = attention_backward_call(
        grad, later0, all_gains[1, 0], matrix(qkv1), stack(out1), first1, common,
        Both(
            ReduceWeights(columns=wide(g_gu1), open=True, at=(0, 4, 4, 5, 5, 9, 10, 11, 99)),
            FinishColumns(two_down1, at=(1, 3, 4, 6)),
            SwapRows(later1, 4),
        ), 6,
    )
    (grad, gain01, g_gu0, two_down0), (s_qkv1,) = feed_backward_call(
        grad, middle0, all_gains[0, 1], matrix(gu0), stack(down0), second0,
        ReduceWeights(columns=wide(g_qkv1), at=(0, 2, 2, 3, 3, 4, 4, 7, 99)), 7,
    )
    (grad, gain00, g_qkv0, s_out0), (two_gu0, s_down0, s_gu1) = attention_backward_call(
        grad, start, all_gains[0, 0], matrix(qkv0), stack(out0), first0, common,
        Both(
            ReduceWeights(columns=wide(g_gu0), open=True, at=(0, 4, 4, 5, 5, 9, 10, 11, 99)),
            FinishColumns(two_down0, at=(1, 3, 4, 6)),
            FinishColumns(two_gu1, at=(2, 4, 5, 9)),
        ), 8, BF,
    )
    terms = jnp.concatenate([gain00, gain01, gain10, gain11]).reshape(2 * LAYERS, -1, owned).transpose(1, 0, 2)
    terms = jnp.pad(terms, ((0, 0), (0, 8 - 2 * LAYERS), (0, lane_width - owned)))
    split = lambda g: g.reshape(2, 2, rows, -1)
    s_gu0, s_qkv0, s_gains, s_gu1, s_qkv1, input_grad = links_call(
        Both(
            FinishColumns(two_gu0, collect=True, at=(0, 1, 1, 4)),
            ReduceWeights(columns=wide(g_qkv0), gains=terms, collect=True, at=(0, 2, 2, 3, 3, 3, 3, 5, 7)),
            CollectColumns(split(s_gu1), split(s_qkv1), at=1),
            SwapRows(grad, 2),
        ),
        "last_gradients",
        9,
    )
    flat = lambda g: g.reshape(-1, D)
    update = {
        "qkv": (s_qkv0, s_qkv1),
        "out": (s_out0, s_out1),
        "gateup": (s_gu0, s_gu1),
        "down": (flat(s_down0), flat(s_down1)),
        "gains": s_gains[: 2 * LAYERS, :owned].reshape(LAYERS, 2, owned),
    }
    return (layer_output, input_grad.astype(F32)) + update_all(
        (w_qkv, w_out, w_gateup, w_down, norm_gains), moments, update
    )


def update_all(stacked, moments, update):
    step_rates = (D ** (-0.5), 4.0 * D ** (-0.5), D ** (-0.5), FF ** (-0.5), 0.5)
    shrinks = (decay_rate, decay_rate, decay_rate, decay_rate, 0.0)
    ways = (update_qkv, update_rows, update_gateup, update_rows, adam_step)
    results = []
    for kind, (name, way) in enumerate(zip(update, ways)):
        weight, first, second = stacked[kind], moments[kind], moments[5 + kind]
        if kind == 4:
            results.append(way(weight, update[name], first, second, step_rates[kind], shrinks[kind]))
        else:
            results.append(way(weight, first, second, update[name], step_rates[kind], shrinks[kind]))
    return tuple(results[kind][part] for part in range(3) for kind in range(5))


def solution(mesh):
    in_specs = (
        P(("fsdp", "seq"), None),
        P(("fsdp", "seq"), None),
        P("fsdp", None),
        P(None, ("fsdp", "seq"), None),
        P(None, ("fsdp", "seq"), None),
        P(None, ("fsdp", "seq"), None),
        P(None, ("fsdp", "seq"), None),
        P(None, None, ("fsdp", "seq")),
        P(None, ("fsdp", "seq"), None),
        P(None, ("fsdp", "seq"), None),
        P(None, ("fsdp", "seq"), None),
        P(None, ("fsdp", "seq"), None),
        P(None, None, ("fsdp", "seq")),
        P(None, ("fsdp", "seq"), None),
        P(None, ("fsdp", "seq"), None),
        P(None, ("fsdp", "seq"), None),
        P(None, ("fsdp", "seq"), None),
        P(None, None, ("fsdp", "seq")),
    )
    out_specs = (
        P(("fsdp", "seq"), None),
        P(("fsdp", "seq"), None),
        P(None, ("fsdp", "seq"), None),
        P(None, ("fsdp", "seq"), None),
        P(None, ("fsdp", "seq"), None),
        P(None, ("fsdp", "seq"), None),
        P(None, None, ("fsdp", "seq")),
        P(None, ("fsdp", "seq"), None),
        P(None, ("fsdp", "seq"), None),
        P(None, ("fsdp", "seq"), None),
        P(None, ("fsdp", "seq"), None),
        P(None, None, ("fsdp", "seq")),
        P(None, ("fsdp", "seq"), None),
        P(None, ("fsdp", "seq"), None),
        P(None, ("fsdp", "seq"), None),
        P(None, ("fsdp", "seq"), None),
        P(None, None, ("fsdp", "seq")),
    )
    whole_tiles = (D // mesh.size) % 16 == 0 and mesh.shape["seq"] == 4 and mesh.size == 32
    body = fast_shards if whole_tiles else shards
    return jax.shard_map(body, mesh=mesh, in_specs=in_specs, out_specs=out_specs, check_vma=False)
```

```python
import functools

import jax
import jax.numpy as jnp
from jax import lax
from jax.experimental import pallas as pl
from jax.experimental.pallas import tpu as pltpu
from jax.sharding import PartitionSpec as P

D = 1536
QUERY_HEAD_COUNT = 16
KEY_VALUE_HEADS = 8
HEAD_SIZE = 96
FF = 4096
LAYERS = 2
STEP = 6


eps_norm = 1e-05
rope_base = 100000.0
beta_one = 0.9
beta_two = 0.95
adam_eps = 1e-08
decay_rate = 0.1
masked_score = -1e30
lane_width = 128


def layout(length_row, places):
    seq_ends = jnp.cumsum(length_row, dtype=jnp.int32)
    passed = (places[:, None] >= seq_ends[None, :]).astype(jnp.int32)
    segment = jnp.sum(passed, axis=1, dtype=jnp.int32)
    begins = jnp.sum(passed * length_row[None, :], axis=1, dtype=jnp.int32)
    return (segment, places - begins)


def tables(positions):
    freq_index = jnp.arange(HEAD_SIZE // 2, dtype=jnp.float32)
    inverse = rope_base ** (-2.0 * freq_index / HEAD_SIZE)
    angles = positions.astype(jnp.float32)[:, None] * inverse[None, :]
    angles = jnp.concatenate([angles, angles], axis=-1)
    return (jnp.cos(angles)[:, None, :], jnp.sin(angles)[:, None, :])


def apply_rotary(values, rotary_cosines, rotary_sines):
    half_width = values.shape[-1] // 2
    turned = jnp.concatenate([-values[..., half_width:], values[..., :half_width]], axis=-1)
    return values * rotary_cosines + turned * rotary_sines


def invert_rotary(values, rotary_cosines, rotary_sines):
    half_width = values.shape[-1] // 2
    scaled_sine = values * rotary_sines
    turned = jnp.concatenate(
        [scaled_sine[..., half_width:], -scaled_sine[..., :half_width]], axis=-1
    )
    return values * rotary_cosines + turned


def normalize(residual):
    return residual * lax.rsqrt(jnp.mean(residual * residual, axis=-1, keepdims=True) + eps_norm)


def norm_back(grad_normed, normed, residual):
    inverse = lax.rsqrt(jnp.mean(residual * residual, axis=-1, keepdims=True) + eps_norm)
    return inverse * (grad_normed - normed * jnp.mean(grad_normed * normed, axis=-1, keepdims=True))


def product(lhs_matrix, rhs_matrix):
    return jnp.dot(lhs_matrix, rhs_matrix, preferred_element_type=jnp.float32)


def attention_scores(query_head_rows, key_head_rows, allowed):
    scores = jnp.einsum(
        "qgrd,kgd->grqk", query_head_rows, key_head_rows, preferred_element_type=jnp.float32
    ) * HEAD_SIZE ** (-0.5)
    return jnp.where(allowed[None, None], scores, masked_score)


def wire_pieces(stacked, layer_index):
    return tuple((shard_piece[layer_index].astype(jnp.bfloat16) for shard_piece in stacked))


def fetch_forward(stacked, layer_index):
    qkv_piece, out_piece, gateup_piece, down_piece, gain_piece = wire_pieces(stacked, layer_index)
    return (
        lax.all_gather(qkv_piece, ("fsdp", "seq"), axis=0, tiled=True),
        lax.all_gather(out_piece, ("fsdp", "seq"), axis=0, tiled=True),
        lax.all_gather(gateup_piece, ("fsdp", "seq"), axis=0, tiled=True),
        lax.all_gather(down_piece, ("fsdp", "seq"), axis=0, tiled=True),
        lax.all_gather(gain_piece, ("fsdp", "seq"), axis=1, tiled=True),
    )


def fetch_backward(stacked, layer_index):
    qkv_piece, out_piece, gateup_piece, down_piece, gain_piece = wire_pieces(stacked, layer_index)
    return (
        lax.all_gather(qkv_piece, ("fsdp", "seq"), axis=0, tiled=True),
        lax.all_gather(out_piece, ("fsdp", "seq"), axis=0, tiled=True),
        lax.all_gather(gateup_piece, ("fsdp", "seq"), axis=0, tiled=True),
        lax.all_gather(down_piece, ("fsdp", "seq"), axis=0, tiled=True),
        lax.all_gather(gain_piece, ("fsdp", "seq"), axis=1, tiled=True),
    )


def flat_lanes(matrix):
    return matrix.reshape(-1, lane_width)


def reduce_grads(grad_terms):
    grad_qkv, grad_out_proj, grad_gateup, grad_down, grad_gains = grad_terms
    widths = (grad_qkv.shape[1], grad_out_proj.shape[1], grad_gateup.shape[1], grad_down.shape[1])
    flat_qkv = flat_lanes(grad_qkv)
    flat_out = flat_lanes(grad_out_proj)
    flat_gateup = flat_lanes(grad_gateup)
    flat_down = flat_lanes(grad_down)
    summed = (
        lax.psum_scatter(flat_qkv, ("fsdp", "seq"), scatter_dimension=0, tiled=True),
        lax.psum_scatter(flat_out, ("fsdp", "seq"), scatter_dimension=0, tiled=True),
        lax.psum_scatter(flat_gateup, ("fsdp", "seq"), scatter_dimension=0, tiled=True),
        lax.psum_scatter(flat_down, ("fsdp", "seq"), scatter_dimension=0, tiled=True),
        lax.psum_scatter(grad_gains, ("fsdp", "seq"), scatter_dimension=1, tiled=True),
    )
    owned = tuple((summed[kind_index].reshape(-1, widths[kind_index]) for kind_index in range(4)))
    return owned + (summed[4],)


def layer_forward(residual, gathered, allowed, rotary_cosines, rotary_sines):
    w_qkv, w_out, w_gateup, w_down, gain_pair = gathered
    count_of_rows = residual.shape[0]
    heads_per_group = QUERY_HEAD_COUNT // KEY_VALUE_HEADS
    gain_float = gain_pair.astype(jnp.float32)
    normed_one = normalize(residual)
    input_one = (normed_one * gain_float[0]).astype(jnp.bfloat16)
    query_key_value_rows = product(input_one, w_qkv)
    query_head_rows = apply_rotary(
        query_key_value_rows[:, : QUERY_HEAD_COUNT * HEAD_SIZE].reshape(
            count_of_rows, QUERY_HEAD_COUNT, HEAD_SIZE
        ),
        rotary_cosines,
        rotary_sines,
    ).astype(jnp.bfloat16)
    key_row_block = apply_rotary(
        query_key_value_rows[
            :, QUERY_HEAD_COUNT * HEAD_SIZE : (QUERY_HEAD_COUNT + KEY_VALUE_HEADS) * HEAD_SIZE
        ].reshape(count_of_rows, KEY_VALUE_HEADS, HEAD_SIZE),
        rotary_cosines,
        rotary_sines,
    ).astype(jnp.bfloat16)
    value_row_block = query_key_value_rows[
        :, (QUERY_HEAD_COUNT + KEY_VALUE_HEADS) * HEAD_SIZE :
    ].astype(jnp.bfloat16)
    every_key, every_value = (
        lax.all_gather(
            key_row_block.reshape(count_of_rows, KEY_VALUE_HEADS * HEAD_SIZE),
            "seq",
            axis=0,
            tiled=True,
        ),
        lax.all_gather(value_row_block, "seq", axis=0, tiled=True),
    )
    key_head_rows = every_key.reshape(-1, KEY_VALUE_HEADS, HEAD_SIZE)
    value_head_rows = every_value.reshape(-1, KEY_VALUE_HEADS, HEAD_SIZE)
    query_head_rows = query_head_rows.reshape(
        count_of_rows, KEY_VALUE_HEADS, heads_per_group, HEAD_SIZE
    )
    scores = attention_scores(query_head_rows, key_head_rows, allowed)
    row_max = jnp.max(scores, axis=-1, keepdims=True)
    shifted = jnp.exp(scores - row_max)
    row_sum = jnp.sum(shifted, axis=-1, keepdims=True)
    log_total = row_max + jnp.log(row_sum)
    attn_weights = (shifted / row_sum).astype(jnp.bfloat16)
    attended = jnp.einsum(
        "grqk,kgd->qgrd", attn_weights, value_head_rows, preferred_element_type=jnp.float32
    )
    attended = attended.reshape(count_of_rows, QUERY_HEAD_COUNT * HEAD_SIZE).astype(jnp.bfloat16)
    middle = residual + product(attended, w_out)
    normed_two = normalize(middle)
    input_two = (normed_two * gain_float[1]).astype(jnp.bfloat16)
    gate_up = product(input_two, w_gateup)
    gate_pre = gate_up[:, :FF]
    up_proj = gate_up[:, FF:]
    hidden = (jax.nn.silu(gate_pre) * up_proj).astype(jnp.bfloat16)
    layer_out = middle + product(hidden, w_down)
    saved_layer = (
        residual,
        normed_one,
        input_one,
        query_head_rows,
        key_head_rows,
        value_head_rows,
        log_total,
        attended,
        middle,
        normed_two,
        input_two,
        gate_pre,
        up_proj,
        hidden,
    )
    return (saved_layer, layer_out)


def layer_backward(grad_out, saved_layer, gathered, allowed, rotary_cosines, rotary_sines):
    w_qkv, w_out, w_gateup, w_down, gain_pair = gathered
    (
        residual,
        normed_one,
        input_one,
        query_head_rows,
        key_head_rows,
        value_head_rows,
        log_total,
        attended,
        middle,
        normed_two,
        input_two,
        gate_pre,
        up_proj,
        hidden,
    ) = saved_layer
    count_of_rows = grad_out.shape[0]
    heads_per_group = QUERY_HEAD_COUNT // KEY_VALUE_HEADS
    gain_float = gain_pair.astype(jnp.float32)
    grad_branch = grad_out.astype(jnp.bfloat16)
    grad_down = jnp.einsum("tf,td->fd", hidden, grad_branch, preferred_element_type=jnp.float32)
    grad_hidden = jnp.einsum("td,fd->tf", grad_branch, w_down, preferred_element_type=jnp.float32)
    sigmoid_gate = jax.nn.sigmoid(gate_pre)
    grad_gate = grad_hidden * up_proj * sigmoid_gate * (1.0 + gate_pre * (1.0 - sigmoid_gate))
    grad_up = grad_hidden * gate_pre * sigmoid_gate
    grad_pair = jnp.concatenate([grad_gate, grad_up], axis=1).astype(jnp.bfloat16)
    grad_gateup = jnp.einsum("td,tf->df", input_two, grad_pair, preferred_element_type=jnp.float32)
    grad_input_two = jnp.einsum(
        "tf,df->td", grad_pair, w_gateup, preferred_element_type=jnp.float32
    )
    grad_gain_two = jnp.sum(grad_input_two * normed_two, axis=0)
    grad_middle = grad_out + norm_back(grad_input_two * gain_float[1], normed_two, middle)
    grad_branch_two = grad_middle.astype(jnp.bfloat16)
    grad_out_proj = jnp.einsum(
        "te,td->ed", attended, grad_branch_two, preferred_element_type=jnp.float32
    )
    attended_gradient = jnp.einsum(
        "td,ed->te", grad_branch_two, w_out, preferred_element_type=jnp.float32
    )
    attended_gradient = attended_gradient.astype(jnp.bfloat16).reshape(
        count_of_rows, KEY_VALUE_HEADS, heads_per_group, HEAD_SIZE
    )
    scores = attention_scores(query_head_rows, key_head_rows, allowed)
    attn_float = jnp.exp(scores - log_total)
    value_gradient = jnp.einsum(
        "grqk,qgrd->kgd",
        attn_float.astype(jnp.bfloat16),
        attended_gradient,
        preferred_element_type=jnp.float32,
    )
    grad_weights = jnp.einsum(
        "qgrd,kgd->grqk", attended_gradient, value_head_rows, preferred_element_type=jnp.float32
    )
    inner_sum = jnp.sum(attn_float * grad_weights, axis=-1, keepdims=True)
    grad_scores = (attn_float * (grad_weights - inner_sum)).astype(jnp.bfloat16)
    grad_query = jnp.einsum(
        "grqk,kgd->qgrd", grad_scores, key_head_rows, preferred_element_type=jnp.float32
    ) * HEAD_SIZE ** (-0.5)
    gradient_keys = jnp.einsum(
        "grqk,qgrd->kgd", grad_scores, query_head_rows, preferred_element_type=jnp.float32
    ) * HEAD_SIZE ** (-0.5)
    shared_keys, value_share = (
        lax.psum_scatter(
            gradient_keys.reshape(-1, KEY_VALUE_HEADS * HEAD_SIZE).astype(jnp.bfloat16),
            "seq",
            scatter_dimension=0,
            tiled=True,
        ).astype(jnp.float32),
        lax.psum_scatter(
            value_gradient.reshape(-1, KEY_VALUE_HEADS * HEAD_SIZE).astype(jnp.bfloat16),
            "seq",
            scatter_dimension=0,
            tiled=True,
        ).astype(jnp.float32),
    )
    grad_q = invert_rotary(
        grad_query.reshape(count_of_rows, QUERY_HEAD_COUNT, HEAD_SIZE), rotary_cosines, rotary_sines
    ).reshape(count_of_rows, QUERY_HEAD_COUNT * HEAD_SIZE)
    key_gradient = invert_rotary(
        shared_keys.reshape(count_of_rows, KEY_VALUE_HEADS, HEAD_SIZE), rotary_cosines, rotary_sines
    ).reshape(count_of_rows, KEY_VALUE_HEADS * HEAD_SIZE)
    grad_rows = jnp.concatenate([grad_q, key_gradient, value_share], axis=1).astype(jnp.bfloat16)
    grad_qkv = jnp.einsum("td,tf->df", input_one, grad_rows, preferred_element_type=jnp.float32)
    grad_input_one = jnp.einsum("tf,df->td", grad_rows, w_qkv, preferred_element_type=jnp.float32)
    grad_gain_one = jnp.sum(grad_input_one * normed_one, axis=0)
    grad_in = grad_middle + norm_back(grad_input_one * gain_float[0], normed_one, residual)
    return (
        grad_in,
        (
            grad_qkv,
            grad_out_proj,
            grad_gateup,
            grad_down,
            jnp.stack([grad_gain_one, grad_gain_two]),
        ),
    )


def adam_step(weight, gradient, first_moment, second_moment, step_rate, shrink):
    first_moment = beta_one * first_moment + (1.0 - beta_one) * gradient
    second_moment = beta_two * second_moment + (1.0 - beta_two) * gradient * gradient
    first_hat = first_moment / (1.0 - beta_one**STEP)
    second_hat = second_moment / (1.0 - beta_two**STEP)
    weight = weight - step_rate * (first_hat / (jnp.sqrt(second_hat) + adam_eps) + shrink * weight)
    return (weight, first_moment, second_moment)


def shards(
    tokens,
    cotangent,
    lengths,
    w_qkv,
    w_out,
    w_gateup,
    w_down,
    norm_gains,
    first_qkv,
    first_out,
    first_gateup,
    first_down,
    first_gains,
    second_qkv,
    second_out,
    second_gateup,
    second_down,
    second_gains,
):
    count_of_rows = tokens.shape[0]
    group_rows = count_of_rows * lax.axis_size("seq")
    place_rows = lax.axis_index("seq") * count_of_rows + jnp.arange(count_of_rows, dtype=jnp.int32)
    key_places = jnp.arange(group_rows, dtype=jnp.int32)
    seg_rows, positions = layout(lengths[0], place_rows)
    seg_keys = layout(lengths[0], key_places)[0]
    allowed = (seg_rows[:, None] == seg_keys[None, :]) & (
        key_places[None, :] <= place_rows[:, None]
    )
    rotary_cosines, rotary_sines = tables(positions)
    stacked = (w_qkv, w_out, w_gateup, w_down, norm_gains)
    residual = tokens.astype(jnp.float32)
    saved_all = []
    for layer_index in range(LAYERS):
        gathered = fetch_forward(stacked, layer_index)
        saved_layer, residual = layer_forward(
            residual, gathered, allowed, rotary_cosines, rotary_sines
        )
        saved_all.append(saved_layer)
    grad_state = cotangent.astype(jnp.float32)
    updates = [None] * LAYERS
    for layer_index in reversed(range(LAYERS)):
        gathered = fetch_backward(stacked, layer_index)
        grad_state, grad_terms = layer_backward(
            grad_state, saved_all[layer_index], gathered, allowed, rotary_cosines, rotary_sines
        )
        updates[layer_index] = reduce_grads(grad_terms)
    step_rates = (D ** (-0.5), 4.0 * D ** (-0.5), D ** (-0.5), FF ** (-0.5), 0.5)
    shrinks = (decay_rate, decay_rate, decay_rate, decay_rate, 0.0)
    firsts = (first_qkv, first_out, first_gateup, first_down, first_gains)
    seconds = (second_qkv, second_out, second_gateup, second_down, second_gains)
    new_weights = []
    new_firsts = []
    new_seconds = []
    for kind_index in range(5):
        grads_kind = jnp.stack([updates[layer_index][kind_index] for layer_index in range(LAYERS)])
        weight, first_moment, second_moment = adam_step(
            stacked[kind_index],
            grads_kind,
            firsts[kind_index],
            seconds[kind_index],
            step_rates[kind_index],
            shrinks[kind_index],
        )
        new_weights.append(weight)
        new_firsts.append(first_moment)
        new_seconds.append(second_moment)
    outputs = [residual.astype(jnp.bfloat16), grad_state] + new_weights + new_firsts + new_seconds
    return tuple(outputs)


MESH = pl.DeviceIdType.MESH
BF = jnp.bfloat16
F32 = jnp.float32
KV_RANK = KEY_VALUE_HEADS // 4
Q_RANK = QUERY_HEAD_COUNT // 4
ANY = pl.BlockSpec(memory_space=pl.ANY)
VM = pl.BlockSpec(memory_space=pltpu.VMEM)
DMA = pltpu.SemaphoreType.DMA


class Place:
    def __init__(self):
        f, z = lax.axis_index("fsdp"), lax.axis_index("seq")
        self.y, self.x, self.c = lax.div(f, 4), lax.rem(lax.div(f, 2), 2), lax.rem(f, 2)
        self.z1, self.z0 = lax.div(z, 2), lax.rem(z, 2)
        self.rank = 2 * self.c + self.z0
        self.inner = self.z1 != self.z0
        self.sibling, self.over = 2 * (1 - self.c) + self.z0, 2 * self.c + 1 - self.z0
        self.diagonal = 2 * (1 - self.c) + 1 - self.z0
        self.peer = {
            "y": (f + 4 - 8 * self.y, z),
            "x": (f + 2 - 4 * self.x, z),
            "c": (f + 1 - 2 * self.c, z),
            "z1": (f, z + 2 - 4 * self.z1),
            "z0": (f, z + 1 - 2 * self.z0),
            "cz": (f + 1 - 2 * self.c, z + 1 - 2 * self.z0),
            "swap": (f - self.c + self.z1, 2 * self.c + self.z0),
            "mid": (f, 3 - z),
        }


def greet(place, names):
    barrier = pltpu.get_barrier_semaphore()
    partial = {"swap": place.c != place.z1, "mid": place.inner}
    amount = len([n for n in names if n not in partial])
    for name in names:
        if name not in partial:
            pl.semaphore_signal(barrier, inc=1, device_id=place.peer[name], device_id_type=MESH)
    for name, holds in partial.items():
        if name in names:
            amount = amount + holds.astype(jnp.int32)

            @pl.when(holds)
            def _(name=name):
                pl.semaphore_signal(barrier, inc=1, device_id=place.peer[name], device_id_type=MESH)

    pl.semaphore_wait(barrier, amount)


def remote(src, dst, send_sem, recv_sem, device):
    return pltpu.make_async_remote_copy(
        src_ref=src, dst_ref=dst, send_sem=send_sem, recv_sem=recv_sem, device_id=device, device_id_type=MESH
    )


def columns_index(y, x, z1, h):
    return ((y * 2 + x) * 2 + h) * 2 + z1


def rows_index(y, x, z1, h):
    return ((y * 2 + x) * 2 + z1) * 2 + h


class Cross:
    def __init__(self, place, src, dst_there, dst_here, relay, send, recv):
        self.p, self.src, self.dst_there, self.dst_here, self.relay = place, src, dst_there, dst_here, relay
        self.send, self.recv = send, recv

    def copy(self, k):
        p, relay = self.p, self.relay
        src, dst, peer = (
            (self.src, relay.at[0], "z0"),
            (self.src, relay.at[1], "mid"),
            (relay.at[0], self.dst_there, "mid"),
            (relay.at[1], self.dst_here, "z0"),
        )[k]
        return remote(src, dst, self.send.at[k], self.recv.at[k], p.peer[peer])

    def start(self):
        @pl.when(self.p.inner)
        def _():
            self.copy(1).start()

        @pl.when(jnp.logical_not(self.p.inner))
        def _():
            self.copy(0).start()

    def bring(self):
        @pl.when(self.p.inner)
        def _():
            self.copy(1).wait_recv()
            self.copy(3).start()

    def take(self):
        @pl.when(self.p.inner)
        def _():
            self.copy(0).wait_recv()
            self.copy(2).start()

    def wait(self):
        @pl.when(self.p.inner)
        def _():
            self.copy(2).wait_recv()

        @pl.when(jnp.logical_not(self.p.inner))
        def _():
            self.copy(3).wait_recv()

    def finish(self):
        @pl.when(self.p.inner)
        def _():
            for k in (1, 2, 3):
                self.copy(k).wait_send()

        @pl.when(jnp.logical_not(self.p.inner))
        def _():
            self.copy(0).wait_send()


class Gather:
    def __init__(self, place, ref, index, send, recv, local, relay, src=None, met=None):
        self.p, self.ref, self.index, self.send, self.recv = place, ref, index, send, recv
        self.local, self.src, self.met = local, src, met
        self.cross = []
        for h in (0, 1) if met is None else ():
            block = self.at((), h)
            self.cross.append(
                Cross(
                    place,
                    block if src is None else src.at[h],
                    block,
                    self.at(("z1",), h),
                    relay.at[h],
                    *[s.at[pl.ds(14 + 4 * h, 4)] for s in (send, recv)],
                )
            )

    def at(self, flips, h):
        p = self.p
        flip = lambda v, name: 1 - v if name in flips else v
        return self.ref.at[self.index(flip(p.y, "y"), flip(p.x, "x"), flip(p.z1, "z1"), h)]

    def route(self, h):
        a, b = ("y", "x") if h == 0 else ("x", "y")
        return (
            ("z1", ()),
            (a, ()),
            (a, ("z1",)),
            (b, ()),
            (b, ("z1",)),
            (b, (a,)),
            (b, (a, "z1")),
        )

    def out(self, h, m):
        axis, flips = self.route(h)[m]
        dst = src = self.at(flips, h)
        if self.src is not None and not flips:
            src = self.src.at[h]
        if self.met is not None and flips == ("z1",):
            src = self.met.at[h]
        return remote(src, dst, self.send.at[7 * h + m], self.recv.at[7 * h + m], self.p.peer[axis])

    def into(self, h, m):
        axis, flips = self.route(h)[m]
        ref = self.at(flips + (axis,), h)
        return remote(ref, ref, self.send.at[7 * h + m], self.recv.at[7 * h + m], self.p.peer[axis])

    def keep(self, h):
        kept = []
        if self.src is not None:
            kept.append(pltpu.make_async_copy(self.src.at[h], self.at((), h), self.local.at[h]))
        if self.met is not None:
            kept.append(pltpu.make_async_copy(self.met.at[h], self.at(("z1",), h), self.local.at[2 + h]))
        return kept

    def first(self):
        for c in self.cross:
            c.start()

    def second(self):
        for m in (1, 3) if self.met is None else (1, 3, 2, 4):
            for h in (0, 1):
                self.out(h, m).start()
        for h in (0, 1):
            for copy in self.keep(h):
                copy.start()

    def turned(self, h):
        self.cross[h].wait()
        for m in (2, 4):
            self.out(h, m).start()

    def on(self, h, got, gives):
        self.into(h, got).wait_recv()
        for m in gives:
            self.out(h, m).start()

    def last(self):
        for h in (0, 1):
            for m in (3, 4, 5, 6):
                self.into(h, m).wait_recv()
            for m in range(1, 7):
                self.out(h, m).wait_send()
            if self.met is None:
                self.cross[h].finish()
            for copy in self.keep(h):
                copy.wait()

    def steps(self, when):
        part = functools.partial
        acts = [(when["start"], self.first), (when["start"], self.second)]
        for h in (0, 1):
            if self.met is None:
                acts.append((when["bring"][h], self.cross[h].bring))
                acts.append((when["take"][h], self.cross[h].take))
                acts.append((when["turn"][h], part(self.turned, h)))
            acts.append((when["five"], part(self.on, h, 1, (5,))))
            acts.append((when["six"][h], part(self.on, h, 2, (6,))))
        return acts + [(when["last"], self.last)]


def times(start, bring, take, five, turn, six, last=99):
    return dict(start=start, bring=bring, take=take, five=five, turn=turn, six=six, last=last)


class Spread:
    def __init__(self, place, src, target, send, recv, local):
        self.p, self.src, self.target, self.send, self.recv, self.local = place, src, target, send, recv, local

    def copy(self, k, arriving=False):
        p = self.p
        name, fc, fz = (("c", 1, 0), ("z0", 0, 1), ("cz", 1, 1))[k]
        c = 1 - p.c if fc else p.c
        z0 = 1 - p.z0 if fz else p.z0
        src = self.src(c, z0)
        dst = self.target(c, z0) if arriving else self.target(p.c, p.z0)
        return remote(src, dst, self.send.at[k], self.recv.at[k], p.peer[name])

    def own(self):
        p = self.p
        return pltpu.make_async_copy(self.src(p.c, p.z0), self.target(p.c, p.z0), self.local)

    def start(self):
        for k in range(3):
            self.copy(k).start()
        self.own().start()

    def wait(self):
        for k in range(3):
            self.copy(k, True).wait_recv()
        self.own().wait()

    def finish(self):
        for k in range(3):
            self.copy(k).wait_send()


def add_to(dst, src):
    dst[...] = (dst[...].astype(F32) + src[...].astype(F32)).astype(dst.dtype)


class Reduce:
    def __init__(self, place, ref, index, out, mine, one, two, three, relay, send, recv, local):
        self.cross = [
            Cross(
                place, two.at[h, 0], three.at[h], three.at[h], relay.at[h], *[s.at[pl.ds(14 + 4 * h, 4)] for s in (send, recv)]
            )
            for h in ((0, 1) if out.shape != two.shape else ())
        ]
        self.p, self.ref, self.index, self.result = place, ref, index, out
        self.mine, self.one, self.two, self.three = mine, one, two, three
        self.send, self.recv, self.local = send, recv, local
        self.open = out.shape == two.shape

    def block(self, h, far_a, m):
        p = self.p
        a, b = (p.x, p.y) if h == 0 else (p.y, p.x)
        a = 1 - a if far_a else a
        b = 1 - b if m < 2 else b
        z1 = 1 - p.z1 if m % 2 == 0 else p.z1
        y, x = (b, a) if h == 0 else (a, b)
        return self.ref.at[self.index(y, x, z1, h)]

    def copy(self, h, m):
        p = self.p
        name_a, name_b = ("x", "y") if h == 0 else ("y", "x")
        sems = self.send.at[7 * h + m], self.recv.at[7 * h + m]
        if m < 4:
            return remote(self.block(h, True, m), self.one.at[h, m], *sems, p.peer[name_a])
        return remote(self.one.at[h, m - 4], self.two.at[h, m - 4], *sems, p.peer[name_b])

    def near(self, h, m):
        return self.block(h, False, m) if self.mine is None else self.mine.at[h, m]

    def load(self, h, m):
        return pltpu.make_async_copy(self.block(h, False, m), self.mine.at[h, m], self.local.at[4 * h + m])

    def first(self):
        for m in range(4):
            for h in (0, 1):
                self.copy(h, m).start()
                if self.mine is not None:
                    self.load(h, m).start()

    def second(self, h, m):
        self.copy(h, m).wait_recv()
        if self.mine is not None:
            self.load(h, m).wait()
        add_to(self.one.at[h, m], self.near(h, m))
        if m < 2:
            self.copy(h, 4 + m).start()

    def third(self, h, k):
        self.copy(h, 4 + k).wait_recv()
        add_to(self.two.at[h, k], self.one.at[h, 2 + k])
        if k == 0 and not self.open:
            self.cross[h].start()

    def fourth(self, h):
        self.cross[h].wait()
        add_to(self.three.at[h], self.two.at[h, 1])

    def finish(self):
        for h in (0, 1):
            for m in range(6):
                self.copy(h, m).wait_send()
            if not self.open:
                self.cross[h].finish()

    def store(self):
        src = self.two if self.result.shape == self.two.shape else self.three
        return pltpu.make_async_copy(src, self.result, self.local.at[8])


def out_gather_steps(p, src, ref, send, recv, local):
    home = p.x == p.z0
    away = jnp.logical_not(home)
    at = lambda fy, fz: ref.at[(1 - p.y if fy else p.y) * 2 + (1 - p.z1 if fz else p.z1)]
    pair = lambda half: remote(src, at(0, 0).at[half], send.at[0], recv.at[0], p.peer["z0"])
    z1_copy = lambda fz: remote(at(0, fz), at(0, fz), send.at[1], recv.at[1], p.peer["z1"])
    x_copy = lambda k: remote(at(0, k), at(0, k), send.at[2 + k], recv.at[2 + k], p.peer["x"])
    y_copy = lambda k, fy: remote(at(fy, k), at(fy, k), send.at[4 + k], recv.at[4 + k], p.peer["y"])
    own = pltpu.make_async_copy(src, at(0, 0).at[p.z0], local)

    def zero():
        @pl.when(home)
        def _():
            own.start()

        @pl.when(away)
        def _():
            pair(p.z0).start()

    def one():
        @pl.when(home)
        def _():
            own.wait()
            pair(1 - p.z0).wait_recv()
            z1_copy(0).start()
            x_copy(0).start()
            y_copy(0, 0).start()

    def two():
        @pl.when(home)
        def _():
            z1_copy(1).wait_recv()
            x_copy(1).start()
            y_copy(1, 0).start()

    def three():
        @pl.when(away)
        def _():
            for k in (0, 1):
                x_copy(k).wait_recv()
                y_copy(k, 0).start()

    def last():
        for k in (0, 1):
            y_copy(k, 1).wait_recv()
            y_copy(k, 0).wait_send()

        @pl.when(home)
        def _():
            z1_copy(0).wait_send()
            for k in (0, 1):
                x_copy(k).wait_send()

        @pl.when(away)
        def _():
            pair(p.z0).wait_send()

    return [zero, one, two, three, last]


def out_reduce_steps(p, ref, out, one, two, three, got, send, recv, local):
    home = p.x == p.z0
    away = jnp.logical_not(home)
    y_copy = lambda k: remote(ref.at[(1 - p.y) * 2 + k], one.at[k], send.at[k], recv.at[k], p.peer["y"])
    x_copy = lambda k: remote(one.at[k], two.at[k], send.at[2 + k], recv.at[2 + k], p.peer["x"])
    z1_copy = remote(two.at[1 - p.z1], three, send.at[4], recv.at[4], p.peer["z1"])
    rows = three.shape[0] // 2
    half = lambda z0: three.at[pl.ds(pl.multiple_of(z0 * rows, rows), rows)]
    pair = remote(half(1 - p.z0), got, send.at[5], recv.at[5], p.peer["z0"])
    keep = pltpu.make_async_copy(half(p.z0), out, local.at[0])
    take = pltpu.make_async_copy(got, out, local.at[0])

    def zero():
        for k in (0, 1):
            y_copy(k).start()

    def first():
        for k in (0, 1):
            y_copy(k).wait_recv()
            add_to(one.at[k], ref.at[p.y * 2 + k])

            @pl.when(away)
            def _(k=k):
                x_copy(k).start()

    def second():
        @pl.when(home)
        def _():
            for k in (0, 1):
                x_copy(k).wait_recv()
                add_to(two.at[k], one.at[k])
            z1_copy.start()

    def third():
        @pl.when(home)
        def _():
            z1_copy.wait_recv()
            add_to(three, two.at[p.z1])
            pair.start()
            keep.start()

    def last():
        for k in (0, 1):
            y_copy(k).wait_send()

        @pl.when(home)
        def _():
            keep.wait()
            z1_copy.wait_send()
            pair.wait_send()

        @pl.when(away)
        def _():
            pair.wait_recv()
            take.start()
            for k in (0, 1):
                x_copy(k).wait_send()
            take.wait()

    return [zero, first, second, third, last]


def out_reduce_scratch(wide):
    return [
        pltpu.VMEM((4,) + wide, BF),
        pltpu.VMEM((2,) + wide, BF),
        pltpu.VMEM((2,) + wide, BF),
        pltpu.VMEM(wide, BF),
        pltpu.VMEM((wide[0] // 2, wide[1]), BF),
        DMA((6,)),
        DMA((6,)),
        DMA((1,)),
    ]


def gains_gather(p, src, ref, send, recv, local):
    me = ((p.y * 2 + p.x) * 2 + p.c) * 4 + p.z1 * 2 + p.z0
    own = pltpu.make_async_copy(src, ref.at[me], local)
    names = ("z0", "z1", "c", "x", "y")

    def span(k, other):
        size = 1 << k
        start = lax.div(me, size) * size
        if other:
            bit = lax.rem(lax.div(me, size), 2)
            start = start + size - 2 * size * bit
        return ref.at[pl.ds(start, size)]

    def copy(k, other):
        return remote(span(k, other), span(k, other), send.at[k], recv.at[k], p.peer[names[k]])

    def step(k):
        def run():
            if k == 0:
                own.start()
                own.wait()
            else:
                copy(k - 1, True).wait_recv()
            if k < 5:
                copy(k, False).start()
            else:
                for j in range(5):
                    copy(j, False).wait_send()

        return run

    return [step(k) for k in range(6)]


def gains_reduce(p, src, out, base, halves, send, recv, local):
    names, bits = ("y", "x", "c", "z1", "z0"), (p.y, p.x, p.c, p.z1, p.z0)
    load = pltpu.make_async_copy(src, base, local.at[0])
    keep = pltpu.make_async_copy(halves[4].at[0], out, local.at[0])

    def part(k, bit):
        source, size = (base if k == 0 else halves[k - 1]), 16 >> k
        return source.at[pl.ds(bit * size, size)]

    def copy(k):
        return remote(part(k, 1 - bits[k]), halves[k], send.at[k], recv.at[k], p.peer[names[k]])

    def step(k):
        def run():
            if k > 0:
                copy(k - 1).wait_recv()
                halves[k - 1][...] += part(k - 1, bits[k - 1])[...]
            else:
                load.start()
                load.wait()
            if k < 5:
                copy(k).start()
            else:
                keep.start()
                for j in range(5):
                    copy(j).wait_send()
                keep.wait()

        return run

    return [step(k) for k in range(6)]


GROUP = ("c", "z0", "cz")
EIGHT = ("z1", "y", "x")


CHUNKS = 2


class ShareRows:
    def __init__(self, p, dst, send, recv):
        self.p, self.dst, self.send, self.recv = p, dst, send, recv
        self.rows = dst.shape[1] // CHUNKS

    def chunk(self, rank, k):
        return self.dst.at[rank, pl.ds(k * self.rows, self.rows)]

    def over(self, k, arriving=False):
        p = self.p
        ref = self.chunk(p.over if arriving else p.rank, k)
        return remote(ref, ref, self.send.at[k], self.recv.at[k], p.peer["z0"])

    def across(self, arriving=False):
        p = self.p
        ref = self.dst.at[p.sibling if arriving else p.rank]
        return remote(ref, ref, self.send.at[CHUNKS], self.recv.at[CHUNKS], p.peer["c"])

    def onward(self, k, arriving=False):
        p = self.p
        ours, theirs = 2 * p.c + 1 - p.z0, 2 * (1 - p.c) + 1 - p.z0
        ref = self.chunk(theirs if arriving else ours, k)
        return remote(ref, ref, self.send.at[CHUNKS + 1 + k], self.recv.at[CHUNKS + 1 + k], p.peer["c"])

    def start(self):
        for k in range(CHUNKS):
            self.over(k).start()
        self.across().start()

    def pass_on(self, k):
        self.over(k, True).wait_recv()
        self.onward(k).start()

    def far(self, k):
        self.onward(k, True).wait_recv()

    def finish(self):
        for k in range(CHUNKS):
            self.over(k).wait_send()
            self.onward(k).wait_send()
        self.across().wait_send()


class SumRows:
    def __init__(self, p, terms, near, cross, far, send, recv):
        self.p, self.terms, self.near, self.cross, self.far, self.send, self.recv = p, terms, near, cross, far, send, recv
        self.rows = near.shape[0] // CHUNKS

    def diagonal(self, k):
        p = self.p
        part = pl.ds(k * self.rows, self.rows)
        rank = 2 * (1 - p.c) + 1 - p.z0
        return remote(self.terms.at[rank, part], self.cross.at[part], self.send.at[k], self.recv.at[k], p.peer["c"])

    def sibling(self):
        p = self.p
        rank, at = 2 * (1 - p.c) + p.z0, CHUNKS
        return remote(self.terms.at[rank], self.near, self.send.at[at], self.recv.at[at], p.peer["c"])

    def over(self, k):
        p, at = self.p, CHUNKS + 1 + k
        part = pl.ds(k * self.rows, self.rows)
        return remote(self.cross.at[part], self.far.at[part], self.send.at[at], self.recv.at[at], p.peer["z0"])

    def relay(self, k):
        p = self.p
        self.diagonal(k).wait_recv()
        part = pl.ds(k * self.rows, self.rows)
        add_to(self.cross.at[part], self.terms.at[2 * p.c + 1 - p.z0, part])
        self.over(k).start()

    def finish(self):
        for k in range(CHUNKS):
            self.diagonal(k).wait_send()
            self.over(k).wait_send()
        self.sibling().wait_send()


def swap_pairs(count_fsdp, count_seq):
    pairs = []
    for f in range(count_fsdp):
        for z in range(count_seq):
            c, z1 = f % 2, z // 2
            pairs.append((f * count_seq + z, (f - c + z1) * count_seq + c * 2 + z % 2))
    return pairs


TILE = 256
UP_TILE = 512
DOWN_TILE = 768
GRAD_TILE = 512
HALVES = 2


def wide_params(collective_id):
    return pltpu.CompilerParams(
        collective_id=collective_id, has_side_effects=True, vmem_limit_bytes=61 * 2**20
    )


def dot(a, b, contract=((1,), (0,))):
    return lax.dot_general(a, b, (contract, ((), ())), preferred_element_type=F32)


def row_normalize(ref, gain, out, rows=32):
    def step(k, _):
        at = pl.ds(pl.multiple_of(k * rows, rows), rows)
        value = ref[at, :].astype(F32)
        out[at, :] = (normalize(value) * gain[...]).astype(out.dtype)
        return 0

    lax.fori_loop(0, ref.shape[0] // rows, step, 0)


def column_tiles(width, tile, step):
    def run(j, _):
        step(pl.multiple_of(j * tile, tile))
        return 0

    lax.fori_loop(0, width // tile, run, 0)


def exchange(p, share, total, compute, advance):
    rows = total.near.shape[0]
    part = rows // CHUNKS
    share.start()
    advance()
    compute([(p.rank, 0)], rows)
    advance()
    share.across(True).wait_recv()
    compute([(p.sibling, 0)], rows)
    total.sibling().start()
    advance()
    for k in range(CHUNKS):
        share.pass_on(k)
        share.far(k)
        compute([(p.diagonal, k * part), (p.over, k * part)], part)
        total.diagonal(k).start()
        total.relay(k)
        advance()


def gather_pieces(ref, pieces, count, *index):
    parts = [ref[(rank, pl.ds(first, count)) + index] for rank, first in pieces]
    return parts[0] if len(parts) == 1 else jnp.concatenate(parts, axis=0)


def scatter_pieces(ref, pieces, count, value, *index):
    for k, (rank, first) in enumerate(pieces):
        ref[(rank, pl.ds(first, count)) + index] = value[k * count : (k + 1) * count]


def token_rows(pieces, count, rows):
    return [pl.ds(pl.multiple_of(rank * rows + first, count), count) for rank, first in pieces]


def collect(p, total, write, rows=32):
    total.sibling().wait_recv()
    for k in range(CHUNKS):
        total.over(k).wait_recv()

        def step(j, _, k=k):
            at = pl.ds(pl.multiple_of(k * total.rows + j * rows, rows), rows)
            value = total.terms[p.rank, at, :].astype(F32) + total.near[at, :].astype(F32)
            write(at, value + total.far[at, :].astype(F32))
            return 0

        lax.fori_loop(0, total.rows // rows, step, 0)


def exchange_scratch(rows):
    part = pltpu.VMEM((rows, D), BF)
    sems = DMA((2 * CHUNKS + 1,))
    return [pltpu.VMEM((4, rows, D), BF), part, part, part, sems, sems, sems, sems]


def exchange_of(p, every, refs):
    terms, near, cross, far, send, recv, t_send, t_recv = refs
    share = ShareRows(p, every, send, recv)
    return every.at[p.rank], terms, share, SumRows(p, terms, near, cross, far, t_send, t_recv)


class Nothing:
    names, args, specs, shapes, scratch = (), (), (), (), ()

    def steps(self, p, ins, outs, scratch):
        return []


class Clock:
    def __init__(self, steps):
        self.steps, self.now = sorted(steps, key=lambda s: s[0]), 0

    def __call__(self):
        while self.steps and self.steps[0][0] <= self.now:
            self.steps.pop(0)[1]()
        self.now += 1

    def finish(self):
        for _, act in self.steps:
            act()
        self.steps = []


class Staged:
    def __init__(self, ins, in_sems, outs, out_sems):
        self.loads = {k: pltpu.make_async_copy(src, dst, in_sems.at[n]) for n, (k, src, dst) in enumerate(ins)}
        self.stores = {k: pltpu.make_async_copy(src, dst, out_sems.at[n]) for n, (k, src, dst) in enumerate(outs)}
        self.started = []
        for load in self.loads.values():
            load.start()

    def ready(self, *ks):
        for k in ks:
            if k in self.loads:
                self.loads.pop(k).wait()

    def flush(self, *ks):
        for k in ks:
            store = self.stores.pop(k)
            store.start()
            self.started.append(store)

    def finish(self):
        self.ready(*list(self.loads))
        self.flush(*list(self.stores))
        for store in self.started:
            store.wait()


def beside_call(
    body, args, late, shapes, later, scratch, beside, name, collective_id, flops, peers=("c", "z0"), specs=None
):
    n_ins, n_outs = len(args), len(shapes)
    buffers = [pltpu.VMEM(args[k].shape, args[k].dtype) for k in late]
    buffers += [pltpu.VMEM(shapes[k].shape, shapes[k].dtype) for k in later]
    sems = [DMA((max(len(late), 1),)), DMA((max(len(later), 1),))]
    counts = [n_ins, len(beside.args), n_outs, len(beside.shapes), len(scratch), len(buffers), 2, len(beside.scratch)]

    def whole(*refs):
        groups, at = [], 0
        for n in counts:
            groups.append(list(refs[at : at + n]))
            at += n
        ins, b_ins, outs, b_outs, own, held, (in_sems, out_sems), b_scratch = groups
        moved_in = [(k, ins[k], held[n]) for n, k in enumerate(late)]
        moved_out = [(k, held[len(late) + n], outs[k]) for n, k in enumerate(later)]
        staged = Staged(moved_in, in_sems, moved_out, out_sems)
        for k, _, dst in moved_in:
            ins[k] = dst
        for k, src, _ in moved_out:
            outs[k] = src
        p = Place()
        greet(p, tuple(peers) + tuple(n for n in beside.names if n not in peers))
        body(p, ins, outs, own, Clock(beside.steps(p, b_ins, b_outs, b_scratch)), staged)
        staged.finish()

    specs = specs or {}
    out = pl.pallas_call(
        whole,
        out_shape=list(shapes) + list(beside.shapes),
        in_specs=[ANY if k in late else VM for k in range(n_ins)] + list(beside.specs),
        out_specs=[ANY if k in later else specs.get(k, VM) for k in range(n_outs)] + [ANY] * len(beside.shapes),
        scratch_shapes=list(scratch) + buffers + sems + list(beside.scratch),
        compiler_params=wide_params(collective_id),
        cost_estimate=pl.CostEstimate(flops=flops, bytes_accessed=20 * 2**20, transcendentals=0),
        name=name,
    )(*args, *beside.args)
    return out[:n_outs], out[n_outs:]


def feed_forward_call(middle, gain, w_gateup, w_down, beside, collective_id, dtype=F32):
    rows, wide = middle.shape[0], w_down.shape[0]

    def body(p, ins, outs, scratch, advance, staged):
        mid_ref, gain_ref, gu_ref, down_ref = ins
        new_ref, every, gate_ref, up_ref, hid_ref = outs
        own, terms, share, total = exchange_of(p, every, scratch)

        def compute(pieces, count):
            staged.ready(2, 3)

            def up_tile(j):
                cols, far = pl.ds(j, UP_TILE), pl.ds(wide + j, UP_TILE)
                x = gather_pieces(every, pieces, count)
                gate, up = dot(x, gu_ref[:, cols]), dot(x, gu_ref[:, far])
                scatter_pieces(gate_ref, pieces, count, gate.astype(BF), cols)
                scatter_pieces(up_ref, pieces, count, up.astype(BF), cols)
                hidden = (gate / (1.0 + jnp.exp(-gate)) * up).astype(BF)
                scatter_pieces(hid_ref, pieces, count, hidden, cols)

            column_tiles(wide, UP_TILE, up_tile)

            def down_tile(j):
                cols = pl.ds(j, DOWN_TILE)
                value = dot(gather_pieces(hid_ref, pieces, count), down_ref[:, cols]).astype(BF)
                scatter_pieces(terms, pieces, count, value, cols)

            column_tiles(D, DOWN_TILE, down_tile)

        row_normalize(mid_ref, gain_ref, own)
        exchange(p, share, total, compute, advance)
        staged.flush(1, 2, 3, 4)

        def write(at, value):
            new_ref[at, :] = (mid_ref[at, :] + value).astype(dtype)

        collect(p, total, write)
        advance.finish()
        share.finish()
        total.finish()

    return beside_call(
        body,
        (middle, gain.reshape(1, D), w_gateup, w_down),
        (2, 3),
        [
            jax.ShapeDtypeStruct((rows, D), dtype),
            jax.ShapeDtypeStruct((4, rows, D), BF),
            jax.ShapeDtypeStruct((4, rows, wide), BF),
            jax.ShapeDtypeStruct((4, rows, wide), BF),
            jax.ShapeDtypeStruct((4, rows, wide), BF),
        ],
        (1, 2, 3, 4),
        exchange_scratch(rows),
        beside,
        "feed_forward",
        collective_id,
        6 * 4 * rows * wide * D,
    )


def feed_backward_call(grad, middle, gain, w_gateup, w_down, kept, beside, collective_id):
    every, gate, up, hidden = kept
    rows, wide = middle.shape[0], w_down.shape[0]
    block = (wide // 16, D)

    def body(p, ins, outs, scratch, advance, staged):
        grad_ref, mid_ref, gain_ref, gu_ref, down_ref, every_ref, gate_ref, up_ref, hid_ref = ins
        new_ref, gain_out, g_gu, two_down = outs
        e, pair, g_down, one, two, send, recv, local = scratch[:8]
        own, terms, share, total = exchange_of(p, e, scratch[8:])
        reduce = Reduce(p, g_down, rows_index, two_down, None, one, two, None, None, send, recv, local)

        def compute(pieces, count):
            staged.ready(4, 6, 7, 3)

            def up_tile(j):
                cols, far = pl.ds(j, UP_TILE), pl.ds(wide + j, UP_TILE)
                grad_hidden = dot(gather_pieces(e, pieces, count), down_ref[cols, :], ((1,), (1,)))
                g = gather_pieces(gate_ref, pieces, count, cols).astype(F32)
                u = gather_pieces(up_ref, pieces, count, cols).astype(F32)
                s = 1.0 / (1.0 + jnp.exp(-g))
                grad_gate = (grad_hidden * u * s * (1.0 + g * (1.0 - s))).astype(BF)
                scatter_pieces(pair, pieces, count, grad_gate, cols)
                scatter_pieces(pair, pieces, count, (grad_hidden * g * s).astype(BF), far)

            column_tiles(wide, UP_TILE, up_tile)

            def down_tile(j):
                cols = pl.ds(j, DOWN_TILE)
                value = dot(gather_pieces(pair, pieces, count), gu_ref[cols, :], ((1,), (1,))).astype(BF)
                scatter_pieces(terms, pieces, count, value, cols)

            column_tiles(D, DOWN_TILE, down_tile)

        def weight_grads():
            tokens = 4 * rows
            e_all, pair_all, x_all, hid_all = (
                r.reshape(tokens, r.shape[2]) for r in (e, pair, every_ref, hid_ref)
            )

            part = g_down.shape[1]
            staged.ready(8, 5)

            def down_grad(j):
                value = dot(hid_all[:, pl.ds(j, GRAD_TILE)], e_all[...], ((0,), (0,))).astype(BF)
                g_down[pl.ds(lax.div(j, part), GRAD_TILE // part)] = value.reshape(GRAD_TILE // part, part, D)

            column_tiles(wide, GRAD_TILE, down_grad)
            reduce.first()
            for k in range(D // GRAD_TILE):
                cols = slice(k * GRAD_TILE, (k + 1) * GRAD_TILE)
                g_gu[cols, :] = dot(x_all[:, cols], pair_all[...], ((0,), (0,))).astype(BF)
                advance()
                if k < 2:
                    for m in (2 * k, 2 * k + 1):
                        for h in (0, 1):
                            reduce.second(h, m)
            staged.flush(2)

        def copy_own(k, _):
            at = pl.ds(pl.multiple_of(k * 32, 32), 32)
            own[at, :] = grad_ref[at, :].astype(BF)
            return 0

        lax.fori_loop(0, rows // 32, copy_own, 0)
        exchange(p, share, total, compute, advance)
        weight_grads()
        gain_out[...] = jnp.zeros_like(gain_out)

        def write(at, value):
            mid = mid_ref[at, :]
            normed = normalize(mid)
            gain_out[...] += jnp.sum(value * normed, axis=0, keepdims=True)
            new_ref[at, :] = grad_ref[at, :] + norm_back(value * gain_ref[...], normed, mid)

        collect(p, total, write)
        for k in (0, 1):
            for h in (0, 1):
                reduce.third(h, k)
        advance.finish()
        reduce.store().start()
        reduce.finish()
        reduce.store().wait()
        share.finish()
        total.finish()

    return beside_call(
        body,
        (grad, middle, gain.reshape(1, D), w_gateup, w_down, every, gate, up, hidden),
        (4, 6, 7, 3, 8, 5),
        [
            jax.ShapeDtypeStruct((rows, D), F32),
            jax.ShapeDtypeStruct((1, D), F32),
            jax.ShapeDtypeStruct((D, 2 * wide), BF),
            jax.ShapeDtypeStruct((2, 2) + block, BF),
        ],
        (2,),
        [
            pltpu.VMEM((4, rows, D), BF),
            pltpu.VMEM((4, rows, 2 * wide), BF),
            pltpu.VMEM((16,) + block, BF),
            pltpu.VMEM((2, 4) + block, BF),
            pltpu.VMEM((2, 2) + block, BF),
            DMA((14,)),
            DMA((14,)),
            DMA((9,)),
        ]
        + exchange_scratch(rows),
        beside,
        "feed_backward",
        collective_id,
        12 * 4 * rows * wide * D,
        ("c", "z0", "x", "y"),
        {3: ANY},
    )


class Both:
    def __init__(self, *parts):
        self.parts = parts
        self.names = tuple(dict.fromkeys(n for p in parts for n in p.names))
        self.args = tuple(a for p in parts for a in p.args)
        self.specs = tuple(a for p in parts for a in p.specs)
        self.shapes = tuple(s for p in parts for s in p.shapes)
        self.scratch = tuple(s for p in parts for s in p.scratch)

    def steps(self, p, ins, outs, scratch):
        waves, at = [], [0, 0, 0]
        for part in self.parts:
            ends = [at[0] + len(part.args), at[1] + len(part.shapes), at[2] + len(part.scratch)]
            waves += part.steps(p, ins[at[0] : ends[0]], outs[at[1] : ends[1]], scratch[at[2] : ends[2]])
            at = ends
        return waves


class SwapRows:
    names = ("swap",)

    def __init__(self, rows, at=0):
        self.args, self.specs, self.time = (rows,), (VM,), at
        self.shapes = (jax.ShapeDtypeStruct(rows.shape, rows.dtype),)
        self.scratch = (DMA((1,)), DMA((1,)), DMA((1,)))

    def steps(self, p, ins, outs, scratch):
        send, recv, local = (s.at[0] for s in scratch)
        away = p.c != p.z1
        move = remote(ins[0], outs[0], send, recv, p.peer["swap"])
        stay = pltpu.make_async_copy(ins[0], outs[0], local)

        def first():
            @pl.when(away)
            def _():
                move.start()

            @pl.when(jnp.logical_not(away))
            def _():
                stay.start()

        def last():
            @pl.when(away)
            def _():
                move.wait()

            @pl.when(jnp.logical_not(away))
            def _():
                stay.wait()

        return [(self.time, first), (99, last)]


class SpreadColumns:
    names = GROUP

    def __init__(self, *blocks):
        self.args, self.specs = blocks, (VM,) * len(blocks)
        self.shapes = tuple(jax.ShapeDtypeStruct((2, 2) + b.shape[1:], BF) for b in blocks)
        self.scratch = (DMA((3 * len(blocks),)), DMA((3 * len(blocks),)), DMA((len(blocks),)))

    def steps(self, p, ins, outs, scratch):
        send, recv, local = scratch
        made = []
        for k, (src, dst) in enumerate(zip(ins, outs)):
            sems = [s.at[pl.ds(3 * k, 3)] for s in (send, recv)]
            made.append(
                Spread(
                    p, lambda c, z0, s=src: s.at[2 * c + z0], lambda c, z0, d=dst: d.at[c, z0], *sems, local.at[k]
                )
            )

        def first():
            for m in made:
                m.start()

        def last():
            for m in made:
                m.wait()
                m.finish()

        return [(0, first), (99, last)]


class CollectColumns:
    names = GROUP

    def __init__(self, *blocks, at=0):
        self.time = at
        self.args, self.specs = blocks, (VM,) * len(blocks)
        self.shapes = tuple(jax.ShapeDtypeStruct((4,) + b.shape[2:], BF) for b in blocks)
        self.scratch = (DMA((3 * len(blocks),)), DMA((3 * len(blocks),)), DMA((len(blocks),)))

    def steps(self, p, ins, outs, scratch):
        send, recv, local = scratch
        made = []
        for k, (src, dst) in enumerate(zip(ins, outs)):
            sems = [s.at[pl.ds(3 * k, 3)] for s in (send, recv)]
            made.append(
                Spread(
                    p, lambda c, z0, s=src: s.at[c, z0], lambda c, z0, d=dst: d.at[2 * c + z0], *sems, local.at[k]
                )
            )

        def first():
            for m in made:
                m.start()

        def last():
            for m in made:
                m.wait()
                m.finish()

        return [(self.time, first), (99, last)]


class MeetBlocks:
    names = ("mid", "z0")

    def __init__(self, *blocks, at=(0, 1, 2)):
        self.args, self.specs, self.times = blocks, (VM,) * len(blocks), at
        self.shapes = tuple(jax.ShapeDtypeStruct(b.shape, BF) for b in blocks)
        self.scratch = tuple(pltpu.VMEM((2,) + b.shape, BF) for b in blocks)
        self.scratch += (DMA((8 * len(blocks),)), DMA((8 * len(blocks),)))

    def steps(self, p, ins, outs, scratch):
        relays, (send, recv) = scratch[:-2], scratch[-2:]
        acts = []
        for k, (src, dst, relay) in enumerate(zip(ins, outs, relays)):
            for h in (0, 1):
                sems = [s.at[pl.ds(8 * k + 4 * h, 4)] for s in (send, recv)]
                c = Cross(p, src.at[h], dst.at[h], dst.at[h], relay.at[:, h], *sems)
                acts += list(zip(self.times, (c.start, c.bring, c.take))) + [(99, c.wait), (99, c.finish)]
        return acts


class MeetOut:
    names = ("z0", "z1")

    def __init__(self, out, at=(0, 4)):
        self.args, self.specs, self.times = (out,), (VM,), at
        self.shapes = (jax.ShapeDtypeStruct((2, 2) + out.shape, BF),)
        self.scratch = (DMA((2,)), DMA((2,)), DMA((1,)))

    def steps(self, p, ins, outs, scratch):
        src, met = ins[0], outs[0]
        send, recv, local = scratch
        home = p.x == p.z0
        away = jnp.logical_not(home)
        pair = lambda half: remote(src, met.at[0, half], send.at[0], recv.at[0], p.peer["z0"])
        over = remote(met.at[0], met.at[1], send.at[1], recv.at[1], p.peer["z1"])
        own = pltpu.make_async_copy(src, met.at[0, p.z0], local.at[0])

        def first():
            pl.when(home)(own.start)
            pl.when(away)(lambda: pair(p.z0).start())

        def second():
            @pl.when(home)
            def _():
                own.wait()
                pair(1 - p.z0).wait_recv()
                over.start()

        def last():
            pl.when(home)(over.wait)
            pl.when(away)(lambda: pair(p.z0).wait_send())

        return [(self.times[0], first), (self.times[1], second), (99, last)]


class GatherOut:
    names = ("x", "y")

    def __init__(self, met, at=(0, 3)):
        self.args, self.specs, self.times = (met,), (VM,), at
        self.shapes = (jax.ShapeDtypeStruct((4,) + met.shape[1:], BF),)
        self.scratch = (DMA((4,)), DMA((4,)), DMA((2,)))

    def steps(self, p, ins, outs, scratch):
        met, ref = ins[0], outs[0]
        send, recv, local = scratch
        home = p.x == p.z0
        away = jnp.logical_not(home)
        at = lambda fy, k: ref.at[(1 - p.y if fy else p.y) * 2 + (1 - p.z1 if k else p.z1)]
        x_copy = lambda k: remote(met.at[k], at(0, k), send.at[k], recv.at[k], p.peer["x"])
        y_copy = lambda k, src, fy=0: remote(src, at(fy, k), send.at[2 + k], recv.at[2 + k], p.peer["y"])
        keep = lambda k: pltpu.make_async_copy(met.at[k], at(0, k), local.at[k])

        def first():
            @pl.when(home)
            def _():
                for k in (0, 1):
                    x_copy(k).start()
                    y_copy(k, met.at[k]).start()
                    keep(k).start()

        def second():
            @pl.when(away)
            def _():
                for k in (0, 1):
                    x_copy(k).wait_recv()
                    y_copy(k, at(0, k)).start()

        def last():
            for k in (0, 1):
                y_copy(k, at(1, k), 1).wait_recv()
                y_copy(k, at(0, k)).wait_send()

            @pl.when(home)
            def _():
                for k in (0, 1):
                    x_copy(k).wait_send()
                    keep(k).wait()

        return [(self.times[0], first), (self.times[1], second), (99, last)]


class GatherWeights:
    def __init__(
        self, columns=None, down=None, out=None, gains=None, columns_at=None, down_at=None, out_at=None, gains_at=None, met=None
    ):
        self.has = columns is not None, down is not None, out is not None, gains is not None
        self.spread = columns is not None and len(columns.shape) == 3
        self.times = columns_at, down_at, out_at, gains_at
        self.names = EIGHT + (("mid",) if met is None else ()) + ("z0",) + (GROUP if self.spread else ())
        self.met = met is not None
        self.args = tuple(a for a in (columns, down, out, gains) if a is not None) + tuple(met or ())
        self.specs = (VM,) * len(self.args)
        shapes, scratch = [], []
        sems = lambda n: [DMA((n,)), DMA((n,)), DMA((4,))]
        if columns is not None:
            block = (2,) + columns.shape[-2:]
            shapes.append((16,) + block)
            scratch += sems(22) + [pltpu.VMEM((2, 2) + block, BF)] + sems(3)
        if down is not None:
            shapes.append((16,) + down.shape[1:])
            scratch += sems(22) + [pltpu.VMEM((2, 2) + down.shape[1:], BF)]
        if out is not None:
            shapes.append((4, 2) + out.shape)
            scratch += sems(8)
        if gains is not None:
            shapes.append((32,) + gains.shape)
            scratch += sems(5)
        self.shapes = tuple(jax.ShapeDtypeStruct(s, BF) for s in shapes)
        self.scratch = tuple(scratch)

    def steps(self, p, ins, outs, scratch):
        ins, outs, scratch = list(ins), list(outs), list(scratch)
        take = lambda n: [scratch.pop(0) for _ in range(n)]
        acts = []
        met = [ins.pop() if self.met and has else None for has in self.has[1::-1]][::-1]
        if self.has[0]:
            src, ref = ins.pop(0), outs.pop(0)
            sems, s_sems, when = take(4), take(3), self.times[0]
            if self.spread:
                at = lambda c, z0, ref=ref: ref.at[columns_index(p.y, p.x, p.z1, c), z0]
                spread = Spread(p, lambda c, z0, src=src: src.at[2 * c + z0], at, *s_sems[:2], s_sems[2].at[0])
                acts += [(-1, spread.start), (when["start"], spread.wait), (99, spread.finish)]
                src = None
            acts += Gather(p, ref, columns_index, *sems, src, met[0]).steps(when)
        if self.has[1]:
            src, ref = ins.pop(0), outs.pop(0)
            acts += Gather(p, ref, rows_index, *take(4), src, met[1]).steps(self.times[1])
        if self.has[2]:
            acts += zip(self.times[2], out_gather_steps(p, ins.pop(0), outs.pop(0), *take(2), take(1)[0].at[0]))
        if self.has[3]:
            acts += zip(self.times[3], gains_gather(p, ins.pop(0), outs.pop(0), *take(2), take(1)[0].at[0]))
        return acts


class ReduceWeights:
    def __init__(self, columns, gains=None, collect=False, open=False, at=range(9)):
        self.gains = gains is not None
        self.collect, self.open, self.times = collect, open, tuple(at)
        self.names = EIGHT + ("mid", "z0") + (GROUP if collect else ())
        self.args = tuple(a for a in (columns, gains) if a is not None)
        self.specs = (ANY,) * len(self.args)
        shapes, scratch = [], []
        b = columns.shape[1:]
        shape = (4, b[0] // 2, b[1]) if collect else (2, 2) + b if open else (2,) + b
        shapes.append(jax.ShapeDtypeStruct(shape, BF))
        scratch += [pltpu.VMEM(n + b, BF) for n in ((2, 4), (2, 4), (2, 2), (2,))]
        scratch += [pltpu.VMEM((1, 1, 16, 128) if open else (2, 2) + b, BF), DMA((22,)), DMA((22,)), DMA((9,))]
        if collect:
            scratch += [DMA((3,)), DMA((3,)), DMA((1,))]
        if gains is not None:
            shapes.append(jax.ShapeDtypeStruct(gains.shape[1:], F32))
            scratch += [pltpu.VMEM(gains.shape, F32)]
            scratch += [pltpu.VMEM((16 >> k,) + gains.shape[1:], F32) for k in range(5)]
            scratch += [DMA((5,)), DMA((5,)), DMA((1,))]
        self.shapes, self.scratch = tuple(shapes), tuple(scratch)

    def steps(self, p, ins, outs, scratch):
        ins, outs, scratch = list(ins), list(outs), list(scratch)
        take = lambda n: [scratch.pop(0) for _ in range(n)]
        waves = [[] for _ in range(9)]
        part = functools.partial
        both = (0, 1)
        columns = Reduce(p, ins.pop(0), columns_index, outs.pop(0), *take(8))
        waves[0].append(columns.first)
        for m in range(4):
            waves[1 + m] += [part(columns.second, h, m) for h in both]
        for k in both:
            waves[5 + k] += [part(columns.third, h, k) for h in both]
        if self.collect:
            send, recv, local = take(3)
            rows = columns.three.shape[1] // 2
            piece = lambda c, z0: columns.three.at[c, pl.ds(pl.multiple_of(z0 * rows, rows), rows)]
            spread = Spread(p, piece, lambda c, z0: columns.result.at[2 * c + z0], send, recv, local.at[0])
            waves[7] += [c.bring for c in columns.cross] + [c.take for c in columns.cross]
            waves[8] += [part(columns.fourth, h) for h in both] + [spread.start, spread.wait, spread.finish]
        elif not self.open:
            waves[7] += [c.bring for c in columns.cross] + [c.take for c in columns.cross]
            waves[8] += [part(columns.fourth, h) for h in both]
        if not self.collect:
            waves[8] += [lambda: columns.store().start(), lambda: columns.store().wait()]
        waves[8].append(columns.finish)
        if self.gains:
            parts = take(9)
            steps = gains_reduce(p, ins.pop(0), outs.pop(0), parts[0], parts[1:6], *parts[6:])
            for k, act in zip((0, 2, 3, 4, 6, 8), steps):
                waves[k].append(act)
        return [(t, act) for t, wave in zip(self.times, waves) for act in wave]


class FinishColumns:
    def __init__(self, two, collect=False, at=(0, 1, 2, 99)):
        self.names = ("mid", "z0") + (GROUP if collect else ())
        self.collect, self.times = collect, at
        b = two.shape[2:]
        self.args, self.specs = (two,), (ANY,)
        self.shapes = (jax.ShapeDtypeStruct((4, b[0] // 2, b[1]) if collect else (2,) + b, BF),)
        self.scratch = (pltpu.VMEM((2,) + b, BF), pltpu.VMEM((2,) + b, BF), pltpu.VMEM((2, 2) + b, BF))
        self.scratch += (DMA((8,)), DMA((8,)), DMA((3,)), DMA((3,)), DMA((3,)), DMA((1,)))

    def steps(self, p, ins, outs, scratch):
        mine, three, relay, send, recv, local, s_send, s_recv, s_local = scratch
        two, result = ins[0], outs[0]
        crosses = [
            Cross(p, two.at[h, 0], three.at[h], three.at[h], relay.at[h], *[s.at[pl.ds(4 * h, 4)] for s in (send, recv)])
            for h in (0, 1)
        ]
        loads = [pltpu.make_async_copy(two.at[h, 1], mine.at[h], local.at[h]) for h in (0, 1)]
        rows = three.shape[1] // 2
        piece = lambda c, z0: three.at[c, pl.ds(pl.multiple_of(z0 * rows, rows), rows)]
        spread = Spread(p, piece, lambda c, z0: result.at[2 * c + z0], s_send, s_recv, s_local.at[0])
        store = lambda: pltpu.make_async_copy(three, result, local.at[2])

        def first():
            for c in crosses + loads:
                c.start()

        def last():
            for h in (0, 1):
                crosses[h].wait()
                loads[h].wait()
                add_to(three.at[h], mine.at[h])
            if self.collect:
                spread.start()
                spread.wait()
                spread.finish()
            else:
                store().start()
                store().wait()
            for c in crosses:
                c.finish()

        acts = [(self.times[0], first)]
        acts += [(self.times[1], c.bring) for c in crosses] + [(self.times[2], c.take) for c in crosses]
        return acts + [(self.times[3], last)]


LANES = 128
HEADS = Q_RANK + 2 * KV_RANK


def head_lanes():
    half = HEAD_SIZE // 2
    column = jnp.arange(HEADS * HEAD_SIZE, dtype=jnp.int32)
    head, inner = column // HEAD_SIZE, column % HEAD_SIZE
    lane = head * LANES + jnp.where(inner < half, inner, inner - half + LANES // 2)
    return (lane[:, None] == jnp.arange(HEADS * LANES, dtype=jnp.int32)[None, :]).astype(BF)


def pad_weights(lanes_ref, qkv_ref, out_ref, qkv_wide, out_wide):
    def qkv_tile(j):
        at = pl.ds(j, TILE)
        qkv_wide[at, :] = dot(qkv_ref[at, :], lanes_ref[...]).astype(BF)

    column_tiles(D, TILE, qkv_tile)
    heads = lanes_ref[: Q_RANK * HEAD_SIZE, : Q_RANK * LANES]

    def out_tile(j):
        cols = pl.ds(j, TILE)
        out_wide[:, cols] = dot(heads, out_ref[:, cols], ((0,), (0,))).astype(BF)

    column_tiles(D, TILE, out_tile)


def masked(scores, first, start_ref):
    count, keys = scores.shape
    query = lax.broadcasted_iota(jnp.int32, scores.shape, 0) + first
    key = lax.broadcasted_iota(jnp.int32, scores.shape, 1)
    start = start_ref[first : first + count, :]
    return jnp.where((key <= query) & (key >= start), scores, masked_score)


def attention_forward_call(residual, gain, w_qkv, w_out, common, beside, collective_id):
    lanes, cosines, sines, starts = common
    rows = residual.shape[0]
    count = 4 * rows
    scale = HEAD_SIZE ** (-0.5)

    def body(p, ins, outs, scratch, advance, staged):
        res_ref, gain_ref, qkv_ref, out_ref, lanes_ref, cos_ref, sin_ref, start_ref = ins
        new_ref, every, heads_ref, att_ref = outs
        qkv_wide, out_wide = scratch[:2]
        own, terms, share, total = exchange_of(p, every, scratch[2:])

        def project(pieces, n):
            places = token_rows(pieces, n, rows)
            both = lambda ref: jnp.concatenate([ref[at, :] for at in places], axis=0)
            cos, sin = both(cos_ref), both(sin_ref)
            x = gather_pieces(every, pieces, n)
            for j in range(0, HEADS, 4):
                wide = dot(x, qkv_wide[:, j * LANES : (j + 4) * LANES])
                for k in range(4):
                    value = wide[:, k * LANES : (k + 1) * LANES]
                    if j + k < Q_RANK + KV_RANK:
                        value = value * cos + pltpu.roll(value, LANES // 2, 1) * sin
                    for m, at in enumerate(places):
                        heads_ref[j + k, at, :] = value[m * n : (m + 1) * n].astype(BF)

        def attend(j, _):
            g = lax.div(j, Q_RANK // KV_RANK)
            for first in range(0, count, rows):
                n = first + rows
                q = heads_ref[j, first:n, :]
                scores = dot(q, heads_ref[Q_RANK + g, :n, :], ((1,), (1,))) * scale
                scores = masked(scores, first, start_ref)
                top = jnp.max(scores, axis=1, keepdims=True)
                shifted = jnp.exp(scores - top)
                amount = jnp.sum(shifted, axis=1, keepdims=True)
                weights = (shifted / amount).astype(BF)
                att_ref[j, first:n, :] = dot(weights, heads_ref[Q_RANK + KV_RANK + g, :n, :]).astype(BF)
            return 0

        def project_out(pieces, n):
            places = token_rows(pieces, n, rows)
            wide = jnp.concatenate(
                [jnp.concatenate([att_ref[j, at, :] for j in range(Q_RANK)], axis=1) for at in places], axis=0
            )

            def tile(j):
                cols = pl.ds(j, DOWN_TILE)
                scatter_pieces(terms, pieces, n, dot(wide, out_wide[:, cols]).astype(BF), cols)

            column_tiles(D, DOWN_TILE, tile)

        row_normalize(res_ref, gain_ref, own)
        share.start()
        advance()
        staged.ready(2, 3, 4)
        pad_weights(lanes_ref, qkv_ref, out_ref, qkv_wide, out_wide)
        staged.ready(5, 6)
        project([(p.rank, 0)], rows)
        share.across(True).wait_recv()
        project([(p.sibling, 0)], rows)
        advance()
        part = rows // CHUNKS
        for k in range(CHUNKS):
            share.pass_on(k)
            share.far(k)
            project([(p.diagonal, k * part), (p.over, k * part)], part)
            advance()
        staged.flush(1, 2)
        for j in range(0, Q_RANK, 2):
            lax.fori_loop(j, j + 2, attend, 0)
            advance()
        for k in range(CHUNKS):
            project_out([(p.diagonal, k * part), (p.over, k * part)], part)
            total.diagonal(k).start()
            total.relay(k)
            advance()
        staged.flush(3)
        project_out([(p.sibling, 0)], rows)
        total.sibling().start()
        project_out([(p.rank, 0)], rows)
        advance()

        def write(at, value):
            new_ref[at, :] = res_ref[at, :] + value

        collect(p, total, write)
        advance.finish()
        share.finish()
        total.finish()

    return beside_call(
        body,
        (residual, gain.reshape(1, D), w_qkv, w_out, lanes, cosines, sines, starts),
        (4, 2, 3, 5, 6),
        [
            jax.ShapeDtypeStruct((rows, D), F32),
            jax.ShapeDtypeStruct((4, rows, D), BF),
            jax.ShapeDtypeStruct((HEADS, count, LANES), BF),
            jax.ShapeDtypeStruct((Q_RANK, count, LANES), BF),
        ],
        (1, 2, 3),
        [pltpu.VMEM((D, HEADS * LANES), BF), pltpu.VMEM((Q_RANK * LANES, D), BF)] + exchange_scratch(rows),
        beside,
        "attention_forward",
        collective_id,
        2 * count * D * (HEADS + Q_RANK) * LANES,
    )


def attention_backward_call(grad, residual, gain, w_qkv, w_out, kept, common, beside, collective_id, dtype=F32):
    lanes, cosines, sines, starts = common
    every, heads, attended = kept
    rows = residual.shape[0]
    count = 4 * rows
    scale = HEAD_SIZE ** (-0.5)

    def body(p, ins, outs, scratch, advance, staged):
        (grad_ref, res_ref, gain_ref, qkv_ref, out_ref, lanes_ref, cos_ref, sin_ref, start_ref) = ins[:9]
        every_ref, heads_ref, att_ref = ins[9:]
        new_ref, gain_out, g_qkv, s_out = outs
        qkv_wide, out_wide, e, d_att, d_k, d_v, d_heads = scratch[:7]
        soft, g_out = scratch[7:9]
        reduce = out_reduce_steps(p, g_out, s_out, *scratch[9:16])
        own, terms, share, total = exchange_of(p, e, scratch[16:])

        def copy_own(k, _):
            at = pl.ds(pl.multiple_of(k * 32, 32), 32)
            own[at, :] = grad_ref[at, :].astype(BF)
            return 0

        lax.fori_loop(0, rows // 32, copy_own, 0)

        def back_out(pieces, n):
            wide = dot(gather_pieces(e, pieces, n), out_wide[...], ((1,), (1,)))
            for m, at in enumerate(token_rows(pieces, n, rows)):
                for j in range(Q_RANK):
                    d_att[j, at, :] = wide[m * n : (m + 1) * n, j * LANES : (j + 1) * LANES].astype(BF)

        def attend(j, _):
            g = lax.div(j, Q_RANK // KV_RANK)
            for first in range(0, count, rows):
                n = first + rows
                q, d_o = heads_ref[j, first:n, :], d_att[j, first:n, :]
                k, v = heads_ref[Q_RANK + g, :n, :], heads_ref[Q_RANK + KV_RANK + g, :n, :]
                rounded = soft[j, :, soft_lanes(first)]
                weights = rounded.astype(F32)
                d_weights = dot(d_o, v, ((1,), (1,)))
                inner = jnp.sum(weights * d_weights, axis=1, keepdims=True)
                d_scores = (weights * (d_weights - inner)).astype(BF)
                d_v[g, :n, :] += dot(rounded, d_o, ((0,), (0,)))
                d_k[g, :n, :] += dot(d_scores, q, ((0,), (0,)))
                d_q = dot(d_scores, k) * scale
                d_heads[j, first:n, :] = turn_back(d_q, cos_ref[first:n, :], sin_ref[first:n, :])
            return 0

        def soft_lanes(first):
            k = first // rows
            at = k * (k + 1) // 2 * rows
            return slice(at, at + first + rows)

        def keep_weights(j, _):
            g = lax.div(j, Q_RANK // KV_RANK)
            for first in range(0, count, rows):
                n = first + rows
                scores = dot(heads_ref[j, first:n, :], heads_ref[Q_RANK + g, :n, :], ((1,), (1,))) * scale
                scores = masked(scores, first, start_ref)
                shifted = jnp.exp(scores - jnp.max(scores, axis=1, keepdims=True))
                amount = jnp.sum(shifted, axis=1, keepdims=True)
                soft[j, :, soft_lanes(first)] = (shifted / amount).astype(BF)
            return 0

        def turn_back(value, cos, sin):
            return (value * cos - pltpu.roll(value, LANES // 2, 1) * sin).astype(BF)

        def keys_back():
            for g in range(KV_RANK):
                for first in range(0, count, rows):
                    at = slice(first, first + rows)
                    d_heads[Q_RANK + g, at, :] = turn_back(d_k[g, at, :] * scale, cos_ref[at, :], sin_ref[at, :])
                    d_heads[Q_RANK + KV_RANK + g, at, :] = d_v[g, at, :].astype(BF)

        def project_back(pieces, n):
            wide = jnp.concatenate(
                [
                    jnp.concatenate([d_heads[j, at, :] for j in range(HEADS)], axis=1)
                    for at in token_rows(pieces, n, rows)
                ],
                axis=0,
            )

            def tile(j):
                cols = pl.ds(j, DOWN_TILE)
                value = dot(wide, qkv_wide[cols, :], ((1,), (1,))).astype(BF)
                scatter_pieces(terms, pieces, n, value, cols)

            column_tiles(D, DOWN_TILE, tile)

        def out_grads():
            e_all = e.reshape(count, D)

            def out_grad(j):
                cols = pl.ds(j, TILE)
                wide = jnp.concatenate(
                    [dot(att_ref[h], e_all[:, cols], ((0,), (0,))) for h in range(Q_RANK)], axis=0
                ).astype(BF)
                value = dot(lanes_ref[: Q_RANK * HEAD_SIZE, : Q_RANK * LANES], wide).astype(BF)
                for h in range(Q_RANK):
                    g_out[h, :, cols] = value[h * HEAD_SIZE : (h + 1) * HEAD_SIZE]

            column_tiles(D, TILE, out_grad)

        def weight_grads():
            x_all = every_ref.reshape(count, D)

            def qkv_grad(j):
                cols = pl.ds(j, TILE)
                wide = jnp.concatenate(
                    [dot(x_all[:, cols], d_heads[h], ((0,), (0,))) for h in range(HEADS)], axis=1
                ).astype(BF)
                g_qkv[cols, :] = dot(wide, lanes_ref[...], ((1,), (1,))).astype(BF)

            column_tiles(D, TILE, qkv_grad)

        share.start()
        advance()
        staged.ready(3, 4, 5)
        pad_weights(lanes_ref, qkv_ref, out_ref, qkv_wide, out_wide)
        staged.ready(10)
        lax.fori_loop(0, Q_RANK, keep_weights, 0)
        d_k[...] = jnp.zeros_like(d_k)
        d_v[...] = jnp.zeros_like(d_v)
        back_out([(p.rank, 0)], rows)
        share.across(True).wait_recv()
        back_out([(p.sibling, 0)], rows)
        advance()
        part = rows // CHUNKS
        for k in range(CHUNKS):
            share.pass_on(k)
            share.far(k)
            back_out([(p.diagonal, k * part), (p.over, k * part)], part)
            advance()
        staged.ready(11)
        out_grads()
        reduce[0]()
        staged.ready(6, 7)
        for j in range(0, Q_RANK, 2):
            lax.fori_loop(j, j + 2, attend, 0)
            advance()
        reduce[1]()
        keys_back()
        for k in range(CHUNKS):
            project_back([(p.diagonal, k * part), (p.over, k * part)], part)
            total.diagonal(k).start()
            total.relay(k)
            advance()
        project_back([(p.sibling, 0)], rows)
        total.sibling().start()
        project_back([(p.rank, 0)], rows)
        advance()
        reduce[2]()
        staged.ready(9)
        weight_grads()
        staged.flush(2)
        reduce[3]()
        advance()
        gain_out[...] = jnp.zeros_like(gain_out)

        def write(at, value):
            res = res_ref[at, :].astype(F32)
            normed = normalize(res)
            gain_out[...] += jnp.sum(value * normed, axis=0, keepdims=True)
            back = norm_back(value * gain_ref[...], normed, res)
            new_ref[at, :] = (grad_ref[at, :] + back).astype(dtype)

        collect(p, total, write)
        advance.finish()
        reduce[4]()
        share.finish()
        total.finish()

    return beside_call(
        body,
        (grad, residual, gain.reshape(1, D), w_qkv, w_out, lanes, cosines, sines, starts, every, heads, attended),
        (5, 3, 4, 10, 11, 6, 7, 9),
        [
            jax.ShapeDtypeStruct((rows, D), dtype),
            jax.ShapeDtypeStruct((1, D), F32),
            jax.ShapeDtypeStruct((D, HEADS * HEAD_SIZE), BF),
            jax.ShapeDtypeStruct((HEAD_SIZE // 2, D), BF),
        ],
        (2,),
        [
            pltpu.VMEM((D, HEADS * LANES), BF),
            pltpu.VMEM((Q_RANK * LANES, D), BF),
            pltpu.VMEM((4, rows, D), BF),
            pltpu.VMEM((Q_RANK, count, LANES), BF),
            pltpu.VMEM((KV_RANK, count, LANES), F32),
            pltpu.VMEM((KV_RANK, count, LANES), F32),
            pltpu.VMEM((HEADS, count, LANES), BF),
            pltpu.VMEM((Q_RANK, rows, 10 * rows), BF),
        ]
        + out_reduce_scratch((HEAD_SIZE, D))
        + exchange_scratch(rows),
        beside,
        "attention_backward",
        collective_id,
        6 * count * D * (HEADS + Q_RANK) * LANES,
        ("c", "z0", "x", "y", "z1"),
        {3: ANY},
    )


def lane_rows():
    half, space = HEAD_SIZE // 2, LANES // 2 - HEAD_SIZE // 2
    index = jnp.arange(half, dtype=jnp.float32)
    inverse = jnp.pad(rope_base ** (-2.0 * index / HEAD_SIZE), (0, space))
    ones = jnp.pad(jnp.ones(half, F32), (0, space))
    row = lambda a, b: jnp.concatenate([a, b])
    return jnp.stack([row(inverse, inverse), row(ones, ones), row(-ones, ones)])


def rank_columns(ref, l, c, x):
    pieces = []
    for start, width in (
        (0, 2 * HEAD_SIZE),
        (QUERY_HEAD_COUNT * HEAD_SIZE, HEAD_SIZE),
        ((QUERY_HEAD_COUNT + KEY_VALUE_HEADS) * HEAD_SIZE, HEAD_SIZE),
    ):
        for y in (0, 1):
            at = start + (4 * y + 2 * x + c) * width
            pieces.append(ref[l][:, at : at + width])
    return jnp.concatenate(pieces, axis=1).astype(BF)


def first_call(tokens, lengths, w_qkv, w_out, w_gateup, w_down, gains, collective_id):
    rows = w_qkv.shape[1]
    count = 4 * tokens.shape[0]
    ranks = lambda w: jax.ShapeDtypeStruct((4, rows, w.shape[2] // 4), BF)
    shard = jax.ShapeDtypeStruct(w_out.shape[1:], BF)
    down_rows = w_down.shape[1] // 2
    half = jax.ShapeDtypeStruct((2, down_rows, D), BF)
    gather = GatherWeights(
        columns=ranks(w_qkv), out=shard, gains=gains, columns_at=times(1, (2, 2), (2, 2), 3, (4, 4), (6, 6)),
        out_at=(-1, 1, 3, 5, 99), gains_at=(1, 2, 3, 4, 5, 99),
    )
    meet = MeetBlocks(half, at=(0, 1, 1))
    spread = SpreadColumns(ranks(w_gateup), ranks(w_qkv), ranks(w_gateup))
    swap = SwapRows(tokens)
    works = (gather, spread, swap, meet)
    unit = w_gateup.shape[2] // 64

    def body(*refs):
        refs = list(refs)
        take = lambda n: [refs.pop(0) for _ in range(n)]
        tokens_ref, lengths_ref, qkv_ref, out_ref, gu_ref, down_ref, gains_ref, lanes_ref = take(8)
        down0, down1, out1, cos_ref, sin_ref, start_ref = take(6)
        outs = [take(len(w.shapes)) for w in works]
        qkv0, qkv1, gu0, gu1, out0 = take(5)
        scratch = [take(len(w.scratch)) for w in works]
        p = Place()
        greet(p, EIGHT + GROUP + ("swap", "mid"))
        clock = Clock(gather.steps(p, [qkv0, out0, gains_ref], outs[0], scratch[0]))

        def pack_heads(l, dst):
            for c in (0, 1):
                for x in (0, 1):
                    dst[2 * c + x] = rank_columns(qkv_ref, l, c, x)

        def pack_units(l, dst):
            for chunk in range(64):
                z0, z1, c, rest = chunk % 2, chunk // 2 % 2, chunk // 4 % 2, chunk // 8
                at = (rest * 2 + z1) * unit
                dst[2 * c + z0, :, at : at + unit] = gu_ref[l, :, chunk * unit : (chunk + 1) * unit].astype(BF)

        pack_heads(0, qkv0)
        out0[...] = out_ref[0].astype(BF)
        clock()
        clock()
        for h in (0, 1):
            part = slice(h * down_rows, (h + 1) * down_rows)
            down0[h] = down_ref[0, part, :].astype(BF)
            down1[h] = down_ref[1, part, :].astype(BF)
        out1[...] = out_ref[1].astype(BF)
        pack_units(0, gu0)
        pack_heads(1, qkv1)
        pack_units(1, gu1)
        clock()
        later = Clock(
            meet.steps(p, [down0], outs[3], scratch[3])
            + spread.steps(p, [gu0, qkv1, gu1], outs[1], scratch[1])
            + swap.steps(p, [tokens_ref], outs[2], scratch[2])
        )
        later()

        def begin(places):
            start, end = jnp.zeros_like(places), 0
            for k in range(lengths.shape[1]):
                length = lengths_ref[0, k]
                end = end + length
                start = start + jnp.where(places >= end, length, 0)
            return start

        def table(k, _):
            at = pl.ds(pl.multiple_of(k * TILE, TILE), TILE)
            places = lax.broadcasted_iota(jnp.int32, (TILE, LANES), 0) + k * TILE
            angles = (places - begin(places)).astype(F32) * lanes_ref[0:1, :]
            cos_ref[at, :] = jnp.cos(angles) * lanes_ref[1:2, :]
            sin_ref[at, :] = jnp.sin(angles) * lanes_ref[2:3, :]
            start_ref[at, :] = begin(lax.broadcasted_iota(jnp.int32, (TILE, 1), 0) + k * TILE)
            return 0

        lax.fori_loop(0, count // TILE, table, 0)
        later()
        clock.finish()
        later.finish()

    vmem = lambda s: pltpu.VMEM(s.shape, BF)
    made = [half, half, shard, *([jax.ShapeDtypeStruct((count, LANES), F32)] * 2), jax.ShapeDtypeStruct((count, 1), jnp.int32)]
    out = pl.pallas_call(
        body,
        out_shape=made + [s for w in works for s in w.shapes],
        in_specs=[VM, pl.BlockSpec(memory_space=pltpu.SMEM)] + [VM] * 6,
        out_specs=[VM] * len(made) + [ANY for w in works for _ in w.shapes],
        scratch_shapes=[vmem(ranks(w_qkv)), vmem(ranks(w_qkv)), vmem(ranks(w_gateup)), vmem(ranks(w_gateup)), vmem(shard)]
        + [s for w in works for s in w.scratch],
        compiler_params=wide_params(collective_id),
        name="first_weights",
    )(tokens, lengths, w_qkv, w_out, w_gateup, w_down, gains, lane_rows())
    return out


def stepped(weight, gradient, first, second, rate, shrink):
    return adam_step(weight, gradient.astype(F32), first, second, rate, shrink)


def update_gateup(weight, first, second, parts, rate, shrink):
    rows, columns = weight.shape[1:]
    blocks = 8
    wide, thin = columns // blocks, columns // 4 // blocks
    unit = thin // 2

    def body(w_ref, m_ref, v_ref, *refs):
        grads, (w_out, m_out, v_out) = refs[:-3], refs[-3:]

        def run(g_ref):
            for c in (0, 1):
                for z1 in (0, 1):
                    for z0 in (0, 1):
                        at = pl.ds(((c * 2 + z1) * 2 + z0) * unit, unit)
                        grad = g_ref[2 * c + z0, :, pl.ds(z1 * unit, unit)]
                        new = stepped(w_ref[0, :, at], grad, m_ref[0, :, at], v_ref[0, :, at], rate, shrink)
                        w_out[0, :, at], m_out[0, :, at], v_out[0, :, at] = new

        for l, g_ref in enumerate(grads):
            pl.when(pl.program_id(0) == l)(functools.partial(run, g_ref))

    big = pl.BlockSpec((1, rows, wide), lambda l, j: (l, 0, j))
    small = [
        pl.BlockSpec((4, rows, thin), lambda l, j, k=k: (0, 0, jnp.where(l == k, j, 0 if k else blocks - 1)))
        for k in range(LAYERS)
    ]
    return pl.pallas_call(
        body,
        grid=(LAYERS, blocks),
        in_specs=[big] * 3 + small,
        out_specs=[big] * 3,
        out_shape=[jax.ShapeDtypeStruct(weight.shape, F32)] * 3,
        compiler_params=pltpu.CompilerParams(vmem_limit_bytes=32 * 2**20),
        name="update_gateup",
    )(weight, first, second, *parts)


def update_rows(weight, first, second, parts, rate, shrink):
    rows, columns = weight.shape[1:]
    blocks = 2
    wide = columns // blocks

    def body(w_ref, m_ref, v_ref, *refs):
        grads, (w_out, m_out, v_out) = refs[:-3], refs[-3:]

        def run(g_ref):
            w_out[0], m_out[0], v_out[0] = stepped(w_ref[0], g_ref[...], m_ref[0], v_ref[0], rate, shrink)

        for l, g_ref in enumerate(grads):
            pl.when(pl.program_id(0) == l)(functools.partial(run, g_ref))

    big = pl.BlockSpec((1, rows, wide), lambda l, j: (l, 0, j))
    small = [
        pl.BlockSpec((rows, wide), lambda l, j, k=k: (0, jnp.where(l == k, j, 0 if k else blocks - 1)))
        for k in range(LAYERS)
    ]
    return pl.pallas_call(
        body,
        grid=(LAYERS, blocks),
        in_specs=[big] * 3 + small,
        out_specs=[big] * 3,
        out_shape=[jax.ShapeDtypeStruct(weight.shape, F32)] * 3,
        compiler_params=pltpu.CompilerParams(vmem_limit_bytes=32 * 2**20),
        name="update_rows",
    )(weight, first, second, *parts)


def update_qkv(weight, first, second, parts, rate, shrink):
    rows, columns = weight.shape[1:]
    q_wide, kv_wide = QUERY_HEAD_COUNT * HEAD_SIZE, KEY_VALUE_HEADS * HEAD_SIZE

    def body(w_ref, m_ref, v_ref, *refs):
        grads, (w_out, m_out, v_out) = refs[:-3], refs[-3:]

        def run(g_ref):
            pieces = []
            for start, width in ((0, 2 * HEAD_SIZE), (4 * HEAD_SIZE, HEAD_SIZE), (6 * HEAD_SIZE, HEAD_SIZE)):
                for y in (0, 1):
                    for x in (0, 1):
                        for c in (0, 1):
                            at = start + y * width
                            pieces.append(g_ref[2 * c + x].astype(F32)[:, at : at + width])
            grad = jnp.concatenate(pieces, axis=1)
            w_out[0], m_out[0], v_out[0] = stepped(w_ref[0], grad, m_ref[0], v_ref[0], rate, shrink)

        for l, g_ref in enumerate(grads):
            pl.when(pl.program_id(0) == l)(functools.partial(run, g_ref))

    big = pl.BlockSpec((1, rows, columns), lambda l: (l, 0, 0))
    small = [pl.BlockSpec((4, rows, columns // 4), lambda l: (0, 0, 0))] * LAYERS
    return pl.pallas_call(
        body,
        grid=(LAYERS,),
        in_specs=[big] * 3 + small,
        out_specs=[big] * 3,
        out_shape=[jax.ShapeDtypeStruct(weight.shape, F32)] * 3,
        compiler_params=pltpu.CompilerParams(vmem_limit_bytes=32 * 2**20),
        name="update_qkv",
    )(weight, first, second, *parts)


def links_call(beside, name, collective_id):
    return beside_call(
        lambda p, ins, outs, scratch, advance, staged: advance.finish(),
        (), (), [], (), [], beside, name, collective_id, 0, peers=(),
    )[1]


def fast_shards(
    tokens, cotangent, lengths, w_qkv, w_out, w_gateup, w_down, norm_gains, *moments
):
    axes = ("fsdp", "seq")
    pairs = swap_pairs(lax.axis_size("fsdp"), lax.axis_size("seq"))
    lengths = lax.ppermute(lengths, axes, pairs)
    rows, owned = w_qkv.shape[1], norm_gains.shape[2]
    own_gains = jnp.pad(
        norm_gains.reshape(2 * LAYERS, owned).astype(BF), ((0, 16 - 2 * LAYERS), (0, lane_width - owned))
    )
    own_down0, own_down1, own_out1, *places, qkv0, out0, got_gains, own_gu0, own_qkv1, own_gu1, start, met_down0 = (
        first_call(tokens, lengths, w_qkv, w_out, w_gateup, w_down, own_gains, 0)
    )
    common = (head_lanes(), *places)
    all_gains = got_gains[:, : 2 * LAYERS, :owned].transpose(1, 0, 2).reshape(LAYERS, 2, D).astype(F32)
    matrix = lambda g: g.reshape(D, -1)
    stack = lambda g: g.reshape(-1, D)
    alone = times(0, (1, 1), (3, 4), 3, (4, 5), (7, 8))
    ahead = times(0, None, None, 3, None, (4, 4))
    (middle0, *first0), (gu0, down0, met_qkv1, met_down1, met_out1) = attention_forward_call(
        start, all_gains[0, 0], matrix(qkv0), stack(out0), common,
        Both(
            GatherWeights(columns=own_gu0, columns_at=alone),
            GatherWeights(down=own_down0, met=(met_down0,), down_at=times(0, None, None, 3, None, (5, 5))),
            MeetBlocks(own_qkv1, own_down1, at=(0, 4, 6)),
            MeetOut(own_out1, at=(0, 5)),
        ), 1,
    )
    (later0, *second0), (out1, qkv1, down1, met_gu1) = feed_forward_call(
        middle0, all_gains[0, 1], matrix(gu0), stack(down0),
        Both(
            GatherOut(met_out1),
            GatherWeights(columns=own_qkv1, met=(met_qkv1,), columns_at=ahead),
            GatherWeights(down=own_down1, met=(met_down1,), down_at=ahead),
            MeetBlocks(own_gu1, at=(0, 3, 4)),
        ), 2,
    )
    (middle1, *first1), (gu1, cotangent) = attention_forward_call(
        later0, all_gains[1, 0], matrix(qkv1), stack(out1), common,
        Both(
            GatherWeights(columns=own_gu1, met=(met_gu1,), columns_at=times(0, None, None, 3, None, (6, 7))),
            SwapRows(cotangent, 3),
        ), 3,
    )
    (later1, *second1), _ = feed_forward_call(
        middle1, all_gains[1, 1], matrix(gu1), stack(down1), Nothing(), 4, BF
    )
    wide = lambda g: g.reshape(16, 2 * rows, -1)
    (grad, gain11, g_gu1, two_down1), _ = feed_backward_call(
        cotangent, middle1, all_gains[1, 1], matrix(gu1), stack(down1), second1, Nothing(), 5
    )
    (grad, gain10, g_qkv1, s_out1), (two_gu1, s_down1, layer_output) = attention_backward_call(
        grad, later0, all_gains[1, 0], matrix(qkv1), stack(out1), first1, common,
        Both(
            ReduceWeights(columns=wide(g_gu1), open=True, at=(0, 4, 4, 5, 5, 9, 10, 11, 99)),
            FinishColumns(two_down1, at=(1, 3, 4, 6)),
            SwapRows(later1, 4),
        ), 6,
    )
    (grad, gain01, g_gu0, two_down0), (s_qkv1,) = feed_backward_call(
        grad, middle0, all_gains[0, 1], matrix(gu0), stack(down0), second0,
        ReduceWeights(columns=wide(g_qkv1), at=(0, 2, 2, 3, 3, 4, 4, 7, 99)), 7,
    )
    (grad, gain00, g_qkv0, s_out0), (two_gu0, s_down0, s_gu1) = attention_backward_call(
        grad, start, all_gains[0, 0], matrix(qkv0), stack(out0), first0, common,
        Both(
            ReduceWeights(columns=wide(g_gu0), open=True, at=(0, 4, 4, 5, 5, 9, 10, 11, 99)),
            FinishColumns(two_down0, at=(1, 3, 4, 6)),
            FinishColumns(two_gu1, at=(2, 4, 5, 9)),
        ), 8, BF,
    )
    terms = jnp.concatenate([gain00, gain01, gain10, gain11]).reshape(2 * LAYERS, -1, owned).transpose(1, 0, 2)
    terms = jnp.pad(terms, ((0, 0), (0, 8 - 2 * LAYERS), (0, lane_width - owned)))
    split = lambda g: g.reshape(2, 2, rows, -1)
    s_gu0, s_qkv0, s_gains, s_gu1, s_qkv1, input_grad = links_call(
        Both(
            FinishColumns(two_gu0, collect=True, at=(0, 1, 1, 4)),
            ReduceWeights(columns=wide(g_qkv0), gains=terms, collect=True, at=(0, 2, 2, 3, 3, 3, 3, 5, 7)),
            CollectColumns(split(s_gu1), split(s_qkv1), at=1),
            SwapRows(grad, 2),
        ),
        "last_gradients",
        9,
    )
    flat = lambda g: g.reshape(-1, D)
    update = {
        "qkv": (s_qkv0, s_qkv1),
        "out": (s_out0, s_out1),
        "gateup": (s_gu0, s_gu1),
        "down": (flat(s_down0), flat(s_down1)),
        "gains": s_gains[: 2 * LAYERS, :owned].reshape(LAYERS, 2, owned),
    }
    return (layer_output, input_grad.astype(F32)) + update_all(
        (w_qkv, w_out, w_gateup, w_down, norm_gains), moments, update
    )


def update_all(stacked, moments, update):
    step_rates = (D ** (-0.5), 4.0 * D ** (-0.5), D ** (-0.5), FF ** (-0.5), 0.5)
    shrinks = (decay_rate, decay_rate, decay_rate, decay_rate, 0.0)
    ways = (update_qkv, update_rows, update_gateup, update_rows, adam_step)
    results = []
    for kind, (name, way) in enumerate(zip(update, ways)):
        weight, first, second = stacked[kind], moments[kind], moments[5 + kind]
        if kind == 4:
            results.append(way(weight, update[name], first, second, step_rates[kind], shrinks[kind]))
        else:
            results.append(way(weight, first, second, update[name], step_rates[kind], shrinks[kind]))
    return tuple(results[kind][part] for part in range(3) for kind in range(5))


def solution(mesh):
    in_specs = (
        P(("fsdp", "seq"), None),
        P(("fsdp", "seq"), None),
        P("fsdp", None),
        P(None, ("fsdp", "seq"), None),
        P(None, ("fsdp", "seq"), None),
        P(None, ("fsdp", "seq"), None),
        P(None, ("fsdp", "seq"), None),
        P(None, None, ("fsdp", "seq")),
        P(None, ("fsdp", "seq"), None),
        P(None, ("fsdp", "seq"), None),
        P(None, ("fsdp", "seq"), None),
        P(None, ("fsdp", "seq"), None),
        P(None, None, ("fsdp", "seq")),
        P(None, ("fsdp", "seq"), None),
        P(None, ("fsdp", "seq"), None),
        P(None, ("fsdp", "seq"), None),
        P(None, ("fsdp", "seq"), None),
        P(None, None, ("fsdp", "seq")),
    )
    out_specs = (
        P(("fsdp", "seq"), None),
        P(("fsdp", "seq"), None),
        P(None, ("fsdp", "seq"), None),
        P(None, ("fsdp", "seq"), None),
        P(None, ("fsdp", "seq"), None),
        P(None, ("fsdp", "seq"), None),
        P(None, None, ("fsdp", "seq")),
        P(None, ("fsdp", "seq"), None),
        P(None, ("fsdp", "seq"), None),
        P(None, ("fsdp", "seq"), None),
        P(None, ("fsdp", "seq"), None),
        P(None, None, ("fsdp", "seq")),
        P(None, ("fsdp", "seq"), None),
        P(None, ("fsdp", "seq"), None),
        P(None, ("fsdp", "seq"), None),
        P(None, ("fsdp", "seq"), None),
        P(None, None, ("fsdp", "seq")),
    )
    whole_tiles = (D // mesh.size) % 16 == 0 and mesh.shape["seq"] == 4 and mesh.size == 32
    body = fast_shards if whole_tiles else shards
    return jax.shard_map(body, mesh=mesh, in_specs=in_specs, out_specs=out_specs, check_vma=False)
```

```python
import functools

import jax
import jax.numpy as jnp
from jax import lax
from jax.experimental import pallas as pl
from jax.experimental.pallas import tpu as pltpu
from jax.sharding import PartitionSpec as P

D = 1536
QUERY_HEAD_COUNT = 16
KEY_VALUE_HEADS = 8
HEAD_SIZE = 96
FF = 4096
LAYERS = 2
STEP = 6


eps_norm = 1e-05
rope_base = 100000.0
beta_one = 0.9
beta_two = 0.95
adam_eps = 1e-08
decay_rate = 0.1
masked_score = -1e30
lane_width = 128


def layout(length_row, places):
    seq_ends = jnp.cumsum(length_row, dtype=jnp.int32)
    passed = (places[:, None] >= seq_ends[None, :]).astype(jnp.int32)
    segment = jnp.sum(passed, axis=1, dtype=jnp.int32)
    begins = jnp.sum(passed * length_row[None, :], axis=1, dtype=jnp.int32)
    return (segment, places - begins)


def tables(positions):
    freq_index = jnp.arange(HEAD_SIZE // 2, dtype=jnp.float32)
    inverse = rope_base ** (-2.0 * freq_index / HEAD_SIZE)
    angles = positions.astype(jnp.float32)[:, None] * inverse[None, :]
    angles = jnp.concatenate([angles, angles], axis=-1)
    return (jnp.cos(angles)[:, None, :], jnp.sin(angles)[:, None, :])


def apply_rotary(values, rotary_cosines, rotary_sines):
    half_width = values.shape[-1] // 2
    turned = jnp.concatenate([-values[..., half_width:], values[..., :half_width]], axis=-1)
    return values * rotary_cosines + turned * rotary_sines


def invert_rotary(values, rotary_cosines, rotary_sines):
    half_width = values.shape[-1] // 2
    scaled_sine = values * rotary_sines
    turned = jnp.concatenate(
        [scaled_sine[..., half_width:], -scaled_sine[..., :half_width]], axis=-1
    )
    return values * rotary_cosines + turned


def normalize(residual):
    return residual * lax.rsqrt(jnp.mean(residual * residual, axis=-1, keepdims=True) + eps_norm)


def norm_back(grad_normed, normed, residual):
    inverse = lax.rsqrt(jnp.mean(residual * residual, axis=-1, keepdims=True) + eps_norm)
    return inverse * (grad_normed - normed * jnp.mean(grad_normed * normed, axis=-1, keepdims=True))


def product(lhs_matrix, rhs_matrix):
    return jnp.dot(lhs_matrix, rhs_matrix, preferred_element_type=jnp.float32)


def attention_scores(query_head_rows, key_head_rows, allowed):
    scores = jnp.einsum(
        "qgrd,kgd->grqk", query_head_rows, key_head_rows, preferred_element_type=jnp.float32
    ) * HEAD_SIZE ** (-0.5)
    return jnp.where(allowed[None, None], scores, masked_score)


def wire_pieces(stacked, layer_index):
    return tuple((shard_piece[layer_index].astype(jnp.bfloat16) for shard_piece in stacked))


def fetch_forward(stacked, layer_index):
    qkv_piece, out_piece, gateup_piece, down_piece, gain_piece = wire_pieces(stacked, layer_index)
    return (
        lax.all_gather(qkv_piece, ("fsdp", "seq"), axis=0, tiled=True),
        lax.all_gather(out_piece, ("fsdp", "seq"), axis=0, tiled=True),
        lax.all_gather(gateup_piece, ("fsdp", "seq"), axis=0, tiled=True),
        lax.all_gather(down_piece, ("fsdp", "seq"), axis=0, tiled=True),
        lax.all_gather(gain_piece, ("fsdp", "seq"), axis=1, tiled=True),
    )


def fetch_backward(stacked, layer_index):
    qkv_piece, out_piece, gateup_piece, down_piece, gain_piece = wire_pieces(stacked, layer_index)
    return (
        lax.all_gather(qkv_piece, ("fsdp", "seq"), axis=0, tiled=True),
        lax.all_gather(out_piece, ("fsdp", "seq"), axis=0, tiled=True),
        lax.all_gather(gateup_piece, ("fsdp", "seq"), axis=0, tiled=True),
        lax.all_gather(down_piece, ("fsdp", "seq"), axis=0, tiled=True),
        lax.all_gather(gain_piece, ("fsdp", "seq"), axis=1, tiled=True),
    )


def flat_lanes(matrix):
    return matrix.reshape(-1, lane_width)


def reduce_grads(grad_terms):
    grad_qkv, grad_out_proj, grad_gateup, grad_down, grad_gains = grad_terms
    widths = (grad_qkv.shape[1], grad_out_proj.shape[1], grad_gateup.shape[1], grad_down.shape[1])
    flat_qkv = flat_lanes(grad_qkv)
    flat_out = flat_lanes(grad_out_proj)
    flat_gateup = flat_lanes(grad_gateup)
    flat_down = flat_lanes(grad_down)
    summed = (
        lax.psum_scatter(flat_qkv, ("fsdp", "seq"), scatter_dimension=0, tiled=True),
        lax.psum_scatter(flat_out, ("fsdp", "seq"), scatter_dimension=0, tiled=True),
        lax.psum_scatter(flat_gateup, ("fsdp", "seq"), scatter_dimension=0, tiled=True),
        lax.psum_scatter(flat_down, ("fsdp", "seq"), scatter_dimension=0, tiled=True),
        lax.psum_scatter(grad_gains, ("fsdp", "seq"), scatter_dimension=1, tiled=True),
    )
    owned = tuple((summed[kind_index].reshape(-1, widths[kind_index]) for kind_index in range(4)))
    return owned + (summed[4],)


def layer_forward(residual, gathered, allowed, rotary_cosines, rotary_sines):
    w_qkv, w_out, w_gateup, w_down, gain_pair = gathered
    count_of_rows = residual.shape[0]
    heads_per_group = QUERY_HEAD_COUNT // KEY_VALUE_HEADS
    gain_float = gain_pair.astype(jnp.float32)
    normed_one = normalize(residual)
    input_one = (normed_one * gain_float[0]).astype(jnp.bfloat16)
    query_key_value_rows = product(input_one, w_qkv)
    query_head_rows = apply_rotary(
        query_key_value_rows[:, : QUERY_HEAD_COUNT * HEAD_SIZE].reshape(
            count_of_rows, QUERY_HEAD_COUNT, HEAD_SIZE
        ),
        rotary_cosines,
        rotary_sines,
    ).astype(jnp.bfloat16)
    key_row_block = apply_rotary(
        query_key_value_rows[
            :, QUERY_HEAD_COUNT * HEAD_SIZE : (QUERY_HEAD_COUNT + KEY_VALUE_HEADS) * HEAD_SIZE
        ].reshape(count_of_rows, KEY_VALUE_HEADS, HEAD_SIZE),
        rotary_cosines,
        rotary_sines,
    ).astype(jnp.bfloat16)
    value_row_block = query_key_value_rows[
        :, (QUERY_HEAD_COUNT + KEY_VALUE_HEADS) * HEAD_SIZE :
    ].astype(jnp.bfloat16)
    every_key, every_value = (
        lax.all_gather(
            key_row_block.reshape(count_of_rows, KEY_VALUE_HEADS * HEAD_SIZE),
            "seq",
            axis=0,
            tiled=True,
        ),
        lax.all_gather(value_row_block, "seq", axis=0, tiled=True),
    )
    key_head_rows = every_key.reshape(-1, KEY_VALUE_HEADS, HEAD_SIZE)
    value_head_rows = every_value.reshape(-1, KEY_VALUE_HEADS, HEAD_SIZE)
    query_head_rows = query_head_rows.reshape(
        count_of_rows, KEY_VALUE_HEADS, heads_per_group, HEAD_SIZE
    )
    scores = attention_scores(query_head_rows, key_head_rows, allowed)
    row_max = jnp.max(scores, axis=-1, keepdims=True)
    shifted = jnp.exp(scores - row_max)
    row_sum = jnp.sum(shifted, axis=-1, keepdims=True)
    log_total = row_max + jnp.log(row_sum)
    attn_weights = (shifted / row_sum).astype(jnp.bfloat16)
    attended = jnp.einsum(
        "grqk,kgd->qgrd", attn_weights, value_head_rows, preferred_element_type=jnp.float32
    )
    attended = attended.reshape(count_of_rows, QUERY_HEAD_COUNT * HEAD_SIZE).astype(jnp.bfloat16)
    middle = residual + product(attended, w_out)
    normed_two = normalize(middle)
    input_two = (normed_two * gain_float[1]).astype(jnp.bfloat16)
    gate_up = product(input_two, w_gateup)
    gate_pre = gate_up[:, :FF]
    up_proj = gate_up[:, FF:]
    hidden = (jax.nn.silu(gate_pre) * up_proj).astype(jnp.bfloat16)
    layer_out = middle + product(hidden, w_down)
    saved_layer = (
        residual,
        normed_one,
        input_one,
        query_head_rows,
        key_head_rows,
        value_head_rows,
        log_total,
        attended,
        middle,
        normed_two,
        input_two,
        gate_pre,
        up_proj,
        hidden,
    )
    return (saved_layer, layer_out)


def layer_backward(grad_out, saved_layer, gathered, allowed, rotary_cosines, rotary_sines):
    w_qkv, w_out, w_gateup, w_down, gain_pair = gathered
    (
        residual,
        normed_one,
        input_one,
        query_head_rows,
        key_head_rows,
        value_head_rows,
        log_total,
        attended,
        middle,
        normed_two,
        input_two,
        gate_pre,
        up_proj,
        hidden,
    ) = saved_layer
    count_of_rows = grad_out.shape[0]
    heads_per_group = QUERY_HEAD_COUNT // KEY_VALUE_HEADS
    gain_float = gain_pair.astype(jnp.float32)
    grad_branch = grad_out.astype(jnp.bfloat16)
    grad_down = jnp.einsum("tf,td->fd", hidden, grad_branch, preferred_element_type=jnp.float32)
    grad_hidden = jnp.einsum("td,fd->tf", grad_branch, w_down, preferred_element_type=jnp.float32)
    sigmoid_gate = jax.nn.sigmoid(gate_pre)
    grad_gate = grad_hidden * up_proj * sigmoid_gate * (1.0 + gate_pre * (1.0 - sigmoid_gate))
    grad_up = grad_hidden * gate_pre * sigmoid_gate
    grad_pair = jnp.concatenate([grad_gate, grad_up], axis=1).astype(jnp.bfloat16)
    grad_gateup = jnp.einsum("td,tf->df", input_two, grad_pair, preferred_element_type=jnp.float32)
    grad_input_two = jnp.einsum(
        "tf,df->td", grad_pair, w_gateup, preferred_element_type=jnp.float32
    )
    grad_gain_two = jnp.sum(grad_input_two * normed_two, axis=0)
    grad_middle = grad_out + norm_back(grad_input_two * gain_float[1], normed_two, middle)
    grad_branch_two = grad_middle.astype(jnp.bfloat16)
    grad_out_proj = jnp.einsum(
        "te,td->ed", attended, grad_branch_two, preferred_element_type=jnp.float32
    )
    attended_gradient = jnp.einsum(
        "td,ed->te", grad_branch_two, w_out, preferred_element_type=jnp.float32
    )
    attended_gradient = attended_gradient.astype(jnp.bfloat16).reshape(
        count_of_rows, KEY_VALUE_HEADS, heads_per_group, HEAD_SIZE
    )
    scores = attention_scores(query_head_rows, key_head_rows, allowed)
    attn_float = jnp.exp(scores - log_total)
    value_gradient = jnp.einsum(
        "grqk,qgrd->kgd",
        attn_float.astype(jnp.bfloat16),
        attended_gradient,
        preferred_element_type=jnp.float32,
    )
    grad_weights = jnp.einsum(
        "qgrd,kgd->grqk", attended_gradient, value_head_rows, preferred_element_type=jnp.float32
    )
    inner_sum = jnp.sum(attn_float * grad_weights, axis=-1, keepdims=True)
    grad_scores = (attn_float * (grad_weights - inner_sum)).astype(jnp.bfloat16)
    grad_query = jnp.einsum(
        "grqk,kgd->qgrd", grad_scores, key_head_rows, preferred_element_type=jnp.float32
    ) * HEAD_SIZE ** (-0.5)
    gradient_keys = jnp.einsum(
        "grqk,qgrd->kgd", grad_scores, query_head_rows, preferred_element_type=jnp.float32
    ) * HEAD_SIZE ** (-0.5)
    shared_keys, value_share = (
        lax.psum_scatter(
            gradient_keys.reshape(-1, KEY_VALUE_HEADS * HEAD_SIZE).astype(jnp.bfloat16),
            "seq",
            scatter_dimension=0,
            tiled=True,
        ).astype(jnp.float32),
        lax.psum_scatter(
            value_gradient.reshape(-1, KEY_VALUE_HEADS * HEAD_SIZE).astype(jnp.bfloat16),
            "seq",
            scatter_dimension=0,
            tiled=True,
        ).astype(jnp.float32),
    )
    grad_q = invert_rotary(
        grad_query.reshape(count_of_rows, QUERY_HEAD_COUNT, HEAD_SIZE), rotary_cosines, rotary_sines
    ).reshape(count_of_rows, QUERY_HEAD_COUNT * HEAD_SIZE)
    key_gradient = invert_rotary(
        shared_keys.reshape(count_of_rows, KEY_VALUE_HEADS, HEAD_SIZE), rotary_cosines, rotary_sines
    ).reshape(count_of_rows, KEY_VALUE_HEADS * HEAD_SIZE)
    grad_rows = jnp.concatenate([grad_q, key_gradient, value_share], axis=1).astype(jnp.bfloat16)
    grad_qkv = jnp.einsum("td,tf->df", input_one, grad_rows, preferred_element_type=jnp.float32)
    grad_input_one = jnp.einsum("tf,df->td", grad_rows, w_qkv, preferred_element_type=jnp.float32)
    grad_gain_one = jnp.sum(grad_input_one * normed_one, axis=0)
    grad_in = grad_middle + norm_back(grad_input_one * gain_float[0], normed_one, residual)
    return (
        grad_in,
        (
            grad_qkv,
            grad_out_proj,
            grad_gateup,
            grad_down,
            jnp.stack([grad_gain_one, grad_gain_two]),
        ),
    )


def adam_step(weight, gradient, first_moment, second_moment, step_rate, shrink):
    first_moment = beta_one * first_moment + (1.0 - beta_one) * gradient
    second_moment = beta_two * second_moment + (1.0 - beta_two) * gradient * gradient
    first_hat = first_moment / (1.0 - beta_one**STEP)
    second_hat = second_moment / (1.0 - beta_two**STEP)
    weight = weight - step_rate * (first_hat / (jnp.sqrt(second_hat) + adam_eps) + shrink * weight)
    return (weight, first_moment, second_moment)


def shards(
    tokens,
    cotangent,
    lengths,
    w_qkv,
    w_out,
    w_gateup,
    w_down,
    norm_gains,
    first_qkv,
    first_out,
    first_gateup,
    first_down,
    first_gains,
    second_qkv,
    second_out,
    second_gateup,
    second_down,
    second_gains,
):
    count_of_rows = tokens.shape[0]
    group_rows = count_of_rows * lax.axis_size("seq")
    place_rows = lax.axis_index("seq") * count_of_rows + jnp.arange(count_of_rows, dtype=jnp.int32)
    key_places = jnp.arange(group_rows, dtype=jnp.int32)
    seg_rows, positions = layout(lengths[0], place_rows)
    seg_keys = layout(lengths[0], key_places)[0]
    allowed = (seg_rows[:, None] == seg_keys[None, :]) & (
        key_places[None, :] <= place_rows[:, None]
    )
    rotary_cosines, rotary_sines = tables(positions)
    stacked = (w_qkv, w_out, w_gateup, w_down, norm_gains)
    residual = tokens.astype(jnp.float32)
    saved_all = []
    for layer_index in range(LAYERS):
        gathered = fetch_forward(stacked, layer_index)
        saved_layer, residual = layer_forward(
            residual, gathered, allowed, rotary_cosines, rotary_sines
        )
        saved_all.append(saved_layer)
    grad_state = cotangent.astype(jnp.float32)
    updates = [None] * LAYERS
    for layer_index in reversed(range(LAYERS)):
        gathered = fetch_backward(stacked, layer_index)
        grad_state, grad_terms = layer_backward(
            grad_state, saved_all[layer_index], gathered, allowed, rotary_cosines, rotary_sines
        )
        updates[layer_index] = reduce_grads(grad_terms)
    step_rates = (D ** (-0.5), 4.0 * D ** (-0.5), D ** (-0.5), FF ** (-0.5), 0.5)
    shrinks = (decay_rate, decay_rate, decay_rate, decay_rate, 0.0)
    firsts = (first_qkv, first_out, first_gateup, first_down, first_gains)
    seconds = (second_qkv, second_out, second_gateup, second_down, second_gains)
    new_weights = []
    new_firsts = []
    new_seconds = []
    for kind_index in range(5):
        grads_kind = jnp.stack([updates[layer_index][kind_index] for layer_index in range(LAYERS)])
        weight, first_moment, second_moment = adam_step(
            stacked[kind_index],
            grads_kind,
            firsts[kind_index],
            seconds[kind_index],
            step_rates[kind_index],
            shrinks[kind_index],
        )
        new_weights.append(weight)
        new_firsts.append(first_moment)
        new_seconds.append(second_moment)
    outputs = [residual.astype(jnp.bfloat16), grad_state] + new_weights + new_firsts + new_seconds
    return tuple(outputs)


MESH = pl.DeviceIdType.MESH
BF = jnp.bfloat16
F32 = jnp.float32
KV_RANK = KEY_VALUE_HEADS // 4
Q_RANK = QUERY_HEAD_COUNT // 4
ANY = pl.BlockSpec(memory_space=pl.ANY)
VM = pl.BlockSpec(memory_space=pltpu.VMEM)
DMA = pltpu.SemaphoreType.DMA


class Place:
    def __init__(self):
        f, z = lax.axis_index("fsdp"), lax.axis_index("seq")
        self.y, self.x, self.c = lax.div(f, 4), lax.rem(lax.div(f, 2), 2), lax.rem(f, 2)
        self.z1, self.z0 = lax.div(z, 2), lax.rem(z, 2)
        self.rank = 2 * self.c + self.z0
        self.inner = self.z1 != self.z0
        self.sibling, self.over = 2 * (1 - self.c) + self.z0, 2 * self.c + 1 - self.z0
        self.diagonal = 2 * (1 - self.c) + 1 - self.z0
        self.peer = {
            "y": (f + 4 - 8 * self.y, z),
            "x": (f + 2 - 4 * self.x, z),
            "c": (f + 1 - 2 * self.c, z),
            "z1": (f, z + 2 - 4 * self.z1),
            "z0": (f, z + 1 - 2 * self.z0),
            "cz": (f + 1 - 2 * self.c, z + 1 - 2 * self.z0),
            "swap": (f - self.c + self.z1, 2 * self.c + self.z0),
            "mid": (f, 3 - z),
        }


def greet(place, names):
    barrier = pltpu.get_barrier_semaphore()
    partial = {"swap": place.c != place.z1, "mid": place.inner}
    amount = len([n for n in names if n not in partial])
    for name in names:
        if name not in partial:
            pl.semaphore_signal(barrier, inc=1, device_id=place.peer[name], device_id_type=MESH)
    for name, holds in partial.items():
        if name in names:
            amount = amount + holds.astype(jnp.int32)

            @pl.when(holds)
            def _(name=name):
                pl.semaphore_signal(barrier, inc=1, device_id=place.peer[name], device_id_type=MESH)

    pl.semaphore_wait(barrier, amount)


def remote(src, dst, send_sem, recv_sem, device):
    return pltpu.make_async_remote_copy(
        src_ref=src, dst_ref=dst, send_sem=send_sem, recv_sem=recv_sem, device_id=device, device_id_type=MESH
    )


def columns_index(y, x, z1, h):
    return ((y * 2 + x) * 2 + h) * 2 + z1


def rows_index(y, x, z1, h):
    return ((y * 2 + x) * 2 + z1) * 2 + h


class Cross:
    def __init__(self, place, src, dst_there, dst_here, relay, send, recv):
        self.p, self.src, self.dst_there, self.dst_here, self.relay = place, src, dst_there, dst_here, relay
        self.send, self.recv = send, recv

    def copy(self, k):
        p, relay = self.p, self.relay
        src, dst, peer = (
            (self.src, relay.at[0], "z0"),
            (self.src, relay.at[1], "mid"),
            (relay.at[0], self.dst_there, "mid"),
            (relay.at[1], self.dst_here, "z0"),
        )[k]
        return remote(src, dst, self.send.at[k], self.recv.at[k], p.peer[peer])

    def start(self):
        @pl.when(self.p.inner)
        def _():
            self.copy(1).start()

        @pl.when(jnp.logical_not(self.p.inner))
        def _():
            self.copy(0).start()

    def bring(self):
        @pl.when(self.p.inner)
        def _():
            self.copy(1).wait_recv()
            self.copy(3).start()

    def take(self):
        @pl.when(self.p.inner)
        def _():
            self.copy(0).wait_recv()
            self.copy(2).start()

    def wait(self):
        @pl.when(self.p.inner)
        def _():
            self.copy(2).wait_recv()

        @pl.when(jnp.logical_not(self.p.inner))
        def _():
            self.copy(3).wait_recv()

    def finish(self):
        @pl.when(self.p.inner)
        def _():
            for k in (1, 2, 3):
                self.copy(k).wait_send()

        @pl.when(jnp.logical_not(self.p.inner))
        def _():
            self.copy(0).wait_send()


class Gather:
    def __init__(self, place, ref, index, send, recv, local, relay, src=None, met=None):
        self.p, self.ref, self.index, self.send, self.recv = place, ref, index, send, recv
        self.local, self.src, self.met = local, src, met
        self.cross = []
        for h in (0, 1) if met is None else ():
            block = self.at((), h)
            self.cross.append(
                Cross(
                    place,
                    block if src is None else src.at[h],
                    block,
                    self.at(("z1",), h),
                    relay.at[h],
                    *[s.at[pl.ds(14 + 4 * h, 4)] for s in (send, recv)],
                )
            )

    def at(self, flips, h):
        p = self.p
        flip = lambda v, name: 1 - v if name in flips else v
        return self.ref.at[self.index(flip(p.y, "y"), flip(p.x, "x"), flip(p.z1, "z1"), h)]

    def route(self, h):
        a, b = ("y", "x") if h == 0 else ("x", "y")
        return (
            ("z1", ()),
            (a, ()),
            (a, ("z1",)),
            (b, ()),
            (b, ("z1",)),
            (b, (a,)),
            (b, (a, "z1")),
        )

    def out(self, h, m):
        axis, flips = self.route(h)[m]
        dst = src = self.at(flips, h)
        if self.src is not None and not flips:
            src = self.src.at[h]
        if self.met is not None and flips == ("z1",):
            src = self.met.at[h]
        return remote(src, dst, self.send.at[7 * h + m], self.recv.at[7 * h + m], self.p.peer[axis])

    def into(self, h, m):
        axis, flips = self.route(h)[m]
        ref = self.at(flips + (axis,), h)
        return remote(ref, ref, self.send.at[7 * h + m], self.recv.at[7 * h + m], self.p.peer[axis])

    def keep(self, h):
        kept = []
        if self.src is not None:
            kept.append(pltpu.make_async_copy(self.src.at[h], self.at((), h), self.local.at[h]))
        if self.met is not None:
            kept.append(pltpu.make_async_copy(self.met.at[h], self.at(("z1",), h), self.local.at[2 + h]))
        return kept

    def first(self):
        for c in self.cross:
            c.start()

    def second(self):
        for m in (1, 3) if self.met is None else (1, 3, 2, 4):
            for h in (0, 1):
                self.out(h, m).start()
        for h in (0, 1):
            for copy in self.keep(h):
                copy.start()

    def turned(self, h):
        self.cross[h].wait()
        for m in (2, 4):
            self.out(h, m).start()

    def on(self, h, got, gives):
        self.into(h, got).wait_recv()
        for m in gives:
            self.out(h, m).start()

    def last(self):
        for h in (0, 1):
            for m in (3, 4, 5, 6):
                self.into(h, m).wait_recv()
            for m in range(1, 7):
                self.out(h, m).wait_send()
            if self.met is None:
                self.cross[h].finish()
            for copy in self.keep(h):
                copy.wait()

    def steps(self, when):
        part = functools.partial
        acts = [(when["start"], self.first), (when["start"], self.second)]
        for h in (0, 1):
            if self.met is None:
                acts.append((when["bring"][h], self.cross[h].bring))
                acts.append((when["take"][h], self.cross[h].take))
                acts.append((when["turn"][h], part(self.turned, h)))
            acts.append((when["five"], part(self.on, h, 1, (5,))))
            acts.append((when["six"][h], part(self.on, h, 2, (6,))))
        return acts + [(when["last"], self.last)]


def times(start, bring, take, five, turn, six, last=99):
    return dict(start=start, bring=bring, take=take, five=five, turn=turn, six=six, last=last)


class Spread:
    def __init__(self, place, src, target, send, recv, local):
        self.p, self.src, self.target, self.send, self.recv, self.local = place, src, target, send, recv, local

    def copy(self, k, arriving=False):
        p = self.p
        name, fc, fz = (("c", 1, 0), ("z0", 0, 1), ("cz", 1, 1))[k]
        c = 1 - p.c if fc else p.c
        z0 = 1 - p.z0 if fz else p.z0
        src = self.src(c, z0)
        dst = self.target(c, z0) if arriving else self.target(p.c, p.z0)
        return remote(src, dst, self.send.at[k], self.recv.at[k], p.peer[name])

    def own(self):
        p = self.p
        return pltpu.make_async_copy(self.src(p.c, p.z0), self.target(p.c, p.z0), self.local)

    def start(self):
        for k in range(3):
            self.copy(k).start()
        self.own().start()

    def wait(self):
        for k in range(3):
            self.copy(k, True).wait_recv()
        self.own().wait()

    def finish(self):
        for k in range(3):
            self.copy(k).wait_send()


def add_to(dst, src):
    dst[...] = (dst[...].astype(F32) + src[...].astype(F32)).astype(dst.dtype)


class Reduce:
    def __init__(self, place, ref, index, out, mine, one, two, three, relay, send, recv, local):
        self.cross = [
            Cross(
                place, two.at[h, 0], three.at[h], three.at[h], relay.at[h], *[s.at[pl.ds(14 + 4 * h, 4)] for s in (send, recv)]
            )
            for h in ((0, 1) if out.shape != two.shape else ())
        ]
        self.p, self.ref, self.index, self.result = place, ref, index, out
        self.mine, self.one, self.two, self.three = mine, one, two, three
        self.send, self.recv, self.local = send, recv, local
        self.open = out.shape == two.shape

    def block(self, h, far_a, m):
        p = self.p
        a, b = (p.x, p.y) if h == 0 else (p.y, p.x)
        a = 1 - a if far_a else a
        b = 1 - b if m < 2 else b
        z1 = 1 - p.z1 if m % 2 == 0 else p.z1
        y, x = (b, a) if h == 0 else (a, b)
        return self.ref.at[self.index(y, x, z1, h)]

    def copy(self, h, m):
        p = self.p
        name_a, name_b = ("x", "y") if h == 0 else ("y", "x")
        sems = self.send.at[7 * h + m], self.recv.at[7 * h + m]
        if m < 4:
            return remote(self.block(h, True, m), self.one.at[h, m], *sems, p.peer[name_a])
        return remote(self.one.at[h, m - 4], self.two.at[h, m - 4], *sems, p.peer[name_b])

    def near(self, h, m):
        return self.block(h, False, m) if self.mine is None else self.mine.at[h, m]

    def load(self, h, m):
        return pltpu.make_async_copy(self.block(h, False, m), self.mine.at[h, m], self.local.at[4 * h + m])

    def first(self):
        for m in range(4):
            for h in (0, 1):
                self.copy(h, m).start()
                if self.mine is not None:
                    self.load(h, m).start()

    def second(self, h, m):
        self.copy(h, m).wait_recv()
        if self.mine is not None:
            self.load(h, m).wait()
        add_to(self.one.at[h, m], self.near(h, m))
        if m < 2:
            self.copy(h, 4 + m).start()

    def third(self, h, k):
        self.copy(h, 4 + k).wait_recv()
        add_to(self.two.at[h, k], self.one.at[h, 2 + k])
        if k == 0 and not self.open:
            self.cross[h].start()

    def fourth(self, h):
        self.cross[h].wait()
        add_to(self.three.at[h], self.two.at[h, 1])

    def finish(self):
        for h in (0, 1):
            for m in range(6):
                self.copy(h, m).wait_send()
            if not self.open:
                self.cross[h].finish()

    def store(self):
        src = self.two if self.result.shape == self.two.shape else self.three
        return pltpu.make_async_copy(src, self.result, self.local.at[8])


def out_gather_steps(p, src, ref, send, recv, local):
    home = p.x == p.z0
    away = jnp.logical_not(home)
    at = lambda fy, fz: ref.at[(1 - p.y if fy else p.y) * 2 + (1 - p.z1 if fz else p.z1)]
    pair = lambda half: remote(src, at(0, 0).at[half], send.at[0], recv.at[0], p.peer["z0"])
    z1_copy = lambda fz: remote(at(0, fz), at(0, fz), send.at[1], recv.at[1], p.peer["z1"])
    x_copy = lambda k: remote(at(0, k), at(0, k), send.at[2 + k], recv.at[2 + k], p.peer["x"])
    y_copy = lambda k, fy: remote(at(fy, k), at(fy, k), send.at[4 + k], recv.at[4 + k], p.peer["y"])
    own = pltpu.make_async_copy(src, at(0, 0).at[p.z0], local)

    def zero():
        @pl.when(home)
        def _():
            own.start()

        @pl.when(away)
        def _():
            pair(p.z0).start()

    def one():
        @pl.when(home)
        def _():
            own.wait()
            pair(1 - p.z0).wait_recv()
            z1_copy(0).start()
            x_copy(0).start()
            y_copy(0, 0).start()

    def two():
        @pl.when(home)
        def _():
            z1_copy(1).wait_recv()
            x_copy(1).start()
            y_copy(1, 0).start()

    def three():
        @pl.when(away)
        def _():
            for k in (0, 1):
                x_copy(k).wait_recv()
                y_copy(k, 0).start()

    def last():
        for k in (0, 1):
            y_copy(k, 1).wait_recv()
            y_copy(k, 0).wait_send()

        @pl.when(home)
        def _():
            z1_copy(0).wait_send()
            for k in (0, 1):
                x_copy(k).wait_send()

        @pl.when(away)
        def _():
            pair(p.z0).wait_send()

    return [zero, one, two, three, last]


def out_reduce_steps(p, ref, out, one, two, three, got, send, recv, local):
    home = p.x == p.z0
    away = jnp.logical_not(home)
    y_copy = lambda k: remote(ref.at[(1 - p.y) * 2 + k], one.at[k], send.at[k], recv.at[k], p.peer["y"])
    x_copy = lambda k: remote(one.at[k], two.at[k], send.at[2 + k], recv.at[2 + k], p.peer["x"])
    z1_copy = remote(two.at[1 - p.z1], three, send.at[4], recv.at[4], p.peer["z1"])
    rows = three.shape[0] // 2
    half = lambda z0: three.at[pl.ds(pl.multiple_of(z0 * rows, rows), rows)]
    pair = remote(half(1 - p.z0), got, send.at[5], recv.at[5], p.peer["z0"])
    keep = pltpu.make_async_copy(half(p.z0), out, local.at[0])
    take = pltpu.make_async_copy(got, out, local.at[0])

    def zero():
        for k in (0, 1):
            y_copy(k).start()

    def first():
        for k in (0, 1):
            y_copy(k).wait_recv()
            add_to(one.at[k], ref.at[p.y * 2 + k])

            @pl.when(away)
            def _(k=k):
                x_copy(k).start()

    def second():
        @pl.when(home)
        def _():
            for k in (0, 1):
                x_copy(k).wait_recv()
                add_to(two.at[k], one.at[k])
            z1_copy.start()

    def third():
        @pl.when(home)
        def _():
            z1_copy.wait_recv()
            add_to(three, two.at[p.z1])
            pair.start()
            keep.start()

    def last():
        for k in (0, 1):
            y_copy(k).wait_send()

        @pl.when(home)
        def _():
            keep.wait()
            z1_copy.wait_send()
            pair.wait_send()

        @pl.when(away)
        def _():
            pair.wait_recv()
            take.start()
            for k in (0, 1):
                x_copy(k).wait_send()
            take.wait()

    return [zero, first, second, third, last]


def out_reduce_scratch(wide):
    return [
        pltpu.VMEM((4,) + wide, BF),
        pltpu.VMEM((2,) + wide, BF),
        pltpu.VMEM((2,) + wide, BF),
        pltpu.VMEM(wide, BF),
        pltpu.VMEM((wide[0] // 2, wide[1]), BF),
        DMA((6,)),
        DMA((6,)),
        DMA((1,)),
    ]


def gains_gather(p, src, ref, send, recv, local):
    me = ((p.y * 2 + p.x) * 2 + p.c) * 4 + p.z1 * 2 + p.z0
    own = pltpu.make_async_copy(src, ref.at[me], local)
    names = ("z0", "z1", "c", "x", "y")

    def span(k, other):
        size = 1 << k
        start = lax.div(me, size) * size
        if other:
            bit = lax.rem(lax.div(me, size), 2)
            start = start + size - 2 * size * bit
        return ref.at[pl.ds(start, size)]

    def copy(k, other):
        return remote(span(k, other), span(k, other), send.at[k], recv.at[k], p.peer[names[k]])

    def step(k):
        def run():
            if k == 0:
                own.start()
                own.wait()
            else:
                copy(k - 1, True).wait_recv()
            if k < 5:
                copy(k, False).start()
            else:
                for j in range(5):
                    copy(j, False).wait_send()

        return run

    return [step(k) for k in range(6)]


def gains_reduce(p, src, out, base, halves, send, recv, local):
    names, bits = ("y", "x", "c", "z1", "z0"), (p.y, p.x, p.c, p.z1, p.z0)
    load = pltpu.make_async_copy(src, base, local.at[0])
    keep = pltpu.make_async_copy(halves[4].at[0], out, local.at[0])

    def part(k, bit):
        source, size = (base if k == 0 else halves[k - 1]), 16 >> k
        return source.at[pl.ds(bit * size, size)]

    def copy(k):
        return remote(part(k, 1 - bits[k]), halves[k], send.at[k], recv.at[k], p.peer[names[k]])

    def step(k):
        def run():
            if k > 0:
                copy(k - 1).wait_recv()
                halves[k - 1][...] += part(k - 1, bits[k - 1])[...]
            else:
                load.start()
                load.wait()
            if k < 5:
                copy(k).start()
            else:
                keep.start()
                for j in range(5):
                    copy(j).wait_send()
                keep.wait()

        return run

    return [step(k) for k in range(6)]


GROUP = ("c", "z0", "cz")
EIGHT = ("z1", "y", "x")


CHUNKS = 2


class ShareRows:
    def __init__(self, p, dst, send, recv):
        self.p, self.dst, self.send, self.recv = p, dst, send, recv
        self.rows = dst.shape[1] // CHUNKS

    def chunk(self, rank, k):
        return self.dst.at[rank, pl.ds(k * self.rows, self.rows)]

    def over(self, k, arriving=False):
        p = self.p
        ref = self.chunk(p.over if arriving else p.rank, k)
        return remote(ref, ref, self.send.at[k], self.recv.at[k], p.peer["z0"])

    def across(self, arriving=False):
        p = self.p
        ref = self.dst.at[p.sibling if arriving else p.rank]
        return remote(ref, ref, self.send.at[CHUNKS], self.recv.at[CHUNKS], p.peer["c"])

    def onward(self, k, arriving=False):
        p = self.p
        ours, theirs = 2 * p.c + 1 - p.z0, 2 * (1 - p.c) + 1 - p.z0
        ref = self.chunk(theirs if arriving else ours, k)
        return remote(ref, ref, self.send.at[CHUNKS + 1 + k], self.recv.at[CHUNKS + 1 + k], p.peer["c"])

    def start(self):
        for k in range(CHUNKS):
            self.over(k).start()
        self.across().start()

    def pass_on(self, k):
        self.over(k, True).wait_recv()
        self.onward(k).start()

    def far(self, k):
        self.onward(k, True).wait_recv()

    def finish(self):
        for k in range(CHUNKS):
            self.over(k).wait_send()
            self.onward(k).wait_send()
        self.across().wait_send()


class SumRows:
    def __init__(self, p, terms, near, cross, far, send, recv):
        self.p, self.terms, self.near, self.cross, self.far, self.send, self.recv = p, terms, near, cross, far, send, recv
        self.rows = near.shape[0] // CHUNKS

    def diagonal(self, k):
        p = self.p
        part = pl.ds(k * self.rows, self.rows)
        rank = 2 * (1 - p.c) + 1 - p.z0
        return remote(self.terms.at[rank, part], self.cross.at[part], self.send.at[k], self.recv.at[k], p.peer["c"])

    def sibling(self):
        p = self.p
        rank, at = 2 * (1 - p.c) + p.z0, CHUNKS
        return remote(self.terms.at[rank], self.near, self.send.at[at], self.recv.at[at], p.peer["c"])

    def over(self, k):
        p, at = self.p, CHUNKS + 1 + k
        part = pl.ds(k * self.rows, self.rows)
        return remote(self.cross.at[part], self.far.at[part], self.send.at[at], self.recv.at[at], p.peer["z0"])

    def relay(self, k):
        p = self.p
        self.diagonal(k).wait_recv()
        part = pl.ds(k * self.rows, self.rows)
        add_to(self.cross.at[part], self.terms.at[2 * p.c + 1 - p.z0, part])
        self.over(k).start()

    def finish(self):
        for k in range(CHUNKS):
            self.diagonal(k).wait_send()
            self.over(k).wait_send()
        self.sibling().wait_send()


def swap_pairs(count_fsdp, count_seq):
    pairs = []
    for f in range(count_fsdp):
        for z in range(count_seq):
            c, z1 = f % 2, z // 2
            pairs.append((f * count_seq + z, (f - c + z1) * count_seq + c * 2 + z % 2))
    return pairs


TILE = 256
UP_TILE = 512
DOWN_TILE = 768
GRAD_TILE = 512
HALVES = 2


def wide_params(collective_id):
    return pltpu.CompilerParams(
        collective_id=collective_id, has_side_effects=True, vmem_limit_bytes=61 * 2**20
    )


def dot(a, b, contract=((1,), (0,))):
    return lax.dot_general(a, b, (contract, ((), ())), preferred_element_type=F32)


def row_normalize(ref, gain, out, rows=32):
    def step(k, _):
        at = pl.ds(pl.multiple_of(k * rows, rows), rows)
        value = ref[at, :].astype(F32)
        out[at, :] = (normalize(value) * gain[...]).astype(out.dtype)
        return 0

    lax.fori_loop(0, ref.shape[0] // rows, step, 0)


def column_tiles(width, tile, step):
    def run(j, _):
        step(pl.multiple_of(j * tile, tile))
        return 0

    lax.fori_loop(0, width // tile, run, 0)


def exchange(p, share, total, compute, advance):
    rows = total.near.shape[0]
    part = rows // CHUNKS
    share.start()
    advance()
    compute([(p.rank, 0)], rows)
    advance()
    share.across(True).wait_recv()
    compute([(p.sibling, 0)], rows)
    total.sibling().start()
    advance()
    for k in range(CHUNKS):
        share.pass_on(k)
        share.far(k)
        compute([(p.diagonal, k * part), (p.over, k * part)], part)
        total.diagonal(k).start()
        total.relay(k)
        advance()


def gather_pieces(ref, pieces, count, *index):
    parts = [ref[(rank, pl.ds(first, count)) + index] for rank, first in pieces]
    return parts[0] if len(parts) == 1 else jnp.concatenate(parts, axis=0)


def scatter_pieces(ref, pieces, count, value, *index):
    for k, (rank, first) in enumerate(pieces):
        ref[(rank, pl.ds(first, count)) + index] = value[k * count : (k + 1) * count]


def token_rows(pieces, count, rows):
    return [pl.ds(pl.multiple_of(rank * rows + first, count), count) for rank, first in pieces]


def collect(p, total, write, rows=32):
    total.sibling().wait_recv()
    for k in range(CHUNKS):
        total.over(k).wait_recv()

        def step(j, _, k=k):
            at = pl.ds(pl.multiple_of(k * total.rows + j * rows, rows), rows)
            value = total.terms[p.rank, at, :].astype(F32) + total.near[at, :].astype(F32)
            write(at, value + total.far[at, :].astype(F32))
            return 0

        lax.fori_loop(0, total.rows // rows, step, 0)


def exchange_scratch(rows):
    part = pltpu.VMEM((rows, D), BF)
    sems = DMA((2 * CHUNKS + 1,))
    return [pltpu.VMEM((4, rows, D), BF), part, part, part, sems, sems, sems, sems]


def exchange_of(p, every, refs):
    terms, near, cross, far, send, recv, t_send, t_recv = refs
    share = ShareRows(p, every, send, recv)
    return every.at[p.rank], terms, share, SumRows(p, terms, near, cross, far, t_send, t_recv)


class Nothing:
    names, args, specs, shapes, scratch = (), (), (), (), ()

    def steps(self, p, ins, outs, scratch):
        return []


class Clock:
    def __init__(self, steps):
        self.steps, self.now = sorted(steps, key=lambda s: s[0]), 0

    def __call__(self):
        while self.steps and self.steps[0][0] <= self.now:
            self.steps.pop(0)[1]()
        self.now += 1

    def finish(self):
        for _, act in self.steps:
            act()
        self.steps = []


class Staged:
    def __init__(self, ins, in_sems, outs, out_sems):
        self.loads = {k: pltpu.make_async_copy(src, dst, in_sems.at[n]) for n, (k, src, dst) in enumerate(ins)}
        self.stores = {k: pltpu.make_async_copy(src, dst, out_sems.at[n]) for n, (k, src, dst) in enumerate(outs)}
        self.started = []
        for load in self.loads.values():
            load.start()

    def ready(self, *ks):
        for k in ks:
            if k in self.loads:
                self.loads.pop(k).wait()

    def flush(self, *ks):
        for k in ks:
            store = self.stores.pop(k)
            store.start()
            self.started.append(store)

    def finish(self):
        self.ready(*list(self.loads))
        self.flush(*list(self.stores))
        for store in self.started:
            store.wait()


def beside_call(
    body, args, late, shapes, later, scratch, beside, name, collective_id, flops, peers=("c", "z0"), specs=None
):
    n_ins, n_outs = len(args), len(shapes)
    buffers = [pltpu.VMEM(args[k].shape, args[k].dtype) for k in late]
    buffers += [pltpu.VMEM(shapes[k].shape, shapes[k].dtype) for k in later]
    sems = [DMA((max(len(late), 1),)), DMA((max(len(later), 1),))]
    counts = [n_ins, len(beside.args), n_outs, len(beside.shapes), len(scratch), len(buffers), 2, len(beside.scratch)]

    def whole(*refs):
        groups, at = [], 0
        for n in counts:
            groups.append(list(refs[at : at + n]))
            at += n
        ins, b_ins, outs, b_outs, own, held, (in_sems, out_sems), b_scratch = groups
        moved_in = [(k, ins[k], held[n]) for n, k in enumerate(late)]
        moved_out = [(k, held[len(late) + n], outs[k]) for n, k in enumerate(later)]
        staged = Staged(moved_in, in_sems, moved_out, out_sems)
        for k, _, dst in moved_in:
            ins[k] = dst
        for k, src, _ in moved_out:
            outs[k] = src
        p = Place()
        greet(p, tuple(peers) + tuple(n for n in beside.names if n not in peers))
        body(p, ins, outs, own, Clock(beside.steps(p, b_ins, b_outs, b_scratch)), staged)
        staged.finish()

    specs = specs or {}
    out = pl.pallas_call(
        whole,
        out_shape=list(shapes) + list(beside.shapes),
        in_specs=[ANY if k in late else VM for k in range(n_ins)] + list(beside.specs),
        out_specs=[ANY if k in later else specs.get(k, VM) for k in range(n_outs)] + [ANY] * len(beside.shapes),
        scratch_shapes=list(scratch) + buffers + sems + list(beside.scratch),
        compiler_params=wide_params(collective_id),
        cost_estimate=pl.CostEstimate(flops=flops, bytes_accessed=20 * 2**20, transcendentals=0),
        name=name,
    )(*args, *beside.args)
    return out[:n_outs], out[n_outs:]


def feed_forward_call(middle, gain, w_gateup, w_down, beside, collective_id, dtype=F32):
    rows, wide = middle.shape[0], w_down.shape[0]

    def body(p, ins, outs, scratch, advance, staged):
        mid_ref, gain_ref, gu_ref, down_ref = ins
        new_ref, every, gate_ref, up_ref, hid_ref = outs
        own, terms, share, total = exchange_of(p, every, scratch)

        def compute(pieces, count):
            staged.ready(2, 3)

            def up_tile(j):
                cols, far = pl.ds(j, UP_TILE), pl.ds(wide + j, UP_TILE)
                x = gather_pieces(every, pieces, count)
                gate, up = dot(x, gu_ref[:, cols]), dot(x, gu_ref[:, far])
                scatter_pieces(gate_ref, pieces, count, gate.astype(BF), cols)
                scatter_pieces(up_ref, pieces, count, up.astype(BF), cols)
                hidden = (gate / (1.0 + jnp.exp(-gate)) * up).astype(BF)
                scatter_pieces(hid_ref, pieces, count, hidden, cols)

            column_tiles(wide, UP_TILE, up_tile)

            def down_tile(j):
                cols = pl.ds(j, DOWN_TILE)
                value = dot(gather_pieces(hid_ref, pieces, count), down_ref[:, cols]).astype(BF)
                scatter_pieces(terms, pieces, count, value, cols)

            column_tiles(D, DOWN_TILE, down_tile)

        row_normalize(mid_ref, gain_ref, own)
        exchange(p, share, total, compute, advance)
        staged.flush(1, 2, 3, 4)

        def write(at, value):
            new_ref[at, :] = (mid_ref[at, :] + value).astype(dtype)

        collect(p, total, write)
        advance.finish()
        share.finish()
        total.finish()

    return beside_call(
        body,
        (middle, gain.reshape(1, D), w_gateup, w_down),
        (2, 3),
        [
            jax.ShapeDtypeStruct((rows, D), dtype),
            jax.ShapeDtypeStruct((4, rows, D), BF),
            jax.ShapeDtypeStruct((4, rows, wide), BF),
            jax.ShapeDtypeStruct((4, rows, wide), BF),
            jax.ShapeDtypeStruct((4, rows, wide), BF),
        ],
        (1, 2, 3, 4),
        exchange_scratch(rows),
        beside,
        "feed_forward",
        collective_id,
        6 * 4 * rows * wide * D,
    )


def feed_backward_call(grad, middle, gain, w_gateup, w_down, kept, beside, collective_id):
    every, gate, up, hidden = kept
    rows, wide = middle.shape[0], w_down.shape[0]
    block = (wide // 16, D)

    def body(p, ins, outs, scratch, advance, staged):
        grad_ref, mid_ref, gain_ref, gu_ref, down_ref, every_ref, gate_ref, up_ref, hid_ref = ins
        new_ref, gain_out, g_gu, two_down = outs
        e, pair, g_down, one, two, send, recv, local = scratch[:8]
        own, terms, share, total = exchange_of(p, e, scratch[8:])
        reduce = Reduce(p, g_down, rows_index, two_down, None, one, two, None, None, send, recv, local)

        def compute(pieces, count):
            staged.ready(4, 6, 7, 3)

            def up_tile(j):
                cols, far = pl.ds(j, UP_TILE), pl.ds(wide + j, UP_TILE)
                grad_hidden = dot(gather_pieces(e, pieces, count), down_ref[cols, :], ((1,), (1,)))
                g = gather_pieces(gate_ref, pieces, count, cols).astype(F32)
                u = gather_pieces(up_ref, pieces, count, cols).astype(F32)
                s = 1.0 / (1.0 + jnp.exp(-g))
                grad_gate = (grad_hidden * u * s * (1.0 + g * (1.0 - s))).astype(BF)
                scatter_pieces(pair, pieces, count, grad_gate, cols)
                scatter_pieces(pair, pieces, count, (grad_hidden * g * s).astype(BF), far)

            column_tiles(wide, UP_TILE, up_tile)

            def down_tile(j):
                cols = pl.ds(j, DOWN_TILE)
                value = dot(gather_pieces(pair, pieces, count), gu_ref[cols, :], ((1,), (1,))).astype(BF)
                scatter_pieces(terms, pieces, count, value, cols)

            column_tiles(D, DOWN_TILE, down_tile)

        def weight_grads():
            tokens = 4 * rows
            e_all, pair_all, x_all, hid_all = (
                r.reshape(tokens, r.shape[2]) for r in (e, pair, every_ref, hid_ref)
            )

            part = g_down.shape[1]
            staged.ready(8, 5)

            def down_grad(j):
                value = dot(hid_all[:, pl.ds(j, GRAD_TILE)], e_all[...], ((0,), (0,))).astype(BF)
                g_down[pl.ds(lax.div(j, part), GRAD_TILE // part)] = value.reshape(GRAD_TILE // part, part, D)

            column_tiles(wide, GRAD_TILE, down_grad)
            reduce.first()
            for k in range(D // GRAD_TILE):
                cols = slice(k * GRAD_TILE, (k + 1) * GRAD_TILE)
                g_gu[cols, :] = dot(x_all[:, cols], pair_all[...], ((0,), (0,))).astype(BF)
                advance()
                if k < 2:
                    for m in (2 * k, 2 * k + 1):
                        for h in (0, 1):
                            reduce.second(h, m)
            staged.flush(2)

        def copy_own(k, _):
            at = pl.ds(pl.multiple_of(k * 32, 32), 32)
            own[at, :] = grad_ref[at, :].astype(BF)
            return 0

        lax.fori_loop(0, rows // 32, copy_own, 0)
        exchange(p, share, total, compute, advance)
        weight_grads()
        gain_out[...] = jnp.zeros_like(gain_out)

        def write(at, value):
            mid = mid_ref[at, :]
            normed = normalize(mid)
            gain_out[...] += jnp.sum(value * normed, axis=0, keepdims=True)
            new_ref[at, :] = grad_ref[at, :] + norm_back(value * gain_ref[...], normed, mid)

        collect(p, total, write)
        for k in (0, 1):
            for h in (0, 1):
                reduce.third(h, k)
        advance.finish()
        reduce.store().start()
        reduce.finish()
        reduce.store().wait()
        share.finish()
        total.finish()

    return beside_call(
        body,
        (grad, middle, gain.reshape(1, D), w_gateup, w_down, every, gate, up, hidden),
        (4, 6, 7, 3, 8, 5),
        [
            jax.ShapeDtypeStruct((rows, D), F32),
            jax.ShapeDtypeStruct((1, D), F32),
            jax.ShapeDtypeStruct((D, 2 * wide), BF),
            jax.ShapeDtypeStruct((2, 2) + block, BF),
        ],
        (2,),
        [
            pltpu.VMEM((4, rows, D), BF),
            pltpu.VMEM((4, rows, 2 * wide), BF),
            pltpu.VMEM((16,) + block, BF),
            pltpu.VMEM((2, 4) + block, BF),
            pltpu.VMEM((2, 2) + block, BF),
            DMA((14,)),
            DMA((14,)),
            DMA((9,)),
        ]
        + exchange_scratch(rows),
        beside,
        "feed_backward",
        collective_id,
        12 * 4 * rows * wide * D,
        ("c", "z0", "x", "y"),
        {3: ANY},
    )


class Both:
    def __init__(self, *parts):
        self.parts = parts
        self.names = tuple(dict.fromkeys(n for p in parts for n in p.names))
        self.args = tuple(a for p in parts for a in p.args)
        self.specs = tuple(a for p in parts for a in p.specs)
        self.shapes = tuple(s for p in parts for s in p.shapes)
        self.scratch = tuple(s for p in parts for s in p.scratch)

    def steps(self, p, ins, outs, scratch):
        waves, at = [], [0, 0, 0]
        for part in self.parts:
            ends = [at[0] + len(part.args), at[1] + len(part.shapes), at[2] + len(part.scratch)]
            waves += part.steps(p, ins[at[0] : ends[0]], outs[at[1] : ends[1]], scratch[at[2] : ends[2]])
            at = ends
        return waves


class SwapRows:
    names = ("swap",)

    def __init__(self, rows, at=0):
        self.args, self.specs, self.time = (rows,), (VM,), at
        self.shapes = (jax.ShapeDtypeStruct(rows.shape, rows.dtype),)
        self.scratch = (DMA((1,)), DMA((1,)), DMA((1,)))

    def steps(self, p, ins, outs, scratch):
        send, recv, local = (s.at[0] for s in scratch)
        away = p.c != p.z1
        move = remote(ins[0], outs[0], send, recv, p.peer["swap"])
        stay = pltpu.make_async_copy(ins[0], outs[0], local)

        def first():
            @pl.when(away)
            def _():
                move.start()

            @pl.when(jnp.logical_not(away))
            def _():
                stay.start()

        def last():
            @pl.when(away)
            def _():
                move.wait()

            @pl.when(jnp.logical_not(away))
            def _():
                stay.wait()

        return [(self.time, first), (99, last)]


class SpreadColumns:
    names = GROUP

    def __init__(self, *blocks):
        self.args, self.specs = blocks, (VM,) * len(blocks)
        self.shapes = tuple(jax.ShapeDtypeStruct((2, 2) + b.shape[1:], BF) for b in blocks)
        self.scratch = (DMA((3 * len(blocks),)), DMA((3 * len(blocks),)), DMA((len(blocks),)))

    def steps(self, p, ins, outs, scratch):
        send, recv, local = scratch
        made = []
        for k, (src, dst) in enumerate(zip(ins, outs)):
            sems = [s.at[pl.ds(3 * k, 3)] for s in (send, recv)]
            made.append(
                Spread(
                    p, lambda c, z0, s=src: s.at[2 * c + z0], lambda c, z0, d=dst: d.at[c, z0], *sems, local.at[k]
                )
            )

        def first():
            for m in made:
                m.start()

        def last():
            for m in made:
                m.wait()
                m.finish()

        return [(0, first), (99, last)]


class CollectColumns:
    names = GROUP

    def __init__(self, *blocks, at=0):
        self.time = at
        self.args, self.specs = blocks, (VM,) * len(blocks)
        self.shapes = tuple(jax.ShapeDtypeStruct((4,) + b.shape[2:], BF) for b in blocks)
        self.scratch = (DMA((3 * len(blocks),)), DMA((3 * len(blocks),)), DMA((len(blocks),)))

    def steps(self, p, ins, outs, scratch):
        send, recv, local = scratch
        made = []
        for k, (src, dst) in enumerate(zip(ins, outs)):
            sems = [s.at[pl.ds(3 * k, 3)] for s in (send, recv)]
            made.append(
                Spread(
                    p, lambda c, z0, s=src: s.at[c, z0], lambda c, z0, d=dst: d.at[2 * c + z0], *sems, local.at[k]
                )
            )

        def first():
            for m in made:
                m.start()

        def last():
            for m in made:
                m.wait()
                m.finish()

        return [(self.time, first), (99, last)]


class MeetBlocks:
    names = ("mid", "z0")

    def __init__(self, *blocks, at=(0, 1, 2)):
        self.args, self.specs, self.times = blocks, (VM,) * len(blocks), at
        self.shapes = tuple(jax.ShapeDtypeStruct(b.shape, BF) for b in blocks)
        self.scratch = tuple(pltpu.VMEM((2,) + b.shape, BF) for b in blocks)
        self.scratch += (DMA((8 * len(blocks),)), DMA((8 * len(blocks),)))

    def steps(self, p, ins, outs, scratch):
        relays, (send, recv) = scratch[:-2], scratch[-2:]
        acts = []
        for k, (src, dst, relay) in enumerate(zip(ins, outs, relays)):
            for h in (0, 1):
                sems = [s.at[pl.ds(8 * k + 4 * h, 4)] for s in (send, recv)]
                c = Cross(p, src.at[h], dst.at[h], dst.at[h], relay.at[:, h], *sems)
                acts += list(zip(self.times, (c.start, c.bring, c.take))) + [(99, c.wait), (99, c.finish)]
        return acts


class MeetOut:
    names = ("z0", "z1")

    def __init__(self, out, at=(0, 4)):
        self.args, self.specs, self.times = (out,), (VM,), at
        self.shapes = (jax.ShapeDtypeStruct((2, 2) + out.shape, BF),)
        self.scratch = (DMA((2,)), DMA((2,)), DMA((1,)))

    def steps(self, p, ins, outs, scratch):
        src, met = ins[0], outs[0]
        send, recv, local = scratch
        home = p.x == p.z0
        away = jnp.logical_not(home)
        pair = lambda half: remote(src, met.at[0, half], send.at[0], recv.at[0], p.peer["z0"])
        over = remote(met.at[0], met.at[1], send.at[1], recv.at[1], p.peer["z1"])
        own = pltpu.make_async_copy(src, met.at[0, p.z0], local.at[0])

        def first():
            pl.when(home)(own.start)
            pl.when(away)(lambda: pair(p.z0).start())

        def second():
            @pl.when(home)
            def _():
                own.wait()
                pair(1 - p.z0).wait_recv()
                over.start()

        def last():
            pl.when(home)(over.wait)
            pl.when(away)(lambda: pair(p.z0).wait_send())

        return [(self.times[0], first), (self.times[1], second), (99, last)]


class GatherOut:
    names = ("x", "y")

    def __init__(self, met, at=(0, 3)):
        self.args, self.specs, self.times = (met,), (VM,), at
        self.shapes = (jax.ShapeDtypeStruct((4,) + met.shape[1:], BF),)
        self.scratch = (DMA((4,)), DMA((4,)), DMA((2,)))

    def steps(self, p, ins, outs, scratch):
        met, ref = ins[0], outs[0]
        send, recv, local = scratch
        home = p.x == p.z0
        away = jnp.logical_not(home)
        at = lambda fy, k: ref.at[(1 - p.y if fy else p.y) * 2 + (1 - p.z1 if k else p.z1)]
        x_copy = lambda k: remote(met.at[k], at(0, k), send.at[k], recv.at[k], p.peer["x"])
        y_copy = lambda k, src, fy=0: remote(src, at(fy, k), send.at[2 + k], recv.at[2 + k], p.peer["y"])
        keep = lambda k: pltpu.make_async_copy(met.at[k], at(0, k), local.at[k])

        def first():
            @pl.when(home)
            def _():
                for k in (0, 1):
                    x_copy(k).start()
                    y_copy(k, met.at[k]).start()
                    keep(k).start()

        def second():
            @pl.when(away)
            def _():
                for k in (0, 1):
                    x_copy(k).wait_recv()
                    y_copy(k, at(0, k)).start()

        def last():
            for k in (0, 1):
                y_copy(k, at(1, k), 1).wait_recv()
                y_copy(k, at(0, k)).wait_send()

            @pl.when(home)
            def _():
                for k in (0, 1):
                    x_copy(k).wait_send()
                    keep(k).wait()

        return [(self.times[0], first), (self.times[1], second), (99, last)]


class GatherWeights:
    def __init__(
        self, columns=None, down=None, out=None, gains=None, columns_at=None, down_at=None, out_at=None, gains_at=None, met=None
    ):
        self.has = columns is not None, down is not None, out is not None, gains is not None
        self.spread = columns is not None and len(columns.shape) == 3
        self.times = columns_at, down_at, out_at, gains_at
        self.names = EIGHT + (("mid",) if met is None else ()) + ("z0",) + (GROUP if self.spread else ())
        self.met = met is not None
        self.args = tuple(a for a in (columns, down, out, gains) if a is not None) + tuple(met or ())
        self.specs = (VM,) * len(self.args)
        shapes, scratch = [], []
        sems = lambda n: [DMA((n,)), DMA((n,)), DMA((4,))]
        if columns is not None:
            block = (2,) + columns.shape[-2:]
            shapes.append((16,) + block)
            scratch += sems(22) + [pltpu.VMEM((2, 2) + block, BF)] + sems(3)
        if down is not None:
            shapes.append((16,) + down.shape[1:])
            scratch += sems(22) + [pltpu.VMEM((2, 2) + down.shape[1:], BF)]
        if out is not None:
            shapes.append((4, 2) + out.shape)
            scratch += sems(8)
        if gains is not None:
            shapes.append((32,) + gains.shape)
            scratch += sems(5)
        self.shapes = tuple(jax.ShapeDtypeStruct(s, BF) for s in shapes)
        self.scratch = tuple(scratch)

    def steps(self, p, ins, outs, scratch):
        ins, outs, scratch = list(ins), list(outs), list(scratch)
        take = lambda n: [scratch.pop(0) for _ in range(n)]
        acts = []
        met = [ins.pop() if self.met and has else None for has in self.has[1::-1]][::-1]
        if self.has[0]:
            src, ref = ins.pop(0), outs.pop(0)
            sems, s_sems, when = take(4), take(3), self.times[0]
            if self.spread:
                at = lambda c, z0, ref=ref: ref.at[columns_index(p.y, p.x, p.z1, c), z0]
                spread = Spread(p, lambda c, z0, src=src: src.at[2 * c + z0], at, *s_sems[:2], s_sems[2].at[0])
                acts += [(-1, spread.start), (when["start"], spread.wait), (99, spread.finish)]
                src = None
            acts += Gather(p, ref, columns_index, *sems, src, met[0]).steps(when)
        if self.has[1]:
            src, ref = ins.pop(0), outs.pop(0)
            acts += Gather(p, ref, rows_index, *take(4), src, met[1]).steps(self.times[1])
        if self.has[2]:
            acts += zip(self.times[2], out_gather_steps(p, ins.pop(0), outs.pop(0), *take(2), take(1)[0].at[0]))
        if self.has[3]:
            acts += zip(self.times[3], gains_gather(p, ins.pop(0), outs.pop(0), *take(2), take(1)[0].at[0]))
        return acts


class ReduceWeights:
    def __init__(self, columns, gains=None, collect=False, open=False, at=range(9)):
        self.gains = gains is not None
        self.collect, self.open, self.times = collect, open, tuple(at)
        self.names = EIGHT + ("mid", "z0") + (GROUP if collect else ())
        self.args = tuple(a for a in (columns, gains) if a is not None)
        self.specs = (ANY,) * len(self.args)
        shapes, scratch = [], []
        b = columns.shape[1:]
        shape = (4, b[0] // 2, b[1]) if collect else (2, 2) + b if open else (2,) + b
        shapes.append(jax.ShapeDtypeStruct(shape, BF))
        scratch += [pltpu.VMEM(n + b, BF) for n in ((2, 4), (2, 4), (2, 2), (2,))]
        scratch += [pltpu.VMEM((1, 1, 16, 128) if open else (2, 2) + b, BF), DMA((22,)), DMA((22,)), DMA((9,))]
        if collect:
            scratch += [DMA((3,)), DMA((3,)), DMA((1,))]
        if gains is not None:
            shapes.append(jax.ShapeDtypeStruct(gains.shape[1:], F32))
            scratch += [pltpu.VMEM(gains.shape, F32)]
            scratch += [pltpu.VMEM((16 >> k,) + gains.shape[1:], F32) for k in range(5)]
            scratch += [DMA((5,)), DMA((5,)), DMA((1,))]
        self.shapes, self.scratch = tuple(shapes), tuple(scratch)

    def steps(self, p, ins, outs, scratch):
        ins, outs, scratch = list(ins), list(outs), list(scratch)
        take = lambda n: [scratch.pop(0) for _ in range(n)]
        waves = [[] for _ in range(9)]
        part = functools.partial
        both = (0, 1)
        columns = Reduce(p, ins.pop(0), columns_index, outs.pop(0), *take(8))
        waves[0].append(columns.first)
        for m in range(4):
            waves[1 + m] += [part(columns.second, h, m) for h in both]
        for k in both:
            waves[5 + k] += [part(columns.third, h, k) for h in both]
        if self.collect:
            send, recv, local = take(3)
            rows = columns.three.shape[1] // 2
            piece = lambda c, z0: columns.three.at[c, pl.ds(pl.multiple_of(z0 * rows, rows), rows)]
            spread = Spread(p, piece, lambda c, z0: columns.result.at[2 * c + z0], send, recv, local.at[0])
            waves[7] += [c.bring for c in columns.cross] + [c.take for c in columns.cross]
            waves[8] += [part(columns.fourth, h) for h in both] + [spread.start, spread.wait, spread.finish]
        elif not self.open:
            waves[7] += [c.bring for c in columns.cross] + [c.take for c in columns.cross]
            waves[8] += [part(columns.fourth, h) for h in both]
        if not self.collect:
            waves[8] += [lambda: columns.store().start(), lambda: columns.store().wait()]
        waves[8].append(columns.finish)
        if self.gains:
            parts = take(9)
            steps = gains_reduce(p, ins.pop(0), outs.pop(0), parts[0], parts[1:6], *parts[6:])
            for k, act in zip((0, 2, 3, 4, 6, 8), steps):
                waves[k].append(act)
        return [(t, act) for t, wave in zip(self.times, waves) for act in wave]


class FinishColumns:
    def __init__(self, two, collect=False, at=(0, 1, 2, 99)):
        self.names = ("mid", "z0") + (GROUP if collect else ())
        self.collect, self.times = collect, at
        b = two.shape[2:]
        self.args, self.specs = (two,), (ANY,)
        self.shapes = (jax.ShapeDtypeStruct((4, b[0] // 2, b[1]) if collect else (2,) + b, BF),)
        self.scratch = (pltpu.VMEM((2,) + b, BF), pltpu.VMEM((2,) + b, BF), pltpu.VMEM((2, 2) + b, BF))
        self.scratch += (DMA((8,)), DMA((8,)), DMA((3,)), DMA((3,)), DMA((3,)), DMA((1,)))

    def steps(self, p, ins, outs, scratch):
        mine, three, relay, send, recv, local, s_send, s_recv, s_local = scratch
        two, result = ins[0], outs[0]
        crosses = [
            Cross(p, two.at[h, 0], three.at[h], three.at[h], relay.at[h], *[s.at[pl.ds(4 * h, 4)] for s in (send, recv)])
            for h in (0, 1)
        ]
        loads = [pltpu.make_async_copy(two.at[h, 1], mine.at[h], local.at[h]) for h in (0, 1)]
        rows = three.shape[1] // 2
        piece = lambda c, z0: three.at[c, pl.ds(pl.multiple_of(z0 * rows, rows), rows)]
        spread = Spread(p, piece, lambda c, z0: result.at[2 * c + z0], s_send, s_recv, s_local.at[0])
        store = lambda: pltpu.make_async_copy(three, result, local.at[2])

        def first():
            for c in crosses + loads:
                c.start()

        def last():
            for h in (0, 1):
                crosses[h].wait()
                loads[h].wait()
                add_to(three.at[h], mine.at[h])
            if self.collect:
                spread.start()
                spread.wait()
                spread.finish()
            else:
                store().start()
                store().wait()
            for c in crosses:
                c.finish()

        acts = [(self.times[0], first)]
        acts += [(self.times[1], c.bring) for c in crosses] + [(self.times[2], c.take) for c in crosses]
        return acts + [(self.times[3], last)]


LANES = 128
HEADS = Q_RANK + 2 * KV_RANK


def head_lanes():
    half = HEAD_SIZE // 2
    column = jnp.arange(HEADS * HEAD_SIZE, dtype=jnp.int32)
    head, inner = column // HEAD_SIZE, column % HEAD_SIZE
    lane = head * LANES + jnp.where(inner < half, inner, inner - half + LANES // 2)
    return (lane[:, None] == jnp.arange(HEADS * LANES, dtype=jnp.int32)[None, :]).astype(BF)


def pad_weights(lanes_ref, qkv_ref, out_ref, qkv_wide, out_wide):
    def qkv_tile(j):
        at = pl.ds(j, TILE)
        qkv_wide[at, :] = dot(qkv_ref[at, :], lanes_ref[...]).astype(BF)

    column_tiles(D, TILE, qkv_tile)
    heads = lanes_ref[: Q_RANK * HEAD_SIZE, : Q_RANK * LANES]

    def out_tile(j):
        cols = pl.ds(j, TILE)
        out_wide[:, cols] = dot(heads, out_ref[:, cols], ((0,), (0,))).astype(BF)

    column_tiles(D, TILE, out_tile)


def masked(scores, first, start_ref):
    count, keys = scores.shape
    query = lax.broadcasted_iota(jnp.int32, scores.shape, 0) + first
    key = lax.broadcasted_iota(jnp.int32, scores.shape, 1)
    start = start_ref[first : first + count, :]
    return jnp.where((key <= query) & (key >= start), scores, masked_score)


def attention_forward_call(residual, gain, w_qkv, w_out, common, beside, collective_id):
    lanes, cosines, sines, starts = common
    rows = residual.shape[0]
    count = 4 * rows
    scale = HEAD_SIZE ** (-0.5)

    def body(p, ins, outs, scratch, advance, staged):
        res_ref, gain_ref, qkv_ref, out_ref, lanes_ref, cos_ref, sin_ref, start_ref = ins
        new_ref, every, heads_ref, att_ref = outs
        qkv_wide, out_wide = scratch[:2]
        own, terms, share, total = exchange_of(p, every, scratch[2:])

        def project(pieces, n):
            places = token_rows(pieces, n, rows)
            both = lambda ref: jnp.concatenate([ref[at, :] for at in places], axis=0)
            cos, sin = both(cos_ref), both(sin_ref)
            x = gather_pieces(every, pieces, n)
            for j in range(0, HEADS, 4):
                wide = dot(x, qkv_wide[:, j * LANES : (j + 4) * LANES])
                for k in range(4):
                    value = wide[:, k * LANES : (k + 1) * LANES]
                    if j + k < Q_RANK + KV_RANK:
                        value = value * cos + pltpu.roll(value, LANES // 2, 1) * sin
                    for m, at in enumerate(places):
                        heads_ref[j + k, at, :] = value[m * n : (m + 1) * n].astype(BF)

        def attend(j, _):
            g = lax.div(j, Q_RANK // KV_RANK)
            for first in range(0, count, rows):
                n = first + rows
                q = heads_ref[j, first:n, :]
                scores = dot(q, heads_ref[Q_RANK + g, :n, :], ((1,), (1,))) * scale
                scores = masked(scores, first, start_ref)
                top = jnp.max(scores, axis=1, keepdims=True)
                shifted = jnp.exp(scores - top)
                amount = jnp.sum(shifted, axis=1, keepdims=True)
                weights = (shifted / amount).astype(BF)
                att_ref[j, first:n, :] = dot(weights, heads_ref[Q_RANK + KV_RANK + g, :n, :]).astype(BF)
            return 0

        def project_out(pieces, n):
            places = token_rows(pieces, n, rows)
            wide = jnp.concatenate(
                [jnp.concatenate([att_ref[j, at, :] for j in range(Q_RANK)], axis=1) for at in places], axis=0
            )

            def tile(j):
                cols = pl.ds(j, DOWN_TILE)
                scatter_pieces(terms, pieces, n, dot(wide, out_wide[:, cols]).astype(BF), cols)

            column_tiles(D, DOWN_TILE, tile)

        row_normalize(res_ref, gain_ref, own)
        share.start()
        advance()
        staged.ready(2, 3, 4)
        pad_weights(lanes_ref, qkv_ref, out_ref, qkv_wide, out_wide)
        staged.ready(5, 6)
        project([(p.rank, 0)], rows)
        share.across(True).wait_recv()
        project([(p.sibling, 0)], rows)
        advance()
        part = rows // CHUNKS
        for k in range(CHUNKS):
            share.pass_on(k)
            share.far(k)
            project([(p.diagonal, k * part), (p.over, k * part)], part)
            advance()
        staged.flush(1, 2)
        for j in range(0, Q_RANK, 2):
            lax.fori_loop(j, j + 2, attend, 0)
            advance()
        for k in range(CHUNKS):
            project_out([(p.diagonal, k * part), (p.over, k * part)], part)
            total.diagonal(k).start()
            total.relay(k)
            advance()
        staged.flush(3)
        project_out([(p.sibling, 0)], rows)
        total.sibling().start()
        project_out([(p.rank, 0)], rows)
        advance()

        def write(at, value):
            new_ref[at, :] = res_ref[at, :] + value

        collect(p, total, write)
        advance.finish()
        share.finish()
        total.finish()

    return beside_call(
        body,
        (residual, gain.reshape(1, D), w_qkv, w_out, lanes, cosines, sines, starts),
        (4, 2, 3, 5, 6),
        [
            jax.ShapeDtypeStruct((rows, D), F32),
            jax.ShapeDtypeStruct((4, rows, D), BF),
            jax.ShapeDtypeStruct((HEADS, count, LANES), BF),
            jax.ShapeDtypeStruct((Q_RANK, count, LANES), BF),
        ],
        (1, 2, 3),
        [pltpu.VMEM((D, HEADS * LANES), BF), pltpu.VMEM((Q_RANK * LANES, D), BF)] + exchange_scratch(rows),
        beside,
        "attention_forward",
        collective_id,
        2 * count * D * (HEADS + Q_RANK) * LANES,
    )


def attention_backward_call(grad, residual, gain, w_qkv, w_out, kept, common, beside, collective_id, dtype=F32):
    lanes, cosines, sines, starts = common
    every, heads, attended = kept
    rows = residual.shape[0]
    count = 4 * rows
    scale = HEAD_SIZE ** (-0.5)

    def body(p, ins, outs, scratch, advance, staged):
        (grad_ref, res_ref, gain_ref, qkv_ref, out_ref, lanes_ref, cos_ref, sin_ref, start_ref) = ins[:9]
        every_ref, heads_ref, att_ref = ins[9:]
        new_ref, gain_out, g_qkv, s_out = outs
        qkv_wide, out_wide, e, d_att, d_k, d_v, d_heads = scratch[:7]
        soft, g_out = scratch[7:9]
        reduce = out_reduce_steps(p, g_out, s_out, *scratch[9:16])
        own, terms, share, total = exchange_of(p, e, scratch[16:])

        def copy_own(k, _):
            at = pl.ds(pl.multiple_of(k * 32, 32), 32)
            own[at, :] = grad_ref[at, :].astype(BF)
            return 0

        lax.fori_loop(0, rows // 32, copy_own, 0)

        def back_out(pieces, n):
            wide = dot(gather_pieces(e, pieces, n), out_wide[...], ((1,), (1,)))
            for m, at in enumerate(token_rows(pieces, n, rows)):
                for j in range(Q_RANK):
                    d_att[j, at, :] = wide[m * n : (m + 1) * n, j * LANES : (j + 1) * LANES].astype(BF)

        def attend(j, _):
            g = lax.div(j, Q_RANK // KV_RANK)
            for first in range(0, count, rows):
                n = first + rows
                q, d_o = heads_ref[j, first:n, :], d_att[j, first:n, :]
                k, v = heads_ref[Q_RANK + g, :n, :], heads_ref[Q_RANK + KV_RANK + g, :n, :]
                rounded = soft[j, :, soft_lanes(first)]
                weights = rounded.astype(F32)
                d_weights = dot(d_o, v, ((1,), (1,)))
                inner = jnp.sum(weights * d_weights, axis=1, keepdims=True)
                d_scores = (weights * (d_weights - inner)).astype(BF)
                d_v[g, :n, :] += dot(rounded, d_o, ((0,), (0,)))
                d_k[g, :n, :] += dot(d_scores, q, ((0,), (0,)))
                d_q = dot(d_scores, k) * scale
                d_heads[j, first:n, :] = turn_back(d_q, cos_ref[first:n, :], sin_ref[first:n, :])
            return 0

        def soft_lanes(first):
            k = first // rows
            at = k * (k + 1) // 2 * rows
            return slice(at, at + first + rows)

        def keep_weights(j, _):
            g = lax.div(j, Q_RANK // KV_RANK)
            for first in range(0, count, rows):
                n = first + rows
                scores = dot(heads_ref[j, first:n, :], heads_ref[Q_RANK + g, :n, :], ((1,), (1,))) * scale
                scores = masked(scores, first, start_ref)
                shifted = jnp.exp(scores - jnp.max(scores, axis=1, keepdims=True))
                amount = jnp.sum(shifted, axis=1, keepdims=True)
                soft[j, :, soft_lanes(first)] = (shifted / amount).astype(BF)
            return 0

        def turn_back(value, cos, sin):
            return (value * cos - pltpu.roll(value, LANES // 2, 1) * sin).astype(BF)

        def keys_back():
            for g in range(KV_RANK):
                for first in range(0, count, rows):
                    at = slice(first, first + rows)
                    d_heads[Q_RANK + g, at, :] = turn_back(d_k[g, at, :] * scale, cos_ref[at, :], sin_ref[at, :])
                    d_heads[Q_RANK + KV_RANK + g, at, :] = d_v[g, at, :].astype(BF)

        def project_back(pieces, n):
            wide = jnp.concatenate(
                [
                    jnp.concatenate([d_heads[j, at, :] for j in range(HEADS)], axis=1)
                    for at in token_rows(pieces, n, rows)
                ],
                axis=0,
            )

            def tile(j):
                cols = pl.ds(j, DOWN_TILE)
                value = dot(wide, qkv_wide[cols, :], ((1,), (1,))).astype(BF)
                scatter_pieces(terms, pieces, n, value, cols)

            column_tiles(D, DOWN_TILE, tile)

        def out_grads():
            e_all = e.reshape(count, D)

            def out_grad(j):
                cols = pl.ds(j, TILE)
                heads = jnp.concatenate([att_ref[h] for h in range(Q_RANK)], axis=1)
                wide = dot(heads, e_all[:, cols], ((0,), (0,))).astype(BF)
                value = dot(lanes_ref[: Q_RANK * HEAD_SIZE, : Q_RANK * LANES], wide).astype(BF)
                for h in range(Q_RANK):
                    g_out[h, :, cols] = value[h * HEAD_SIZE : (h + 1) * HEAD_SIZE]

            column_tiles(D, TILE, out_grad)

        def weight_grads():
            x_all = every_ref.reshape(count, D)

            def qkv_grad(j):
                cols = pl.ds(j, TILE)
                wide = jnp.concatenate(
                    [
                        dot(x_all[:, cols], jnp.concatenate([d_heads[h], d_heads[h + 1]], axis=1), ((0,), (0,)))
                        for h in range(0, HEADS, 2)
                    ],
                    axis=1,
                ).astype(BF)
                g_qkv[cols, :] = dot(wide, lanes_ref[...], ((1,), (1,))).astype(BF)

            column_tiles(D, TILE, qkv_grad)

        share.start()
        advance()
        staged.ready(3, 4, 5)
        pad_weights(lanes_ref, qkv_ref, out_ref, qkv_wide, out_wide)
        staged.ready(10)
        lax.fori_loop(0, Q_RANK, keep_weights, 0)
        d_k[...] = jnp.zeros_like(d_k)
        d_v[...] = jnp.zeros_like(d_v)
        back_out([(p.rank, 0)], rows)
        share.across(True).wait_recv()
        back_out([(p.sibling, 0)], rows)
        advance()
        part = rows // CHUNKS
        for k in range(CHUNKS):
            share.pass_on(k)
            share.far(k)
            back_out([(p.diagonal, k * part), (p.over, k * part)], part)
            advance()
        staged.ready(11)
        out_grads()
        reduce[0]()
        staged.ready(6, 7)
        for j in range(0, Q_RANK, 2):
            lax.fori_loop(j, j + 2, attend, 0)
            advance()
        reduce[1]()
        keys_back()
        for k in range(CHUNKS):
            project_back([(p.diagonal, k * part), (p.over, k * part)], part)
            total.diagonal(k).start()
            total.relay(k)
            advance()
        project_back([(p.sibling, 0)], rows)
        total.sibling().start()
        project_back([(p.rank, 0)], rows)
        advance()
        reduce[2]()
        staged.ready(9)
        weight_grads()
        staged.flush(2)
        reduce[3]()
        advance()
        gain_out[...] = jnp.zeros_like(gain_out)

        def write(at, value):
            res = res_ref[at, :].astype(F32)
            normed = normalize(res)
            gain_out[...] += jnp.sum(value * normed, axis=0, keepdims=True)
            back = norm_back(value * gain_ref[...], normed, res)
            new_ref[at, :] = (grad_ref[at, :] + back).astype(dtype)

        collect(p, total, write)
        advance.finish()
        reduce[4]()
        share.finish()
        total.finish()

    return beside_call(
        body,
        (grad, residual, gain.reshape(1, D), w_qkv, w_out, lanes, cosines, sines, starts, every, heads, attended),
        (5, 3, 4, 10, 11, 6, 7, 9),
        [
            jax.ShapeDtypeStruct((rows, D), dtype),
            jax.ShapeDtypeStruct((1, D), F32),
            jax.ShapeDtypeStruct((D, HEADS * HEAD_SIZE), BF),
            jax.ShapeDtypeStruct((HEAD_SIZE // 2, D), BF),
        ],
        (2,),
        [
            pltpu.VMEM((D, HEADS * LANES), BF),
            pltpu.VMEM((Q_RANK * LANES, D), BF),
            pltpu.VMEM((4, rows, D), BF),
            pltpu.VMEM((Q_RANK, count, LANES), BF),
            pltpu.VMEM((KV_RANK, count, LANES), F32),
            pltpu.VMEM((KV_RANK, count, LANES), F32),
            pltpu.VMEM((HEADS, count, LANES), BF),
            pltpu.VMEM((Q_RANK, rows, 10 * rows), BF),
        ]
        + out_reduce_scratch((HEAD_SIZE, D))
        + exchange_scratch(rows),
        beside,
        "attention_backward",
        collective_id,
        6 * count * D * (HEADS + Q_RANK) * LANES,
        ("c", "z0", "x", "y", "z1"),
        {3: ANY},
    )


def lane_rows():
    half, space = HEAD_SIZE // 2, LANES // 2 - HEAD_SIZE // 2
    index = jnp.arange(half, dtype=jnp.float32)
    inverse = jnp.pad(rope_base ** (-2.0 * index / HEAD_SIZE), (0, space))
    ones = jnp.pad(jnp.ones(half, F32), (0, space))
    row = lambda a, b: jnp.concatenate([a, b])
    return jnp.stack([row(inverse, inverse), row(ones, ones), row(-ones, ones)])


def rank_columns(ref, l, c, x):
    pieces = []
    for start, width in (
        (0, 2 * HEAD_SIZE),
        (QUERY_HEAD_COUNT * HEAD_SIZE, HEAD_SIZE),
        ((QUERY_HEAD_COUNT + KEY_VALUE_HEADS) * HEAD_SIZE, HEAD_SIZE),
    ):
        for y in (0, 1):
            at = start + (4 * y + 2 * x + c) * width
            pieces.append(ref[l][:, at : at + width])
    return jnp.concatenate(pieces, axis=1).astype(BF)


def first_call(tokens, lengths, w_qkv, w_out, w_gateup, w_down, gains, collective_id):
    rows = w_qkv.shape[1]
    count = 4 * tokens.shape[0]
    ranks = lambda w: jax.ShapeDtypeStruct((4, rows, w.shape[2] // 4), BF)
    shard = jax.ShapeDtypeStruct(w_out.shape[1:], BF)
    down_rows = w_down.shape[1] // 2
    half = jax.ShapeDtypeStruct((2, down_rows, D), BF)
    gather = GatherWeights(
        columns=ranks(w_qkv), out=shard, gains=gains, columns_at=times(1, (2, 2), (2, 2), 3, (4, 4), (6, 6)),
        out_at=(-1, 1, 3, 5, 99), gains_at=(1, 2, 3, 4, 5, 99),
    )
    meet = MeetBlocks(half, at=(0, 1, 1))
    spread = SpreadColumns(ranks(w_gateup), ranks(w_qkv), ranks(w_gateup))
    swap = SwapRows(tokens)
    works = (gather, spread, swap, meet)
    unit = w_gateup.shape[2] // 64

    def body(*refs):
        refs = list(refs)
        take = lambda n: [refs.pop(0) for _ in range(n)]
        tokens_ref, lengths_ref, qkv_ref, out_ref, gu_ref, down_ref, gains_ref, lanes_ref = take(8)
        down0, down1, out1, cos_ref, sin_ref, start_ref = take(6)
        outs = [take(len(w.shapes)) for w in works]
        qkv0, qkv1, gu0, gu1, out0 = take(5)
        scratch = [take(len(w.scratch)) for w in works]
        p = Place()
        greet(p, EIGHT + GROUP + ("swap", "mid"))
        clock = Clock(gather.steps(p, [qkv0, out0, gains_ref], outs[0], scratch[0]))

        def pack_heads(l, dst):
            for c in (0, 1):
                for x in (0, 1):
                    dst[2 * c + x] = rank_columns(qkv_ref, l, c, x)

        def pack_units(l, dst):
            for chunk in range(64):
                z0, z1, c, rest = chunk % 2, chunk // 2 % 2, chunk // 4 % 2, chunk // 8
                at = (rest * 2 + z1) * unit
                dst[2 * c + z0, :, at : at + unit] = gu_ref[l, :, chunk * unit : (chunk + 1) * unit].astype(BF)

        pack_heads(0, qkv0)
        out0[...] = out_ref[0].astype(BF)
        clock()
        clock()
        for h in (0, 1):
            part = slice(h * down_rows, (h + 1) * down_rows)
            down0[h] = down_ref[0, part, :].astype(BF)
            down1[h] = down_ref[1, part, :].astype(BF)
        out1[...] = out_ref[1].astype(BF)
        pack_units(0, gu0)
        pack_heads(1, qkv1)
        pack_units(1, gu1)
        clock()
        later = Clock(
            meet.steps(p, [down0], outs[3], scratch[3])
            + spread.steps(p, [gu0, qkv1, gu1], outs[1], scratch[1])
            + swap.steps(p, [tokens_ref], outs[2], scratch[2])
        )
        later()

        def begin(places):
            start, end = jnp.zeros_like(places), 0
            for k in range(lengths.shape[1]):
                length = lengths_ref[0, k]
                end = end + length
                start = start + jnp.where(places >= end, length, 0)
            return start

        def table(k, _):
            at = pl.ds(pl.multiple_of(k * TILE, TILE), TILE)
            places = lax.broadcasted_iota(jnp.int32, (TILE, LANES), 0) + k * TILE
            angles = (places - begin(places)).astype(F32) * lanes_ref[0:1, :]
            cos_ref[at, :] = jnp.cos(angles) * lanes_ref[1:2, :]
            sin_ref[at, :] = jnp.sin(angles) * lanes_ref[2:3, :]
            start_ref[at, :] = begin(lax.broadcasted_iota(jnp.int32, (TILE, 1), 0) + k * TILE)
            return 0

        lax.fori_loop(0, count // TILE, table, 0)
        later()
        clock.finish()
        later.finish()

    vmem = lambda s: pltpu.VMEM(s.shape, BF)
    made = [half, half, shard, *([jax.ShapeDtypeStruct((count, LANES), F32)] * 2), jax.ShapeDtypeStruct((count, 1), jnp.int32)]
    out = pl.pallas_call(
        body,
        out_shape=made + [s for w in works for s in w.shapes],
        in_specs=[VM, pl.BlockSpec(memory_space=pltpu.SMEM)] + [VM] * 6,
        out_specs=[VM] * len(made) + [ANY for w in works for _ in w.shapes],
        scratch_shapes=[vmem(ranks(w_qkv)), vmem(ranks(w_qkv)), vmem(ranks(w_gateup)), vmem(ranks(w_gateup)), vmem(shard)]
        + [s for w in works for s in w.scratch],
        compiler_params=wide_params(collective_id),
        name="first_weights",
    )(tokens, lengths, w_qkv, w_out, w_gateup, w_down, gains, lane_rows())
    return out


def stepped(weight, gradient, first, second, rate, shrink):
    return adam_step(weight, gradient.astype(F32), first, second, rate, shrink)


def update_gateup(weight, first, second, parts, rate, shrink):
    rows, columns = weight.shape[1:]
    blocks = 8
    wide, thin = columns // blocks, columns // 4 // blocks
    unit = thin // 2

    def body(w_ref, m_ref, v_ref, *refs):
        grads, (w_out, m_out, v_out) = refs[:-3], refs[-3:]

        def run(g_ref):
            for c in (0, 1):
                for z1 in (0, 1):
                    for z0 in (0, 1):
                        at = pl.ds(((c * 2 + z1) * 2 + z0) * unit, unit)
                        grad = g_ref[2 * c + z0, :, pl.ds(z1 * unit, unit)]
                        new = stepped(w_ref[0, :, at], grad, m_ref[0, :, at], v_ref[0, :, at], rate, shrink)
                        w_out[0, :, at], m_out[0, :, at], v_out[0, :, at] = new

        for l, g_ref in enumerate(grads):
            pl.when(pl.program_id(0) == l)(functools.partial(run, g_ref))

    big = pl.BlockSpec((1, rows, wide), lambda l, j: (l, 0, j))
    small = [
        pl.BlockSpec((4, rows, thin), lambda l, j, k=k: (0, 0, jnp.where(l == k, j, 0 if k else blocks - 1)))
        for k in range(LAYERS)
    ]
    return pl.pallas_call(
        body,
        grid=(LAYERS, blocks),
        in_specs=[big] * 3 + small,
        out_specs=[big] * 3,
        out_shape=[jax.ShapeDtypeStruct(weight.shape, F32)] * 3,
        compiler_params=pltpu.CompilerParams(vmem_limit_bytes=32 * 2**20),
        name="update_gateup",
    )(weight, first, second, *parts)


def update_rows(weight, first, second, parts, rate, shrink):
    rows, columns = weight.shape[1:]
    blocks = 2
    wide = columns // blocks

    def body(w_ref, m_ref, v_ref, *refs):
        grads, (w_out, m_out, v_out) = refs[:-3], refs[-3:]

        def run(g_ref):
            w_out[0], m_out[0], v_out[0] = stepped(w_ref[0], g_ref[...], m_ref[0], v_ref[0], rate, shrink)

        for l, g_ref in enumerate(grads):
            pl.when(pl.program_id(0) == l)(functools.partial(run, g_ref))

    big = pl.BlockSpec((1, rows, wide), lambda l, j: (l, 0, j))
    small = [
        pl.BlockSpec((rows, wide), lambda l, j, k=k: (0, jnp.where(l == k, j, 0 if k else blocks - 1)))
        for k in range(LAYERS)
    ]
    return pl.pallas_call(
        body,
        grid=(LAYERS, blocks),
        in_specs=[big] * 3 + small,
        out_specs=[big] * 3,
        out_shape=[jax.ShapeDtypeStruct(weight.shape, F32)] * 3,
        compiler_params=pltpu.CompilerParams(vmem_limit_bytes=32 * 2**20),
        name="update_rows",
    )(weight, first, second, *parts)


def update_qkv(weight, first, second, parts, rate, shrink):
    rows, columns = weight.shape[1:]
    q_wide, kv_wide = QUERY_HEAD_COUNT * HEAD_SIZE, KEY_VALUE_HEADS * HEAD_SIZE

    def body(w_ref, m_ref, v_ref, *refs):
        grads, (w_out, m_out, v_out) = refs[:-3], refs[-3:]

        def run(g_ref):
            pieces = []
            for start, width in ((0, 2 * HEAD_SIZE), (4 * HEAD_SIZE, HEAD_SIZE), (6 * HEAD_SIZE, HEAD_SIZE)):
                for y in (0, 1):
                    for x in (0, 1):
                        for c in (0, 1):
                            at = start + y * width
                            pieces.append(g_ref[2 * c + x].astype(F32)[:, at : at + width])
            grad = jnp.concatenate(pieces, axis=1)
            w_out[0], m_out[0], v_out[0] = stepped(w_ref[0], grad, m_ref[0], v_ref[0], rate, shrink)

        for l, g_ref in enumerate(grads):
            pl.when(pl.program_id(0) == l)(functools.partial(run, g_ref))

    big = pl.BlockSpec((1, rows, columns), lambda l: (l, 0, 0))
    small = [pl.BlockSpec((4, rows, columns // 4), lambda l: (0, 0, 0))] * LAYERS
    return pl.pallas_call(
        body,
        grid=(LAYERS,),
        in_specs=[big] * 3 + small,
        out_specs=[big] * 3,
        out_shape=[jax.ShapeDtypeStruct(weight.shape, F32)] * 3,
        compiler_params=pltpu.CompilerParams(vmem_limit_bytes=32 * 2**20),
        name="update_qkv",
    )(weight, first, second, *parts)


def links_call(beside, name, collective_id):
    return beside_call(
        lambda p, ins, outs, scratch, advance, staged: advance.finish(),
        (), (), [], (), [], beside, name, collective_id, 0, peers=(),
    )[1]


def fast_shards(
    tokens, cotangent, lengths, w_qkv, w_out, w_gateup, w_down, norm_gains, *moments
):
    axes = ("fsdp", "seq")
    pairs = swap_pairs(lax.axis_size("fsdp"), lax.axis_size("seq"))
    lengths = lax.ppermute(lengths, axes, pairs)
    rows, owned = w_qkv.shape[1], norm_gains.shape[2]
    own_gains = jnp.pad(
        norm_gains.reshape(2 * LAYERS, owned).astype(BF), ((0, 16 - 2 * LAYERS), (0, lane_width - owned))
    )
    own_down0, own_down1, own_out1, *places, qkv0, out0, got_gains, own_gu0, own_qkv1, own_gu1, start, met_down0 = (
        first_call(tokens, lengths, w_qkv, w_out, w_gateup, w_down, own_gains, 0)
    )
    common = (head_lanes(), *places)
    all_gains = got_gains[:, : 2 * LAYERS, :owned].transpose(1, 0, 2).reshape(LAYERS, 2, D).astype(F32)
    matrix = lambda g: g.reshape(D, -1)
    stack = lambda g: g.reshape(-1, D)
    alone = times(0, (1, 1), (3, 4), 3, (4, 5), (7, 8))
    ahead = times(0, None, None, 3, None, (4, 4))
    (middle0, *first0), (gu0, down0, met_qkv1, met_down1, met_out1) = attention_forward_call(
        start, all_gains[0, 0], matrix(qkv0), stack(out0), common,
        Both(
            GatherWeights(columns=own_gu0, columns_at=alone),
            GatherWeights(down=own_down0, met=(met_down0,), down_at=times(0, None, None, 3, None, (5, 5))),
            MeetBlocks(own_qkv1, own_down1, at=(0, 4, 6)),
            MeetOut(own_out1, at=(0, 5)),
        ), 1,
    )
    (later0, *second0), (out1, qkv1, down1, met_gu1) = feed_forward_call(
        middle0, all_gains[0, 1], matrix(gu0), stack(down0),
        Both(
            GatherOut(met_out1),
            GatherWeights(columns=own_qkv1, met=(met_qkv1,), columns_at=ahead),
            GatherWeights(down=own_down1, met=(met_down1,), down_at=ahead),
            MeetBlocks(own_gu1, at=(0, 3, 4)),
        ), 2,
    )
    (middle1, *first1), (gu1, cotangent) = attention_forward_call(
        later0, all_gains[1, 0], matrix(qkv1), stack(out1), common,
        Both(
            GatherWeights(columns=own_gu1, met=(met_gu1,), columns_at=times(0, None, None, 3, None, (6, 7))),
            SwapRows(cotangent, 3),
        ), 3,
    )
    (later1, *second1), _ = feed_forward_call(
        middle1, all_gains[1, 1], matrix(gu1), stack(down1), Nothing(), 4, BF
    )
    wide = lambda g: g.reshape(16, 2 * rows, -1)
    (grad, gain11, g_gu1, two_down1), _ = feed_backward_call(
        cotangent, middle1, all_gains[1, 1], matrix(gu1), stack(down1), second1, Nothing(), 5
    )
    (grad, gain10, g_qkv1, s_out1), (two_gu1, s_down1, layer_output) = attention_backward_call(
        grad, later0, all_gains[1, 0], matrix(qkv1), stack(out1), first1, common,
        Both(
            ReduceWeights(columns=wide(g_gu1), open=True, at=(0, 4, 4, 5, 5, 9, 10, 11, 99)),
            FinishColumns(two_down1, at=(1, 3, 4, 6)),
            SwapRows(later1, 4),
        ), 6,
    )
    (grad, gain01, g_gu0, two_down0), (s_qkv1,) = feed_backward_call(
        grad, middle0, all_gains[0, 1], matrix(gu0), stack(down0), second0,
        ReduceWeights(columns=wide(g_qkv1), at=(0, 2, 2, 3, 3, 4, 4, 7, 99)), 7,
    )
    (grad, gain00, g_qkv0, s_out0), (two_gu0, s_down0, s_gu1) = attention_backward_call(
        grad, start, all_gains[0, 0], matrix(qkv0), stack(out0), first0, common,
        Both(
            ReduceWeights(columns=wide(g_gu0), open=True, at=(0, 4, 4, 5, 5, 9, 10, 11, 99)),
            FinishColumns(two_down0, at=(1, 3, 4, 6)),
            FinishColumns(two_gu1, at=(2, 4, 5, 9)),
        ), 8, BF,
    )
    terms = jnp.concatenate([gain00, gain01, gain10, gain11]).reshape(2 * LAYERS, -1, owned).transpose(1, 0, 2)
    terms = jnp.pad(terms, ((0, 0), (0, 8 - 2 * LAYERS), (0, lane_width - owned)))
    split = lambda g: g.reshape(2, 2, rows, -1)
    s_gu0, s_qkv0, s_gains, s_gu1, s_qkv1, input_grad = links_call(
        Both(
            FinishColumns(two_gu0, collect=True, at=(0, 1, 1, 4)),
            ReduceWeights(columns=wide(g_qkv0), gains=terms, collect=True, at=(0, 2, 2, 3, 3, 3, 3, 5, 7)),
            CollectColumns(split(s_gu1), split(s_qkv1), at=1),
            SwapRows(grad, 2),
        ),
        "last_gradients",
        9,
    )
    flat = lambda g: g.reshape(-1, D)
    update = {
        "qkv": (s_qkv0, s_qkv1),
        "out": (s_out0, s_out1),
        "gateup": (s_gu0, s_gu1),
        "down": (flat(s_down0), flat(s_down1)),
        "gains": s_gains[: 2 * LAYERS, :owned].reshape(LAYERS, 2, owned),
    }
    return (layer_output, input_grad.astype(F32)) + update_all(
        (w_qkv, w_out, w_gateup, w_down, norm_gains), moments, update
    )


def update_all(stacked, moments, update):
    step_rates = (D ** (-0.5), 4.0 * D ** (-0.5), D ** (-0.5), FF ** (-0.5), 0.5)
    shrinks = (decay_rate, decay_rate, decay_rate, decay_rate, 0.0)
    ways = (update_qkv, update_rows, update_gateup, update_rows, adam_step)
    results = []
    for kind, (name, way) in enumerate(zip(update, ways)):
        weight, first, second = stacked[kind], moments[kind], moments[5 + kind]
        if kind == 4:
            results.append(way(weight, update[name], first, second, step_rates[kind], shrinks[kind]))
        else:
            results.append(way(weight, first, second, update[name], step_rates[kind], shrinks[kind]))
    return tuple(results[kind][part] for part in range(3) for kind in range(5))


def solution(mesh):
    in_specs = (
        P(("fsdp", "seq"), None),
        P(("fsdp", "seq"), None),
        P("fsdp", None),
        P(None, ("fsdp", "seq"), None),
        P(None, ("fsdp", "seq"), None),
        P(None, ("fsdp", "seq"), None),
        P(None, ("fsdp", "seq"), None),
        P(None, None, ("fsdp", "seq")),
        P(None, ("fsdp", "seq"), None),
        P(None, ("fsdp", "seq"), None),
        P(None, ("fsdp", "seq"), None),
        P(None, ("fsdp", "seq"), None),
        P(None, None, ("fsdp", "seq")),
        P(None, ("fsdp", "seq"), None),
        P(None, ("fsdp", "seq"), None),
        P(None, ("fsdp", "seq"), None),
        P(None, ("fsdp", "seq"), None),
        P(None, None, ("fsdp", "seq")),
    )
    out_specs = (
        P(("fsdp", "seq"), None),
        P(("fsdp", "seq"), None),
        P(None, ("fsdp", "seq"), None),
        P(None, ("fsdp", "seq"), None),
        P(None, ("fsdp", "seq"), None),
        P(None, ("fsdp", "seq"), None),
        P(None, None, ("fsdp", "seq")),
        P(None, ("fsdp", "seq"), None),
        P(None, ("fsdp", "seq"), None),
        P(None, ("fsdp", "seq"), None),
        P(None, ("fsdp", "seq"), None),
        P(None, None, ("fsdp", "seq")),
        P(None, ("fsdp", "seq"), None),
        P(None, ("fsdp", "seq"), None),
        P(None, ("fsdp", "seq"), None),
        P(None, ("fsdp", "seq"), None),
        P(None, None, ("fsdp", "seq")),
    )
    whole_tiles = (D // mesh.size) % 16 == 0 and mesh.shape["seq"] == 4 and mesh.size == 32
    body = fast_shards if whole_tiles else shards
    return jax.shard_map(body, mesh=mesh, in_specs=in_specs, out_specs=out_specs, check_vma=False)
```
